32 devices in a mesh: dp: 4 (over y, core), fsdp: 8 (over z, x).
Axes of the slice: x: 2, y: 2, z: 4, core: 2. Of those that a mesh axis runs over, the one named last changes fastest.
Arguments:
- decoder_in: bfloat16 [16384, 768], P(('dp', 'fsdp')), may hold values from -6 to 6
- encoder_out: bfloat16 [256, 512, 768], P(('dp', 'fsdp')), may hold values from -6 to 6
- decoder_lengths: int32 [32, 8], P(('dp', 'fsdp')), may hold values from 1 to 128, 512 in all within a row
- encoder_lengths: int32 [256], P(('dp', 'fsdp')), may hold values from 1 to 512, as said below
- norm_gains: float32 [3, 768], P(None, 'fsdp'), may hold values from 0.25 to 1.75
- rel_table: float32 [32, 12], P('dp'), may hold values from -4 to 4
- query_self: float32 [768, 768], P('dp', 'fsdp'), may hold values from -0.109375 to 0.109375
- key_self: float32 [768, 768], P('dp', 'fsdp'), may hold values from -0.109375 to 0.109375
- value_self: float32 [768, 768], P('dp', 'fsdp'), may hold values from -0.21875 to 0.21875
- out_self: float32 [768, 768], P('dp', 'fsdp'), may hold values from -0.4375 to 0.4375
- query_cross: float32 [768, 768], P('dp', 'fsdp'), may hold values from -0.109375 to 0.109375
- key_cross: float32 [768, 768], P('dp', 'fsdp'), may hold values from -0.109375 to 0.109375
- value_cross: float32 [768, 768], P('dp', 'fsdp'), may hold values from -0.21875 to 0.21875
- out_cross: float32 [768, 768], P('dp', 'fsdp'), may hold values from -0.4375 to 0.4375
- feed_in: float32 [768, 3072], P('dp', 'fsdp'), may hold values from -0.21875 to 0.21875
- feed_out: float32 [3072, 768], P('dp', 'fsdp'), may hold values from -0.21875 to 0.21875
- upstream: bfloat16 [16384, 768], P(('dp', 'fsdp')), may hold values from -12 to 12
Outputs:
- decoder_out: bfloat16 [16384, 768], P(('dp', 'fsdp'))
- decoder_gradient: bfloat16 [16384, 768], P(('dp', 'fsdp'))
- encoder_gradient: bfloat16 [256, 512, 768], P(('dp', 'fsdp'))
- gains_gradient: float32 [3, 768], P(None, 'fsdp')
- table_gradient: float32 [32, 12], P('dp')
- query_self_gradient: float32 [768, 768], P('dp', 'fsdp')
- key_self_gradient: float32 [768, 768], P('dp', 'fsdp')
- value_self_gradient: float32 [768, 768], P('dp', 'fsdp')
- out_self_gradient: float32 [768, 768], P('dp', 'fsdp')
- query_cross_gradient: float32 [768, 768], P('dp', 'fsdp')
- key_cross_gradient: float32 [768, 768], P('dp', 'fsdp')
- value_cross_gradient: float32 [768, 768], P('dp', 'fsdp')
- out_cross_gradient: float32 [768, 768], P('dp', 'fsdp')
- feed_in_gradient: float32 [768, 3072], P('dp', 'fsdp')
- feed_out_gradient: float32 [3072, 768], P('dp', 'fsdp')
The draws below stay inside these ranges and needn't reach their ends.
Inputs may be any that keep to these rules, and one draw needn't show every extreme that they name: `decoder_lengths`: in each row the 8 lengths sum to 512. `encoder_lengths`: in every row one of its 8 examples has all 512 encoder positions valid.
All inputs are finite; a program needn't handle non-finite values.
Results may differ from the reference program's by a relative error of at most 0.025.
The reference program's roundings to bfloat16 on the way count: a program that leaves them out, or rounds other values in their place, can miss the bound.
Values may be sent and summed in bfloat16 or wider, within the bound.
A program may use at most 512 MiB of HBM per device.

```python
import math
import jax
import jax.numpy as jnp
import numpy as np
from jax import lax

D = 768
HEADS = 12
HEAD_DIM = 64
FF = 3072
BUCKETS = 32
MAX_DIST = 128
INNER = 768
ROW = 512
EX_ROW = 8
ENC = 512
MOST = 128
ROWS = 32
TOKENS = 16384
EXAMPLES = 256


def draw_encoder_lengths(key, part):
    key = jax.random.fold_in(key, 11)
    key_lengths, key_full = jax.random.split(key)
    lengths_drawn = jax.random.randint(key_lengths, (ROWS, EX_ROW), 1, ENC + 1)
    full_at = jax.random.randint(key_full, (ROWS, 1), 0, EX_ROW)
    columns = jnp.arange(EX_ROW, dtype=jnp.int32)[None, :]
    return jnp.where(columns == full_at, ENC, lengths_drawn).reshape(ROWS * EX_ROW).astype(jnp.int32)


def spiked(values, key, source, target, shards_of, factor):
    def block_of(axis_at):
        return (jnp.arange(values.shape[axis_at]) // (values.shape[axis_at] // shards_of)).reshape((-1,) + (1,) * (values.ndim - 1 - axis_at))

    near = jax.random.permutation(key, shards_of)[block_of(target)]
    far = (block_of(target) + shards_of // 2) % shards_of
    return jnp.where((block_of(source) == near) | (block_of(source) == far), factor * values, values)


def block_levels(key, dims, cuts, low, largest):
    def one(position, shards_of):
        draws = jax.random.uniform(jax.random.fold_in(jax.random.fold_in(key, 6), position), (shards_of,), jnp.float32, low / len(cuts), largest / len(cuts))
        return jnp.repeat(jnp.exp(draws), dims[position] // shards_of).reshape((-1,) + (1,) * (len(dims) - position - 1))

    gain = one(*cuts[0])
    for cut in cuts[1:]:
        gain = gain * one(*cut)
    return gain


def length_profile(number_of, total, most, slope):
    portions = [(1 << 20) // math.isqrt(standing ** slope) + 1 for standing in range(2, number_of + 1)]
    surplus, holding = total - most - (number_of - 1), [1] * (number_of - 1)
    while surplus > 0:
        candidates = [i for i in range(number_of - 1) if holding[i] < most]
        mass, left = sum([portions[i] for i in candidates]), surplus
        for i in candidates:
            extra = min(most - holding[i], max(1, left * portions[i] // mass), surplus)
            holding[i] = holding[i] + extra
            surplus = surplus - extra
    return np.array([most] + holding)


def uneven(stream_key, number_of, total, reach, skew):
    if number_of == 2:
        one = jax.random.randint(stream_key, (), max(1, total - reach), min(reach, total - 1) + 1)
        return jnp.stack([one, total - one])
    sizes = jnp.asarray(length_profile(number_of, total, reach, skew), jnp.int32)
    twos = (number_of - 1) // 2
    source_of, receiver = sizes[1:1 + 2 * twos:2], sizes[2:2 + 2 * twos:2]
    margin = jnp.minimum(source_of - 1, reach - receiver)
    moved = jax.random.randint(jax.random.fold_in(stream_key, 1), (twos,), 0, 1 << 20) % (margin + 1)
    sizes = sizes.at[1:1 + 2 * twos:2].set(source_of - moved).at[2:2 + 2 * twos:2].set(receiver + moved)
    return sizes[jax.random.permutation(jax.random.fold_in(stream_key, 2), number_of)]


def gaussian(key, dims, width, reach, cuts=(), kind=jnp.bfloat16):
    array = width * jax.random.normal(key, dims, jnp.float32)
    if cuts:
        array = array * block_levels(key, dims, cuts, -0.22, 0.18)
    return jnp.clip(array, -reach, reach).astype(kind)


def bell_draw_with(key, shape, spread, limit, shards, heavy, kind=jnp.bfloat16):
    drawn = spread * jax.random.normal(key, shape, jnp.float32)
    if shards:
        drawn = drawn * block_levels(key, shape, shards, -0.22, 0.18)
    return jnp.clip(spiked(drawn, jax.random.fold_in(key, 3), *heavy), -limit, limit).astype(kind)


def setup_inputs(seed: int = 0) -> dict:
    seeds = jax.random.split(jax.random.key(seed), 18)
    return {
        "decoder_in": gaussian(seeds[0], (TOKENS, D), 1.0, 6.0, ((0, 32),)),
        "encoder_out": gaussian(seeds[1], (EXAMPLES, ENC, D), 1.0, 6.0, ((0, 32),)),
        "decoder_lengths": jax.vmap(lambda own: uneven(own, EX_ROW, ROW, MOST, 1))(jax.random.split(seeds[2], ROWS)).reshape((ROWS, EX_ROW)).astype(jnp.int32),
        "encoder_lengths": draw_encoder_lengths(jax.random.fold_in(seeds[17], 71), 0),
        "norm_gains": jnp.clip(1.0 + 0.15 * jax.random.normal(seeds[4], (3, D), jnp.float32), 0.25, 1.75),
        "rel_table": gaussian(seeds[5], (BUCKETS, HEADS), 1.0, 4.0, ((0, 4),), jnp.float32),
        "query_self": gaussian(seeds[6], (D, INNER), (4 * D) ** -0.5, 0.109375, ((0, 4), (1, 8)), jnp.float32),
        "key_self": gaussian(seeds[7], (D, INNER), (4 * D) ** -0.5, 0.109375, ((0, 4), (1, 8)), jnp.float32),
        "value_self": gaussian(seeds[8], (D, INNER), D ** -0.5, 0.21875, ((0, 4), (1, 8)), jnp.float32),
        "out_self": gaussian(seeds[9], (INNER, D), (INNER // 4) ** -0.5, 0.4375, ((0, 4), (1, 8)), jnp.float32),
        "query_cross": gaussian(seeds[10], (D, INNER), (4 * D) ** -0.5, 0.109375, ((0, 4), (1, 8)), jnp.float32),
        "key_cross": gaussian(seeds[11], (D, INNER), (4 * D) ** -0.5, 0.109375, ((0, 4), (1, 8)), jnp.float32),
        "value_cross": gaussian(seeds[12], (D, INNER), D ** -0.5, 0.21875, ((0, 4), (1, 8)), jnp.float32),
        "out_cross": gaussian(seeds[13], (INNER, D), (INNER // 4) ** -0.5, 0.4375, ((0, 4), (1, 8)), jnp.float32),
        "feed_in": gaussian(seeds[14], (D, FF), D ** -0.5, 0.21875, ((0, 4), (1, 8)), jnp.float32),
        "feed_out": gaussian(seeds[15], (FF, D), (FF // 4) ** -0.5, 0.21875, ((0, 4), (1, 8)), jnp.float32),
        "upstream": bell_draw_with(seeds[16], (TOKENS, D), 1.0, 12.0, ((0, 32),), (0, 1, 32, 2.75)),
    }


@jax.custom_vjp
def low(v):
    return lax.optimization_barrier(v.astype(jnp.bfloat16)).astype(jnp.float32)

@jax.custom_vjp
def low_back(v):
    return v

def low_keep(v):
    return (low(v), None)

def low_pass(kept, grad):
    return (grad,)

def back_keep(v):
    return (v, None)

def back_low(kept, grad):
    return (low(grad),)
low.defvjp(low_keep, low_pass)
low_back.defvjp(back_keep, back_low)
epsilon = 1e-06
highest = lax.Precision.HIGHEST

def matmul(left_rows, right_rows):
    return jnp.dot(left_rows, right_rows, precision=highest, preferred_element_type=jnp.float32)

def bucket_of(distance):
    half_count = BUCKETS // 2
    counted = jnp.zeros_like(distance)
    for section_index in range(1, half_count):
        edge_at = int(math.ceil(half_count * (MAX_DIST / half_count) ** (section_index / half_count)))
        counted = counted + (distance >= edge_at).astype(jnp.int32)
    return jnp.where(distance < half_count, distance, half_count + counted)

def rms_norm(hidden, gain_row):
    factor = lax.rsqrt(lax.optimization_barrier(jnp.mean(hidden * hidden, axis=-1, keepdims=True)) + epsilon)
    return hidden * factor * gain_row

def attend(queries, key_rows, value_rows, visible, bias_full):
    scores = low_back(jnp.einsum('qhd,khd->hqk', queries, key_rows, precision=highest)) + bias_full
    row_max = lax.optimization_barrier(jnp.max(jnp.where(visible[None], scores, -jnp.inf), axis=-1, keepdims=True))
    raised = jnp.where(visible[None], jnp.exp(scores - row_max), 0.0)
    attention = low(raised / lax.optimization_barrier(jnp.sum(raised, axis=-1, keepdims=True)))
    mixed_rows = jnp.einsum('hqk,khd->qhd', attention, value_rows, precision=highest)
    return mixed_rows.reshape(mixed_rows.shape[0], HEADS * HEAD_DIM)

def one_row(row_item, weights):
    hidden, encoder_rows, segment, valid_keys = row_item
    norm_gains, rel_table, query_self, key_self, value_self, out_self, query_cross, key_cross, value_cross, out_cross, feed_in, feed_out = weights
    places = jnp.arange(ROW, dtype=jnp.int32)
    distance = places[:, None] - places[None, :]
    visible = (distance >= 0) & (segment[:, None] == segment[None, :])
    bias_full = jnp.transpose(rel_table[bucket_of(jnp.maximum(distance, 0))], (2, 0, 1))
    normed = low(rms_norm(hidden, norm_gains[0]))
    queries = low_back(low(matmul(normed, query_self))).reshape(ROW, HEADS, HEAD_DIM)
    key_rows = low_back(low(matmul(normed, key_self))).reshape(ROW, HEADS, HEAD_DIM)
    value_rows = low_back(low(matmul(normed, value_self))).reshape(ROW, HEADS, HEAD_DIM)
    attended = low_back(low(attend(queries, key_rows, value_rows, visible, bias_full)))
    hidden = hidden + low_back(matmul(attended, out_self))
    normed = low(rms_norm(hidden, norm_gains[1]))
    queries = low_back(low(matmul(normed, query_cross))).reshape(ROW, HEADS, HEAD_DIM)
    key_rows = low_back(low(matmul(encoder_rows, key_cross))).reshape(EX_ROW * ENC, HEADS, HEAD_DIM)
    value_rows = low_back(low(matmul(encoder_rows, value_cross))).reshape(EX_ROW * ENC, HEADS, HEAD_DIM)
    key_example = jnp.arange(EX_ROW * ENC, dtype=jnp.int32) // ENC
    visible = (segment[:, None] == key_example[None, :]) & valid_keys[None, :]
    attended = low_back(low(attend(queries, key_rows, value_rows, visible, 0.0)))
    hidden = hidden + low_back(matmul(attended, out_cross))
    normed = low(rms_norm(hidden, norm_gains[2]))
    pre_act = low_back(matmul(normed, feed_in))
    active = low(jax.nn.gelu(pre_act, approximate=True))
    return hidden + low_back(matmul(active, feed_out))

def reference(decoder_in, encoder_out, decoder_lengths, encoder_lengths, norm_gains, rel_table, query_self, key_self, value_self, out_self, query_cross, key_cross, value_cross, out_cross, feed_in, feed_out, upstream):
    places = jnp.arange(ROW, dtype=jnp.int32)
    seg_ends = jnp.cumsum(decoder_lengths, axis=1, dtype=jnp.int32)
    segment = lax.optimization_barrier(jnp.sum((places[None, :, None] >= seg_ends[:, None, :]).astype(jnp.int32), axis=-1))
    valid_keys = (jnp.arange(ENC, dtype=jnp.int32)[None, :] < encoder_lengths[:, None]).reshape(ROWS, EX_ROW * ENC)

    def forward(decoder_rows, encoder_rows, *parameters):
        weights = tuple((low(parameter) for parameter in parameters))

        def row_step(row_item):
            return one_row(row_item, weights)
        outputs = lax.map(jax.checkpoint(row_step), (decoder_rows.reshape(ROWS, ROW, D), encoder_rows.reshape(ROWS, EX_ROW * ENC, D), segment, valid_keys))
        return outputs.reshape(ROWS * ROW, D)
    primals = (decoder_in.astype(jnp.float32), encoder_out.astype(jnp.float32), norm_gains, rel_table, query_self, key_self, value_self, out_self, query_cross, key_cross, value_cross, out_cross, feed_in, feed_out)
    decoder_out, pullback = jax.vjp(forward, *primals)
    deltas = pullback(upstream.astype(jnp.float32))
    return (decoder_out.astype(jnp.bfloat16), deltas[0].astype(jnp.bfloat16), deltas[1].astype(jnp.bfloat16), deltas[2], deltas[3], deltas[4], deltas[5], deltas[6], deltas[7], deltas[8], deltas[9], deltas[10], deltas[11], deltas[12], deltas[13])
```

```python
import functools
import math

import jax
import jax.numpy as jnp
from jax import lax
from jax.experimental import pallas as pl
from jax.experimental.pallas import tpu as pltpu
from jax.sharding import PartitionSpec as P

HEADS = 12
HEAD_DIM = 64
BUCKETS = 32
MAX_DIST = 128
MOST = 128
PAIRS = HEADS // 2
EPSILON = 1e-06
HIDDEN_SCORE = -1e30
BF = jnp.bfloat16
F32 = jnp.float32
VMEM_LIMIT = 60 * 1024 * 1024


def nn(a, b):
    return lax.dot_general(a, b, (((1,), (0,)), ((), ())), preferred_element_type=F32)


def nt(a, b):
    return lax.dot_general(a, b, (((1,), (1,)), ((), ())), preferred_element_type=F32)


def tn(a, b):
    return lax.dot_general(a, b, (((0,), (0,)), ((), ())), preferred_element_type=F32)


def rms(z, gain):
    factor = lax.rsqrt(jnp.mean(z * z, axis=-1, keepdims=True) + EPSILON)
    return z * factor * gain


def rms_back(z, gain, dy):
    factor = lax.rsqrt(jnp.mean(z * z, axis=-1, keepdims=True) + EPSILON)
    wdy = dy * gain
    inner = jnp.mean(z * wdy, axis=-1, keepdims=True)
    dz = factor * wdy - z * (factor * factor * factor * inner)
    return dz, jnp.sum(dy * z * factor, axis=0, keepdims=True)


def split_heads(rows):
    first = lax.broadcasted_iota(jnp.int32, rows.shape, 1) < HEAD_DIM
    zero = jnp.zeros_like(rows)
    return jnp.concatenate([jnp.where(first, rows, zero), jnp.where(first, zero, rows)], axis=0)


def join_heads(rows):
    half = rows.shape[0] // 2
    first = lax.broadcasted_iota(jnp.int32, (half, rows.shape[1]), 1) < HEAD_DIM
    return jnp.where(first, rows[:half], rows[half:])


def softmax(scores):
    raised = jnp.exp(scores - jnp.max(scores, axis=-1, keepdims=True))
    return raised * (1.0 / jnp.sum(raised, axis=-1, keepdims=True))


def lanes(index, width):
    return pl.ds(pl.multiple_of(index * width, width), width)


def loop(count, step):
    def run(index, carry):
        step(index)
        return carry

    lax.fori_loop(0, count, run, 0)


def bucket_of(distance):
    half_count = BUCKETS // 2
    counted = jnp.zeros_like(distance)
    for section_index in range(1, half_count):
        edge_at = int(
            math.ceil(half_count * (MAX_DIST / half_count) ** (section_index / half_count))
        )
        counted = counted + (distance >= edge_at).astype(jnp.int32)
    return jnp.where(distance < half_count, distance, half_count + counted)


def distance_hot():
    distance = jnp.maximum(MOST - jnp.arange(2 * MOST, dtype=jnp.int32), 0)
    return (bucket_of(distance)[:, None] == jnp.arange(BUCKETS, dtype=jnp.int32)[None, :]).astype(F32)


def self_masks(seg_col, seg_row, mask_ref):
    blocks = mask_ref.shape[0]
    a = lax.broadcasted_iota(jnp.int32, (MOST, 2 * MOST), 0)
    b = lax.broadcasted_iota(jnp.int32, (MOST, 2 * MOST), 1)
    causal = b <= a + MOST
    for i in range(blocks):
        same = seg_col[MOST * i : MOST * (i + 1), :] == seg_row[:, MOST * i : MOST * (i + 2)]
        mask_ref[i] = jnp.where(causal & same, 0.0, HIDDEN_SCORE)


def pair_bias(dist_ref, pair):
    parts = []
    for h in range(2):
        row = dist_ref[pl.ds(2 * pair + h, 1), :]
        parts.append(
            pltpu.roll(jnp.broadcast_to(row, (MOST, 2 * MOST)), 0, 1, stride=1, stride_axis=0)
        )
    return jnp.concatenate(parts, axis=0)


def masked_scores(scores, bias, mask):
    both = scores + bias
    return (both.reshape(2, MOST, 2 * MOST) + mask[None]).reshape(2 * MOST, 2 * MOST)


def front_kernel(
    x_ref, gains_ref, dist_ref, segc_ref, segr_ref, w_ref,
    n1_ref, q1_ref, k1_ref, v1_ref, a1_ref, h1_ref, n2_ref, q2_ref,
    mask_ref,
):
    rows, width = x_ref.shape
    blocks = rows // MOST
    n1_ref[...] = rms(x_ref[...].astype(F32), gains_ref[0:1, :]).astype(BF)
    k1_ref[0:MOST, :] = jnp.zeros((MOST, width), BF)
    v1_ref[0:MOST, :] = jnp.zeros((MOST, width), BF)

    def qkv(j):
        n1 = n1_ref[...]
        at = lanes(j, 256)
        q1_ref[:, at] = nt(n1, w_ref[0, at, :]).astype(BF)
        k1_ref[MOST:, at] = nt(n1, w_ref[1, at, :]).astype(BF)
        v1_ref[MOST:, at] = nt(n1, w_ref[2, at, :]).astype(BF)

    loop(width // 256, qkv)
    self_masks(segc_ref[...], segr_ref[...], mask_ref)

    def attend(pair):
        at = lanes(pair, 128)
        bias = pair_bias(dist_ref, pair)
        for i in range(blocks):
            queries = split_heads(q1_ref[MOST * i : MOST * (i + 1), at])
            keys = k1_ref[MOST * i : MOST * (i + 2), at]
            values = v1_ref[MOST * i : MOST * (i + 2), at]
            probs = softmax(masked_scores(nt(queries, keys), bias, mask_ref[i])).astype(BF)
            a1_ref[MOST * i : MOST * (i + 1), at] = join_heads(nn(probs, values)).astype(BF)

    loop(PAIRS, attend)

    def out(j):
        at = lanes(j, 256)
        h1_ref[:, at] = x_ref[:, at].astype(F32) + nt(a1_ref[...], w_ref[3, at, :])

    loop(width // 256, out)
    n2_ref[...] = rms(h1_ref[...], gains_ref[1:2, :]).astype(BF)

    def query(j):
        at = lanes(j, 256)
        q2_ref[:, at] = nt(n2_ref[...], w_ref[4, at, :]).astype(BF)

    loop(width // 256, query)


def example_rows(segr_ref, offr_ref, example, total):
    place = lax.broadcasted_iota(jnp.int32, (MOST, total), 0)
    return ((segr_ref[...] == example) & (offr_ref[...] == place)).astype(F32).astype(BF)


def cross_kernel(
    enc_ref, q2_ref, segr_ref, offr_ref, valid_ref, w_ref,
    k2_ref, v2_ref, a2_ref,
    qe_ref, ae_ref, sum_ref,
):
    e = pl.program_id(0)
    rows, width = q2_ref.shape
    keys_n = enc_ref.shape[0]

    @pl.when(e == 0)
    def _():
        sum_ref[...] = jnp.zeros_like(sum_ref)

    def project(j):
        at = lanes(j, 256)
        k2_ref[:, at] = nt(enc_ref[...], w_ref[0, at, :]).astype(BF)
        v2_ref[:, at] = nt(enc_ref[...], w_ref[1, at, :]).astype(BF)

    loop(width // 256, project)
    pick = example_rows(segr_ref, offr_ref, e, rows)
    qe_ref[...] = nn(pick, q2_ref[...]).astype(BF)
    hidden = valid_ref[pl.ds(e, 1), :]

    def attend(pair):
        at = lanes(pair, 128)
        probs = softmax(nt(split_heads(qe_ref[:, at]), k2_ref[:, at]) + hidden).astype(BF)
        ae_ref[:, at] = join_heads(nn(probs, v2_ref[:, at])).astype(BF)

    loop(PAIRS, attend)
    sum_ref[...] += tn(pick, ae_ref[...])

    @pl.when(e == pl.num_programs(0) - 1)
    def _():
        a2_ref[...] = sum_ref[...].astype(BF)


GELU_A = math.sqrt(2.0 / math.pi)
GELU_B = 0.044715


def feed_kernel(
    a2_ref, h1_ref, c_ref, gains_ref, w_ref, win_ref, wout_ref,
    out_ref, dwin_ref, dwout_ref, dwoc_ref, da2_ref, dh2_ref, gain_ref,
    h2_ref, n3_ref, sum_ref, back_ref,
):
    rows, width = a2_ref.shape
    hidden = win_ref.shape[1]

    def cross_out(j):
        at = lanes(j, 256)
        h2_ref[:, at] = h1_ref[:, at] + nt(a2_ref[...], w_ref[0, at, :])

    loop(width // 256, cross_out)
    n3_ref[...] = rms(h2_ref[...], gains_ref[2:3, :]).astype(BF)
    sum_ref[...] = h2_ref[...]
    back_ref[...] = jnp.zeros_like(back_ref)

    def part(j):
        at = lanes(j, 256)
        u = nn(n3_ref[...], win_ref[:, at])
        t = jnp.tanh(GELU_A * (u + GELU_B * (u * u * u)))
        g = (0.5 * u * (1.0 + t)).astype(BF)
        slope = 0.5 * (1.0 + t) + 0.5 * u * (1.0 - t * t) * (
            GELU_A * (1.0 + (3.0 * GELU_B) * (u * u))
        )
        du = (nn(c_ref[...], wout_ref[:, at]) * slope).astype(BF)
        dwout_ref[:, at] = tn(c_ref[...], g).astype(BF)
        dwin_ref[:, at] = tn(n3_ref[...], du).astype(BF)
        sum_ref[...] += nt(g, wout_ref[:, at])
        back_ref[...] += nt(du, win_ref[:, at])

    loop(hidden // 256, part)
    out_ref[...] = sum_ref[...].astype(BF)
    dz, dw = rms_back(h2_ref[...], gains_ref[2:3, :], back_ref[...])
    gain_ref[...] = dw
    dh2_ref[...] = c_ref[...].astype(F32) + dz

    def tail(j):
        at = lanes(j, 256)
        da2_ref[:, at] = nn(dh2_ref[...].astype(BF), w_ref[0, :, at]).astype(BF)
        dwoc_ref[at, :] = tn(dh2_ref[:, at].astype(BF), a2_ref[...]).astype(BF)

    loop(width // 256, tail)


def cross_back_kernel(
    enc_ref, k2_ref, v2_ref, q2_ref, da2_ref, segr_ref, offr_ref, valid_ref, w_ref,
    denc_ref, dq2_ref, dw_ref,
    qe_ref, dae_ref, dqe_ref, dk_ref, dv_ref, sum_ref, dwsum_ref,
):
    e = pl.program_id(0)
    rows, width = q2_ref.shape

    @pl.when(e == 0)
    def _():
        sum_ref[...] = jnp.zeros_like(sum_ref)
        dwsum_ref[...] = jnp.zeros_like(dwsum_ref)

    pick = example_rows(segr_ref, offr_ref, e, rows)
    qe_ref[...] = nn(pick, q2_ref[...]).astype(BF)
    dae_ref[...] = nn(pick, da2_ref[...]).astype(BF)
    hidden = valid_ref[pl.ds(e, 1), :]

    def attend(pair):
        at = lanes(pair, 128)
        queries = split_heads(qe_ref[:, at])
        deltas = split_heads(dae_ref[:, at])
        probs = softmax(nt(queries, k2_ref[:, at]) + hidden)
        dprobs = nt(deltas, v2_ref[:, at])
        low = (probs * (dprobs - jnp.sum(dprobs * probs, axis=-1, keepdims=True))).astype(BF)
        dv_ref[:, at] = tn(probs.astype(BF), deltas).astype(BF)
        dk_ref[:, at] = tn(low, queries).astype(BF)
        dqe_ref[:, at] = join_heads(nn(low, k2_ref[:, at])).astype(BF)

    loop(PAIRS, attend)
    sum_ref[...] += tn(pick, dqe_ref[...])

    def dense(j):
        at = lanes(j, 256)
        denc_ref[:, at] = (nn(dk_ref[...], w_ref[0, :, at]) + nn(dv_ref[...], w_ref[1, :, at])).astype(BF)
        dwsum_ref[0, at, :] += tn(dk_ref[:, at], enc_ref[...])
        dwsum_ref[1, at, :] += tn(dv_ref[:, at], enc_ref[...])

    loop(width // 256, dense)

    @pl.when(e == pl.num_programs(0) - 1)
    def _():
        dq2_ref[...] = sum_ref[...].astype(BF)
        dw_ref[...] = dwsum_ref[...].astype(BF)


def self_back_kernel(
    dq2_ref, n2_ref, h1_ref, dh2_ref, x_ref, n1_ref, q1_ref, k1_ref, v1_ref, a1_ref,
    gains_ref, dist_ref, segc_ref, segr_ref, w_ref,
    dx_ref, dw_ref, gain_ref, dist_out_ref,
    mask_ref, dh1_ref, b1_ref, da1_ref, dq_ref, dk_ref, dv_ref, dksum_ref, dvsum_ref, back_ref,
):
    rows, width = x_ref.shape
    blocks = rows // MOST

    def query(j):
        at = lanes(j, 256)
        dw_ref[4, at, :] = tn(dq2_ref[:, at], n2_ref[...]).astype(BF)
        back_ref[:, at] = nn(dq2_ref[...], w_ref[4, :, at])

    loop(width // 256, query)
    dz, dw = rms_back(h1_ref[...], gains_ref[1:2, :], back_ref[...])
    gain_ref[1:2, :] = dw
    dh1_ref[...] = dh2_ref[...] + dz
    b1_ref[...] = dh1_ref[...].astype(BF)

    def out(j):
        at = lanes(j, 256)
        dw_ref[3, at, :] = tn(b1_ref[:, at], a1_ref[...]).astype(BF)
        da1_ref[:, at] = nn(b1_ref[...], w_ref[3, :, at]).astype(BF)

    loop(width // 256, out)
    self_masks(segc_ref[...], segr_ref[...], mask_ref)

    def attend(pair):
        at = lanes(pair, 128)
        bias = pair_bias(dist_ref, pair)
        dksum_ref[...] = jnp.zeros_like(dksum_ref)
        dvsum_ref[...] = jnp.zeros_like(dvsum_ref)
        skewed = jnp.zeros((2 * MOST, 2 * MOST), F32)
        for i in range(blocks):
            own = slice(MOST * i, MOST * (i + 1))
            band = slice(MOST * i, MOST * (i + 2))
            queries = split_heads(q1_ref[own, at])
            deltas = split_heads(da1_ref[own, at])
            keys = k1_ref[band, at]
            probs = softmax(masked_scores(nt(queries, keys), bias, mask_ref[i]))
            dprobs = nt(deltas, v1_ref[band, at])
            dscores = probs * (dprobs - jnp.sum(dprobs * probs, axis=-1, keepdims=True))
            low = dscores.astype(BF)
            skewed = skewed + dscores
            dvsum_ref[band, :] += tn(probs.astype(BF), deltas)
            dksum_ref[band, :] += tn(low, queries)
            dq_ref[own, at] = join_heads(nn(low, keys)).astype(BF)
        dk_ref[:, at] = dksum_ref[MOST:, :].astype(BF)
        dv_ref[:, at] = dvsum_ref[MOST:, :].astype(BF)
        a = lax.broadcasted_iota(jnp.int32, (MOST, MOST), 0)
        b = lax.broadcasted_iota(jnp.int32, (MOST, MOST), 1)
        flip = (a + b == MOST - 1).astype(F32)
        for h in range(2):
            flipped = jnp.dot(
                flip,
                skewed[MOST * h : MOST * (h + 1)],
                precision=lax.Precision.HIGHEST,
                preferred_element_type=F32,
            )
            straight = pltpu.roll(flipped, MOST + 1, 1, stride=1, stride_axis=0)
            dist_out_ref[pl.ds(2 * pair + h, 1), :] = jnp.sum(straight, axis=0, keepdims=True)

    loop(PAIRS, attend)

    def qkv(j):
        at = lanes(j, 256)
        dw_ref[0, at, :] = tn(dq_ref[:, at], n1_ref[...]).astype(BF)
        dw_ref[1, at, :] = tn(dk_ref[:, at], n1_ref[...]).astype(BF)
        dw_ref[2, at, :] = tn(dv_ref[:, at], n1_ref[...]).astype(BF)
        back_ref[:, at] = (
            nn(dq_ref[...], w_ref[0, :, at])
            + nn(dk_ref[...], w_ref[1, :, at])
            + nn(dv_ref[...], w_ref[2, :, at])
        )

    loop(width // 256, qkv)
    dz, dw = rms_back(x_ref[...].astype(F32), gains_ref[0:1, :], back_ref[...])
    gain_ref[0:1, :] = dw
    dx_ref[...] = (dh1_ref[...] + dz).astype(BF)


def whole():
    return pl.BlockSpec(memory_space=pltpu.VMEM)


def call(kernel, outs, scratch, args, specs=None, grid=None, out_specs=None, name=None, flops=0):
    specs = specs or [whole()] * len(args)
    out_specs = out_specs or [whole()] * len(outs)
    return pl.pallas_call(
        kernel,
        grid=grid or (),
        in_specs=specs,
        out_specs=out_specs,
        out_shape=[jax.ShapeDtypeStruct(shape, kind) for shape, kind in outs],
        scratch_shapes=[pltpu.VMEM(shape, kind) for shape, kind in scratch],
        compiler_params=pltpu.CompilerParams(vmem_limit_bytes=VMEM_LIMIT),
        cost_estimate=pl.CostEstimate(flops=flops, bytes_accessed=20_000_000, transcendentals=0),
        name=name,
    )(*args)


def square_spec(first, count, width):
    return pl.BlockSpec((count, width, width), lambda *_: (first // count, 0, 0))


def body(decoder_in, encoder_out, decoder_lengths, encoder_lengths, norm_gains, rel_table,
         query_self, key_self, value_self, out_self, query_cross, key_cross, value_cross, out_cross,
         feed_in, feed_out, upstream):
    rows, width = decoder_in.shape
    row_count, examples = decoder_lengths.shape
    keys_n = encoder_out.shape[1]

    order = (query_self, key_self, value_self, out_self, query_cross, out_cross, key_cross, value_cross)
    square = jnp.stack([m.astype(BF).T for m in order])
    square = lax.all_gather(square, "fsdp", axis=1, tiled=True)
    square = lax.all_gather(square, "dp", axis=2, tiled=True)
    win = lax.all_gather(feed_in.astype(BF), "fsdp", axis=1, tiled=True)
    win = lax.all_gather(win, "dp", axis=0, tiled=True)
    wout = lax.all_gather(feed_out.astype(BF).T, "fsdp", axis=0, tiled=True)
    wout = lax.all_gather(wout, "dp", axis=1, tiled=True)
    gains = lax.all_gather(norm_gains.astype(BF), "fsdp", axis=1, tiled=True).astype(F32)
    table = lax.all_gather(rel_table.astype(BF), "dp", axis=0, tiled=True).astype(F32)
    hidden = win.shape[1]

    places = jnp.arange(rows, dtype=jnp.int32)
    ends = jnp.cumsum(decoder_lengths[0], dtype=jnp.int32)
    segment = jnp.sum((places[:, None] >= ends[None, :]).astype(jnp.int32), axis=-1)
    starts = ends - decoder_lengths[0]
    offset = places - jnp.sum(
        jnp.where(segment[:, None] == jnp.arange(examples)[None, :], starts[None, :], 0), axis=-1
    )
    seg_col = segment[:, None]
    seg_row = segment[None, :]
    off_row = offset[None, :]
    seg_band = jnp.concatenate([jnp.full((1, MOST), -1, jnp.int32), seg_row], axis=1)
    valid = jnp.where(
        jnp.arange(keys_n, dtype=jnp.int32)[None, :] < encoder_lengths[:, None], 0.0, HIDDEN_SCORE
    )
    hot = distance_hot()
    dist = jnp.dot(hot, table, precision=lax.Precision.HIGHEST).T

    small = (rows, width)
    n1, q1, k1, v1, a1, h1, n2, q2 = call(
        front_kernel,
        [(small, BF), (small, BF), ((rows + MOST, width), BF), ((rows + MOST, width), BF), (small, BF),
         (small, F32), (small, BF), (small, BF)],
        [((rows // MOST, MOST, 2 * MOST), F32)],
        (decoder_in, gains, dist, seg_col, seg_band, square),
        specs=[whole()] * 5 + [square_spec(0, 5, width)],
        grid=(1,),
        name="front",
    )
    enc = encoder_out.reshape(-1, width)
    per_example = pl.BlockSpec((keys_n, width), lambda e: (e, 0))
    k2, v2, a2 = call(
        cross_kernel,
        [(enc.shape, BF), (enc.shape, BF), (small, BF)],
        [((MOST, width), BF), ((MOST, width), BF), (small, F32)],
        (enc, q2, seg_row, off_row, valid, square),
        specs=[per_example] + [whole()] * 4 + [square_spec(6, 2, width)],
        out_specs=[per_example, per_example, whole()],
        grid=(examples,),
        name="cross",
    )
    out, dwin, dwout, dwoc, da2, dh2, gain3 = call(
        feed_kernel,
        [(small, BF), (win.shape, BF), (wout.shape, BF), ((width, width), BF), (small, BF), (small, F32),
         ((1, width), F32)],
        [(small, F32), (small, BF), (small, F32), (small, F32)],
        (a2, h1, upstream, gains, square, win, wout),
        specs=[whole()] * 4 + [square_spec(5, 1, width)] + [whole()] * 2,
        grid=(1,),
        name="feed",
    )
    denc, dq2, dw_kv = call(
        cross_back_kernel,
        [(enc.shape, BF), (small, BF), ((2, width, width), BF)],
        [((MOST, width), BF), ((MOST, width), BF), ((MOST, width), BF), ((keys_n, width), BF),
         ((keys_n, width), BF), (small, F32), ((2, width, width), F32)],
        (enc, k2, v2, q2, da2, seg_row, off_row, valid, square),
        specs=[per_example] * 3 + [whole()] * 5 + [square_spec(6, 2, width)],
        out_specs=[per_example, whole(), whole()],
        grid=(examples,),
        name="cross_back",
    )
    dx, dw_five, gain12, dist_sum = call(
        self_back_kernel,
        [(small, BF), ((5, width, width), BF), ((2, width), F32), ((HEADS, 2 * MOST), F32)],
        [((rows // MOST, MOST, 2 * MOST), F32), (small, F32), (small, BF), (small, BF), (small, BF),
         (small, BF), (small, BF), ((rows + MOST, 128), F32), ((rows + MOST, 128), F32), (small, F32)],
        (dq2, n2, h1, dh2, decoder_in, n1, q1, k1, v1, a1, gains, dist, seg_col, seg_band, square),
        specs=[whole()] * 14 + [square_spec(0, 5, width)],
        grid=(1,),
        name="self_back",
    )

    dsquare = jnp.concatenate([dw_five, dwoc[None], dw_kv], axis=0)
    dsquare = lax.psum_scatter(dsquare, "dp", scatter_dimension=2, tiled=True)
    dsquare = lax.psum_scatter(dsquare, "fsdp", scatter_dimension=1, tiled=True)
    dwin = lax.psum_scatter(dwin, "dp", scatter_dimension=0, tiled=True)
    dwin = lax.psum_scatter(dwin, "fsdp", scatter_dimension=1, tiled=True)
    dwout = lax.psum_scatter(dwout, "dp", scatter_dimension=1, tiled=True)
    dwout = lax.psum_scatter(dwout, "fsdp", scatter_dimension=0, tiled=True)
    gains_delta = lax.psum(jnp.concatenate([gain12, gain3], axis=0), "dp")
    gains_delta = lax.psum_scatter(gains_delta, "fsdp", scatter_dimension=1, tiled=True)
    table_delta = jnp.dot(dist_sum, hot, precision=lax.Precision.HIGHEST).T
    table_delta = lax.psum_scatter(table_delta, "dp", scatter_dimension=0, tiled=True)
    table_delta = lax.psum(table_delta, "fsdp")
    squares = [dsquare[i].astype(F32).T for i in range(8)]
    q_s, k_s, v_s, o_s, q_c, o_c, k_c, v_c = squares
    return (out, dx, denc.reshape(encoder_out.shape), gains_delta, table_delta,
            q_s, k_s, v_s, o_s, q_c, k_c, v_c, o_c, dwin.astype(F32), dwout.astype(F32).T)


def solution(mesh):
    tokens = P(("dp", "fsdp"), None)
    weight = P("dp", "fsdp")
    return jax.shard_map(
        body,
        mesh=mesh,
        in_specs=(tokens, P(("dp", "fsdp"), None, None), tokens, P(("dp", "fsdp")), P(None, "fsdp"),
                  P("dp", None)) + (weight,) * 10 + (tokens,),
        out_specs=(tokens, tokens, P(("dp", "fsdp"), None, None), P(None, "fsdp"), P("dp", None))
        + (weight,) * 10,
        check_vma=False,
    )
```

```python
import functools
import math

import jax
import jax.numpy as jnp
from jax import lax
from jax.experimental import pallas as pl
from jax.experimental.pallas import tpu as pltpu
from jax.sharding import PartitionSpec as P

HEADS = 12
HEAD_DIM = 64
BUCKETS = 32
MAX_DIST = 128
MOST = 128
PAIRS = HEADS // 2
EPSILON = 1e-06
HIDDEN_SCORE = -1e30
BF = jnp.bfloat16
F32 = jnp.float32
VMEM_LIMIT = 60 * 1024 * 1024


def nn(a, b):
    return lax.dot_general(a, b, (((1,), (0,)), ((), ())), preferred_element_type=F32)


def nt(a, b):
    return lax.dot_general(a, b, (((1,), (1,)), ((), ())), preferred_element_type=F32)


def tn(a, b):
    return lax.dot_general(a, b, (((0,), (0,)), ((), ())), preferred_element_type=F32)


def rms(z, gain):
    factor = lax.rsqrt(jnp.mean(z * z, axis=-1, keepdims=True) + EPSILON)
    return z * factor * gain


def rms_back(z, gain, dy):
    factor = lax.rsqrt(jnp.mean(z * z, axis=-1, keepdims=True) + EPSILON)
    wdy = dy * gain
    inner = jnp.mean(z * wdy, axis=-1, keepdims=True)
    dz = factor * wdy - z * (factor * factor * factor * inner)
    return dz, jnp.sum(dy * z * factor, axis=0, keepdims=True)


def split_heads(rows):
    first = lax.broadcasted_iota(jnp.int32, rows.shape, 1) < HEAD_DIM
    zero = jnp.zeros_like(rows)
    return jnp.concatenate([jnp.where(first, rows, zero), jnp.where(first, zero, rows)], axis=0)


def join_heads(rows):
    half = rows.shape[0] // 2
    first = lax.broadcasted_iota(jnp.int32, (half, rows.shape[1]), 1) < HEAD_DIM
    return jnp.where(first, rows[:half], rows[half:])


def softmax(scores):
    raised = jnp.exp(scores - jnp.max(scores, axis=-1, keepdims=True))
    return raised * (1.0 / jnp.sum(raised, axis=-1, keepdims=True))


def lanes(index, width):
    return pl.ds(pl.multiple_of(index * width, width), width)


def loop(count, step):
    def run(index, carry):
        step(index)
        return carry

    lax.fori_loop(0, count, run, 0)


def bucket_of(distance):
    half_count = BUCKETS // 2
    counted = jnp.zeros_like(distance)
    for section_index in range(1, half_count):
        edge_at = int(
            math.ceil(half_count * (MAX_DIST / half_count) ** (section_index / half_count))
        )
        counted = counted + (distance >= edge_at).astype(jnp.int32)
    return jnp.where(distance < half_count, distance, half_count + counted)


def distance_hot():
    distance = jnp.maximum(MOST - jnp.arange(2 * MOST, dtype=jnp.int32), 0)
    return (bucket_of(distance)[:, None] == jnp.arange(BUCKETS, dtype=jnp.int32)[None, :]).astype(F32)


def self_masks(seg_col, seg_row, mask_ref):
    blocks = mask_ref.shape[0]
    a = lax.broadcasted_iota(jnp.int32, (MOST, 2 * MOST), 0)
    b = lax.broadcasted_iota(jnp.int32, (MOST, 2 * MOST), 1)
    causal = b <= a + MOST
    for i in range(blocks):
        same = seg_col[MOST * i : MOST * (i + 1), :] == seg_row[:, MOST * i : MOST * (i + 2)]
        mask_ref[i] = jnp.where(causal & same, 0.0, HIDDEN_SCORE)


def pair_bias(dist_ref, pair):
    parts = []
    for h in range(2):
        row = dist_ref[pl.ds(2 * pair + h, 1), :]
        parts.append(
            pltpu.roll(jnp.broadcast_to(row, (MOST, 2 * MOST)), 0, 1, stride=1, stride_axis=0)
        )
    return jnp.concatenate(parts, axis=0)


def masked_scores(scores, bias, mask):
    both = scores + bias
    return (both.reshape(2, MOST, 2 * MOST) + mask[None]).reshape(2 * MOST, 2 * MOST)


def front_kernel(
    x_ref, gains_ref, dist_ref, segc_ref, segr_ref, w_ref,
    n1_ref, q1_ref, k1_ref, v1_ref, a1_ref, h1_ref, n2_ref, q2_ref,
    mask_ref,
):
    rows, width = x_ref.shape
    blocks = rows // MOST
    n1_ref[...] = rms(x_ref[...].astype(F32), gains_ref[0:1, :]).astype(BF)
    k1_ref[0:MOST, :] = jnp.zeros((MOST, width), BF)
    v1_ref[0:MOST, :] = jnp.zeros((MOST, width), BF)

    def qkv(j):
        n1 = n1_ref[...]
        at = lanes(j, 256)
        q1_ref[:, at] = nt(n1, w_ref[0, at, :]).astype(BF)
        k1_ref[MOST:, at] = nt(n1, w_ref[1, at, :]).astype(BF)
        v1_ref[MOST:, at] = nt(n1, w_ref[2, at, :]).astype(BF)

    loop(width // 256, qkv)
    self_masks(segc_ref[...], segr_ref[...], mask_ref)

    def attend(pair):
        at = lanes(pair, 128)
        bias = pair_bias(dist_ref, pair)
        for i in range(blocks):
            queries = split_heads(q1_ref[MOST * i : MOST * (i + 1), at])
            keys = k1_ref[MOST * i : MOST * (i + 2), at]
            values = v1_ref[MOST * i : MOST * (i + 2), at]
            probs = softmax(masked_scores(nt(queries, keys), bias, mask_ref[i])).astype(BF)
            a1_ref[MOST * i : MOST * (i + 1), at] = join_heads(nn(probs, values)).astype(BF)

    loop(PAIRS, attend)

    def out(j):
        at = lanes(j, 256)
        h1_ref[:, at] = x_ref[:, at].astype(F32) + nt(a1_ref[...], w_ref[3, at, :])

    loop(width // 256, out)
    n2_ref[...] = rms(h1_ref[...], gains_ref[1:2, :]).astype(BF)

    def query(j):
        at = lanes(j, 256)
        q2_ref[:, at] = nt(n2_ref[...], w_ref[4, at, :]).astype(BF)

    loop(width // 256, query)


def example_rows(segr_ref, offr_ref, example, total):
    place = lax.broadcasted_iota(jnp.int32, (MOST, total), 0)
    return ((segr_ref[...] == example) & (offr_ref[...] == place)).astype(F32).astype(BF)


def cross_kernel(
    enc_ref, q2_ref, segr_ref, offr_ref, valid_ref, w_ref,
    k2_ref, v2_ref, a2_ref,
    qe_ref, ae_ref, sum_ref,
):
    e = pl.program_id(0)
    rows, width = q2_ref.shape
    keys_n = enc_ref.shape[0]

    @pl.when(e == 0)
    def _():
        sum_ref[...] = jnp.zeros_like(sum_ref)

    def project(j):
        at = lanes(j, 256)
        k2_ref[:, at] = nt(enc_ref[...], w_ref[0, at, :]).astype(BF)
        v2_ref[:, at] = nt(enc_ref[...], w_ref[1, at, :]).astype(BF)

    loop(width // 256, project)
    pick = example_rows(segr_ref, offr_ref, e, rows)
    qe_ref[...] = nn(pick, q2_ref[...]).astype(BF)
    hidden = valid_ref[pl.ds(e, 1), :]

    def attend(pair):
        at = lanes(pair, 128)
        probs = softmax(nt(split_heads(qe_ref[:, at]), k2_ref[:, at]) + hidden).astype(BF)
        ae_ref[:, at] = join_heads(nn(probs, v2_ref[:, at])).astype(BF)

    loop(PAIRS, attend)
    sum_ref[...] += tn(pick, ae_ref[...])

    @pl.when(e == pl.num_programs(0) - 1)
    def _():
        a2_ref[...] = sum_ref[...].astype(BF)


GELU_A = math.sqrt(2.0 / math.pi)
GELU_B = 0.044715


def feed_kernel(
    a2_ref, h1_ref, c_ref, gains_ref, w_ref, win_ref, wout_ref,
    out_ref, dwin_ref, dwout_ref, dwoc_ref, da2_ref, dh2_ref, gain_ref,
    h2_ref, n3_ref, sum_ref, back_ref,
):
    rows, width = a2_ref.shape
    hidden = win_ref.shape[0]

    def cross_out(j):
        at = lanes(j, 256)
        h2_ref[:, at] = h1_ref[:, at] + nt(a2_ref[...], w_ref[0, at, :])

    loop(width // 256, cross_out)
    n3_ref[...] = rms(h2_ref[...], gains_ref[2:3, :]).astype(BF)
    sum_ref[...] = h2_ref[...]
    back_ref[...] = jnp.zeros_like(back_ref)

    def part(j):
        at = lanes(j, 256)
        u = nt(n3_ref[...], win_ref[at, :])
        t = jnp.tanh(GELU_A * (u + GELU_B * (u * u * u)))
        g = (0.5 * u * (1.0 + t)).astype(BF)
        slope = 0.5 * (1.0 + t) + 0.5 * u * (1.0 - t * t) * (
            GELU_A * (1.0 + (3.0 * GELU_B) * (u * u))
        )
        du = (nn(c_ref[...], wout_ref[:, at]) * slope).astype(BF)
        dwout_ref[:, at] = tn(c_ref[...], g).astype(BF)
        dwin_ref[at, :] = tn(du, n3_ref[...]).astype(BF)
        sum_ref[...] += nt(g, wout_ref[:, at])
        back_ref[...] += nn(du, win_ref[at, :])

    loop(hidden // 256, part)
    out_ref[...] = sum_ref[...].astype(BF)
    dz, dw = rms_back(h2_ref[...], gains_ref[2:3, :], back_ref[...])
    gain_ref[...] = dw
    dh2_ref[...] = c_ref[...].astype(F32) + dz

    def tail(j):
        at = lanes(j, 256)
        da2_ref[:, at] = nn(dh2_ref[...].astype(BF), w_ref[0, :, at]).astype(BF)
        dwoc_ref[at, :] = tn(dh2_ref[:, at].astype(BF), a2_ref[...]).astype(BF)

    loop(width // 256, tail)


def cross_back_kernel(
    enc_ref, k2_ref, v2_ref, q2_ref, da2_ref, segr_ref, offr_ref, valid_ref, w_ref,
    denc_ref, dq2_ref, dw_ref,
    qe_ref, dae_ref, dqe_ref, dk_ref, dv_ref, sum_ref, dwsum_ref,
):
    e = pl.program_id(0)
    rows, width = q2_ref.shape

    @pl.when(e == 0)
    def _():
        sum_ref[...] = jnp.zeros_like(sum_ref)
        dwsum_ref[...] = jnp.zeros_like(dwsum_ref)

    pick = example_rows(segr_ref, offr_ref, e, rows)
    qe_ref[...] = nn(pick, q2_ref[...]).astype(BF)
    dae_ref[...] = nn(pick, da2_ref[...]).astype(BF)
    hidden = valid_ref[pl.ds(e, 1), :]

    def attend(pair):
        at = lanes(pair, 128)
        queries = split_heads(qe_ref[:, at])
        deltas = split_heads(dae_ref[:, at])
        probs = softmax(nt(queries, k2_ref[:, at]) + hidden)
        dprobs = nt(deltas, v2_ref[:, at])
        low = (probs * (dprobs - jnp.sum(dprobs * probs, axis=-1, keepdims=True))).astype(BF)
        dv_ref[:, at] = tn(probs.astype(BF), deltas).astype(BF)
        dk_ref[:, at] = tn(low, queries).astype(BF)
        dqe_ref[:, at] = join_heads(nn(low, k2_ref[:, at])).astype(BF)

    loop(PAIRS, attend)
    sum_ref[...] += tn(pick, dqe_ref[...])

    def dense(j):
        at = lanes(j, 256)
        denc_ref[:, at] = (nn(dk_ref[...], w_ref[0, :, at]) + nn(dv_ref[...], w_ref[1, :, at])).astype(BF)
        dwsum_ref[0, at, :] += tn(dk_ref[:, at], enc_ref[...])
        dwsum_ref[1, at, :] += tn(dv_ref[:, at], enc_ref[...])

    loop(width // 256, dense)

    @pl.when(e == pl.num_programs(0) - 1)
    def _():
        dq2_ref[...] = sum_ref[...].astype(BF)
        dw_ref[...] = dwsum_ref[...].astype(BF)


def self_back_kernel(
    dq2_ref, n2_ref, h1_ref, dh2_ref, x_ref, n1_ref, q1_ref, k1_ref, v1_ref, a1_ref,
    gains_ref, dist_ref, segc_ref, segr_ref, w_ref,
    dx_ref, dw_ref, gain_ref, dist_out_ref,
    mask_ref, dh1_ref, b1_ref, da1_ref, dq_ref, dk_ref, dv_ref, dksum_ref, dvsum_ref, back_ref,
):
    rows, width = x_ref.shape
    blocks = rows // MOST

    def query(j):
        at = lanes(j, 256)
        dw_ref[4, at, :] = tn(dq2_ref[:, at], n2_ref[...]).astype(BF)
        back_ref[:, at] = nn(dq2_ref[...], w_ref[4, :, at])

    loop(width // 256, query)
    dz, dw = rms_back(h1_ref[...], gains_ref[1:2, :], back_ref[...])
    gain_ref[1:2, :] = dw
    dh1_ref[...] = dh2_ref[...] + dz
    b1_ref[...] = dh1_ref[...].astype(BF)

    def out(j):
        at = lanes(j, 256)
        dw_ref[3, at, :] = tn(b1_ref[:, at], a1_ref[...]).astype(BF)
        da1_ref[:, at] = nn(b1_ref[...], w_ref[3, :, at]).astype(BF)

    loop(width // 256, out)
    self_masks(segc_ref[...], segr_ref[...], mask_ref)

    def attend(pair):
        at = lanes(pair, 128)
        bias = pair_bias(dist_ref, pair)
        dksum_ref[...] = jnp.zeros_like(dksum_ref)
        dvsum_ref[...] = jnp.zeros_like(dvsum_ref)
        skewed = jnp.zeros((2 * MOST, 2 * MOST), F32)
        for i in range(blocks):
            own = slice(MOST * i, MOST * (i + 1))
            band = slice(MOST * i, MOST * (i + 2))
            queries = split_heads(q1_ref[own, at])
            deltas = split_heads(da1_ref[own, at])
            keys = k1_ref[band, at]
            probs = softmax(masked_scores(nt(queries, keys), bias, mask_ref[i]))
            dprobs = nt(deltas, v1_ref[band, at])
            dscores = probs * (dprobs - jnp.sum(dprobs * probs, axis=-1, keepdims=True))
            low = dscores.astype(BF)
            skewed = skewed + dscores
            dvsum_ref[band, :] += tn(probs.astype(BF), deltas)
            dksum_ref[band, :] += tn(low, queries)
            dq_ref[own, at] = join_heads(nn(low, keys)).astype(BF)
        dk_ref[:, at] = dksum_ref[MOST:, :].astype(BF)
        dv_ref[:, at] = dvsum_ref[MOST:, :].astype(BF)
        a = lax.broadcasted_iota(jnp.int32, (MOST, MOST), 0)
        b = lax.broadcasted_iota(jnp.int32, (MOST, MOST), 1)
        flip = (a + b == MOST - 1).astype(F32)
        for h in range(2):
            flipped = jnp.dot(
                flip,
                skewed[MOST * h : MOST * (h + 1)],
                precision=lax.Precision.HIGHEST,
                preferred_element_type=F32,
            )
            straight = pltpu.roll(flipped, MOST + 1, 1, stride=1, stride_axis=0)
            dist_out_ref[pl.ds(2 * pair + h, 1), :] = jnp.sum(straight, axis=0, keepdims=True)

    loop(PAIRS, attend)

    def qkv(j):
        at = lanes(j, 256)
        dw_ref[0, at, :] = tn(dq_ref[:, at], n1_ref[...]).astype(BF)
        dw_ref[1, at, :] = tn(dk_ref[:, at], n1_ref[...]).astype(BF)
        dw_ref[2, at, :] = tn(dv_ref[:, at], n1_ref[...]).astype(BF)
        back_ref[:, at] = (
            nn(dq_ref[...], w_ref[0, :, at])
            + nn(dk_ref[...], w_ref[1, :, at])
            + nn(dv_ref[...], w_ref[2, :, at])
        )

    loop(width // 256, qkv)
    dz, dw = rms_back(x_ref[...].astype(F32), gains_ref[0:1, :], back_ref[...])
    gain_ref[0:1, :] = dw
    dx_ref[...] = (dh1_ref[...] + dz).astype(BF)


MESH = pl.DeviceIdType.MESH
PIECE = 48
WIDE = 384
UNITS = 16

class Place:
    def __init__(self):
        d, f = lax.axis_index("dp"), lax.axis_index("fsdp")
        self.d, self.f = d, f
        self.y, self.c = d // 2, d % 2
        self.z, self.x = f // 2, f % 2
    def at(self, z=None, x=None, y=None, c=None):
        z = self.z if z is None else z
        x = self.x if x is None else x
        y = self.y if y is None else y
        c = self.c if c is None else c
        return (y * 2 + c, z * 2 + x)

def eye(n):
    a = lax.broadcasted_iota(jnp.int32, (n, n), 0)
    b = lax.broadcasted_iota(jnp.int32, (n, n), 1)
    return (a == b).astype(F32).astype(BF)

def remote(src, dst, send, recv, dev):
    return pltpu.make_async_remote_copy(src_ref=src, dst_ref=dst, send_sem=send, recv_sem=recv,
                                        device_id=dev, device_id_type=MESH)

ALL = slice(None)

def unit_piece(sq, fi, fo, u, z, x, c, y):
    if u < 8:
        return sq.at[u, z, x, c, :, pl.ds(pl.multiple_of(y * WIDE, WIDE), WIDE)]
    if u < 12:
        return fi.at[z, x, c, u - 8, :, pl.ds(pl.multiple_of(y * WIDE, WIDE), WIDE)]
    return fo.at[z, x, c, :, pl.ds(pl.multiple_of(y * (4 * WIDE) + (u - 12) * WIDE, WIDE), WIDE)]

class Gather:
    def __init__(self, place, own, sq, fi, fo, sems):
        self.p, self.own = place, own
        self.bufs = (sq, fi, fo)
        self.sems = sems
        self.made = []
    def piece(self, u, z, x, c, y):
        return unit_piece(*self.bufs, u, z, x, c, y)
    def go(self, u, slot, src, dst, dev):
        copy = remote(src, dst, self.sems[0].at[u, slot], self.sems[1].at[u, slot], dev)
        copy.start()
        self.made.append(copy)
        return copy
    def first(self, u):
        p = self.p
        mine = self.piece(u, p.z, p.x, p.c, p.y)
        self.zc = getattr(self, "zc", {})
        self.zc[u] = [self.go(u, k - 1, self.own.at[u], mine, p.at(z=(p.z + k) % 4)) for k in (1, 2, 3)]
    def even(self, u):
        return u % 2 == 0
    def second(self, u):
        p = self.p
        for copy in self.zc[u]:
            copy.wait_recv()
        here = self.piece(u, ALL, p.x, p.c, p.y)
        dev = p.at(x=1 - p.x) if self.even(u) else p.at(y=1 - p.y)
        self.sc = getattr(self, "sc", {})
        self.sc[u] = self.go(u, 3, here, here, dev)
    def third(self, u):
        p = self.p
        self.sc[u].wait_recv()
        self.tc = getattr(self, "tc", {})
        self.cc = getattr(self, "cc", {})
        if self.even(u):
            here = self.piece(u, ALL, ALL, p.c, p.y)
            self.tc[u] = [self.go(u, 4, here, here, p.at(y=1 - p.y))]
            self.cc[u] = [self.go(u, 6, here, here, p.at(c=1 - p.c))]
        else:
            here = [self.piece(u, ALL, p.x, p.c, y) for y in (0, 1)]
            self.tc[u] = [self.go(u, 4 + y, here[y], here[y], p.at(x=1 - p.x)) for y in (0, 1)]
            self.cc[u] = [self.go(u, 6 + y, here[y], here[y], p.at(c=1 - p.c)) for y in (0, 1)]
    def fourth(self, u):
        p = self.p
        for copy in self.tc[u]:
            copy.wait_recv()
        if self.even(u):
            here = self.piece(u, ALL, ALL, p.c, 1 - p.y)
            self.cc[u] += [self.go(u, 8, here, here, p.at(c=1 - p.c))]
        else:
            here = [self.piece(u, ALL, 1 - p.x, p.c, y) for y in (0, 1)]
            self.cc[u] += [self.go(u, 8 + y, here[y], here[y], p.at(c=1 - p.c)) for y in (0, 1)]
    def fifth(self, u):
        for copy in self.cc[u]:
            copy.wait_recv()
    def drain(self):
        for copy in self.made:
            copy.wait_send()

def ag_kernel(q_s, k_s, v_s, o_s, q_c, o_c, k_c, v_c, f_i, f_o, sq, fi, fo,
              xt, xf, land, landf, own, xsem, lsem, ssem, rsem):
    p = Place()
    barrier = pltpu.get_barrier_semaphore()
    peers = [p.at(z=(p.z + k) % 4) for k in (1, 2, 3)] + [p.at(x=1 - p.x), p.at(y=1 - p.y), p.at(c=1 - p.c)]
    for dev in peers:
        pl.semaphore_signal(barrier, inc=1, device_id=dev, device_id_type=MESH)
    e96 = eye(96)
    for m, ref in enumerate((k_c, v_c, q_s, k_s, v_s, o_s, q_c, o_c)):
        xt[m] = nt(e96, ref[...].astype(BF)).astype(BF).reshape(2, PIECE, 192)
    t = nt(eye(384), f_i[...].astype(BF)).astype(BF).reshape(2, 4, PIECE, 192)
    for s in range(4):
        for h in range(2):
            xt[8 + s, h] = t[h, s]
    xf[...] = nt(e96, f_o[...].astype(BF)).astype(BF).reshape(2, PIECE, 768)
    pl.semaphore_wait(barrier, len(peers))
    sib = p.at(c=1 - p.c)
    ex = [remote(xt.at[:, 1 - p.c], land, xsem.at[0], xsem.at[1], sib),
          remote(xf.at[1 - p.c], landf, xsem.at[2], xsem.at[3], sib)]
    for e in ex:
        e.start()
    ex[0].wait_recv()
    first = p.c == 0
    mine, other = xt[:, pl.ds(p.c, 1)].reshape(12, PIECE, 192), land[...]
    own[0:12] = jnp.concatenate([jnp.where(first, mine, other), jnp.where(first, other, mine)], axis=-1)
    ex[1].wait_recv()
    mine, other = xf[pl.ds(p.c, 1)].reshape(PIECE, 768), landf[...]
    lo, hi = jnp.where(first, mine, other), jnp.where(first, other, mine)
    own[12] = lo[:, :WIDE]
    own[13] = lo[:, WIDE:]
    own[14] = hi[:, :WIDE]
    own[15] = hi[:, WIDE:]
    g = Gather(p, own, sq, fi, fo, (ssem, rsem))
    local = []
    for u in range(UNITS):
        copy = pltpu.make_async_copy(own.at[u], g.piece(u, p.z, p.x, p.c, p.y), lsem.at[u])
        copy.start()
        local.append(copy)
        g.first(u)
    for u in range(UNITS):
        local[u].wait()
    for tick in range(UNITS + 4):
        if tick < UNITS:
            g.second(tick)
        if 0 <= tick - 1 < UNITS:
            g.third(tick - 1)
        if 0 <= tick - 2 < UNITS:
            g.fourth(tick - 2)
    for u in range(UNITS):
        g.fifth(u)
    g.drain()
    for e in ex:
        e.wait_send()

def gather(q_s, k_s, v_s, o_s, q_c, o_c, k_c, v_c, f_i, f_o):
    hbm = pl.BlockSpec(memory_space=pl.ANY)
    vm = pl.BlockSpec(memory_space=pltpu.VMEM)
    return pl.pallas_call(
        ag_kernel,
        out_shape=[jax.ShapeDtypeStruct((8, 4, 2, 2, PIECE, 768), BF),
                   jax.ShapeDtypeStruct((4, 2, 2, 4, PIECE, 768), BF),
                   jax.ShapeDtypeStruct((4, 2, 2, PIECE, 3072), BF)],
        in_specs=[vm] * 10,
        out_specs=[hbm] * 3,
        scratch_shapes=[pltpu.VMEM((12, 2, PIECE, 192), BF), pltpu.VMEM((2, PIECE, 768), BF),
                        pltpu.VMEM((12, PIECE, 192), BF), pltpu.VMEM((PIECE, 768), BF),
                        pltpu.VMEM((UNITS, PIECE, WIDE), BF),
                        pltpu.SemaphoreType.DMA((4,)), pltpu.SemaphoreType.DMA((UNITS,)),
                        pltpu.SemaphoreType.DMA((UNITS, 10)), pltpu.SemaphoreType.DMA((UNITS, 10))],
        compiler_params=pltpu.CompilerParams(collective_id=0, has_side_effects=True, vmem_limit_bytes=60*1024*1024),
        name="gather",
    )(q_s, k_s, v_s, o_s, q_c, o_c, k_c, v_c, f_i, f_o)


class Scatter:
    def __init__(self, place, parts, count, refs, sems):
        self.p, self.parts, self.count = place, parts, count
        self.land, self.acc, self.land1, self.land2, self.land3, self.fin = refs
        self.ssem, self.rsem, self.lsem = sems
        self.c = {}
        self.made = []
    def go(self, u, slot, src, dst, dev):
        copy = remote(src, dst, self.ssem.at[u, slot], self.rsem.at[u, slot], dev)
        copy.start()
        self.made.append(copy)
        self.c.setdefault(u, {})[slot] = copy
    def wait(self, u, slots):
        for s in slots:
            self.c[u][s].wait_recv()
    def r0(self, u):
        p = self.p
        self.c.setdefault(u, {})["l"] = []
        for y in (0, 1):
            self.go(u, y, self.parts(u, 1 - p.c, y), self.land.at[u, y], p.at(c=1 - p.c))
            copy = pltpu.make_async_copy(self.parts(u, p.c, y), self.acc.at[u, y], self.lsem.at[u, y])
            copy.start()
            self.c[u]["l"].append(copy)
    def r1(self, u):
        p = self.p
        self.wait(u, (0, 1))
        for copy in self.c[u]["l"]:
            copy.wait()
        if u % 2 == 0:
            other, own = pl.ds(1 - p.y, 1), pl.ds(p.y, 1)
            self.acc[u, other] = self.acc[u, other] + self.land[u, other]
            self.go(u, 2, self.acc.at[u, 1 - p.y], self.land1.at[u], p.at(y=1 - p.y))
            self.acc[u, own] = self.acc[u, own] + self.land[u, own]
        else:
            for y in (0, 1):
                self.acc[u, y] = self.acc[u, y] + self.land[u, y]
                self.go(u, 2 + y, self.acc.at[u, y, :, 1 - p.x], self.land1.at[u, :, y], p.at(x=1 - p.x))
    def r2(self, u):
        p = self.p
        if u % 2 == 0:
            self.wait(u, (2,))
            own = pl.ds(p.y, 1)
            self.acc[u, own] = self.acc[u, own] + self.land1[u][None]
            self.go(u, 4, self.acc.at[u, p.y, :, 1 - p.x], self.land2.at[u], p.at(x=1 - p.x))
        else:
            self.wait(u, (2, 3))
            x = pl.ds(p.x, 1)
            for y in (0, 1):
                self.acc[u, y, :, x] = self.acc[u, y, :, x] + self.land1[u, :, y][:, None]
            self.go(u, 4, self.acc.at[u, 1 - p.y, :, p.x], self.land2.at[u], p.at(y=1 - p.y))
    def r3(self, u):
        p = self.p
        self.wait(u, (4,))
        y, x = pl.ds(p.y, 1), pl.ds(p.x, 1)
        self.acc[u, y, :, x] = self.acc[u, y, :, x] + self.land2[u][None, :, None]
        for k in (1, 2, 3):
            z = (p.z + k) % 4
            self.go(u, 4 + k, self.acc.at[u, p.y, z, p.x], self.land3.at[u, k - 1], p.at(z=z))
    def r4(self, u):
        p = self.p
        self.wait(u, (5, 6, 7))
        total = self.acc[u, pl.ds(p.y, 1), pl.ds(p.z, 1), pl.ds(p.x, 1)].reshape(PIECE, WIDE).astype(F32)
        for k in range(3):
            total = total + self.land3[u, k].astype(F32)
        self.fin[u] = total.astype(BF)
    def drain(self):
        for copy in self.made:
            copy.wait_send()

def scatter_scratch(count):
    return [pltpu.VMEM((count, 2, 4, 2, PIECE, WIDE), BF), pltpu.VMEM((count, 2, 4, 2, PIECE, WIDE), BF),
            pltpu.VMEM((count, 4, 2, PIECE, WIDE), BF), pltpu.VMEM((count, 4, PIECE, WIDE), BF),
            pltpu.VMEM((count, 3, PIECE, WIDE), BF), pltpu.VMEM((count, PIECE, WIDE), BF),
            pltpu.SemaphoreType.DMA((count, 8)), pltpu.SemaphoreType.DMA((count, 8)), pltpu.SemaphoreType.DMA((count, 2))]

def rs_kernel(sq, fi, fo, *rest):
    outs, scr = rest[:10], rest[10:]
    refs, sems = scr[:6], scr[6:9]
    give, take, giveo, takeo, xsem = scr[9:]
    p = Place()
    barrier = pltpu.get_barrier_semaphore()
    peers = [p.at(z=(p.z + k) % 4) for k in (1, 2, 3)] + [p.at(x=1 - p.x), p.at(y=1 - p.y), p.at(c=1 - p.c)]
    for dev in peers:
        pl.semaphore_signal(barrier, inc=1, device_id=dev, device_id_type=MESH)
    pl.semaphore_wait(barrier, len(peers))
    def parts(u, c, y):
        if u < 8:
            return sq.at[u, :, :, c, :, y * WIDE:(y + 1) * WIDE]
        if u < 12:
            return fi.at[:, :, c, u - 8, :, y * WIDE:(y + 1) * WIDE]
        return fo.at[:, :, c, :, y * 4 * WIDE + (u - 12) * WIDE:y * 4 * WIDE + (u - 11) * WIDE]
    s = Scatter(p, parts, 16, refs, sems)
    P2 = 8
    for t in range(P2 + 4):
        for step, f in ((4, s.r4), (3, s.r3), (2, s.r2), (1, s.r1), (0, s.r0)):
            if 0 <= t - step < P2:
                for u in (2 * (t - step), 2 * (t - step) + 1):
                    f(u)
    fin = refs[5]
    first = p.c == 0
    def trade(lo, n):
        low, high = fin[lo:lo + n, :, :192], fin[lo:lo + n, :, 192:]
        give[lo:lo + n] = jnp.where(first, high, low)
        return jnp.where(first, low, high)
    mine = trade(0, 12)
    sib = p.at(c=1 - p.c)
    giveo[...] = fin[pl.ds(12 + 2 * (1 - p.c), 2)]
    ex = [remote(give, take, xsem.at[0], xsem.at[1], sib), remote(giveo, takeo, xsem.at[2], xsem.at[3], sib)]
    for e in ex: e.start()
    ex[0].wait_recv()
    e192 = eye(192)
    def both(a, b):
        return jnp.concatenate([jnp.where(first, a, b), jnp.where(first, b, a)], axis=0)
    for m in range(8):
        outs[m][...] = nt(e192, both(mine[m], take[m]))
    t = both(mine[8:12].reshape(192, 192), take[8:12].reshape(192, 192))
    outs[8][...] = nt(e192, t)
    ex[1].wait_recv()
    own = fin[pl.ds(12 + 2 * p.c, 2)]
    t = both(jnp.concatenate([own[0], own[1]], axis=1), jnp.concatenate([takeo[0], takeo[1]], axis=1))
    e768 = eye(WIDE)
    outs[9][0:WIDE] = nt(e768, t[:, :WIDE])
    outs[9][WIDE:] = nt(e768, t[:, WIDE:])
    s.drain()
    for e in ex: e.wait_send()

def scatter(sq, fi, fo):
    hbm = pl.BlockSpec(memory_space=pl.ANY)
    vm = pl.BlockSpec(memory_space=pltpu.VMEM)
    return pl.pallas_call(
        rs_kernel,
        out_shape=[jax.ShapeDtypeStruct((192, 96), F32)] * 8 + [jax.ShapeDtypeStruct((192, 384), F32), jax.ShapeDtypeStruct((768, 96), F32)],
        in_specs=[hbm] * 3, out_specs=[vm] * 10,
        scratch_shapes=scatter_scratch(16) + [pltpu.VMEM((12, PIECE, 192), BF), pltpu.VMEM((12, PIECE, 192), BF),
            pltpu.VMEM((2, PIECE, WIDE), BF), pltpu.VMEM((2, PIECE, WIDE), BF), pltpu.SemaphoreType.DMA((4,))],
        compiler_params=pltpu.CompilerParams(collective_id=1, has_side_effects=True, vmem_limit_bytes=60*1024*1024),
        name="scatter",
    )(sq, fi, fo)


def whole():
    return pl.BlockSpec(memory_space=pltpu.VMEM)


def call(kernel, outs, scratch, args, specs=None, grid=None, out_specs=None, name=None, flops=0):
    specs = specs or [whole()] * len(args)
    out_specs = out_specs or [whole()] * len(outs)
    return pl.pallas_call(
        kernel,
        grid=grid or (),
        in_specs=specs,
        out_specs=out_specs,
        out_shape=[jax.ShapeDtypeStruct(shape, kind) for shape, kind in outs],
        scratch_shapes=[pltpu.VMEM(shape, kind) for shape, kind in scratch],
        compiler_params=pltpu.CompilerParams(vmem_limit_bytes=VMEM_LIMIT),
        cost_estimate=pl.CostEstimate(flops=flops, bytes_accessed=20_000_000, transcendentals=0),
        name=name,
    )(*args)


def body(custom, decoder_in, encoder_out, decoder_lengths, encoder_lengths, norm_gains, rel_table,
         query_self, key_self, value_self, out_self, query_cross, key_cross, value_cross, out_cross,
         feed_in, feed_out, upstream):
    rows, width = decoder_in.shape
    row_count, examples = decoder_lengths.shape
    keys_n = encoder_out.shape[1]

    if custom:
        sq, fi, fo = gather(query_self, key_self, value_self, out_self, query_cross, out_cross, key_cross,
                            value_cross, feed_in, feed_out)
        sq, fi, fo = sq.reshape(8, width, width), fi.reshape(-1, width), fo.reshape(width, -1)
    else:
        order = (key_cross, value_cross, query_self, key_self, value_self, out_self, query_cross, out_cross)
        sq = jnp.stack([m.astype(BF).T for m in order])
        sq = lax.all_gather(sq, "fsdp", axis=1, tiled=True)
        sq = lax.all_gather(sq, "dp", axis=2, tiled=True)
        fi = lax.all_gather(feed_in.astype(BF).T, "fsdp", axis=0, tiled=True)
        fi = lax.all_gather(fi, "dp", axis=1, tiled=True)
        fo = lax.all_gather(feed_out.astype(BF).T, "fsdp", axis=0, tiled=True)
        fo = lax.all_gather(fo, "dp", axis=1, tiled=True)
    w_kv, w_five, w_oc = sq[0:2], sq[2:7], sq[7:8]
    gains = lax.all_gather(norm_gains.astype(BF), "fsdp", axis=1, tiled=True).astype(F32)
    table = lax.all_gather(rel_table.astype(BF), "dp", axis=0, tiled=True).astype(F32)

    places = jnp.arange(rows, dtype=jnp.int32)
    ends = jnp.cumsum(decoder_lengths[0], dtype=jnp.int32)
    segment = jnp.sum((places[:, None] >= ends[None, :]).astype(jnp.int32), axis=-1)
    starts = ends - decoder_lengths[0]
    offset = places - jnp.sum(
        jnp.where(segment[:, None] == jnp.arange(examples)[None, :], starts[None, :], 0), axis=-1
    )
    seg_col = segment[:, None]
    seg_row = segment[None, :]
    off_row = offset[None, :]
    seg_band = jnp.concatenate([jnp.full((1, MOST), -1, jnp.int32), seg_row], axis=1)
    valid = jnp.where(
        jnp.arange(keys_n, dtype=jnp.int32)[None, :] < encoder_lengths[:, None], 0.0, HIDDEN_SCORE
    )
    hot = distance_hot()
    dist = jnp.dot(hot, table, precision=lax.Precision.HIGHEST).T

    small = (rows, width)
    n1, q1, k1, v1, a1, h1, n2, q2 = call(
        front_kernel,
        [(small, BF), (small, BF), ((rows + MOST, width), BF), ((rows + MOST, width), BF), (small, BF),
         (small, F32), (small, BF), (small, BF)],
        [((rows // MOST, MOST, 2 * MOST), F32)],
        (decoder_in, gains, dist, seg_col, seg_band, w_five),
        specs=[whole()] * 6,
        grid=(1,),
        name="front",
    )
    enc = encoder_out.reshape(-1, width)
    per_example = pl.BlockSpec((keys_n, width), lambda e: (e, 0))
    k2, v2, a2 = call(
        cross_kernel,
        [(enc.shape, BF), (enc.shape, BF), (small, BF)],
        [((MOST, width), BF), ((MOST, width), BF), (small, F32)],
        (enc, q2, seg_row, off_row, valid, w_kv),
        specs=[per_example] + [whole()] * 5,
        out_specs=[per_example, per_example, whole()],
        grid=(examples,),
        name="cross",
    )
    out, dwin, dwout, dwoc, da2, dh2, gain3 = call(
        feed_kernel,
        [(small, BF), (fi.shape, BF), (fo.shape, BF), ((width, width), BF), (small, BF), (small, F32),
         ((1, width), F32)],
        [(small, F32), (small, BF), (small, F32), (small, F32)],
        (a2, h1, upstream, gains, w_oc, fi, fo),
        specs=[whole()] * 7,
        grid=(1,),
        name="feed",
    )
    denc, dq2, dw_kv = call(
        cross_back_kernel,
        [(enc.shape, BF), (small, BF), ((2, width, width), BF)],
        [((MOST, width), BF), ((MOST, width), BF), ((MOST, width), BF), ((keys_n, width), BF),
         ((keys_n, width), BF), (small, F32), ((2, width, width), F32)],
        (enc, k2, v2, q2, da2, seg_row, off_row, valid, w_kv),
        specs=[per_example] * 3 + [whole()] * 6,
        out_specs=[per_example, whole(), whole()],
        grid=(examples,),
        name="cross_back",
    )
    dx, dw_five, gain12, dist_sum = call(
        self_back_kernel,
        [(small, BF), ((5, width, width), BF), ((2, width), F32), ((HEADS, 2 * MOST), F32)],
        [((rows // MOST, MOST, 2 * MOST), F32), (small, F32), (small, BF), (small, BF), (small, BF),
         (small, BF), (small, BF), ((rows + MOST, 128), F32), ((rows + MOST, 128), F32), (small, F32)],
        (dq2, n2, h1, dh2, decoder_in, n1, q1, k1, v1, a1, gains, dist, seg_col, seg_band, w_five),
        specs=[whole()] * 15,
        grid=(1,),
        name="self_back",
    )

    dsq = jnp.concatenate([dw_kv, dw_five, dwoc[None]], axis=0)
    if custom:
        parts = scatter(dsq.reshape(8, 4, 2, 2, PIECE, width), dwin.reshape(4, 2, 2, 4, PIECE, width),
                        dwout.reshape(4, 2, 2, PIECE, -1))
    else:
        dsq = lax.psum_scatter(dsq, "dp", scatter_dimension=2, tiled=True)
        dsq = lax.psum_scatter(dsq, "fsdp", scatter_dimension=1, tiled=True).astype(F32)
        dwin = lax.psum_scatter(dwin, "dp", scatter_dimension=1, tiled=True)
        dwin = lax.psum_scatter(dwin, "fsdp", scatter_dimension=0, tiled=True)
        dwout = lax.psum_scatter(dwout, "dp", scatter_dimension=1, tiled=True)
        dwout = lax.psum_scatter(dwout, "fsdp", scatter_dimension=0, tiled=True)
        parts = [dsq[i].T for i in range(8)] + [dwin.astype(F32).T, dwout.astype(F32).T]
    k_c, v_c, q_s, k_s, v_s, o_s, q_c, o_c, f_i, f_o = parts
    gains_delta = lax.psum(jnp.concatenate([gain12, gain3], axis=0), "dp")
    gains_delta = lax.psum_scatter(gains_delta, "fsdp", scatter_dimension=1, tiled=True)
    table_delta = jnp.dot(dist_sum, hot, precision=lax.Precision.HIGHEST).T
    table_delta = lax.psum_scatter(table_delta, "dp", scatter_dimension=0, tiled=True)
    table_delta = lax.psum(table_delta, "fsdp")
    return (out, dx, denc.reshape(encoder_out.shape), gains_delta, table_delta,
            q_s, k_s, v_s, o_s, q_c, k_c, v_c, o_c, f_i, f_o)


def solution(mesh):
    tokens = P(("dp", "fsdp"), None)
    weight = P("dp", "fsdp")
    return jax.shard_map(
        functools.partial(body, (mesh.shape["dp"], mesh.shape["fsdp"]) == (4, 8)),
        mesh=mesh,
        in_specs=(tokens, P(("dp", "fsdp"), None, None), tokens, P(("dp", "fsdp")), P(None, "fsdp"),
                  P("dp", None)) + (weight,) * 10 + (tokens,),
        out_specs=(tokens, tokens, P(("dp", "fsdp"), None, None), P(None, "fsdp"), P("dp", None))
        + (weight,) * 10,
        check_vma=False,
    )
```

```python
import functools
import math
import types

import jax
import jax.numpy as jnp
from jax import lax
from jax.experimental import pallas as pl
from jax.experimental.pallas import tpu as pltpu
from jax.sharding import PartitionSpec as P

HEADS = 12
HEAD_DIM = 64
BUCKETS = 32
MAX_DIST = 128
MOST = 128
PAIRS = HEADS // 2
EPSILON = 1e-06
HIDDEN_SCORE = -1e30
BF = jnp.bfloat16
F32 = jnp.float32
VMEM_LIMIT = 60 * 1024 * 1024


def nn(a, b):
    return lax.dot_general(a, b, (((1,), (0,)), ((), ())), preferred_element_type=F32)


def nt(a, b):
    return lax.dot_general(a, b, (((1,), (1,)), ((), ())), preferred_element_type=F32)


def tn(a, b):
    return lax.dot_general(a, b, (((0,), (0,)), ((), ())), preferred_element_type=F32)


def rms(z, gain):
    factor = lax.rsqrt(jnp.mean(z * z, axis=-1, keepdims=True) + EPSILON)
    return z * factor * gain


def rms_back(z, gain, dy):
    factor = lax.rsqrt(jnp.mean(z * z, axis=-1, keepdims=True) + EPSILON)
    wdy = dy * gain
    inner = jnp.mean(z * wdy, axis=-1, keepdims=True)
    dz = factor * wdy - z * (factor * factor * factor * inner)
    return dz, jnp.sum(dy * z * factor, axis=0, keepdims=True)


def split_heads(rows):
    first = lax.broadcasted_iota(jnp.int32, rows.shape, 1) < HEAD_DIM
    zero = jnp.zeros_like(rows)
    return jnp.concatenate([jnp.where(first, rows, zero), jnp.where(first, zero, rows)], axis=0)


def join_heads(rows):
    half = rows.shape[0] // 2
    first = lax.broadcasted_iota(jnp.int32, (half, rows.shape[1]), 1) < HEAD_DIM
    return jnp.where(first, rows[:half], rows[half:])


def softmax(scores):
    raised = jnp.exp(scores - jnp.max(scores, axis=-1, keepdims=True))
    return raised * (1.0 / jnp.sum(raised, axis=-1, keepdims=True))


def lanes(index, width):
    return pl.ds(pl.multiple_of(index * width, width), width)


def loop(low, high, step):
    def run(index, carry):
        step(index)
        return carry

    lax.fori_loop(low, high, run, 0)


def bucket_of(distance):
    half_count = BUCKETS // 2
    counted = jnp.zeros_like(distance)
    for section_index in range(1, half_count):
        edge_at = int(
            math.ceil(half_count * (MAX_DIST / half_count) ** (section_index / half_count))
        )
        counted = counted + (distance >= edge_at).astype(jnp.int32)
    return jnp.where(distance < half_count, distance, half_count + counted)


def distance_hot():
    distance = jnp.maximum(MOST - jnp.arange(2 * MOST, dtype=jnp.int32), 0)
    return (bucket_of(distance)[:, None] == jnp.arange(BUCKETS, dtype=jnp.int32)[None, :]).astype(F32)


def local(src, dst, sem):
    return pltpu.make_async_copy(src, dst, sem)


def w_rows(ref, m, j):
    return ref[m, pl.ds(2 * j, 2)].reshape(2 * WIDE // 2, ref.shape[-1])


def w_lanes(ref, m, at):
    part = ref[m, :, :, :, :, at]
    return part.reshape(-1, part.shape[-1])


MESH = pl.DeviceIdType.MESH
PIECE = 48
WIDE = 384
UNITS = 16
ALL = slice(None)


class Place:
    def __init__(self):
        self.d, self.f = lax.axis_index("dp"), lax.axis_index("fsdp")
        self.y, self.c = self.d // 2, self.d % 2
        self.z, self.x = self.f // 2, self.f % 2

    def at(self, z=None, x=None, y=None, c=None):
        z = self.z if z is None else z
        x = self.x if x is None else x
        y = self.y if y is None else y
        c = self.c if c is None else c
        return (y * 2 + c, z * 2 + x)

    def near(self):
        others = [self.at(z=(self.z + k) % 4) for k in (1, 2, 3)]
        return others + [self.at(x=1 - self.x), self.at(y=1 - self.y), self.at(c=1 - self.c)]


def greet(peers):
    barrier = pltpu.get_barrier_semaphore()
    for dev in peers:
        pl.semaphore_signal(barrier, inc=1, device_id=dev, device_id_type=MESH)
    pl.semaphore_wait(barrier, len(peers))


def eye(n):
    a = lax.broadcasted_iota(jnp.int32, (n, n), 0)
    b = lax.broadcasted_iota(jnp.int32, (n, n), 1)
    return (a == b).astype(F32).astype(BF)


def remote(src, dst, send, recv, dev):
    return pltpu.make_async_remote_copy(
        src_ref=src, dst_ref=dst, send_sem=send, recv_sem=recv, device_id=dev, device_id_type=MESH
    )


class Sends:
    def __init__(self, place, ssem, rsem):
        self.p, self.ssem, self.rsem, self.made = place, ssem, rsem, {}

    def to_x(self):
        return self.p.at(x=1 - self.p.x)

    def to_y(self):
        return self.p.at(y=1 - self.p.y)

    def to_c(self):
        return self.p.at(c=1 - self.p.c)

    def go(self, u, slot, src, dst, dev):
        def make():
            return remote(src(), dst(), self.ssem.at[u, slot], self.rsem.at[u, slot], dev())

        make().start()
        self.made[u, slot] = make

    def wait(self, u, *slots):
        for slot in slots:
            self.made[u, slot]().wait_recv()

    def drain(self):
        for make in self.made.values():
            make().wait_send()


class Gather(Sends):
    def __init__(self, place, own, sq, fi, fo, ssem, rsem):
        super().__init__(place, ssem, rsem)
        self.own, self.sq, self.fi, self.fo = own, sq, fi, fo

    def piece(self, u, z, x, c, y):
        if u < 8:
            return self.sq.at[u, z, x, c, :, pl.ds(pl.multiple_of(y * WIDE, WIDE), WIDE)]
        if u < 12:
            return self.fi.at[z, x, c, u - 8, :, pl.ds(pl.multiple_of(y * WIDE, WIDE), WIDE)]
        at = y * (4 * WIDE) + (u - 12) * WIDE
        return self.fo.at[z, x, c, :, pl.ds(pl.multiple_of(at, WIDE), WIDE)]

    def same(self, u, slot, dev, z, x, c, y):
        def here():
            return self.piece(u, z, x, c, y)

        self.go(u, slot, here, here, dev)

    def first(self, u):
        p = self.p
        for k in (1, 2, 3):
            self.go(
                u, k - 1, lambda: self.own.at[u], lambda: self.piece(u, p.z, p.x, p.c, p.y),
                lambda k=k: p.at(z=(p.z + k) % 4),
            )

    def second(self, u):
        p = self.p
        self.wait(u, 0, 1, 2)
        self.same(u, 3, self.to_x if u % 2 == 0 else self.to_y, ALL, p.x, p.c, p.y)

    def third(self, u):
        p = self.p
        self.wait(u, 3)
        if u % 2 == 0:
            self.same(u, 4, self.to_y, ALL, ALL, p.c, p.y)
            self.same(u, 6, self.to_c, ALL, ALL, p.c, p.y)
        else:
            for y in (0, 1):
                self.same(u, 4 + y, self.to_x, ALL, p.x, p.c, y)
            for y in (0, 1):
                self.same(u, 6 + y, self.to_c, ALL, p.x, p.c, y)

    def fourth(self, u):
        p = self.p
        if u % 2 == 0:
            self.wait(u, 4)
            self.same(u, 8, self.to_c, ALL, ALL, p.c, 1 - p.y)
        else:
            self.wait(u, 4, 5)
            for y in (0, 1):
                self.same(u, 8 + y, self.to_c, ALL, 1 - p.x, p.c, y)

    def fifth(self, u):
        self.wait(u, *((6, 8) if u % 2 == 0 else (6, 7, 8, 9)))

    def tick(self, t):
        for step, act in ((2, self.fourth), (1, self.third), (0, self.second)):
            if 0 <= t - step < UNITS // 2:
                act(2 * (t - step))
                act(2 * (t - step) + 1)


class Scatter(Sends):
    def __init__(self, place, parts, r):
        super().__init__(place, r.ssem, r.rsem)
        self.parts, self.r = parts, r

    def halves(self, u):
        p, r = self.p, self.r
        return [local(self.parts(u, p.c, y), r.acc.at[u, y], r.lsem.at[u, y]) for y in (0, 1)]

    def r0(self, u):
        p, r = self.p, self.r
        for y in (0, 1):
            self.go(
                u, y, lambda y=y: self.parts(u, 1 - p.c, y), lambda y=y: r.land.at[u, y], self.to_c
            )
        for copy in self.halves(u):
            copy.start()

    def r1(self, u):
        p, r = self.p, self.r
        self.wait(u, 0, 1)
        for copy in self.halves(u):
            copy.wait()
        if u % 2 == 0:
            other, own = pl.ds(1 - p.y, 1), pl.ds(p.y, 1)
            r.acc[u, other] = r.acc[u, other] + r.land[u, other]
            self.go(u, 2, lambda: r.acc.at[u, 1 - p.y], lambda: r.land1.at[u], self.to_y)
            r.acc[u, own] = r.acc[u, own] + r.land[u, own]
        else:
            for y in (0, 1):
                r.acc[u, y] = r.acc[u, y] + r.land[u, y]
                self.go(
                    u, 2 + y, lambda y=y: r.acc.at[u, y, :, 1 - p.x], lambda y=y: r.land1.at[u, :, y],
                    self.to_x,
                )

    def r2(self, u):
        p, r = self.p, self.r
        if u % 2 == 0:
            self.wait(u, 2)
            own = pl.ds(p.y, 1)
            r.acc[u, own] = r.acc[u, own] + r.land1[u][None]
            self.go(
                u, 4, lambda: r.acc.at[u, p.y, :, 1 - p.x], lambda: r.land2.at[u], self.to_x
            )
        else:
            self.wait(u, 2, 3)
            x = pl.ds(p.x, 1)
            for y in (0, 1):
                r.acc[u, y, :, x] = r.acc[u, y, :, x] + r.land1[u, :, y][:, None]
            self.go(
                u, 4, lambda: r.acc.at[u, 1 - p.y, :, p.x], lambda: r.land2.at[u], self.to_y
            )

    def r3(self, u):
        p, r = self.p, self.r
        self.wait(u, 4)
        y, x = pl.ds(p.y, 1), pl.ds(p.x, 1)
        r.acc[u, y, :, x] = r.acc[u, y, :, x] + r.land2[u][None, :, None]
        for k in (1, 2, 3):
            self.go(
                u, 4 + k, lambda k=k: r.acc.at[u, p.y, (p.z + k) % 4, p.x],
                lambda k=k: r.land3.at[u, k - 1], lambda k=k: p.at(z=(p.z + k) % 4),
            )

    def r4(self, u):
        p, r = self.p, self.r
        self.wait(u, 5, 6, 7)
        part = r.acc[u, pl.ds(p.y, 1), pl.ds(p.z, 1), pl.ds(p.x, 1)]
        total = part.reshape(PIECE, WIDE).astype(F32)
        for k in range(3):
            total = total + r.land3[u, k].astype(F32)
        r.fin[u] = total.astype(BF)

    def step(self, number, *units):
        act = (self.r0, self.r1, self.r2, self.r3, self.r4)[number]
        for u in units:
            act(u)


def scatter_scratch(count):
    return dict(
        land=pltpu.VMEM((count, 2, 4, 2, PIECE, WIDE), BF),
        acc=pltpu.VMEM((count, 2, 4, 2, PIECE, WIDE), BF),
        land1=pltpu.VMEM((count, 4, 2, PIECE, WIDE), BF),
        land2=pltpu.VMEM((count, 4, PIECE, WIDE), BF),
        land3=pltpu.VMEM((count, 3, PIECE, WIDE), BF),
        ssem=pltpu.SemaphoreType.DMA((count, 8)),
        rsem=pltpu.SemaphoreType.DMA((count, 8)),
        lsem=pltpu.SemaphoreType.DMA((count, 2)),
    )


def self_masks(seg_col, seg_row, mask_ref):
    blocks = mask_ref.shape[0]
    a = lax.broadcasted_iota(jnp.int32, (MOST, 2 * MOST), 0)
    b = lax.broadcasted_iota(jnp.int32, (MOST, 2 * MOST), 1)
    causal = b <= a + MOST
    for i in range(blocks):
        same = seg_col[MOST * i : MOST * (i + 1), :] == seg_row[:, MOST * i : MOST * (i + 2)]
        mask_ref[i] = jnp.where(causal & same, 0.0, HIDDEN_SCORE)


def pair_bias(dist_ref, pair):
    parts = []
    for h in range(2):
        row = dist_ref[pl.ds(2 * pair + h, 1), :]
        parts.append(
            pltpu.roll(jnp.broadcast_to(row, (MOST, 2 * MOST)), 0, 1, stride=1, stride_axis=0)
        )
    return jnp.concatenate(parts, axis=0)


def masked_scores(scores, bias, mask):
    both = scores + bias
    return (both.reshape(2, MOST, 2 * MOST) + mask[None]).reshape(2 * MOST, 2 * MOST)


def example_rows(segr_ref, offr_ref, example, total):
    place = lax.broadcasted_iota(jnp.int32, (MOST, total), 0)
    return ((segr_ref[...] == example) & (offr_ref[...] == place)).astype(F32).astype(BF)


def spread_shards(p, r):
    e96 = eye(96)
    shards = (r.k_c, r.v_c, r.q_s, r.k_s, r.v_s, r.o_s, r.q_c, r.o_c)
    for m, ref in enumerate(shards):
        r.xt[m] = nt(e96, ref[...].astype(BF)).astype(BF).reshape(2, PIECE, 192)
    t = nt(eye(384), r.f_i[...].astype(BF)).astype(BF).reshape(2, 4, PIECE, 192)
    for s in range(4):
        for h in range(2):
            r.xt[8 + s, h] = t[h, s]
    r.xf[...] = nt(e96, r.f_o[...].astype(BF)).astype(BF).reshape(2, PIECE, 768)


def small_sends(p, r):
    made = []
    for k in range(1, 8):
        dev = (p.d, (p.f + k) % 8)
        made.append(
            remote(r.gt.at[p.f], r.gt.at[p.f], r.smsem.at[0, k - 1], r.smsem.at[1, k - 1], dev)
        )
    for k in range(1, 4):
        dev = ((p.d + k) % 4, p.f)
        made.append(
            remote(r.tt.at[p.d], r.tt.at[p.d], r.smsem.at[0, 6 + k], r.smsem.at[1, 6 + k], dev)
        )
    return made


def forward_kernel(comm, r):
    rows, width = r.x.shape
    examples, keys_n = r.valid.shape
    blocks = rows // MOST
    enc_copies = [local(r.enc.at[e], r.encv.at[e], r.esem.at[e]) for e in range(examples)]
    for copy in enc_copies:
        copy.start()

    if comm:
        p = Place()
        peers = [(p.d, (p.f + k) % 8) for k in range(1, 8)] + [((p.d + k) % 4, p.f) for k in range(1, 4)]
        r.gt[pl.ds(p.f, 1)] = jnp.zeros((1, 8, 128), F32)
        r.gt[pl.ds(p.f, 1), 0:3, 0:96] = r.gains_s[...].astype(BF).astype(F32)[None]
        r.tt[pl.ds(p.d, 1)] = jnp.zeros((1, 8, 128), F32)
        r.tt[pl.ds(p.d, 1), :, 0:HEADS] = r.table_s[...].astype(BF).astype(F32)[None]
        spread_shards(p, r)
        greet(peers)
        sib = p.at(c=1 - p.c)
        trade = [
            remote(r.xt.at[:, 1 - p.c], r.took, r.xsem.at[0], r.xsem.at[1], sib),
            remote(r.xf.at[1 - p.c], r.tookf, r.xsem.at[2], r.xsem.at[3], sib),
        ]
        small = small_sends(p, r)
        for copy in trade + small:
            copy.start()
        first = p.c == 0
        trade[0].wait_recv()
        mine, other = r.xt[:, pl.ds(p.c, 1)].reshape(12, PIECE, 192), r.took[...]
        r.own[0:12] = jnp.concatenate(
            [jnp.where(first, mine, other), jnp.where(first, other, mine)], axis=-1
        )
        trade[1].wait_recv()
        mine, other = r.xf[pl.ds(p.c, 1)].reshape(PIECE, 768), r.tookf[...]
        low, high = jnp.where(first, mine, other), jnp.where(first, other, mine)
        r.own[12], r.own[13] = low[:, :WIDE], low[:, WIDE:]
        r.own[14], r.own[15] = high[:, :WIDE], high[:, WIDE:]
        g = Gather(p, r.own, r.sq, r.fi, r.fo, r.ssem, r.rsem)
        placed = [
            local(r.own.at[u], g.piece(u, p.z, p.x, p.c, p.y), r.psem.at[u]) for u in range(UNITS)
        ]
        for u in range(UNITS):
            g.first(u)
            placed[u].start()
        for copy in small:
            copy.wait_recv()
        spot = lax.broadcasted_iota(jnp.int32, (128, width), 1)
        lane = lax.broadcasted_iota(jnp.int32, (128, width), 0)
        gains = jnp.zeros((8, width), F32)
        for f in range(8):
            put = ((spot == lane + 96 * f) & (lane < 96)).astype(F32).astype(BF)
            gains = gains + nn(r.gt[f].astype(BF), put)
        r.gains[...] = gains[0:3]
        table = r.tt[...].reshape(BUCKETS, 128).astype(BF)
        r.dist[...] = tn(table, r.hot[...].astype(BF))[0:HEADS]
        for copy in placed:
            copy.wait()
        tick, arrived = g.tick, g.fifth
    else:
        tick = arrived = lambda index: None

    loads = [local(r.sq.at[m], r.wv.at[m], r.wsem.at[m]) for m in range(7)]

    def fetch(*which):
        for m in which:
            arrived(m)
            loads[m].start()

    def have(*which):
        for m in which:
            loads[m].wait()

    r.n1[...] = rms(r.x[...].astype(F32), r.gains[0:1, :]).astype(BF)
    r.k1[0:MOST, :] = jnp.zeros((MOST, width), BF)
    r.v1[0:MOST, :] = jnp.zeros((MOST, width), BF)
    self_masks(r.seg_col[...], r.seg_band[...], r.mask)
    halves = width // WIDE

    def save(e):
        return [local(r.k2v.at[e], r.k2.at[e], r.ksem.at[e, 0]), local(r.v2v.at[e], r.v2.at[e], r.ksem.at[e, 1])]

    def project(e):
        local(r.enc.at[e], r.encv.at[e], r.esem.at[e]).wait()
        for j in range(halves):
            at = slice(WIDE * j, WIDE * (j + 1))
            r.k2v[e, :, at] = nt(r.encv[e], w_rows(r.wv, 0, j)).astype(BF)
            r.v2v[e, :, at] = nt(r.encv[e], w_rows(r.wv, 1, j)).astype(BF)
        for copy in save(e):
            copy.start()

    tick(0)
    tick(1)
    tick(2)
    fetch(0, 1)
    have(0, 1)
    loop(0, examples // 2, project)
    tick(3)
    fetch(2, 3)
    loop(examples // 2, examples, project)
    tick(4)
    fetch(4, 5)
    have(2, 3, 4)

    for j in range(halves):
        at = slice(WIDE * j, WIDE * (j + 1))
        r.q1[:, at] = nt(r.n1[...], w_rows(r.wv, 2, j)).astype(BF)
        r.k1[MOST:, at] = nt(r.n1[...], w_rows(r.wv, 3, j)).astype(BF)
        r.v1[MOST:, at] = nt(r.n1[...], w_rows(r.wv, 4, j)).astype(BF)

    def attend(pair):
        at = lanes(pair, 128)
        bias = pair_bias(r.dist, pair)
        for i in range(blocks):
            queries = split_heads(r.q1[MOST * i : MOST * (i + 1), at])
            keys = r.k1[MOST * i : MOST * (i + 2), at]
            values = r.v1[MOST * i : MOST * (i + 2), at]
            probs = softmax(masked_scores(nt(queries, keys), bias, r.mask[i])).astype(BF)
            r.a1[MOST * i : MOST * (i + 1), at] = join_heads(nn(probs, values)).astype(BF)

    loop(0, PAIRS // 2, attend)
    tick(5)
    fetch(6)
    loop(PAIRS // 2, PAIRS, attend)
    have(5, 6)
    for j in range(halves):
        at = slice(WIDE * j, WIDE * (j + 1))
        r.h1[:, at] = r.x[:, at].astype(F32) + nt(r.a1[...], w_rows(r.wv, 5, j))
    r.n2[...] = rms(r.h1[...], r.gains[1:2, :]).astype(BF)
    for j in range(halves):
        at = slice(WIDE * j, WIDE * (j + 1))
        r.q2[:, at] = nt(r.n2[...], w_rows(r.wv, 6, j)).astype(BF)

    r.sum[...] = jnp.zeros_like(r.sum)

    def cross(e):
        pick = example_rows(r.seg_row, r.off_row, e, rows)
        r.qe[...] = nn(pick, r.q2[...]).astype(BF)
        hidden = r.valid[pl.ds(e, 1), :]

        def pair_step(pair):
            at = lanes(pair, 128)
            probs = softmax(nt(split_heads(r.qe[:, at]), r.k2v[e, :, at]) + hidden).astype(BF)
            r.ae[:, at] = join_heads(nn(probs, r.v2v[e, :, at])).astype(BF)

        loop(0, PAIRS, pair_step)
        r.sum[...] += tn(pick, r.ae[...])

    tick(6)
    loop(0, 3, cross)
    tick(7)
    loop(3, 6, cross)
    tick(8)
    loop(6, examples, cross)
    r.a2[...] = r.sum[...].astype(BF)
    tick(9)

    def saved(e):
        for copy in save(e):
            copy.wait()

    loop(0, examples, saved)
    if comm:
        for u in range(7, UNITS):
            g.fifth(u)
        g.drain()
        for copy in trade + small:
            copy.wait_send()


GELU_A = math.sqrt(2.0 / math.pi)
GELU_B = 0.044715


def feed_kernel(r):
    rows, width = r.a2.shape
    hidden = r.fi.shape[0]

    def cross_out(j):
        at = lanes(j, 256)
        r.h2[:, at] = r.h1[:, at] + nt(r.a2[...], r.w[0, at, :])

    loop(0, width // 256, cross_out)
    r.n3[...] = rms(r.h2[...], r.gains[2:3, :]).astype(BF)
    r.sum[...] = r.h2[...]
    r.back[...] = jnp.zeros_like(r.back)

    def part(j):
        at = lanes(j, 256)
        u = nt(r.n3[...], r.fi[at, :])
        t = jnp.tanh(GELU_A * (u + GELU_B * (u * u * u)))
        g = (0.5 * u * (1.0 + t)).astype(BF)
        slope = 0.5 * (1.0 + t) + 0.5 * u * (1.0 - t * t) * (
            GELU_A * (1.0 + (3.0 * GELU_B) * (u * u))
        )
        du = (nn(r.c[...], r.fo[:, at]) * slope).astype(BF)
        r.dfo[:, at] = tn(r.c[...], g).astype(BF)
        r.dfi[at, :] = tn(du, r.n3[...]).astype(BF)
        r.sum[...] += nt(g, r.fo[:, at])
        r.back[...] += nn(du, r.fi[at, :])

    loop(0, hidden // 256, part)
    r.out[...] = r.sum[...].astype(BF)
    dz, dw = rms_back(r.h2[...], r.gains[2:3, :], r.back[...])
    r.gain[...] = dw
    r.dh2[...] = r.c[...].astype(F32) + dz

    def tail(j):
        at = lanes(j, 256)
        r.da2[:, at] = nn(r.dh2[...].astype(BF), r.w[0, :, at]).astype(BF)
        r.dwoc[at, :] = tn(r.dh2[:, at].astype(BF), r.a2[...]).astype(BF)

    loop(0, width // 256, tail)


def cross_back_kernel(comm, r):
    rows, width = r.q2.shape
    examples, keys_n = r.valid.shape
    halves = width // WIDE

    def fetches(e):
        return [local(getattr(r, a).at[e], getattr(r, b).at[e], r.esem.at[e, i])
                for i, (a, b) in enumerate((("enc", "encv"), ("k2", "k2v"), ("v2", "v2v")))]

    for e in range(examples):
        for copy in fetches(e):
            copy.start()
    if comm:
        p = Place()

        def parts(u, c, y):
            if u < 4:
                return r.dfi.at[:, :, c, u, :, y * WIDE : (y + 1) * WIDE]
            at = y * 4 * WIDE + (u - 4) * WIDE
            return r.dfo.at[:, :, c, :, at : at + WIDE]

        s = Scatter(p, parts, r)
        greet(p.near())
    r.sum[...] = jnp.zeros_like(r.sum)
    r.dwsum[...] = jnp.zeros_like(r.dwsum)

    def out_copy(e):
        return local(r.denv.at[e % 2], r.denc.at[e], r.dsem.at[e % 2])

    def example(e):
        if comm:
            for t in range(8):

                @pl.when(e == t)
                def _():
                    for number in (4, 3, 2, 1, 0):
                        if 0 <= t - number < 4:
                            s.step(number, t - number, 4 + t - number)

        for copy in fetches(e):
            copy.wait()
        pick = example_rows(r.seg_row, r.off_row, e, rows)
        r.qe[...] = nn(pick, r.q2[...]).astype(BF)
        r.dae[...] = nn(pick, r.da2[...]).astype(BF)
        hidden = r.valid[pl.ds(e, 1), :]

        def attend(pair):
            at = lanes(pair, 128)
            queries = split_heads(r.qe[:, at])
            deltas = split_heads(r.dae[:, at])
            keys = r.k2v[e, :, at]
            probs = softmax(nt(queries, keys) + hidden)
            dprobs = nt(deltas, r.v2v[e, :, at])
            low = (probs * (dprobs - jnp.sum(dprobs * probs, axis=-1, keepdims=True))).astype(BF)
            r.dv[:, at] = tn(probs.astype(BF), deltas).astype(BF)
            r.dk[:, at] = tn(low, queries).astype(BF)
            r.dqe[:, at] = join_heads(nn(low, keys)).astype(BF)

        loop(0, PAIRS, attend)
        r.sum[...] += tn(pick, r.dqe[...])

        @pl.when(e >= 2)
        def _():
            out_copy(e - 2).wait()

        def dense(j):
            at = lanes(j, 256)
            r.denv[e % 2, :, at] = (
                nn(r.dk[...], w_lanes(r.w, 0, at)) + nn(r.dv[...], w_lanes(r.w, 1, at))
            ).astype(BF)
            r.dwsum[0, at, :] += tn(r.dk[:, at], r.encv[e])
            r.dwsum[1, at, :] += tn(r.dv[:, at], r.encv[e])

        loop(0, width // 256, dense)
        out_copy(e).start()

    loop(0, examples, example)
    r.dq2[...] = r.sum[...].astype(BF)
    r.dwkv[...] = r.dwsum[...].astype(BF)
    for e in (examples - 2, examples - 1):
        out_copy(e).wait()
    if comm:
        s.drain()


def self_back_kernel(comm, r):
    rows, width = r.x.shape
    blocks = rows // MOST
    thirds = width // 256
    if comm:
        p = Place()

        def parts(u, c, y):
            at = slice(y * WIDE, (y + 1) * WIDE)
            if u < 2:
                return r.dwkv.at[u, :, :, c, :, at]
            if u == 2:
                return r.dwoc.at[:, :, c, :, at]
            return r.dw.at[u - 3, :, :, c, :, at]

        s = Scatter(p, parts, r)
        greet(p.near())
        step = s.step
    else:
        step = lambda *units: None

    def put(m, j, value):
        if comm:
            r.dw[m, 2 * j : 2 * j + 2] = value.astype(BF).reshape(2, 2, 2, PIECE, width)
        else:
            r.dw[m, WIDE * j : WIDE * (j + 1), :] = value.astype(BF)

    halves = width // WIDE
    step(0, 0, 1, 2)
    for j in range(halves):
        at = slice(WIDE * j, WIDE * (j + 1))
        put(0, j, tn(r.dq2[:, at], r.n2[...]))
    step(0, 3)

    def query(j):
        at = lanes(j, 256)
        r.back[:, at] = nn(r.dq2[...], w_lanes(r.w, 4, at))

    loop(0, thirds, query)
    step(1, 0, 1)
    dz, dw = rms_back(r.h1[...], r.gains[1:2, :], r.back[...])
    r.gain[1:2, :] = dw
    r.dh1[...] = r.dh2[...] + dz
    r.b1[...] = r.dh1[...].astype(BF)
    for j in range(halves):
        at = slice(WIDE * j, WIDE * (j + 1))
        put(1, j, tn(r.b1[:, at], r.a1[...]))
    step(0, 4)
    step(2, 0, 1)

    def out(j):
        at = lanes(j, 256)
        r.da1[:, at] = nn(r.b1[...], w_lanes(r.w, 3, at)).astype(BF)

    loop(0, thirds, out)
    step(1, 2, 3)
    self_masks(r.seg_col[...], r.seg_band[...], r.mask)
    a = lax.broadcasted_iota(jnp.int32, (MOST, MOST), 0)
    b = lax.broadcasted_iota(jnp.int32, (MOST, MOST), 1)
    flip = (a + b == MOST - 1).astype(F32)

    def attend(pair):
        at = lanes(pair, 128)
        bias = pair_bias(r.dist, pair)
        r.dksum[...] = jnp.zeros_like(r.dksum)
        r.dvsum[...] = jnp.zeros_like(r.dvsum)
        skewed = jnp.zeros((2 * MOST, 2 * MOST), F32)
        for i in range(blocks):
            own = slice(MOST * i, MOST * (i + 1))
            band = slice(MOST * i, MOST * (i + 2))
            queries = split_heads(r.q1[own, at])
            deltas = split_heads(r.da1[own, at])
            keys = r.k1[band, at]
            probs = softmax(masked_scores(nt(queries, keys), bias, r.mask[i]))
            dprobs = nt(deltas, r.v1[band, at])
            dscores = probs * (dprobs - jnp.sum(dprobs * probs, axis=-1, keepdims=True))
            low = dscores.astype(BF)
            skewed = skewed + dscores
            r.dvsum[band, :] += tn(probs.astype(BF), deltas)
            r.dksum[band, :] += tn(low, queries)
            r.dq[own, at] = join_heads(nn(low, keys)).astype(BF)
        r.dk[:, at] = r.dksum[MOST:, :].astype(BF)
        r.dv[:, at] = r.dvsum[MOST:, :].astype(BF)
        for h in range(2):
            flipped = jnp.dot(
                flip,
                skewed[MOST * h : MOST * (h + 1)],
                precision=lax.Precision.HIGHEST,
                preferred_element_type=F32,
            )
            straight = pltpu.roll(flipped, MOST + 1, 1, stride=1, stride_axis=0)
            r.distsum[pl.ds(2 * pair + h, 1), :] = jnp.sum(straight, axis=0, keepdims=True)

    loop(0, 2, attend)
    step(3, 0, 1)
    step(2, 2, 3)
    step(1, 4)
    loop(2, 4, attend)
    step(4, 0, 1)
    step(3, 2, 3)
    step(2, 4)
    loop(4, PAIRS, attend)

    for m, ref in ((2, r.dq), (3, r.dk), (4, r.dv)):
        for j in range(halves):
            at = slice(WIDE * j, WIDE * (j + 1))
            put(m, j, tn(ref[:, at], r.n1[...]))
        step(0, 3 + m)
    step(4, 2, 3)
    step(3, 4)
    step(1, 5, 6, 7)

    def qkv(j):
        at = lanes(j, 256)
        r.back[:, at] = (
            nn(r.dq[...], w_lanes(r.w, 0, at))
            + nn(r.dk[...], w_lanes(r.w, 1, at))
            + nn(r.dv[...], w_lanes(r.w, 2, at))
        )

    loop(0, thirds, qkv)
    dz, dw = rms_back(r.x[...].astype(F32), r.gains[0:1, :], r.back[...])
    r.gain[0:1, :] = dw
    r.dx[...] = (r.dh1[...] + dz).astype(BF)
    by_bucket = jnp.dot(
        r.distsum[...], r.hot[...], precision=lax.Precision.HIGHEST, preferred_element_type=F32
    )
    r.small[...] = jnp.zeros_like(r.small)
    r.small[0:2, :] = r.gain[0:2, :]
    r.small[2:3, :] = r.gain3[...]
    r.small[3 : 3 + HEADS, 0:BUCKETS] = by_bucket
    if not comm:
        return

    pairs = [p.at(c=1 - p.c), p.at(y=1 - p.y), p.at(x=1 - p.x),
             p.at(z=p.z + 1 - 2 * (p.z % 2)), p.at(z=(p.z + 2) % 4)]

    def share(i):
        return remote(r.given.at[i], r.gotten.at[i], r.smsem.at[0, i], r.smsem.at[1, i], pairs[i])

    def share_go(i):
        r.given[i] = r.small[...]
        share(i).start()

    def share_end(i):
        share(i).wait_recv()
        r.small[...] = r.small[...] + r.gotten[i]

    share_go(0)
    step(4, 4)
    share_end(0)
    share_go(1)
    step(2, 6, 5)
    share_end(1)
    share_go(2)
    step(2, 7)
    share_end(2)
    share_go(3)
    step(3, 6, 5)
    share_end(3)
    share_go(4)
    step(3, 7)
    share_end(4)
    step(4, 6, 5, 7)

    first = p.c == 0

    def split(ref, n):
        low, high = ref[0:n, :, :192], ref[0:n, :, 192:]
        return jnp.where(first, low, high), jnp.where(first, high, low)

    keep_sq, r.give[0:8] = split(r.fin, 8)
    keep_fi, r.give[8:12] = split(r.finf, 4)
    r.giveo[...] = r.finf[pl.ds(4 + 2 * (1 - p.c), 2)]
    sib = p.at(c=1 - p.c)
    trade = [
        remote(r.give, r.take, r.xsem.at[0], r.xsem.at[1], sib),
        remote(r.giveo, r.takeo, r.xsem.at[2], r.xsem.at[3], sib),
    ]
    for copy in trade:
        copy.start()
    for copy in trade:
        copy.wait_recv()

    def both(a, b, axis):
        return jnp.concatenate([jnp.where(first, a, b), jnp.where(first, b, a)], axis=axis)

    r.tsq[...] = both(keep_sq, r.take[0:8], 1)
    r.tfi[...] = both(keep_fi.reshape(192, 192), r.take[8:12].reshape(192, 192), 0)
    own = r.finf[pl.ds(4 + 2 * p.c, 2)]
    r.tfo[...] = both(
        jnp.concatenate([own[0], own[1]], axis=1), jnp.concatenate([r.takeo[0], r.takeo[1]], axis=1), 0
    )
    s.drain()
    for i in range(5):
        share(i).wait_send()
    for copy in trade:
        copy.wait_send()


def finish_kernel(r):
    e192 = eye(192)
    for m, ref in enumerate((r.k_c, r.v_c, r.o_c, r.q_c, r.o_s, r.q_s, r.k_s, r.v_s)):
        ref[...] = nt(e192, r.tsq[m])
    r.f_i[...] = nt(e192, r.tfi[...])
    e384 = eye(WIDE)
    for j in range(2):
        r.f_o[WIDE * j : WIDE * (j + 1), :] = nt(e384, r.tfo[:, WIDE * j : WIDE * (j + 1)])


VM = pltpu.VMEM
HBM = pl.ANY


def run(kernel, ins, outs, scratch, name, collective=None, flops=0):
    names = list(ins) + list(outs) + list(scratch)

    def wrapped(*refs):
        kernel(types.SimpleNamespace(**dict(zip(names, refs))))

    arrays, specs = [], []
    for value in ins.values():
        array, spec = value if isinstance(value, tuple) else (value, VM)
        arrays.append(array)
        specs.append(spec if isinstance(spec, pl.BlockSpec) else pl.BlockSpec(memory_space=spec))
    results = pl.pallas_call(
        wrapped,
        grid=(1,),
        in_specs=specs,
        out_specs=[pl.BlockSpec(memory_space=(o[2] if len(o) > 2 else VM)) for o in outs.values()],
        out_shape=[jax.ShapeDtypeStruct(o[0], o[1]) for o in outs.values()],
        scratch_shapes=list(scratch.values()),
        compiler_params=pltpu.CompilerParams(
            vmem_limit_bytes=VMEM_LIMIT,
            collective_id=collective,
            has_side_effects=collective is not None,
        ),
        cost_estimate=pl.CostEstimate(flops=flops, bytes_accessed=20_000_000, transcendentals=0),
        name=name,
    )(*arrays)
    return types.SimpleNamespace(**dict(zip(outs, results)))


def dma(*shape):
    return pltpu.SemaphoreType.DMA(shape)


def body(comm, decoder_in, encoder_out, decoder_lengths, encoder_lengths, norm_gains, rel_table,
         query_self, key_self, value_self, out_self, query_cross, key_cross, value_cross, out_cross,
         feed_in, feed_out, upstream):
    rows, width = decoder_in.shape
    row_count, examples = decoder_lengths.shape
    keys_n = encoder_out.shape[1]
    hidden = feed_in.shape[1] * lax.axis_size("fsdp")
    small = (rows, width)
    cut = (4, 2, 2, PIECE, width)

    places = jnp.arange(rows, dtype=jnp.int32)
    ends = jnp.cumsum(decoder_lengths[0], dtype=jnp.int32)
    segment = jnp.sum((places[:, None] >= ends[None, :]).astype(jnp.int32), axis=-1)
    starts = ends - decoder_lengths[0]
    offset = places - jnp.sum(
        jnp.where(segment[:, None] == jnp.arange(examples)[None, :], starts[None, :], 0), axis=-1
    )
    seg_col = segment[:, None]
    seg_row = segment[None, :]
    off_row = offset[None, :]
    seg_band = jnp.concatenate([jnp.full((1, MOST), -1, jnp.int32), seg_row], axis=1)
    valid = jnp.where(
        jnp.arange(keys_n, dtype=jnp.int32)[None, :] < encoder_lengths[:, None], 0.0, HIDDEN_SCORE
    )
    hot = distance_hot()
    index = dict(seg_col=seg_col, seg_band=seg_band)
    by_example = dict(seg_row=seg_row, off_row=off_row, valid=valid)

    acts = dict(n1=(small, BF), q1=(small, BF), k1=((rows + MOST, width), BF), v1=((rows + MOST, width), BF),
                a1=(small, BF), h1=(small, F32), n2=(small, BF), q2=(small, BF), a2=(small, BF),
                k2=(encoder_out.shape, BF, HBM), v2=(encoder_out.shape, BF, HBM))
    scratch = dict(
        encv=VM(encoder_out.shape, BF), k2v=VM(encoder_out.shape, BF), v2v=VM(encoder_out.shape, BF),
        wv=VM((7,) + cut, BF), mask=VM((rows // MOST, MOST, 2 * MOST), F32),
        qe=VM((MOST, width), BF), ae=VM((MOST, width), BF), sum=VM(small, F32),
        esem=dma(examples), wsem=dma(7), ksem=dma(examples, 2),
    )
    ins = dict(x=decoder_in, enc=(encoder_out, HBM), hot=hot.T, **index, **by_example)
    if comm:
        ins |= dict(q_s=query_self, k_s=key_self, v_s=value_self, o_s=out_self, q_c=query_cross,
                    o_c=out_cross, k_c=key_cross, v_c=value_cross, f_i=feed_in, f_o=feed_out,
                    gains_s=norm_gains, table_s=rel_table)
        fwd = run(
            functools.partial(forward_kernel, True), ins,
            acts | dict(sq=((8,) + cut, BF, HBM), fi=((4, 2, 2, 4, PIECE, width), BF, HBM),
                        fo=((4, 2, 2, PIECE, hidden), BF, HBM), gains=((3, width), F32),
                        dist=((HEADS, 2 * MOST), F32)),
            scratch | dict(
                xt=VM((12, 2, PIECE, 192), BF), xf=VM((2, PIECE, 768), BF), took=VM((12, PIECE, 192), BF),
                tookf=VM((PIECE, 768), BF), own=VM((UNITS, PIECE, WIDE), BF), gt=VM((8, 8, 128), F32),
                tt=VM((4, 8, 128), F32), xsem=dma(4), psem=dma(UNITS), smsem=dma(2, 10),
                ssem=dma(UNITS, 10), rsem=dma(UNITS, 10)),
            "forward", collective=0,
        )
        sq, fi, fo, gains, dist = fwd.sq, fwd.fi, fwd.fo, fwd.gains, fwd.dist
    else:
        order = (key_cross, value_cross, query_self, key_self, value_self, out_self, query_cross, out_cross)
        sq = jnp.stack([m.astype(BF).T for m in order])
        sq = lax.all_gather(sq, "fsdp", axis=1, tiled=True)
        sq = lax.all_gather(sq, "dp", axis=2, tiled=True).reshape((8,) + cut)
        fi = lax.all_gather(feed_in.astype(BF).T, "fsdp", axis=0, tiled=True)
        fi = lax.all_gather(fi, "dp", axis=1, tiled=True)
        fo = lax.all_gather(feed_out.astype(BF).T, "fsdp", axis=0, tiled=True)
        fo = lax.all_gather(fo, "dp", axis=1, tiled=True)
        gains = lax.all_gather(norm_gains.astype(BF), "fsdp", axis=1, tiled=True).astype(F32)
        table = lax.all_gather(rel_table.astype(BF), "dp", axis=0, tiled=True).astype(F32)
        dist = jnp.dot(hot, table, precision=lax.Precision.HIGHEST).T
        fwd = run(
            functools.partial(forward_kernel, False),
            ins | dict(sq=(sq, HBM), gains=gains, dist=dist), acts, scratch, "forward",
        )

    feed = run(
        feed_kernel,
        dict(a2=fwd.a2, h1=fwd.h1, c=upstream, gains=gains,
             w=(sq.reshape(8, width, width), pl.BlockSpec((1, width, width), lambda _: (7, 0, 0))),
             fi=fi.reshape(hidden, width), fo=fo.reshape(width, hidden)),
        dict(out=(small, BF), dfi=((hidden, width), BF), dfo=((width, hidden), BF),
             dwoc=((width, width), BF), da2=(small, BF), dh2=(small, F32), gain=((1, width), F32)),
        dict(h2=VM(small, F32), n3=VM(small, BF), sum=VM(small, F32), back=VM(small, F32)),
        "feed",
    )

    cut_spec = pl.BlockSpec((2,) + cut, lambda _: (0,) * 6)
    ins = dict(enc=(encoder_out, HBM), k2=(fwd.k2, HBM), v2=(fwd.v2, HBM), q2=fwd.q2, da2=feed.da2,
               w=(sq, cut_spec), **by_example)
    outs = dict(denc=(encoder_out.shape, BF, HBM), dq2=(small, BF), dwkv=((2, width, width), BF))
    scratch = dict(
        encv=VM(encoder_out.shape, BF), k2v=VM(encoder_out.shape, BF), v2v=VM(encoder_out.shape, BF),
        qe=VM((MOST, width), BF), dae=VM((MOST, width), BF), dqe=VM((MOST, width), BF),
        dk=VM((keys_n, width), BF), dv=VM((keys_n, width), BF), denv=VM((2, keys_n, width), BF),
        sum=VM(small, F32), dwsum=VM((2, width, width), F32), esem=dma(examples, 3), dsem=dma(2),
    )
    fins = {}
    if comm:
        ins |= dict(dfi=(feed.dfi.reshape(4, 2, 2, 4, PIECE, width), HBM),
                    dfo=(feed.dfo.reshape(4, 2, 2, PIECE, hidden), HBM))
        fins = dict(fin=((8, PIECE, WIDE), BF))
        scratch |= scatter_scratch(8)
    mid = run(functools.partial(cross_back_kernel, comm), ins, outs | fins, scratch, "cross_back",
              collective=1 if comm else None)

    five = (5,) + cut if comm else (5, width, width)
    ins = dict(dq2=mid.dq2, n2=fwd.n2, h1=fwd.h1, dh2=feed.dh2, x=decoder_in, n1=fwd.n1, q1=fwd.q1,
               k1=fwd.k1, v1=fwd.v1, a1=fwd.a1, gains=gains, dist=dist, gain3=feed.gain, hot=hot,
               w=(sq[2:7], VM), **index)
    outs = dict(dx=(small, BF), small=((16, width), F32))
    scratch = dict(
        mask=VM((rows // MOST, MOST, 2 * MOST), F32), dh1=VM(small, F32), b1=VM(small, BF),
        da1=VM(small, BF), dq=VM(small, BF), dk=VM(small, BF), dv=VM(small, BF),
        dksum=VM((rows + MOST, 128), F32), dvsum=VM((rows + MOST, 128), F32), back=VM(small, F32),
        gain=VM((2, width), F32), distsum=VM((HEADS, 2 * MOST), F32),
    )
    if comm:
        ins |= dict(dwkv=(mid.dwkv.reshape((2,) + cut), HBM), dwoc=(feed.dwoc.reshape(cut), HBM), finf=mid.fin)
        outs |= dict(tsq=((8, 96, 192), BF), tfi=((384, 192), BF), tfo=((96, 768), BF))
        scratch |= dict(
            dw=VM(five, BF), fin=VM((8, PIECE, WIDE), BF), give=VM((12, PIECE, 192), BF),
            take=VM((12, PIECE, 192), BF), giveo=VM((2, PIECE, WIDE), BF), takeo=VM((2, PIECE, WIDE), BF),
            given=VM((5, 16, width), F32), gotten=VM((5, 16, width), F32), smsem=dma(2, 5), xsem=dma(4),
        ) | scatter_scratch(8)
    else:
        outs |= dict(dw=(five, BF))
    last = run(functools.partial(self_back_kernel, comm), ins, outs, scratch, "self_back",
               collective=2 if comm else None)

    if comm:
        square = ((192, 96), F32)
        done = run(
            finish_kernel, dict(tsq=last.tsq, tfi=last.tfi, tfo=last.tfo),
            {n: square for n in ("k_c", "v_c", "q_s", "k_s", "v_s", "o_s", "q_c", "o_c")}
            | dict(f_i=((192, 384), F32), f_o=((768, 96), F32)),
            {}, "finish",
        )
        grads = (done.q_s, done.k_s, done.v_s, done.o_s, done.q_c, done.k_c, done.v_c, done.o_c,
                 done.f_i, done.f_o)
        d, f = lax.axis_index("dp"), lax.axis_index("fsdp")
        part = norm_gains.shape[1]
        gains_delta = lax.dynamic_slice(last.small[0:3], (0, f * part), (3, part))
        part = rel_table.shape[0]
        table_delta = lax.dynamic_slice(last.small[3 : 3 + HEADS, 0:BUCKETS].T, (d * part, 0), (part, HEADS))
    else:
        def owned(t, rows_axis=0):
            t = lax.psum_scatter(t, "dp", scatter_dimension=1, tiled=True)
            return lax.psum_scatter(t, "fsdp", scatter_dimension=0, tiled=True).astype(F32).T

        dw = last.dw
        grads = tuple(owned(t) for t in (dw[2], dw[3], dw[4], dw[1], dw[0], mid.dwkv[0], mid.dwkv[1],
                                         feed.dwoc, feed.dfi, feed.dfo))
        gains_delta = lax.psum(last.small[0:3], "dp")
        gains_delta = lax.psum_scatter(gains_delta, "fsdp", scatter_dimension=1, tiled=True)
        table_delta = last.small[3 : 3 + HEADS, 0:BUCKETS].T
        table_delta = lax.psum_scatter(table_delta, "dp", scatter_dimension=0, tiled=True)
        table_delta = lax.psum(table_delta, "fsdp")
    return (feed.out, last.dx, mid.denc, gains_delta, table_delta) + grads


def solution(mesh):
    tokens = P(("dp", "fsdp"), None)
    weight = P("dp", "fsdp")
    comm = (mesh.shape["dp"], mesh.shape["fsdp"]) == (4, 8)
    return jax.shard_map(
        functools.partial(body, comm),
        mesh=mesh,
        in_specs=(tokens, P(("dp", "fsdp"), None, None), tokens, P(("dp", "fsdp")), P(None, "fsdp"),
                  P("dp", None)) + (weight,) * 10 + (tokens,),
        out_specs=(tokens, tokens, P(("dp", "fsdp"), None, None), P(None, "fsdp"), P("dp", None))
        + (weight,) * 10,
        check_vma=False,
    )
```

```python
import functools
import math
import types

import jax
import jax.numpy as jnp
from jax import lax
from jax.experimental import pallas as pl
from jax.experimental.pallas import tpu as pltpu
from jax.sharding import PartitionSpec as P

HEADS = 12
HEAD_DIM = 64
BUCKETS = 32
MAX_DIST = 128
MOST = 128
PAIRS = HEADS // 2
EPSILON = 1e-06
HIDDEN_SCORE = -1e30
BF = jnp.bfloat16
F32 = jnp.float32
VMEM_LIMIT = 60 * 1024 * 1024


def nn(a, b):
    return lax.dot_general(a, b, (((1,), (0,)), ((), ())), preferred_element_type=F32)


def nt(a, b):
    return lax.dot_general(a, b, (((1,), (1,)), ((), ())), preferred_element_type=F32)


def tn(a, b):
    return lax.dot_general(a, b, (((0,), (0,)), ((), ())), preferred_element_type=F32)


def rms(z, gain):
    factor = lax.rsqrt(jnp.mean(z * z, axis=-1, keepdims=True) + EPSILON)
    return z * factor * gain


def rms_back(z, gain, dy):
    factor = lax.rsqrt(jnp.mean(z * z, axis=-1, keepdims=True) + EPSILON)
    wdy = dy * gain
    inner = jnp.mean(z * wdy, axis=-1, keepdims=True)
    dz = factor * wdy - z * (factor * factor * factor * inner)
    return dz, jnp.sum(dy * z * factor, axis=0, keepdims=True)


def split_heads(rows):
    first = lax.broadcasted_iota(jnp.int32, rows.shape, 1) < HEAD_DIM
    zero = jnp.zeros_like(rows)
    return jnp.concatenate([jnp.where(first, rows, zero), jnp.where(first, zero, rows)], axis=0)


def join_heads(rows):
    half = rows.shape[0] // 2
    first = lax.broadcasted_iota(jnp.int32, (half, rows.shape[1]), 1) < HEAD_DIM
    return jnp.where(first, rows[:half], rows[half:])


def softmax(scores):
    raised = jnp.exp(scores - jnp.max(scores, axis=-1, keepdims=True))
    return raised * (1.0 / jnp.sum(raised, axis=-1, keepdims=True))


def lanes(index, width):
    return pl.ds(pl.multiple_of(index * width, width), width)


def loop(low, high, step):
    def run(index, carry):
        step(index)
        return carry

    lax.fori_loop(low, high, run, 0)


def bucket_of(distance):
    half_count = BUCKETS // 2
    counted = jnp.zeros_like(distance)
    for section_index in range(1, half_count):
        edge_at = int(
            math.ceil(half_count * (MAX_DIST / half_count) ** (section_index / half_count))
        )
        counted = counted + (distance >= edge_at).astype(jnp.int32)
    return jnp.where(distance < half_count, distance, half_count + counted)


def distance_hot(axis):
    shape = (2 * MOST, BUCKETS) if axis == 0 else (BUCKETS, 2 * MOST)
    distance = jnp.maximum(MOST - lax.broadcasted_iota(jnp.int32, shape, axis), 0)
    return (bucket_of(distance) == lax.broadcasted_iota(jnp.int32, shape, 1 - axis)).astype(F32)


def segments(lengths, shape, axis, shift=0):
    places = lax.broadcasted_iota(jnp.int32, shape, axis) - shift
    end = jnp.zeros((1, 1), jnp.int32)
    example = jnp.where(places < 0, -1, 0)
    start = jnp.zeros(shape, jnp.int32)
    for e in range(lengths.shape[1]):
        length = lengths[:, e : e + 1]
        end = end + length
        example = example + (places >= end).astype(jnp.int32)
        start = start + jnp.where(places >= end, length, 0)
    return example, places - start


def local(src, dst, sem):
    return pltpu.make_async_copy(src, dst, sem)


def w_rows(ref, m, j):
    return ref[m, pl.ds(2 * j, 2)].reshape(2 * WIDE // 2, ref.shape[-1])


def w_lanes(ref, m, at):
    part = ref[m, :, :, :, :, at]
    return part.reshape(-1, part.shape[-1])


MESH = pl.DeviceIdType.MESH
PIECE = 48
WIDE = 384
UNITS = 16
ALL = slice(None)


class Place:
    def __init__(self):
        self.d, self.f = lax.axis_index("dp"), lax.axis_index("fsdp")
        self.y, self.c = self.d // 2, self.d % 2
        self.z, self.x = self.f // 2, self.f % 2
        self.nx, self.ny, self.nc = 1 - self.x, 1 - self.y, 1 - self.c

    def at(self, z=None, x=None, y=None, c=None):
        z = self.z if z is None else z
        x = self.x if x is None else x
        y = self.y if y is None else y
        c = self.c if c is None else c
        return (y * 2 + c, z * 2 + x)

    def near(self):
        others = [self.at(z=(self.z + k) % 4) for k in (1, 2, 3)]
        return others + [self.at(x=1 - self.x), self.at(y=1 - self.y), self.at(c=1 - self.c)]


def greet(peers):
    barrier = pltpu.get_barrier_semaphore()
    for dev in peers:
        pl.semaphore_signal(barrier, inc=1, device_id=dev, device_id_type=MESH)
    pl.semaphore_wait(barrier, len(peers))


def eye(n):
    a = lax.broadcasted_iota(jnp.int32, (n, n), 0)
    b = lax.broadcasted_iota(jnp.int32, (n, n), 1)
    return (a == b).astype(F32).astype(BF)


def remote(src, dst, send, recv, dev):
    return pltpu.make_async_remote_copy(
        src_ref=src, dst_ref=dst, send_sem=send, recv_sem=recv, device_id=dev, device_id_type=MESH
    )


class Sends:
    def __init__(self, place, ssem, rsem):
        self.p, self.ssem, self.rsem, self.made = place, ssem, rsem, {}

    def to_x(self):
        return self.p.at(x=1 - self.p.x)

    def to_y(self):
        return self.p.at(y=1 - self.p.y)

    def to_c(self):
        return self.p.at(c=1 - self.p.c)

    def go(self, u, slot, src, dst, dev):
        def make():
            return remote(src(), dst(), self.ssem.at[u, slot], self.rsem.at[u, slot], dev())

        make().start()
        self.made[u, slot] = make

    def wait(self, u, *slots):
        for slot in slots:
            self.made[u, slot]().wait_recv()

    def drain(self):
        for make in self.made.values():
            make().wait_send()


class Gather(Sends):
    def __init__(self, place, own, sq, fi, fo, ssem, rsem):
        super().__init__(place, ssem, rsem)
        self.own, self.sq, self.fi, self.fo = own, sq, fi, fo

    def piece(self, u, z, x, c, y):
        if u < 8:
            return self.sq.at[u, z, x, c, :, pl.ds(pl.multiple_of(y * WIDE, WIDE), WIDE)]
        if u < 12:
            return self.fi.at[z, x, c, u - 8, :, pl.ds(pl.multiple_of(y * WIDE, WIDE), WIDE)]
        at = y * (4 * WIDE) + (u - 12) * WIDE
        return self.fo.at[z, x, c, :, pl.ds(pl.multiple_of(at, WIDE), WIDE)]

    def same(self, u, slot, dev, z, x, c, y):
        def here():
            return self.piece(u, z, x, c, y)

        self.go(u, slot, here, here, dev)

    def first(self, u):
        p = self.p
        for k in (1, 2, 3):
            self.go(
                u, k - 1, lambda: self.own.at[u], lambda: self.piece(u, p.z, p.x, p.c, p.y),
                lambda k=k: p.at(z=(p.z + k) % 4),
            )

    def second(self, u):
        p = self.p
        self.wait(u, 0, 1, 2)
        self.same(u, 3, self.to_x if u % 2 == 0 else self.to_y, ALL, p.x, p.c, p.y)

    def third(self, u):
        p = self.p
        self.wait(u, 3)
        if u % 2 == 0:
            self.same(u, 4, self.to_y, ALL, ALL, p.c, p.y)
            self.same(u, 6, self.to_c, ALL, ALL, p.c, p.y)
        else:
            for y in (0, 1):
                self.same(u, 4 + y, self.to_x, ALL, p.x, p.c, y)
            for y in (0, 1):
                self.same(u, 6 + y, self.to_c, ALL, p.x, p.c, y)

    def fourth(self, u):
        p = self.p
        if u % 2 == 0:
            self.wait(u, 4)
            self.same(u, 8, self.to_c, ALL, ALL, p.c, p.ny)
        else:
            self.wait(u, 4, 5)
            for y in (0, 1):
                self.same(u, 8 + y, self.to_c, ALL, p.nx, p.c, y)

    def fifth(self, u):
        self.wait(u, *((6, 8) if u % 2 == 0 else (6, 7, 8, 9)))

    def begin(self):
        for act, u in ((self.second, 0), (self.second, 1), (self.third, 0), (self.third, 1),
                       (self.second, 2), (self.second, 3), (self.fourth, 0), (self.fourth, 1), (self.second, 4)):
            act(u)

    def tick(self, t):
        for act, u in ((self.fourth, t), (self.third, t + 2), (self.second, t + 5)):
            low = {self.fourth: 2, self.third: 2, self.second: 5}[act]
            if low <= u < UNITS:
                act(u)


class Scatter(Sends):
    def __init__(self, place, parts, r):
        super().__init__(place, r.ssem, r.rsem)
        self.parts, self.r = parts, r

    def halves(self, u):
        p, r = self.p, self.r
        return [local(self.parts(u, p.c, y), r.acc.at[u, y], r.lsem.at[u, y]) for y in (0, 1)]

    def r0(self, u):
        p, r = self.p, self.r
        for y in (0, 1):
            self.go(
                u, y, lambda y=y: self.parts(u, 1 - p.c, y), lambda y=y: r.land.at[u, y], self.to_c
            )
        for copy in self.halves(u):
            copy.start()

    def r1(self, u):
        p, r = self.p, self.r
        self.wait(u, 0, 1)
        for copy in self.halves(u):
            copy.wait()
        if u % 2 == 0:
            other, own = pl.ds(1 - p.y, 1), pl.ds(p.y, 1)
            r.acc[u, other] = r.acc[u, other] + r.land[u, other]
            self.go(u, 2, lambda: r.acc.at[u, 1 - p.y], lambda: r.land1.at[u], self.to_y)
            r.acc[u, own] = r.acc[u, own] + r.land[u, own]
        else:
            for y in (0, 1):
                r.acc[u, y] = r.acc[u, y] + r.land[u, y]
                self.go(
                    u, 2 + y, lambda y=y: r.acc.at[u, y, :, 1 - p.x], lambda y=y: r.land1.at[u, :, y],
                    self.to_x,
                )

    def r2(self, u):
        p, r = self.p, self.r
        if u % 2 == 0:
            self.wait(u, 2)
            own = pl.ds(p.y, 1)
            r.acc[u, own] = r.acc[u, own] + r.land1[u][None]
            self.go(
                u, 4, lambda: r.acc.at[u, p.y, :, 1 - p.x], lambda: r.land2.at[u], self.to_x
            )
        else:
            self.wait(u, 2, 3)
            x = pl.ds(p.x, 1)
            for y in (0, 1):
                r.acc[u, y, :, x] = r.acc[u, y, :, x] + r.land1[u, :, y][:, None]
            self.go(
                u, 4, lambda: r.acc.at[u, 1 - p.y, :, p.x], lambda: r.land2.at[u], self.to_y
            )

    def r3(self, u):
        p, r = self.p, self.r
        self.wait(u, 4)
        y, x = pl.ds(p.y, 1), pl.ds(p.x, 1)
        r.acc[u, y, :, x] = r.acc[u, y, :, x] + r.land2[u][None, :, None]
        for k in (1, 2, 3):
            self.go(
                u, 4 + k, lambda k=k: r.acc.at[u, p.y, (p.z + k) % 4, p.x],
                lambda k=k: r.land3.at[u, k - 1], lambda k=k: p.at(z=(p.z + k) % 4),
            )

    def r4(self, u):
        p, r = self.p, self.r
        self.wait(u, 5, 6, 7)
        part = r.acc[u, pl.ds(p.y, 1), pl.ds(p.z, 1), pl.ds(p.x, 1)]
        total = part.reshape(PIECE, WIDE).astype(F32)
        for k in range(3):
            total = total + r.land3[u, k].astype(F32)
        r.fin[u] = total.astype(BF)

    def step(self, number, *units):
        act = (self.r0, self.r1, self.r2, self.r3, self.r4)[number]
        for u in units:
            act(u)


def scatter_scratch(count):
    return dict(
        land=pltpu.VMEM((count, 2, 4, 2, PIECE, WIDE), BF),
        acc=pltpu.VMEM((count, 2, 4, 2, PIECE, WIDE), BF),
        land1=pltpu.VMEM((count, 4, 2, PIECE, WIDE), BF),
        land2=pltpu.VMEM((count, 4, PIECE, WIDE), BF),
        land3=pltpu.VMEM((count, 3, PIECE, WIDE), BF),
        ssem=pltpu.SemaphoreType.DMA((count, 8)),
        rsem=pltpu.SemaphoreType.DMA((count, 8)),
        lsem=pltpu.SemaphoreType.DMA((count, 2)),
    )


def self_masks(lengths, mask_ref):
    blocks = mask_ref.shape[0]
    seg_col = segments(lengths, (blocks * MOST, 1), 0)[0]
    seg_row = segments(lengths, (1, (blocks + 1) * MOST), 1, MOST)[0]
    a = lax.broadcasted_iota(jnp.int32, (MOST, 2 * MOST), 0)
    b = lax.broadcasted_iota(jnp.int32, (MOST, 2 * MOST), 1)
    causal = b <= a + MOST
    for i in range(blocks):
        same = seg_col[MOST * i : MOST * (i + 1), :] == seg_row[:, MOST * i : MOST * (i + 2)]
        mask_ref[i] = jnp.where(causal & same, 0.0, HIDDEN_SCORE)


def pair_bias(dist_ref, pair):
    parts = []
    for h in range(2):
        row = dist_ref[pl.ds(2 * pair + h, 1), :]
        parts.append(
            pltpu.roll(jnp.broadcast_to(row, (MOST, 2 * MOST)), 0, 1, stride=1, stride_axis=0)
        )
    return jnp.concatenate(parts, axis=0)


def masked_scores(scores, bias, mask):
    both = scores + bias
    return (both.reshape(2, MOST, 2 * MOST) + mask[None]).reshape(2 * MOST, 2 * MOST)


def example_rows(index_ref, example, total):
    place = lax.broadcasted_iota(jnp.int32, (MOST, total), 0)
    here = (index_ref[0:1, :] == example) & (index_ref[1:2, :] == place)
    return here.astype(F32).astype(BF)


def example_index(r, total):
    r.index[0:1, :], r.index[1:2, :] = segments(r.lengths[...], (1, total), 1)
    examples, keys_n = r.hidden.shape
    place = lax.broadcasted_iota(jnp.int32, (1, keys_n), 1)
    for e in range(examples):
        r.hidden[e : e + 1, :] = jnp.where(place < r.valid[:, e : e + 1], 0.0, HIDDEN_SCORE)


def spread_shards(p, r):
    e96 = eye(96)
    shards = (r.k_c, r.v_c, r.q_s, r.k_s, r.v_s, r.o_s, r.q_c, r.o_c)
    for m, ref in enumerate(shards):
        r.xt[m] = nt(e96, ref[...].astype(BF)).astype(BF).reshape(2, PIECE, 192)
    t = nt(eye(384), r.f_i[...].astype(BF)).astype(BF).reshape(2, 4, PIECE, 192)
    for s in range(4):
        for h in range(2):
            r.xt[8 + s, h] = t[h, s]
    r.xf[...] = r.f_o[...].astype(BF).reshape(2, PIECE, 768)


def small_sends(p, r):
    made = []
    for k in range(1, 8):
        dev = (p.d, (p.f + k) % 8)
        made.append(
            remote(r.gt.at[p.f], r.gt.at[p.f], r.smsem.at[0, k - 1], r.smsem.at[1, k - 1], dev)
        )
    for k in range(1, 4):
        dev = ((p.d + k) % 4, p.f)
        made.append(
            remote(r.tt.at[p.d], r.tt.at[p.d], r.smsem.at[0, 6 + k], r.smsem.at[1, 6 + k], dev)
        )
    return made


def forward_kernel(comm, r):
    rows, width = r.x.shape
    examples, keys_n = r.enc.shape[0], r.enc.shape[1]
    blocks = rows // MOST
    enc_copies = [local(r.enc.at[e], r.encv.at[e], r.esem.at[e]) for e in range(examples)]
    for copy in enc_copies:
        copy.start()

    if comm:
        p = Place()
        peers = [(p.d, (p.f + k) % 8) for k in range(1, 8)] + [((p.d + k) % 4, p.f) for k in range(1, 4)]
        r.gt[pl.ds(p.f, 1)] = jnp.zeros((1, 8, 128), F32)
        r.gt[pl.ds(p.f, 1), 0:3, 0:96] = r.gains_s[...].astype(BF).astype(F32)[None]
        r.tt[pl.ds(p.d, 1)] = jnp.zeros((1, 8, 128), F32)
        r.tt[pl.ds(p.d, 1), :, 0:HEADS] = r.table_s[...].astype(BF).astype(F32)[None]
        spread_shards(p, r)
        greet(peers)
        sib = p.at(c=1 - p.c)
        trade = [
            remote(r.xt.at[:, 1 - p.c], r.took, r.xsem.at[0], r.xsem.at[1], sib),
            remote(r.xf.at[1 - p.c], r.tookf, r.xsem.at[2], r.xsem.at[3], sib),
        ]
        small = small_sends(p, r)
        for copy in trade + small:
            copy.start()
        first = p.c == 0
        trade[0].wait_recv()
        mine, other = r.xt[:, pl.ds(p.c, 1)].reshape(12, PIECE, 192), r.took[...]
        r.own[0:12] = jnp.concatenate(
            [jnp.where(first, mine, other), jnp.where(first, other, mine)], axis=-1
        )
        trade[1].wait_recv()
        mine, other = r.xf[pl.ds(p.c, 1)].reshape(PIECE, 768), r.tookf[...]
        low, high = jnp.where(first, mine, other), jnp.where(first, other, mine)
        r.own[12], r.own[13] = low[:, :WIDE], low[:, WIDE:]
        r.own[14], r.own[15] = high[:, :WIDE], high[:, WIDE:]
        g = Gather(p, r.own, r.sq, r.fi, r.fo, r.ssem, r.rsem)
        placed = [
            local(r.own.at[u], g.piece(u, p.z, p.x, p.c, p.y), r.psem.at[u]) for u in range(UNITS)
        ]
        for u in range(UNITS):
            g.first(u)
            placed[u].start()
        for copy in small:
            copy.wait_recv()
        spot = lax.broadcasted_iota(jnp.int32, (128, width), 1)
        lane = lax.broadcasted_iota(jnp.int32, (128, width), 0)
        gains = jnp.zeros((8, width), F32)
        for f in range(8):
            put = ((spot == lane + 96 * f) & (lane < 96)).astype(F32).astype(BF)
            gains = gains + nn(r.gt[f].astype(BF), put)
        r.gains[...] = gains[0:3]
        table = r.tt[...].reshape(BUCKETS, 128).astype(BF)
        r.dist[...] = tn(table, distance_hot(1).astype(BF))[0:HEADS]
        for copy in placed:
            copy.wait()
        begin, tick, arrived = g.begin, g.tick, g.fifth
    else:
        begin, tick, arrived = (lambda *_: None,) * 3

    loads = [local(r.sq.at[m], r.wv.at[m], r.wsem.at[m]) for m in range(7)]

    def fetch(*which):
        for m in which:
            arrived(m)
            loads[m].start()

    def have(*which):
        for m in which:
            loads[m].wait()

    example_index(r, rows)
    r.n1[...] = rms(r.x[...].astype(F32), r.gains[0:1, :]).astype(BF)
    r.k1[0:MOST, :] = jnp.zeros((MOST, width), BF)
    r.v1[0:MOST, :] = jnp.zeros((MOST, width), BF)
    self_masks(r.lengths[...], r.mask)
    halves = width // WIDE

    def save(e):
        return [local(r.k2v.at[e], r.k2.at[e], r.ksem.at[e, 0]), local(r.v2v.at[e], r.v2.at[e], r.ksem.at[e, 1])]

    def project(e):
        local(r.enc.at[e], r.encv.at[e], r.esem.at[e]).wait()
        for j in range(halves):
            at = slice(WIDE * j, WIDE * (j + 1))
            r.k2v[e, :, at] = nt(r.encv[e], w_rows(r.wv, 0, j)).astype(BF)
            r.v2v[e, :, at] = nt(r.encv[e], w_rows(r.wv, 1, j)).astype(BF)
        for copy in save(e):
            copy.start()

    begin()
    fetch(0, 1)
    have(0, 1)
    for t in range(4):
        tick(t)
        loop(2 * t, 2 * t + 2, project)
    fetch(2, 3)
    tick(4)
    fetch(4)
    have(2, 3, 4)

    for j in range(halves):
        at = slice(WIDE * j, WIDE * (j + 1))
        r.q1[:, at] = nt(r.n1[...], w_rows(r.wv, 2, j)).astype(BF)
        r.k1[MOST:, at] = nt(r.n1[...], w_rows(r.wv, 3, j)).astype(BF)
        r.v1[MOST:, at] = nt(r.n1[...], w_rows(r.wv, 4, j)).astype(BF)

    def attend(pair):
        at = lanes(pair, 128)
        bias = pair_bias(r.dist, pair)
        for i in range(blocks):
            queries = split_heads(r.q1[MOST * i : MOST * (i + 1), at])
            keys = r.k1[MOST * i : MOST * (i + 2), at]
            values = r.v1[MOST * i : MOST * (i + 2), at]
            probs = softmax(masked_scores(nt(queries, keys), bias, r.mask[i])).astype(BF)
            r.a1[MOST * i : MOST * (i + 1), at] = join_heads(nn(probs, values)).astype(BF)

    tick(5)
    loop(0, PAIRS // 2, attend)
    tick(6)
    fetch(5)
    loop(PAIRS // 2, PAIRS, attend)
    tick(7)
    fetch(6)
    have(5, 6)
    for j in range(halves):
        at = slice(WIDE * j, WIDE * (j + 1))
        r.h1[:, at] = r.x[:, at].astype(F32) + nt(r.a1[...], w_rows(r.wv, 5, j))
    r.n2[...] = rms(r.h1[...], r.gains[1:2, :]).astype(BF)
    for j in range(halves):
        at = slice(WIDE * j, WIDE * (j + 1))
        r.q2[:, at] = nt(r.n2[...], w_rows(r.wv, 6, j)).astype(BF)

    r.sum[...] = jnp.zeros_like(r.sum)

    def cross(e):
        pick = example_rows(r.index, e, rows)
        r.qe[...] = nn(pick, r.q2[...]).astype(BF)
        hidden = r.hidden[pl.ds(e, 1), :]

        def pair_step(pair):
            at = lanes(pair, 128)
            probs = softmax(nt(split_heads(r.qe[:, at]), r.k2v[e, :, at]) + hidden).astype(BF)
            r.ae[:, at] = join_heads(nn(probs, r.v2v[e, :, at])).astype(BF)

        loop(0, PAIRS, pair_step)
        r.sum[...] += tn(pick, r.ae[...])

    def cross_tick(e):
        if comm:
            for t in range(examples):
                pl.when(e == t)(functools.partial(tick, t + 8))
        cross(e)

    loop(0, examples, cross_tick)
    r.a2[...] = r.sum[...].astype(BF)

    def saved(e):
        for copy in save(e):
            copy.wait()

    loop(0, examples, saved)
    if comm:
        for u in range(7, UNITS):
            g.fifth(u)
        g.drain()
        for copy in trade + small:
            copy.wait_send()


GELU_A = math.sqrt(2.0 / math.pi)
GELU_B = 0.044715


def feed_kernel(r):
    rows, width = r.a2.shape
    hidden = r.fi.shape[0]

    def cross_out(j):
        at = lanes(j, 256)
        r.h2[:, at] = r.h1[:, at] + nt(r.a2[...], r.w[0, at, :])

    loop(0, width // 256, cross_out)
    r.n3[...] = rms(r.h2[...], r.gains[2:3, :]).astype(BF)
    r.sum[...] = r.h2[...]
    r.back[...] = jnp.zeros_like(r.back)

    def part(j):
        at = lanes(j, 256)
        u = nt(r.n3[...], r.fi[at, :])
        t = jnp.tanh(GELU_A * (u + GELU_B * (u * u * u)))
        g = (0.5 * u * (1.0 + t)).astype(BF)
        slope = 0.5 * (1.0 + t) + 0.5 * u * (1.0 - t * t) * (
            GELU_A * (1.0 + (3.0 * GELU_B) * (u * u))
        )
        du = (nn(r.c[...], r.fo[:, at]) * slope).astype(BF)
        r.dfo[:, at] = tn(r.c[...], g).astype(BF)
        r.dfi[at, :] = tn(du, r.n3[...]).astype(BF)
        r.sum[...] += nt(g, r.fo[:, at])
        r.back[...] += nn(du, r.fi[at, :])

    loop(0, hidden // 256, part)
    r.out[...] = r.sum[...].astype(BF)
    dz, dw = rms_back(r.h2[...], r.gains[2:3, :], r.back[...])
    r.gain[...] = dw
    r.dh2[...] = r.c[...].astype(F32) + dz

    def tail(j):
        at = lanes(j, 256)
        r.da2[:, at] = nn(r.dh2[...].astype(BF), r.w[0, :, at]).astype(BF)
        r.dwoc[at, :] = tn(r.dh2[:, at].astype(BF), r.a2[...]).astype(BF)

    loop(0, width // 256, tail)


def cross_back_kernel(comm, r):
    rows, width = r.q2.shape
    examples, keys_n = r.enc.shape[0], r.enc.shape[1]

    def fetches(e):
        return [local(getattr(r, a).at[e], getattr(r, b).at[e], r.esem.at[e, i])
                for i, (a, b) in enumerate((("enc", "encv"), ("k2", "k2v"), ("v2", "v2v")))]

    for e in range(examples):
        for copy in fetches(e):
            copy.start()
    if comm:
        p = Place()

        def parts(u, c, y):
            if u < 4:
                return r.dfi.at[:, :, c, u, :, y * WIDE : (y + 1) * WIDE]
            at = y * 4 * WIDE + (u - 4) * WIDE
            return r.dfo.at[:, :, c, :, at : at + WIDE]

        s = Scatter(p, parts, r)
        greet(p.near())
    example_index(r, rows)
    r.sum[...] = jnp.zeros_like(r.sum)
    r.dwsum[...] = jnp.zeros_like(r.dwsum)

    def out_copies(e):
        return [
            local(r.dk.at[e % 2], r.dk2.at[e], r.dsem.at[e % 2, 0]),
            local(r.dv.at[e % 2], r.dv2.at[e], r.dsem.at[e % 2, 1]),
        ]

    def tick(at):
        if comm:
            for t in range(2 * examples):

                @pl.when(at == t)
                def _():
                    for number in (4, 3, 2, 1, 0):
                        if 0 <= t - 2 * number < 8:
                            s.step(number, t - 2 * number)

    def example(e):
        tick(2 * e)
        for copy in fetches(e):
            copy.wait()
        pick = example_rows(r.index, e, rows)
        r.qe[...] = nn(pick, r.q2[...]).astype(BF)
        r.dae[...] = nn(pick, r.da2[...]).astype(BF)
        hidden = r.hidden[pl.ds(e, 1), :]

        @pl.when(e >= 2)
        def _():
            for copy in out_copies(e - 2):
                copy.wait()

        def attend(pair):
            at = lanes(pair, 128)
            queries = split_heads(r.qe[:, at])
            deltas = split_heads(r.dae[:, at])
            keys = r.k2v[e, :, at]
            probs = softmax(nt(queries, keys) + hidden)
            dprobs = nt(deltas, r.v2v[e, :, at])
            low = (probs * (dprobs - jnp.sum(dprobs * probs, axis=-1, keepdims=True))).astype(BF)
            r.dv[e % 2, :, at] = tn(probs.astype(BF), deltas).astype(BF)
            r.dk[e % 2, :, at] = tn(low, queries).astype(BF)
            r.dqe[:, at] = join_heads(nn(low, keys)).astype(BF)

        loop(0, PAIRS, attend)
        tick(2 * e + 1)
        for copy in out_copies(e):
            copy.start()
        r.sum[...] += tn(pick, r.dqe[...])

        def dense(j):
            at = lanes(j, 256)
            r.dwsum[0, at, :] += tn(r.dk[e % 2, :, at], r.encv[e])
            r.dwsum[1, at, :] += tn(r.dv[e % 2, :, at], r.encv[e])

        loop(0, width // 256, dense)

    loop(0, examples, example)
    r.dq2[...] = r.sum[...].astype(BF)
    r.dwkv[...] = r.dwsum[...].astype(BF)
    for e in (examples - 2, examples - 1):
        for copy in out_copies(e):
            copy.wait()
    if comm:
        s.drain()


def self_back_kernel(comm, r):
    rows, width = r.x.shape
    blocks = rows // MOST
    thirds = width // 256
    if comm:
        p = Place()

        def parts(u, c, y):
            at = slice(y * WIDE, (y + 1) * WIDE)
            if u < 2:
                return r.dwkv.at[u, :, :, c, :, at]
            if u == 2:
                return r.dwoc.at[:, :, c, :, at]
            return r.dw.at[u - 3, :, :, c, :, at]

        s = Scatter(p, parts, r)
        greet(p.near())
        step = s.step
    else:
        step = lambda *units: None

    def put(m, j, value):
        if comm:
            r.dw[m, 2 * j : 2 * j + 2] = value.astype(BF).reshape(2, 2, 2, PIECE, width)
        else:
            r.dw[m, WIDE * j : WIDE * (j + 1), :] = value.astype(BF)

    halves = width // WIDE
    examples = r.denc.shape[0]
    loads = [local(r.sq.at[m], r.w.at[m], r.wsem.at[m]) for m in range(7)]
    for copy in loads:
        copy.start()

    def fetches(e):
        return [
            local(r.dk2.at[e], r.dkv.at[e % 2, 0], r.esem.at[e % 2, 0]),
            local(r.dv2.at[e], r.dkv.at[e % 2, 1], r.esem.at[e % 2, 1]),
        ]

    def out_copy(e):
        return local(r.denv.at[e % 2], r.denc.at[e], r.dsem.at[e % 2])

    for e in (0, 1):
        for copy in fetches(e):
            copy.start()
    step(0, 0, 1, 2)
    for j in range(halves):
        at = slice(WIDE * j, WIDE * (j + 1))
        put(0, j, tn(r.dq2[:, at], r.n2[...]))
    step(0, 3)
    for copy in loads:
        copy.wait()

    def query(j):
        at = lanes(j, 256)
        r.back[:, at] = nn(r.dq2[...], w_lanes(r.w, 6, at))

    loop(0, thirds, query)
    step(1, 0, 1)
    dz, dw = rms_back(r.h1[...], r.gains[1:2, :], r.back[...])
    r.gain[1:2, :] = dw
    r.dh1[...] = r.dh2[...] + dz
    r.b1[...] = r.dh1[...].astype(BF)
    for j in range(halves):
        at = slice(WIDE * j, WIDE * (j + 1))
        put(1, j, tn(r.b1[:, at], r.a1[...]))
    step(0, 4)
    step(1, 2, 3)

    def out(j):
        at = lanes(j, 256)
        r.da1[:, at] = nn(r.b1[...], w_lanes(r.w, 5, at)).astype(BF)

    loop(0, thirds, out)
    self_masks(r.lengths[...], r.mask)
    a = lax.broadcasted_iota(jnp.int32, (MOST, MOST), 0)
    b = lax.broadcasted_iota(jnp.int32, (MOST, MOST), 1)
    flip = (a + b == MOST - 1).astype(F32)

    def attend(pair):
        at = lanes(pair, 128)
        bias = pair_bias(r.dist, pair)
        r.dksum[...] = jnp.zeros_like(r.dksum)
        r.dvsum[...] = jnp.zeros_like(r.dvsum)
        skewed = jnp.zeros((2 * MOST, 2 * MOST), F32)
        for i in range(blocks):
            own = slice(MOST * i, MOST * (i + 1))
            band = slice(MOST * i, MOST * (i + 2))
            queries = split_heads(r.q1[own, at])
            deltas = split_heads(r.da1[own, at])
            keys = r.k1[band, at]
            probs = softmax(masked_scores(nt(queries, keys), bias, r.mask[i]))
            dprobs = nt(deltas, r.v1[band, at])
            dscores = probs * (dprobs - jnp.sum(dprobs * probs, axis=-1, keepdims=True))
            low = dscores.astype(BF)
            skewed = skewed + dscores
            r.dvsum[band, :] += tn(probs.astype(BF), deltas)
            r.dksum[band, :] += tn(low, queries)
            r.dq[own, at] = join_heads(nn(low, keys)).astype(BF)
        r.dk[:, at] = r.dksum[MOST:, :].astype(BF)
        r.dv[:, at] = r.dvsum[MOST:, :].astype(BF)
        for h in range(2):
            flipped = jnp.dot(
                flip,
                skewed[MOST * h : MOST * (h + 1)],
                precision=lax.Precision.HIGHEST,
                preferred_element_type=F32,
            )
            straight = pltpu.roll(flipped, MOST + 1, 1, stride=1, stride_axis=0)
            r.distsum[pl.ds(2 * pair + h, 1), :] = jnp.sum(straight, axis=0, keepdims=True)

    plan = {
        0: ((2, 0, 1), (1, 4)),
        1: ((2, 2, 3),),
        2: ((3, 0, 1), (2, 4)),
        3: ((3, 2, 3),),
        4: ((4, 0, 1), (3, 4)),
        5: ((4, 2, 3),),
    }

    def attend_tick(pair):
        if comm:
            for t, steps in plan.items():

                @pl.when(pair == t)
                def _():
                    for numbers in steps:
                        step(*numbers)

        attend(pair)

    loop(0, PAIRS, attend_tick)
    step(4, 4)
    for m, ref in ((2, r.dq), (3, r.dk), (4, r.dv)):
        for j in range(halves):
            at = slice(WIDE * j, WIDE * (j + 1))
            put(m, j, tn(ref[:, at], r.n1[...]))
        step(0, 3 + m)
    step(1, 5, 6)

    def qkv(j):
        at = lanes(j, 256)
        r.back[:, at] = (
            nn(r.dq[...], w_lanes(r.w, 2, at))
            + nn(r.dk[...], w_lanes(r.w, 3, at))
            + nn(r.dv[...], w_lanes(r.w, 4, at))
        )

    loop(0, thirds, qkv)
    step(1, 7)
    dz, dw = rms_back(r.x[...].astype(F32), r.gains[0:1, :], r.back[...])
    r.gain[0:1, :] = dw
    r.dx[...] = (r.dh1[...] + dz).astype(BF)
    by_bucket = jnp.dot(
        r.distsum[...], distance_hot(0), precision=lax.Precision.HIGHEST, preferred_element_type=F32
    )
    r.small[...] = jnp.zeros_like(r.small)
    r.small[0:2, :] = r.gain[0:2, :]
    r.small[2:3, :] = r.gain3[...]
    r.small[3 : 3 + HEADS, 0:BUCKETS] = by_bucket

    def encoder(e):
        for copy in fetches(e):
            copy.wait()

        @pl.when(e >= 2)
        def _():
            out_copy(e - 2).wait()

        def dense(j):
            at = lanes(j, 256)
            r.denv[e % 2, :, at] = (
                nn(r.dkv[e % 2, 0], w_lanes(r.w, 0, at)) + nn(r.dkv[e % 2, 1], w_lanes(r.w, 1, at))
            ).astype(BF)

        loop(0, thirds, dense)
        out_copy(e).start()

        @pl.when(e + 2 < examples)
        def _():
            for copy in fetches(e + 2):
                copy.start()

    if comm:
        pairs = [p.at(c=1 - p.c), p.at(y=1 - p.y), p.at(x=1 - p.x),
                 p.at(z=p.z + 1 - 2 * (p.z % 2)), p.at(z=(p.z + 2) % 4)]

        def share(i):
            return remote(r.given.at[i], r.gotten.at[i], r.smsem.at[0, i], r.smsem.at[1, i], pairs[i])

        def share_go(i):
            r.given[i] = r.small[...]
            share(i).start()

        def share_end(i):
            share(i).wait_recv()
            r.small[...] = r.small[...] + r.gotten[i]

        share_go(0)
        loop(0, 2, encoder)
        share_end(0)
        share_go(1)
        step(2, 6, 5)
        loop(2, 3, encoder)
        step(2, 7)
        loop(3, 4, encoder)
        share_end(1)
        share_go(2)
        step(3, 6, 5)
        loop(4, 5, encoder)
        share_end(2)
        share_go(3)
        loop(5, 6, encoder)
        step(3, 7)
        loop(6, 7, encoder)
        share_end(3)
        share_go(4)
        step(4, 6, 5)
        loop(7, examples, encoder)
        share_end(4)
        step(4, 7)
    else:
        loop(0, examples, encoder)
    for e in (examples - 2, examples - 1):
        out_copy(e).wait()
    if not comm:
        return

    first = p.c == 0

    def split(ref, n):
        low, high = ref[0:n, :, :192], ref[0:n, :, 192:]
        return jnp.where(first, low, high), jnp.where(first, high, low)

    keep_sq, r.give[0:8] = split(r.fin, 8)
    keep_fi, r.give[8:12] = split(r.finf, 4)
    r.giveo[...] = r.finf[pl.ds(4 + 2 * (1 - p.c), 2)]
    sib = p.at(c=1 - p.c)
    trade = [
        remote(r.give, r.take, r.xsem.at[0], r.xsem.at[1], sib),
        remote(r.giveo, r.takeo, r.xsem.at[2], r.xsem.at[3], sib),
    ]
    for copy in trade:
        copy.start()
    for copy in trade:
        copy.wait_recv()

    def both(a, b, axis):
        return jnp.concatenate([jnp.where(first, a, b), jnp.where(first, b, a)], axis=axis)

    r.tsq[...] = both(keep_sq, r.take[0:8], 1)
    r.tfi[...] = both(keep_fi.reshape(192, 192), r.take[8:12].reshape(192, 192), 0)
    own = r.finf[pl.ds(4 + 2 * p.c, 2)]
    r.tfo[...] = both(
        jnp.concatenate([own[0], own[1]], axis=1), jnp.concatenate([r.takeo[0], r.takeo[1]], axis=1), 0
    )
    spot = lax.broadcasted_iota(jnp.int32, (width, 128), 0)
    lane = lax.broadcasted_iota(jnp.int32, (width, 128), 1)
    put_gains = ((spot == lane + 96 * p.f) & (lane < 96)).astype(F32)
    r.gains_own[...] = jnp.dot(
        r.small[0:8, :], put_gains, precision=lax.Precision.HIGHEST, preferred_element_type=F32
    )
    spot = lax.broadcasted_iota(jnp.int32, (8, BUCKETS), 1)
    line = lax.broadcasted_iota(jnp.int32, (8, BUCKETS), 0)
    r.table_own[...] = lax.dot_general(
        (spot == line + 8 * p.d).astype(F32), r.small[3 : 3 + HEADS, 0:BUCKETS], (((1,), (1,)), ((), ())),
        precision=lax.Precision.HIGHEST, preferred_element_type=F32,
    )
    s.drain()
    for i in range(5):
        share(i).wait_send()
    for copy in trade:
        copy.wait_send()


def finish_kernel(r):
    examples = r.denc.shape[0]
    ins = [local(r.denc_in.at[e], r.hold.at[e], r.sem.at[e, 0]) for e in range(examples)]
    outs = [local(r.hold.at[e], r.denc.at[e], r.sem.at[e, 1]) for e in range(examples)]
    for copy in ins:
        copy.start()
    r.dx[...] = r.dx_in[...]
    e192 = eye(192)
    for m, ref in enumerate((r.k_c, r.v_c, r.o_c, r.q_c, r.o_s, r.q_s, r.k_s, r.v_s)):
        ref[...] = nt(e192, r.tsq[m])
    r.f_i[...] = nt(e192, r.tfi[...])
    r.f_o[...] = r.tfo[...].astype(F32)
    r.gains[...] = r.gains_in[0:3, 0:96]
    r.table[...] = r.table_in[...]
    for e in range(examples):
        ins[e].wait()
        outs[e].start()
    for copy in outs:
        copy.wait()


VM = pltpu.VMEM
HBM = pl.ANY


def run(kernel, ins, outs, scratch, name, collective=None, flops=0):
    names = list(ins) + list(outs) + list(scratch)

    def wrapped(*refs):
        kernel(types.SimpleNamespace(**dict(zip(names, refs))))

    arrays, specs = [], []
    for value in ins.values():
        array, spec = value if isinstance(value, tuple) else (value, VM)
        arrays.append(array)
        specs.append(spec if isinstance(spec, pl.BlockSpec) else pl.BlockSpec(memory_space=spec))
    results = pl.pallas_call(
        wrapped,
        grid=(1,),
        in_specs=specs,
        out_specs=[pl.BlockSpec(memory_space=(o[2] if len(o) > 2 else VM)) for o in outs.values()],
        out_shape=[jax.ShapeDtypeStruct(o[0], o[1]) for o in outs.values()],
        scratch_shapes=list(scratch.values()),
        compiler_params=pltpu.CompilerParams(
            vmem_limit_bytes=VMEM_LIMIT,
            collective_id=collective,
            has_side_effects=collective is not None,
        ),
        cost_estimate=pl.CostEstimate(flops=flops, bytes_accessed=20_000_000, transcendentals=0),
        name=name,
    )(*arrays)
    return types.SimpleNamespace(**dict(zip(outs, results)))


def dma(*shape):
    return pltpu.SemaphoreType.DMA(shape)


def body(comm, decoder_in, encoder_out, decoder_lengths, encoder_lengths, norm_gains, rel_table,
         query_self, key_self, value_self, out_self, query_cross, key_cross, value_cross, out_cross,
         feed_in, feed_out, upstream):
    rows, width = decoder_in.shape
    row_count, examples = decoder_lengths.shape
    keys_n = encoder_out.shape[1]
    hidden = feed_in.shape[1] * lax.axis_size("fsdp")
    small = (rows, width)
    cut = (4, 2, 2, PIECE, width)

    index = dict(lengths=decoder_lengths, valid=encoder_lengths[None, :])
    index_scratch = dict(index=VM((2, rows), jnp.int32), hidden=VM((examples, keys_n), F32))

    acts = dict(n1=(small, BF), q1=(small, BF), k1=((rows + MOST, width), BF), v1=((rows + MOST, width), BF),
                a1=(small, BF), h1=(small, F32), n2=(small, BF), q2=(small, BF), a2=(small, BF),
                k2=(encoder_out.shape, BF, HBM), v2=(encoder_out.shape, BF, HBM))
    scratch = dict(
        encv=VM(encoder_out.shape, BF), k2v=VM(encoder_out.shape, BF), v2v=VM(encoder_out.shape, BF),
        wv=VM((7,) + cut, BF), mask=VM((rows // MOST, MOST, 2 * MOST), F32),
        qe=VM((MOST, width), BF), ae=VM((MOST, width), BF), sum=VM(small, F32),
        esem=dma(examples), wsem=dma(7), ksem=dma(examples, 2), **index_scratch,
    )
    ins = dict(x=decoder_in, enc=(encoder_out, HBM), **index)
    if comm:
        ins |= dict(q_s=query_self, k_s=key_self, v_s=value_self, o_s=out_self, q_c=query_cross,
                    o_c=out_cross, k_c=key_cross, v_c=value_cross, f_i=feed_in, f_o=feed_out.T,
                    gains_s=norm_gains, table_s=rel_table)
        fwd = run(
            functools.partial(forward_kernel, True), ins,
            acts | dict(sq=((8,) + cut, BF, HBM), fi=((4, 2, 2, 4, PIECE, width), BF, HBM),
                        fo=((4, 2, 2, PIECE, hidden), BF, HBM), gains=((3, width), F32),
                        dist=((HEADS, 2 * MOST), F32)),
            scratch | dict(
                xt=VM((12, 2, PIECE, 192), BF), xf=VM((2, PIECE, 768), BF), took=VM((12, PIECE, 192), BF),
                tookf=VM((PIECE, 768), BF), own=VM((UNITS, PIECE, WIDE), BF), gt=VM((8, 8, 128), F32),
                tt=VM((4, 8, 128), F32), xsem=dma(4), psem=dma(UNITS), smsem=dma(2, 10),
                ssem=dma(UNITS, 10), rsem=dma(UNITS, 10)),
            "forward", collective=0,
        )
        sq, fi, fo, gains, dist = fwd.sq, fwd.fi, fwd.fo, fwd.gains, fwd.dist
    else:
        order = (key_cross, value_cross, query_self, key_self, value_self, out_self, query_cross, out_cross)
        sq = jnp.stack([m.astype(BF).T for m in order])
        sq = lax.all_gather(sq, "fsdp", axis=1, tiled=True)
        sq = lax.all_gather(sq, "dp", axis=2, tiled=True).reshape((8,) + cut)
        fi = lax.all_gather(feed_in.astype(BF).T, "fsdp", axis=0, tiled=True)
        fi = lax.all_gather(fi, "dp", axis=1, tiled=True)
        fo = lax.all_gather(feed_out.astype(BF).T, "fsdp", axis=0, tiled=True)
        fo = lax.all_gather(fo, "dp", axis=1, tiled=True)
        gains = lax.all_gather(norm_gains.astype(BF), "fsdp", axis=1, tiled=True).astype(F32)
        table = lax.all_gather(rel_table.astype(BF), "dp", axis=0, tiled=True).astype(F32)
        dist = jnp.dot(distance_hot(0), table, precision=lax.Precision.HIGHEST).T
        fwd = run(
            functools.partial(forward_kernel, False),
            ins | dict(sq=(sq, HBM), gains=gains, dist=dist), acts, scratch, "forward",
        )

    feed = run(
        feed_kernel,
        dict(a2=fwd.a2, h1=fwd.h1, c=upstream, gains=gains,
             w=(sq.reshape(8, width, width), pl.BlockSpec((1, width, width), lambda _: (7, 0, 0))),
             fi=fi.reshape(hidden, width), fo=fo.reshape(width, hidden)),
        dict(out=(small, BF), dfi=((hidden, width), BF), dfo=((width, hidden), BF),
             dwoc=((width, width), BF), da2=(small, BF), dh2=(small, F32), gain=((1, width), F32)),
        dict(h2=VM(small, F32), n3=VM(small, BF), sum=VM(small, F32), back=VM(small, F32)),
        "feed",
    )

    ins = dict(enc=(encoder_out, HBM), k2=(fwd.k2, HBM), v2=(fwd.v2, HBM), q2=fwd.q2, da2=feed.da2,
               **index)
    outs = dict(dk2=(encoder_out.shape, BF, HBM), dv2=(encoder_out.shape, BF, HBM), dq2=(small, BF),
                dwkv=((2, width, width), BF))
    scratch = dict(
        encv=VM(encoder_out.shape, BF), k2v=VM(encoder_out.shape, BF), v2v=VM(encoder_out.shape, BF),
        qe=VM((MOST, width), BF), dae=VM((MOST, width), BF), dqe=VM((MOST, width), BF),
        dk=VM((2, keys_n, width), BF), dv=VM((2, keys_n, width), BF),
        sum=VM(small, F32), dwsum=VM((2, width, width), F32), esem=dma(examples, 3), dsem=dma(2, 2),
        **index_scratch,
    )
    fins = {}
    if comm:
        ins |= dict(dfi=(feed.dfi.reshape(4, 2, 2, 4, PIECE, width), HBM),
                    dfo=(feed.dfo.reshape(4, 2, 2, PIECE, hidden), HBM))
        fins = dict(fin=((8, PIECE, WIDE), BF))
        scratch |= scatter_scratch(8)
    mid = run(functools.partial(cross_back_kernel, comm), ins, outs | fins, scratch, "cross_back",
              collective=1 if comm else None)

    five = (5,) + cut if comm else (5, width, width)
    ins = dict(dq2=mid.dq2, n2=fwd.n2, h1=fwd.h1, dh2=feed.dh2, x=decoder_in, n1=fwd.n1, q1=fwd.q1,
               k1=fwd.k1, v1=fwd.v1, a1=fwd.a1, gains=gains, dist=dist, gain3=feed.gain,
               sq=(sq, HBM), dk2=(mid.dk2, HBM), dv2=(mid.dv2, HBM), lengths=decoder_lengths)
    outs = dict(dx=(small, BF), small=((16, width), F32), denc=(encoder_out.shape, BF, HBM))
    scratch = dict(
        mask=VM((rows // MOST, MOST, 2 * MOST), F32), dh1=VM(small, F32), b1=VM(small, BF),
        da1=VM(small, BF), dq=VM(small, BF), dk=VM(small, BF), dv=VM(small, BF),
        dksum=VM((rows + MOST, 128), F32), dvsum=VM((rows + MOST, 128), F32), back=VM(small, F32),
        gain=VM((2, width), F32), distsum=VM((HEADS, 2 * MOST), F32), w=VM((7,) + cut, BF),
        dkv=VM((2, 2, keys_n, width), BF), denv=VM((2, keys_n, width), BF), wsem=dma(7), esem=dma(2, 2),
        dsem=dma(2),
    )
    if comm:
        ins |= dict(dwkv=(mid.dwkv.reshape((2,) + cut), HBM), dwoc=(feed.dwoc.reshape(cut), HBM), finf=mid.fin)
        outs |= dict(tsq=((8, 96, 192), BF), tfi=((384, 192), BF), tfo=((96, 768), BF), gains_own=((8, 128), F32),
                     table_own=((8, HEADS), F32))
        scratch |= dict(
            dw=VM(five, BF), fin=VM((8, PIECE, WIDE), BF), give=VM((12, PIECE, 192), BF),
            take=VM((12, PIECE, 192), BF), giveo=VM((2, PIECE, WIDE), BF), takeo=VM((2, PIECE, WIDE), BF),
            given=VM((5, 16, width), F32), gotten=VM((5, 16, width), F32), smsem=dma(2, 5), xsem=dma(4),
        ) | scatter_scratch(8)
    else:
        outs |= dict(dw=(five, BF))
    last = run(functools.partial(self_back_kernel, comm), ins, outs, scratch, "self_back",
               collective=2 if comm else None)

    if comm:
        square = ((192, 96), F32)
        done = run(
            finish_kernel,
            dict(tsq=last.tsq, tfi=last.tfi, tfo=last.tfo, gains_in=last.gains_own, table_in=last.table_own,
                 dx_in=last.dx, denc_in=(last.denc, HBM)),
            {n: square for n in ("k_c", "v_c", "q_s", "k_s", "v_s", "o_s", "q_c", "o_c")}
            | dict(f_i=((192, 384), F32), f_o=((96, 768), F32), gains=((3, 96), F32), table=((8, HEADS), F32),
                   dx=(small, BF), denc=(encoder_out.shape, BF, HBM)),
            dict(sem=dma(examples, 2), hold=VM(encoder_out.shape, BF)), "finish",
        )
        grads = (done.q_s, done.k_s, done.v_s, done.o_s, done.q_c, done.k_c, done.v_c, done.o_c,
                 done.f_i, done.f_o.T)
        gains_delta, table_delta, dx, denc = done.gains, done.table, done.dx, done.denc
    else:
        def owned(t, rows_axis=0):
            t = lax.psum_scatter(t, "dp", scatter_dimension=1, tiled=True)
            return lax.psum_scatter(t, "fsdp", scatter_dimension=0, tiled=True).astype(F32).T

        dw = last.dw
        grads = tuple(owned(t) for t in (dw[2], dw[3], dw[4], dw[1], dw[0], mid.dwkv[0], mid.dwkv[1],
                                         feed.dwoc, feed.dfi, feed.dfo))
        gains_delta = lax.psum(last.small[0:3], "dp")
        gains_delta = lax.psum_scatter(gains_delta, "fsdp", scatter_dimension=1, tiled=True)
        table_delta = last.small[3 : 3 + HEADS, 0:BUCKETS].T
        table_delta = lax.psum_scatter(table_delta, "dp", scatter_dimension=0, tiled=True)
        table_delta = lax.psum(table_delta, "fsdp")
        dx, denc = last.dx, last.denc
    return (feed.out, dx, denc, gains_delta, table_delta) + grads


def solution(mesh):
    tokens = P(("dp", "fsdp"), None)
    weight = P("dp", "fsdp")
    comm = (mesh.shape["dp"], mesh.shape["fsdp"]) == (4, 8)
    return jax.shard_map(
        functools.partial(body, comm),
        mesh=mesh,
        in_specs=(tokens, P(("dp", "fsdp"), None, None), tokens, P(("dp", "fsdp")), P(None, "fsdp"),
                  P("dp", None)) + (weight,) * 10 + (tokens,),
        out_specs=(tokens, tokens, P(("dp", "fsdp"), None, None), P(None, "fsdp"), P("dp", None))
        + (weight,) * 10,
        check_vma=False,
    )
```

```python
import functools
import math
import types

import jax
import jax.numpy as jnp
from jax import lax
from jax.experimental import pallas as pl
from jax.experimental.pallas import tpu as pltpu
from jax.sharding import PartitionSpec as P

HEADS = 12
HEAD_DIM = 64
BUCKETS = 32
MAX_DIST = 128
MOST = 128
PAIRS = HEADS // 2
EPSILON = 1e-06
HIDDEN_SCORE = -1e30
BF = jnp.bfloat16
F32 = jnp.float32
VMEM_LIMIT = 60 * 1024 * 1024


def nn(a, b):
    return lax.dot_general(a, b, (((1,), (0,)), ((), ())), preferred_element_type=F32)


def nt(a, b):
    return lax.dot_general(a, b, (((1,), (1,)), ((), ())), preferred_element_type=F32)


def tn(a, b):
    return lax.dot_general(a, b, (((0,), (0,)), ((), ())), preferred_element_type=F32)


def rms(z, gain):
    factor = lax.rsqrt(jnp.mean(z * z, axis=-1, keepdims=True) + EPSILON)
    return z * factor * gain


def rms_back(z, gain, dy):
    factor = lax.rsqrt(jnp.mean(z * z, axis=-1, keepdims=True) + EPSILON)
    wdy = dy * gain
    inner = jnp.mean(z * wdy, axis=-1, keepdims=True)
    dz = factor * wdy - z * (factor * factor * factor * inner)
    return dz, jnp.sum(dy * z * factor, axis=0, keepdims=True)


def split_heads(rows):
    first = lax.broadcasted_iota(jnp.int32, rows.shape, 1) < HEAD_DIM
    zero = jnp.zeros_like(rows)
    return jnp.concatenate([jnp.where(first, rows, zero), jnp.where(first, zero, rows)], axis=0)


def join_heads(rows):
    half = rows.shape[0] // 2
    first = lax.broadcasted_iota(jnp.int32, (half, rows.shape[1]), 1) < HEAD_DIM
    return jnp.where(first, rows[:half], rows[half:])


def softmax(scores):
    raised = jnp.exp(scores - jnp.max(scores, axis=-1, keepdims=True))
    return raised * (1.0 / jnp.sum(raised, axis=-1, keepdims=True))


def lanes(index, width):
    return pl.ds(pl.multiple_of(index * width, width), width)


def loop(low, high, step, unroll=1):
    def run(index, carry):
        step(index)
        return carry

    lax.fori_loop(low, high, run, 0, unroll=unroll)


def quiet(act):
    act()


def bucket_of(distance):
    half_count = BUCKETS // 2
    counted = jnp.zeros_like(distance)
    for section_index in range(1, half_count):
        edge_at = int(
            math.ceil(half_count * (MAX_DIST / half_count) ** (section_index / half_count))
        )
        counted = counted + (distance >= edge_at).astype(jnp.int32)
    return jnp.where(distance < half_count, distance, half_count + counted)


def distance_hot(axis):
    shape = (2 * MOST, BUCKETS) if axis == 0 else (BUCKETS, 2 * MOST)
    distance = jnp.maximum(MOST - lax.broadcasted_iota(jnp.int32, shape, axis), 0)
    return (bucket_of(distance) == lax.broadcasted_iota(jnp.int32, shape, 1 - axis)).astype(F32)


def segments(lengths, shape, axis, shift=0):
    places = lax.broadcasted_iota(jnp.int32, shape, axis) - shift
    end = jnp.zeros((1, 1), jnp.int32)
    example = jnp.where(places < 0, -1, 0)
    start = jnp.zeros(shape, jnp.int32)
    for e in range(lengths.shape[1]):
        length = lengths[:, e : e + 1]
        end = end + length
        example = example + (places >= end).astype(jnp.int32)
        start = start + jnp.where(places >= end, length, 0)
    return example, places - start


def local(src, dst, sem):
    return pltpu.make_async_copy(src, dst, sem)


def w_rows(ref, m, j):
    return ref[m, pl.ds(2 * j, 2)].reshape(2 * WIDE // 2, ref.shape[-1])


def w_lanes(ref, m, at):
    part = ref[m, :, :, :, :, at]
    return part.reshape(-1, part.shape[-1])


MESH = pl.DeviceIdType.MESH
PIECE = 48
WIDE = 384
UNITS = 16
ALL = slice(None)
LOW, HIGH = slice(0, 2), slice(2, 4)


class Place:
    def __init__(self):
        self.d, self.f = lax.axis_index("dp"), lax.axis_index("fsdp")
        self.y, self.c = self.d // 2, self.d % 2
        self.z, self.x = self.f // 2, self.f % 2
        self.nx, self.ny, self.nc = 1 - self.x, 1 - self.y, 1 - self.c

    def at(self, z=None, x=None, y=None, c=None):
        z = self.z if z is None else z
        x = self.x if x is None else x
        y = self.y if y is None else y
        c = self.c if c is None else c
        return (y * 2 + c, z * 2 + x)

    def near(self):
        others = [self.at(z=(self.z + k) % 4) for k in (1, 2, 3)]
        return others + [self.at(x=1 - self.x), self.at(y=1 - self.y), self.at(c=1 - self.c)]


def greet(peers, between=lambda: None):
    barrier = pltpu.get_barrier_semaphore()
    for dev in peers:
        pl.semaphore_signal(barrier, inc=1, device_id=dev, device_id_type=MESH)
    between()
    pl.semaphore_wait(barrier, len(peers))


def eye(n):
    a = lax.broadcasted_iota(jnp.int32, (n, n), 0)
    b = lax.broadcasted_iota(jnp.int32, (n, n), 1)
    return (a == b).astype(F32).astype(BF)


def remote(src, dst, send, recv, dev):
    return pltpu.make_async_remote_copy(
        src_ref=src, dst_ref=dst, send_sem=send, recv_sem=recv, device_id=dev, device_id_type=MESH
    )


class Sends:
    def __init__(self, place, ssem, rsem):
        self.p, self.ssem, self.rsem, self.made = place, ssem, rsem, {}

    def to_x(self):
        return self.p.at(x=1 - self.p.x)

    def to_y(self):
        return self.p.at(y=1 - self.p.y)

    def to_c(self):
        return self.p.at(c=1 - self.p.c)

    def go(self, u, slot, src, dst, dev):
        def make():
            return remote(src(), dst(), self.ssem.at[u, slot], self.rsem.at[u, slot], dev())

        make().start()
        self.made[u, slot] = make

    def wait(self, u, *slots):
        for slot in slots:
            self.made[u, slot]().wait_recv()

    def drain(self):
        for make in self.made.values():
            make().wait_send()


class Gather(Sends):
    def __init__(self, place, own, sq, fi, fo, ssem, rsem):
        super().__init__(place, ssem, rsem)
        self.own, self.sq, self.fi, self.fo = own, sq, fi, fo

    def piece(self, u, z, x, c, y):
        if u < 8:
            return self.sq.at[u, z, x, c, :, pl.ds(pl.multiple_of(y * WIDE, WIDE), WIDE)]
        if u < 12:
            return self.fi.at[z, x, c, u - 8, :, pl.ds(pl.multiple_of(y * WIDE, WIDE), WIDE)]
        at = y * (4 * WIDE) + (u - 12) * WIDE
        return self.fo.at[z, x, c, :, pl.ds(pl.multiple_of(at, WIDE), WIDE)]

    def same(self, u, slot, dev, z, x, c, y):
        def here():
            return self.piece(u, z, x, c, y)

        self.go(u, slot, here, here, dev)

    def first(self, u):
        p = self.p
        for k in (1, 2, 3):
            self.go(
                u, k - 1, lambda: self.own.at[u], lambda: self.piece(u, p.z, p.x, p.c, p.y),
                lambda k=k: p.at(z=(p.z + k) % 4),
            )

    def second(self, u):
        p = self.p
        self.wait(u, 0, 1, 2)
        self.same(u, 3, self.to_x, LOW, p.x, p.c, p.y)
        self.same(u, 4, self.to_y, HIGH, p.x, p.c, p.y)

    def third(self, u):
        p = self.p
        self.wait(u, 3, 4)
        self.same(u, 5, self.to_y, LOW, ALL, p.c, p.y)
        for y in (0, 1):
            self.same(u, 6 + y, self.to_x, HIGH, p.x, p.c, y)
        self.same(u, 8, self.to_c, LOW, ALL, p.c, p.y)
        for y in (0, 1):
            self.same(u, 9 + y, self.to_c, HIGH, p.x, p.c, y)

    def fourth(self, u):
        p = self.p
        self.wait(u, 5, 6, 7)
        self.same(u, 11, self.to_c, LOW, ALL, p.c, p.ny)
        for y in (0, 1):
            self.same(u, 12 + y, self.to_c, HIGH, p.nx, p.c, y)

    def fifth(self, u):
        self.wait(u, *range(8, 14))

    def begin(self):
        for act, u in ((self.second, 0), (self.second, 1), (self.third, 0),
                       (self.third, 1), (self.second, 2), (self.second, 3), (self.fourth, 0), (self.fourth, 1),
                       (self.second, 4)):
            act(u)

    def tick(self, t):
        if 2 <= t:
            self.fourth(t)
        if t + 2 < UNITS:
            self.third(t + 2)
        if t + 5 < UNITS:
            self.second(t + 5)


class Scatter(Sends):
    def __init__(self, place, parts, staged, r):
        super().__init__(place, r.ssem, r.rsem)
        self.parts, self.staged, self.r = parts, staged, r

    def halves(self, u):
        p, r = self.p, self.r
        return [local(self.parts(u, p.c, y), r.stage.at[u, y], r.lsem.at[u, y]) for y in (0, 1)]

    def own(self, u, y):
        if u < self.staged:
            return self.r.stage[u, pl.ds(y, 1)]
        return self.parts(u, self.p.c, y)[...][None]

    def r0(self, u):
        p, r = self.p, self.r
        for y in (0, 1):
            self.go(
                u, y, lambda y=y: self.parts(u, p.nc, y), lambda y=y: r.land.at[u, y], self.to_c
            )
        if u < self.staged:
            for copy in self.halves(u):
                copy.start()

    def r1(self, u):
        p, r = self.p, self.r
        self.wait(u, 0, 1)
        if u < self.staged:
            for copy in self.halves(u):
                copy.wait()
        for y in (p.ny, p.y):
            at = pl.ds(y, 1)
            r.land[u, at] = r.land[u, at] + self.own(u, y)
            if y is p.ny:
                self.go(
                    u, 2, lambda: r.land.at[u, p.ny, LOW], lambda: r.land1.at[u, LOW], self.to_y
                )
        for y in (0, 1):
            self.go(
                u, 3 + y, lambda y=y: r.land.at[u, y, HIGH, p.nx], lambda y=y: r.land1.at[u, HIGH, y],
                self.to_x,
            )

    def r2(self, u):
        p, r = self.p, self.r
        self.wait(u, 2, 3, 4)
        own, x = pl.ds(p.y, 1), pl.ds(p.x, 1)
        r.land[u, own, LOW] = r.land[u, own, LOW] + r.land1[u, LOW][None]
        for y in (0, 1):
            r.land[u, y, HIGH, x] = r.land[u, y, HIGH, x] + r.land1[u, HIGH, y][:, None]
        self.go(u, 5, lambda: r.land.at[u, p.y, LOW, p.nx], lambda: r.land2.at[u, LOW], self.to_x)
        self.go(u, 6, lambda: r.land.at[u, p.ny, HIGH, p.x], lambda: r.land2.at[u, HIGH], self.to_y)

    def r3(self, u):
        p, r = self.p, self.r
        self.wait(u, 5, 6)
        y, x = pl.ds(p.y, 1), pl.ds(p.x, 1)
        r.land[u, y, :, x] = r.land[u, y, :, x] + r.land2[u][None, :, None]
        for k in (1, 2, 3):
            self.go(
                u, 6 + k, lambda k=k: r.land.at[u, p.y, (p.z + k) % 4, p.x],
                lambda k=k: r.land3.at[u, k - 1], lambda k=k: p.at(z=(p.z + k) % 4),
            )

    def r4(self, u):
        p, r = self.p, self.r
        self.wait(u, 7, 8, 9)
        part = r.land[u, pl.ds(p.y, 1), pl.ds(p.z, 1), pl.ds(p.x, 1)]
        total = part.reshape(PIECE, WIDE).astype(F32)
        for k in range(3):
            total = total + r.land3[u, k].astype(F32)
        r.fin[u] = total.astype(BF)

    def step(self, number, *units):
        act = (self.r0, self.r1, self.r2, self.r3, self.r4)[number]
        for u in units:
            act(u)


def scatter_scratch(count, staged):
    return dict(
        land=pltpu.VMEM((count, 2, 4, 2, PIECE, WIDE), BF),
        stage=pltpu.VMEM((staged, 2, 4, 2, PIECE, WIDE), BF),
        land1=pltpu.VMEM((count, 4, 2, PIECE, WIDE), BF),
        land2=pltpu.VMEM((count, 4, PIECE, WIDE), BF),
        land3=pltpu.VMEM((count, 3, PIECE, WIDE), BF),
        ssem=pltpu.SemaphoreType.DMA((count, 10)),
        rsem=pltpu.SemaphoreType.DMA((count, 10)),
        lsem=pltpu.SemaphoreType.DMA((staged, 2)),
    )


def self_masks(lengths, mask_ref):
    blocks = mask_ref.shape[0]
    seg_col = segments(lengths, (blocks * MOST, 1), 0)[0]
    seg_row = segments(lengths, (1, (blocks + 1) * MOST), 1, MOST)[0]
    a = lax.broadcasted_iota(jnp.int32, (MOST, 2 * MOST), 0)
    b = lax.broadcasted_iota(jnp.int32, (MOST, 2 * MOST), 1)
    causal = b <= a + MOST
    for i in range(blocks):
        same = seg_col[MOST * i : MOST * (i + 1), :] == seg_row[:, MOST * i : MOST * (i + 2)]
        mask_ref[i] = jnp.where(causal & same, 0.0, HIDDEN_SCORE)


def pair_bias(dist_ref, pair):
    parts = []
    for h in range(2):
        row = dist_ref[pl.ds(2 * pair + h, 1), :]
        parts.append(
            pltpu.roll(jnp.broadcast_to(row, (MOST, 2 * MOST)), 0, 1, stride=1, stride_axis=0)
        )
    return jnp.concatenate(parts, axis=0)


def masked_scores(scores, bias, mask):
    both = scores + bias
    return (both.reshape(2, MOST, 2 * MOST) + mask[None]).reshape(2 * MOST, 2 * MOST)


def example_rows(index_ref, example, total):
    place = lax.broadcasted_iota(jnp.int32, (MOST, total), 0)
    here = (index_ref[0:1, :] == example) & (index_ref[1:2, :] == place)
    return here.astype(F32).astype(BF)


def example_index(r, total):
    r.index[0:1, :], r.index[1:2, :] = segments(r.lengths[...], (1, total), 1)
    examples, keys_n = r.hidden.shape
    place = lax.broadcasted_iota(jnp.int32, (1, keys_n), 1)
    for e in range(examples):
        r.hidden[e : e + 1, :] = jnp.where(place < r.valid[:, e : e + 1], 0.0, HIDDEN_SCORE)


def turn_squares(r, *which):
    shards = (r.k_c, r.v_c, r.q_s, r.k_s, r.v_s, r.o_s, r.q_c, r.o_c)
    e96 = eye(96)
    for m in which:
        r.xt[m] = nt(e96, shards[m][...].astype(BF)).astype(BF).reshape(2, PIECE, 192)


def turn_feeds(r):
    t = nt(eye(384), r.f_i[...].astype(BF)).astype(BF).reshape(2, 4, PIECE, 192)
    for s in range(4):
        for h in range(2):
            r.xt[8 + s, h] = t[h, s]
    r.xf[...] = r.f_o[...].astype(BF).reshape(2, PIECE, 768)


def own_parts(p, r, low, high):
    first = p.c == 0
    mine = r.xt[low:high, pl.ds(p.c, 1)].reshape(high - low, PIECE, 192)
    other = r.took[low:high]
    r.own[low:high] = jnp.concatenate(
        [jnp.where(first, mine, other), jnp.where(first, other, mine)], axis=-1
    )


def small_sends(p, r):
    made = []
    for k in range(1, 8):
        dev = (p.d, (p.f + k) % 8)
        made.append(
            remote(r.gt.at[p.f], r.gt.at[p.f], r.smsem.at[0, k - 1], r.smsem.at[1, k - 1], dev)
        )
    for k in range(1, 4):
        dev = ((p.d + k) % 4, p.f)
        made.append(
            remote(r.tt.at[p.d], r.tt.at[p.d], r.smsem.at[0, 6 + k], r.smsem.at[1, 6 + k], dev)
        )
    return made


def forward_kernel(comm, r):
    rows, width = r.x.shape
    examples, keys_n = r.enc.shape[0], r.enc.shape[1]
    blocks = rows // MOST
    enc_copies = [local(r.enc.at[e], r.encv.at[e], r.esem.at[e]) for e in range(examples)]
    for copy in enc_copies:
        copy.start()
    if comm:
        p = Place()
        peers = [(p.d, (p.f + k) % 8) for k in range(1, 8)] + [((p.d + k) % 4, p.f) for k in range(1, 4)]

        def prepare():
            r.gt[pl.ds(p.f, 1)] = jnp.zeros((1, 8, 128), F32)
            r.gt[pl.ds(p.f, 1), 0:3, 0:96] = r.gains_s[...].astype(BF).astype(F32)[None]
            r.tt[pl.ds(p.d, 1)] = jnp.zeros((1, 8, 128), F32)
            r.tt[pl.ds(p.d, 1), :, 0:HEADS] = r.table_s[...].astype(BF).astype(F32)[None]
            turn_squares(r, 0, 1)

        greet(peers, prepare)
        sib = p.at(c=1 - p.c)
        trade = [
            remote(r.xt.at[0:2, 1 - p.c], r.took.at[0:2], r.xsem.at[0], r.xsem.at[1], sib),
            remote(r.xt.at[2:12, 1 - p.c], r.took.at[2:12], r.xsem.at[2], r.xsem.at[3], sib),
            remote(r.xf.at[1 - p.c], r.tookf, r.xsem.at[4], r.xsem.at[5], sib),
        ]
        small = small_sends(p, r)
        for copy in trade[0:1] + small:
            copy.start()
        turn_feeds(r)
        g = Gather(p, r.own, r.sq, r.fi, r.fo, r.ssem, r.rsem)
        placed = [
            local(r.own.at[u], g.piece(u, p.z, p.x, p.c, p.y), r.psem.at[u]) for u in range(UNITS)
        ]
        trade[0].wait_recv()
        own_parts(p, r, 0, 2)
        for u in (0, 1):
            g.first(u)
            placed[u].start()
        turn_squares(r, 2, 3, 4, 5, 6, 7)
        for copy in trade[1:]:
            copy.start()
        first = p.c == 0
        trade[1].wait_recv()
        own_parts(p, r, 2, 12)
        trade[2].wait_recv()
        mine, other = r.xf[pl.ds(p.c, 1)].reshape(PIECE, 768), r.tookf[...]
        low, high = jnp.where(first, mine, other), jnp.where(first, other, mine)
        r.own[12], r.own[13] = low[:, :WIDE], low[:, WIDE:]
        r.own[14], r.own[15] = high[:, :WIDE], high[:, WIDE:]
        for u in range(2, UNITS):
            g.first(u)
            placed[u].start()
        for copy in small:
            copy.wait_recv()
        spot = lax.broadcasted_iota(jnp.int32, (128, width), 1)
        lane = lax.broadcasted_iota(jnp.int32, (128, width), 0)
        gains = jnp.zeros((8, width), F32)
        for f in range(8):
            put = ((spot == lane + 96 * f) & (lane < 96)).astype(F32).astype(BF)
            gains = gains + nn(r.gt[f].astype(BF), put)
        r.gains[...] = gains[0:3]
        table = r.tt[...].reshape(BUCKETS, 128).astype(BF)
        r.dist[...] = tn(table, distance_hot(1).astype(BF))[0:HEADS]
        for copy in placed:
            copy.wait()
        begin, tick, arrived = g.begin, g.tick, g.fifth
    else:
        begin, tick, arrived = (lambda *_: None,) * 3

    loads = [local(r.sq.at[m], r.wv.at[m], r.wsem.at[m]) for m in range(7)]

    def fetch(*which):
        for m in which:
            arrived(m)
            loads[m].start()

    def have(*which):
        for m in which:
            loads[m].wait()

    example_index(r, rows)
    r.n1[...] = rms(r.x[...].astype(F32), r.gains[0:1, :]).astype(BF)
    r.k1[0:MOST, :] = jnp.zeros((MOST, width), BF)
    r.v1[0:MOST, :] = jnp.zeros((MOST, width), BF)
    self_masks(r.lengths[...], r.mask)
    halves = width // WIDE

    def save(e):
        return [local(r.k2v.at[e], r.k2.at[e], r.ksem.at[e, 0]), local(r.v2v.at[e], r.v2.at[e], r.ksem.at[e, 1])]

    def project(e):
        local(r.enc.at[e], r.encv.at[e], r.esem.at[e]).wait()
        for j in range(halves):
            at = slice(WIDE * j, WIDE * (j + 1))
            r.k2v[e, :, at] = nt(r.encv[e], w_rows(r.wv, 0, j)).astype(BF)
            r.v2v[e, :, at] = nt(r.encv[e], w_rows(r.wv, 1, j)).astype(BF)
        for copy in save(e):
            copy.start()

    begin()
    fetch(0, 1)
    have(0, 1)
    for t in range(4):
        tick(t)
        loop(2 * t, 2 * t + 2, project)
    fetch(2, 3)
    tick(4)
    fetch(4)
    have(2, 3, 4)

    for j in range(halves):
        at = slice(WIDE * j, WIDE * (j + 1))
        r.q1[:, at] = nt(r.n1[...], w_rows(r.wv, 2, j)).astype(BF)
        r.k1[MOST:, at] = nt(r.n1[...], w_rows(r.wv, 3, j)).astype(BF)
        r.v1[MOST:, at] = nt(r.n1[...], w_rows(r.wv, 4, j)).astype(BF)

    def attend(pair):
        at = lanes(pair, 128)
        bias = pair_bias(r.dist, pair)
        for i in range(blocks):
            queries = split_heads(r.q1[MOST * i : MOST * (i + 1), at])
            keys = r.k1[MOST * i : MOST * (i + 2), at]
            values = r.v1[MOST * i : MOST * (i + 2), at]
            probs = softmax(masked_scores(nt(queries, keys), bias, r.mask[i])).astype(BF)
            r.a1[MOST * i : MOST * (i + 1), at] = join_heads(nn(probs, values)).astype(BF)

    tick(5)
    loop(0, PAIRS // 2, attend, PAIRS // 2)
    tick(6)
    fetch(5)
    loop(PAIRS // 2, PAIRS, attend, PAIRS // 2)
    tick(7)
    fetch(6)
    have(5, 6)
    for j in range(halves):
        at = slice(WIDE * j, WIDE * (j + 1))
        r.h1[:, at] = r.x[:, at].astype(F32) + nt(r.a1[...], w_rows(r.wv, 5, j))
    r.n2[...] = rms(r.h1[...], r.gains[1:2, :]).astype(BF)
    for j in range(halves):
        at = slice(WIDE * j, WIDE * (j + 1))
        r.q2[:, at] = nt(r.n2[...], w_rows(r.wv, 6, j)).astype(BF)

    r.sum[...] = jnp.zeros_like(r.sum)

    def cross(e):
        pick = example_rows(r.index, e, rows)
        r.qe[...] = nn(pick, r.q2[...]).astype(BF)
        hidden = r.hidden[pl.ds(e, 1), :]

        def pair_step(pair):
            at = lanes(pair, 128)
            probs = softmax(nt(split_heads(r.qe[:, at]), r.k2v[e, :, at]) + hidden).astype(BF)
            r.ae[:, at] = join_heads(nn(probs, r.v2v[e, :, at])).astype(BF)

        loop(0, PAIRS, pair_step, PAIRS)
        r.sum[...] += tn(pick, r.ae[...])

    def cross_tick(e):
        if comm:
            for t in range(examples):
                pl.when(e == t)(functools.partial(tick, t + 8))
        cross(e)

    loop(0, examples, cross_tick)
    r.a2[...] = r.sum[...].astype(BF)

    def saved(e):
        for copy in save(e):
            copy.wait()

    loop(0, examples, saved)
    if comm:
        for u in range(7, UNITS):
            g.fifth(u)
        g.drain()
        for copy in trade + small:
            copy.wait_send()


GELU_A = math.sqrt(2.0 / math.pi)
GELU_B = 0.044715


def feed_kernel(comm, r):
    rows, width = r.a2.shape
    hidden = r.fi.shape[0]
    if comm:
        p = Place()

        def parts(u, c, y):
            at = pl.ds(pl.multiple_of(y * 4 * WIDE + u * WIDE, WIDE), WIDE)
            return r.dfo.at[:, :, c, :, at]

        s = Scatter(p, parts, 0, r)
        greet(p.near())
    step = s.step if comm else lambda *units: None

    def cross_out(j):
        at = lanes(j, 256)
        r.h2[:, at] = r.h1[:, at] + nt(r.a2[...], r.w[0, at, :])

    loop(0, width // 256, cross_out)
    r.n3[...] = rms(r.h2[...], r.gains[2:3, :]).astype(BF)
    r.sum[...] = r.h2[...]
    r.back[...] = jnp.zeros_like(r.back)

    r.ct[...] = r.c[...].T

    def part(turn):
        j = lax.rem(turn, 2) * 2 + turn // 2
        if comm:
            pl.when(turn == 2)(lambda: step(0, 0, 1))
        for i in range(3):
            at = pl.ds(pl.multiple_of(j * width + i * 256, 256), 256)
            here = slice(256 * i, 256 * (i + 1))
            u = nt(r.n3[...], r.fi[at, :])
            t = jnp.tanh(GELU_A * (u + GELU_B * (u * u * u)))
            r.g[:, here] = (0.5 * u * (1.0 + t)).astype(BF)
            slope = 0.5 * (1.0 + t) + 0.5 * u * (1.0 - t * t) * (
                GELU_A * (1.0 + (3.0 * GELU_B) * (u * u))
            )
            r.du[:, here] = (nn(r.c[...], r.fo[:, at]) * slope).astype(BF)
        if comm:
            pl.when(turn == 2)(lambda: step(1, 0, 1))
            pl.when(turn == 3)(lambda: step(2, 0, 1))
        whole_part = lanes(j, width)
        for i in range(3):
            at = pl.ds(pl.multiple_of(j * width + i * 256, 256), 256)
            here = slice(256 * i, 256 * (i + 1))
            r.dfo[:, :, :, :, at] = nn(r.ct[...], r.g[:, here]).astype(BF).reshape(4, 2, 2, PIECE, 256)
            r.dfi[at, :] = tn(r.du[:, here], r.n3[...]).astype(BF)
            r.sum[:, here] += nt(r.g[...], r.fo[here, whole_part])
            r.back[:, here] += nn(r.du[...], r.fi[whole_part, here])

    loop(0, hidden // width, part)
    r.out[...] = r.sum[...].astype(BF)
    step(3, 0, 1)
    dz, dw = rms_back(r.h2[...], r.gains[2:3, :], r.back[...])
    r.gain[...] = dw
    r.dh2[...] = r.c[...].astype(F32) + dz

    def tail(j):
        at = lanes(j, 256)
        r.da2[:, at] = nn(r.dh2[...].astype(BF), r.w[0, :, at]).astype(BF)
        r.dwoc[at, :] = tn(r.dh2[:, at].astype(BF), r.a2[...]).astype(BF)

    loop(0, width // 256, tail)
    step(4, 0, 1)
    if comm:
        s.drain()


def cross_back_kernel(comm, r):
    rows, width = r.q2.shape
    examples, keys_n = r.k2.shape[0], r.k2.shape[1]

    def fetches(e):
        return [local(getattr(r, a).at[e], getattr(r, b).at[e], r.esem.at[e, i])
                for i, (a, b) in enumerate((("k2", "k2v"), ("v2", "v2v")))]

    for e in range(examples):
        for copy in fetches(e):
            copy.start()
    if comm:
        p = Place()

        def parts(u, c, y):
            if u >= 2:
                return r.dfi.at[:, :, c, u - 2, :, y * WIDE : (y + 1) * WIDE]
            at = y * 4 * WIDE + (u + 2) * WIDE
            return r.dfo.at[:, :, c, :, at : at + WIDE]

        s = Scatter(p, parts, 5, r)
        greet(p.near())
    example_index(r, rows)
    r.sum[...] = jnp.zeros_like(r.sum)

    def out_copies(e):
        return [
            local(r.dk.at[e % 2], r.dk2.at[e], r.dsem.at[e % 2, 0]),
            local(r.dv.at[e % 2], r.dv2.at[e], r.dsem.at[e % 2, 1]),
        ]

    def tick(at):
        if comm:
            for t in range(2 * examples):

                @pl.when(at == t)
                def _():
                    for number in (4, 3, 2, 1, 0):
                        for u, at_first in enumerate((0, 1, 3, 5, 7)):
                            if at_first + 2 * number == t:
                                s.step(number, u)

    def example(e):
        tick(2 * e)
        for copy in fetches(e):
            copy.wait()
        pick = example_rows(r.index, e, rows)
        r.qe[...] = nn(pick, r.q2[...]).astype(BF)
        r.dae[...] = nn(pick, r.da2[...]).astype(BF)
        hidden = r.hidden[pl.ds(e, 1), :]

        @pl.when(e >= 2)
        def _():
            for copy in out_copies(e - 2):
                copy.wait()

        def attend(pair):
            at = lanes(pair, 128)
            queries = split_heads(r.qe[:, at])
            deltas = split_heads(r.dae[:, at])
            keys = r.k2v[e, :, at]
            probs = softmax(nt(queries, keys) + hidden)
            dprobs = nt(deltas, r.v2v[e, :, at])
            low = (probs * (dprobs - jnp.sum(dprobs * probs, axis=-1, keepdims=True))).astype(BF)
            r.dv[e % 2, at, :] = tn(deltas, probs.astype(BF)).astype(BF)
            r.dk[e % 2, at, :] = tn(queries, low).astype(BF)
            r.dqe[:, at] = join_heads(nn(low, keys)).astype(BF)

        loop(0, PAIRS, attend, PAIRS)
        tick(2 * e + 1)
        for copy in out_copies(e):
            copy.start()
        r.sum[...] += tn(pick, r.dqe[...])

    loop(0, examples, example)
    r.dq2[...] = r.sum[...].astype(BF)
    for e in (examples - 2, examples - 1):
        for copy in out_copies(e):
            copy.wait()
    if comm:
        s.drain()


def self_back_kernel(comm, r):
    rows, width = r.x.shape
    blocks = rows // MOST
    thirds = width // 256
    if comm:
        p = Place()

        def parts(u, c, y):
            at = pl.ds(pl.multiple_of(y * WIDE, WIDE), WIDE)
            if u == 0:
                return r.dfi.at[:, :, c, 3, :, at]
            if u == 1:
                return r.dwoc.at[:, :, c, :, at]
            return r.dw.at[u - 2, :, :, c, :, at]

        s = Scatter(p, parts, 2, r)
        greet(p.near())
        step = s.step
    else:
        step = lambda *units: None

    def put(m, j, value):
        if comm:
            r.dw[m, 2 * j : 2 * j + 2] = value.astype(BF).reshape(2, 2, 2, PIECE, width)
        else:
            r.dw[m, WIDE * j : WIDE * (j + 1), :] = value.astype(BF)

    halves = width // WIDE
    examples = r.denc.shape[0]
    loads = [local(r.sq.at[2 + m], r.w.at[m], r.wsem.at[m]) for m in range(5)]
    late = [local(r.sq.at[m], r.w.at[3 + m], r.wsem.at[5 + m]) for m in range(2)]
    for copy in loads:
        copy.start()

    passes = ((r.dk2, r.enc), (r.dv2, r.enc), (r.dk2, r.dv2))

    def fetches(number, e):
        places = (r.one, r.three if number == 2 else r.two)
        return [local(passes[number][i].at[e], places[i].at[e % 2], r.esem.at[e % 2, i]) for i in (0, 1)]

    def pass_step(number, e, act):
        for copy in fetches(number, e):
            copy.wait()
        act(e)

        @pl.when(e + 2 < examples)
        def _():
            for copy in fetches(number, e + 2):
                copy.start()

        if number < 2:

            @pl.when(e + 2 >= examples)
            def _():
                for copy in fetches(number + 1, e + 2 - examples):
                    copy.start()

    def out_copy(e):
        return local(r.denv.at[e % 2], r.denc.at[e], r.dsem.at[e % 2])

    for e in (0, 1):
        for copy in fetches(0, e):
            copy.start()
    step(0, 0, 1)
    for j in range(halves):
        at = slice(WIDE * j, WIDE * (j + 1))
        put(0, j, tn(r.dq2[:, at], r.n2[...]))
    step(0, 2)
    for copy in loads:
        copy.wait()

    def query(j):
        at = lanes(j, 256)
        r.back[:, at] = nn(r.dq2[...], w_lanes(r.w, 4, at))

    loop(0, thirds, query)
    step(1, 0, 1)
    dz, dw = rms_back(r.h1[...], r.gains[1:2, :], r.back[...])
    r.gain[1:2, :] = dw
    r.dh1[...] = r.dh2[...] + dz
    r.b1[...] = r.dh1[...].astype(BF)
    for j in range(halves):
        at = slice(WIDE * j, WIDE * (j + 1))
        put(1, j, tn(r.b1[:, at], r.a1[...]))
    step(0, 3)
    step(1, 2)

    def out(j):
        at = lanes(j, 256)
        r.da1[:, at] = nn(r.b1[...], w_lanes(r.w, 3, at)).astype(BF)

    loop(0, thirds, out)
    for copy in late:
        copy.start()
    self_masks(r.lengths[...], r.mask)
    a = lax.broadcasted_iota(jnp.int32, (MOST, MOST), 0)
    b = lax.broadcasted_iota(jnp.int32, (MOST, MOST), 1)
    flip = (a + b == MOST - 1).astype(F32)

    def attend(pair):
        at = lanes(pair, 128)
        bias = pair_bias(r.dist, pair)
        r.dksum[...] = jnp.zeros_like(r.dksum)
        r.dvsum[...] = jnp.zeros_like(r.dvsum)
        skewed = jnp.zeros((2 * MOST, 2 * MOST), F32)
        for i in range(blocks):
            own = slice(MOST * i, MOST * (i + 1))
            band = slice(MOST * i, MOST * (i + 2))
            queries = split_heads(r.q1[own, at])
            deltas = split_heads(r.da1[own, at])
            keys = r.k1[band, at]
            probs = softmax(masked_scores(nt(queries, keys), bias, r.mask[i]))
            dprobs = nt(deltas, r.v1[band, at])
            dscores = probs * (dprobs - jnp.sum(dprobs * probs, axis=-1, keepdims=True))
            low = dscores.astype(BF)
            skewed = skewed + dscores
            r.dvsum[:, band] += tn(deltas, probs.astype(BF))
            r.dksum[:, band] += tn(queries, low)
            r.dq[own, at] = join_heads(nn(low, keys)).astype(BF)
        r.dk[at, :] = r.dksum[:, MOST:].astype(BF)
        r.dv[at, :] = r.dvsum[:, MOST:].astype(BF)
        for h in range(2):
            flipped = jnp.dot(
                flip,
                skewed[MOST * h : MOST * (h + 1)],
                precision=lax.Precision.HIGHEST,
                preferred_element_type=F32,
            )
            straight = pltpu.roll(flipped, MOST + 1, 1, stride=1, stride_axis=0)
            r.distsum[pl.ds(2 * pair + h, 1), :] = jnp.sum(straight, axis=0, keepdims=True)

    plan = {
        0: ((1, 3),),
        1: ((2, 0, 1),),
        2: ((2, 2),),
        3: ((3, 0, 1), (2, 3)),
        4: ((3, 2),),
        5: ((4, 0, 1), (3, 3)),
    }

    def attend_tick(pair):
        if comm:
            for t, steps in plan.items():

                @pl.when(pair == t)
                def _():
                    for numbers in steps:
                        step(*numbers)

        attend(pair)

    loop(0, PAIRS, attend_tick)
    step(4, 2)
    for m, ref in ((2, r.dq), (3, r.dk), (4, r.dv)):
        for j in range(halves):
            at = slice(WIDE * j, WIDE * (j + 1))
            put(m, j, tn(ref[:, at], r.n1[...]) if m == 2 else nn(ref[at, :], r.n1[...]))
        step(0, 2 + m)
    step(4, 3)
    step(1, 4, 5)

    r.b1[...] = r.dk[...].T
    r.da1[...] = r.dv[...].T

    def qkv(j):
        at = lanes(j, 256)
        r.back[:, at] = (
            nn(r.dq[...], w_lanes(r.w, 0, at))
            + nn(r.b1[...], w_lanes(r.w, 1, at))
            + nn(r.da1[...], w_lanes(r.w, 2, at))
        )

    loop(0, thirds, qkv, thirds)
    step(1, 6)
    dz, dw = rms_back(r.x[...].astype(F32), r.gains[0:1, :], r.back[...])
    r.gain[0:1, :] = dw
    r.dx[...] = (r.dh1[...] + dz).astype(BF)
    by_bucket = jnp.dot(
        r.distsum[...], distance_hot(0), precision=lax.Precision.HIGHEST, preferred_element_type=F32
    )
    r.small[...] = jnp.zeros_like(r.small)
    r.small[0:2, :] = r.gain[0:2, :]
    r.small[2:3, :] = r.gain3[...]
    r.small[3 : 3 + HEADS, 0:BUCKETS] = by_bucket

    if comm:
        pairs = [p.at(c=1 - p.c), p.at(y=1 - p.y), p.at(x=1 - p.x),
                 p.at(z=p.z + 1 - 2 * (p.z % 2)), p.at(z=(p.z + 2) % 4)]

        def share(i):
            return remote(r.given.at[i], r.gotten.at[i], r.smsem.at[0, i], r.smsem.at[1, i], pairs[i])

        def share_go(i):
            r.given[i] = r.small[...]
            share(i).start()

        def share_end(i):
            share(i).wait_recv()
            r.small[...] = r.small[...] + r.gotten[i]

        share_go(0)

    def passing(number, act, events):
        def one(e):
            pass_step(number, e, act)
            if comm:
                for at, happens in events.items():
                    pl.when(e == at)(functools.partial(quiet, happens))

        loop(0, examples, one)

    def weight_sum(e):
        def dense(j):
            at = lanes(j, 256)
            r.dwsum[at, :] = nn(r.one[e % 2, at, :], r.two[e % 2]) + jnp.where(e == 0, 0.0, r.dwsum[at, :])

        loop(0, thirds, dense, thirds)

    def share_next(i):
        share_end(i)
        share_go(i + 1)

    events = (
        {0: lambda: share_next(0), 1: lambda: step(2, 4), 2: lambda: step(2, 5), 4: lambda: step(2, 6),
         5: lambda: step(3, 4), 6: lambda: (step(3, 5), share_next(1)), 7: lambda: step(3, 6)},
        {1: lambda: (step(1, 7), step(4, 4)), 2: lambda: step(4, 5), 3: lambda: share_next(2),
         4: lambda: step(4, 6), 5: lambda: step(2, 7), 7: lambda: share_next(3)},
        {0: lambda: step(3, 7), 1: lambda: step(1, 8), 3: lambda: step(4, 7), 4: lambda: share_end(4),
         5: lambda: step(2, 8), 7: lambda: step(3, 8)},
    )

    r.dwsum[...] = jnp.zeros_like(r.dwsum)
    passing(0, weight_sum, events[0])
    for j in range(halves):
        put(5, j, r.dwsum[WIDE * j : WIDE * (j + 1), :])
    step(0, 7)
    passing(1, weight_sum, events[1])
    for j in range(halves):
        put(6, j, r.dwsum[WIDE * j : WIDE * (j + 1), :])
    step(0, 8)
    for copy in late:
        copy.wait()

    def encoder(e):
        @pl.when(e >= 2)
        def _():
            out_copy(e - 2).wait()

        r.b1[...] = r.one[e % 2].T
        r.da1[...] = r.three[e % 2].T

        def dense(j):
            at = lanes(j, 256)
            r.denv[e % 2, :, at] = (
                nn(r.b1[...], w_lanes(r.w, 3, at)) + nn(r.da1[...], w_lanes(r.w, 4, at))
            ).astype(BF)

        loop(0, thirds, dense, thirds)
        out_copy(e).start()

    passing(2, encoder, events[2])
    step(4, 8)
    for e in (examples - 2, examples - 1):
        out_copy(e).wait()
    if not comm:
        return

    first = p.c == 0

    def split(ref, n):
        low, high = ref[0:n, :, :192], ref[0:n, :, 192:]
        return jnp.where(first, low, high), jnp.where(first, high, low)

    r.all[0:8] = r.fin[1:9]
    r.all[8:11] = r.finf[2:5]
    r.all[11] = r.fin[0]
    keep, r.give[...] = split(r.all, 12)
    r.giveo[...] = jnp.where(first, r.finf[0:2], r.fing[...])
    sib = p.at(c=1 - p.c)
    trade = [
        remote(r.give, r.take, r.xsem.at[0], r.xsem.at[1], sib),
        remote(r.giveo, r.takeo, r.xsem.at[2], r.xsem.at[3], sib),
    ]
    for copy in trade:
        copy.start()
    for copy in trade:
        copy.wait_recv()

    def both(a, b, axis):
        return jnp.concatenate([jnp.where(first, a, b), jnp.where(first, b, a)], axis=axis)

    r.tsq[...] = both(keep[0:8], r.take[0:8], 1)
    r.tfi[...] = both(keep[8:12].reshape(192, 192), r.take[8:12].reshape(192, 192), 0)
    own = jnp.where(first, r.fing[...], r.finf[0:2])
    r.tfo[...] = both(
        jnp.concatenate([own[0], own[1]], axis=1), jnp.concatenate([r.takeo[0], r.takeo[1]], axis=1), 0
    )
    spot = lax.broadcasted_iota(jnp.int32, (width, 128), 0)
    lane = lax.broadcasted_iota(jnp.int32, (width, 128), 1)
    put_gains = ((spot == lane + 96 * p.f) & (lane < 96)).astype(F32)
    r.gains_own[...] = jnp.dot(
        r.small[0:8, :], put_gains, precision=lax.Precision.HIGHEST, preferred_element_type=F32
    )
    spot = lax.broadcasted_iota(jnp.int32, (8, BUCKETS), 1)
    line = lax.broadcasted_iota(jnp.int32, (8, BUCKETS), 0)
    r.table_own[...] = lax.dot_general(
        (spot == line + 8 * p.d).astype(F32), r.small[3 : 3 + HEADS, 0:BUCKETS], (((1,), (1,)), ((), ())),
        precision=lax.Precision.HIGHEST, preferred_element_type=F32,
    )
    s.drain()
    for i in range(5):
        share(i).wait_send()
    for copy in trade:
        copy.wait_send()


def finish_kernel(r):
    examples = r.denc.shape[0]
    ins = [local(r.denc_in.at[e], r.hold.at[e], r.sem.at[e, 0]) for e in range(examples)]
    outs = [local(r.hold.at[e], r.denc.at[e], r.sem.at[e, 1]) for e in range(examples)]
    for copy in ins:
        copy.start()
    r.dx[...] = r.dx_in[...]
    r.out[...] = r.out_in[...]
    e192 = eye(192)
    for m, ref in enumerate((r.o_c, r.q_c, r.o_s, r.q_s, r.k_s, r.v_s, r.k_c, r.v_c)):
        ref[...] = nt(e192, r.tsq[m])
    r.f_i[...] = nt(e192, r.tfi[...])
    r.f_o[...] = r.tfo[...].astype(F32)
    r.gains[...] = r.gains_in[0:3, 0:96]
    r.table[...] = r.table_in[...]
    for e in range(examples):
        ins[e].wait()
        outs[e].start()
    for copy in outs:
        copy.wait()


VM = pltpu.VMEM
HBM = pl.ANY


def run(kernel, ins, outs, scratch, name, collective=None, flops=0):
    names = list(ins) + list(outs) + list(scratch)

    def wrapped(*refs):
        kernel(types.SimpleNamespace(**dict(zip(names, refs))))

    arrays, specs = [], []
    for value in ins.values():
        array, spec = value if isinstance(value, tuple) else (value, VM)
        arrays.append(array)
        specs.append(spec if isinstance(spec, pl.BlockSpec) else pl.BlockSpec(memory_space=spec))
    results = pl.pallas_call(
        wrapped,
        grid=(1,),
        in_specs=specs,
        out_specs=[pl.BlockSpec(memory_space=(o[2] if len(o) > 2 else VM)) for o in outs.values()],
        out_shape=[jax.ShapeDtypeStruct(o[0], o[1]) for o in outs.values()],
        scratch_shapes=list(scratch.values()),
        compiler_params=pltpu.CompilerParams(
            vmem_limit_bytes=VMEM_LIMIT,
            collective_id=collective,
            has_side_effects=collective is not None,
        ),
        cost_estimate=pl.CostEstimate(flops=flops, bytes_accessed=20_000_000, transcendentals=0),
        name=name,
    )(*arrays)
    return types.SimpleNamespace(**dict(zip(outs, results)))


def dma(*shape):
    return pltpu.SemaphoreType.DMA(shape)


def body(comm, decoder_in, encoder_out, decoder_lengths, encoder_lengths, norm_gains, rel_table,
         query_self, key_self, value_self, out_self, query_cross, key_cross, value_cross, out_cross,
         feed_in, feed_out, upstream):
    rows, width = decoder_in.shape
    row_count, examples = decoder_lengths.shape
    keys_n = encoder_out.shape[1]
    hidden = feed_in.shape[1] * lax.axis_size("fsdp")
    small = (rows, width)
    cut = (4, 2, 2, PIECE, width)

    index = dict(lengths=decoder_lengths, valid=encoder_lengths[None, :])
    index_scratch = dict(index=VM((2, rows), jnp.int32), hidden=VM((examples, keys_n), F32))

    acts = dict(n1=(small, BF), q1=(small, BF), k1=((rows + MOST, width), BF), v1=((rows + MOST, width), BF),
                a1=(small, BF), h1=(small, F32), n2=(small, BF), q2=(small, BF), a2=(small, BF),
                k2=(encoder_out.shape, BF, HBM), v2=(encoder_out.shape, BF, HBM))
    scratch = dict(
        encv=VM(encoder_out.shape, BF), k2v=VM(encoder_out.shape, BF), v2v=VM(encoder_out.shape, BF),
        wv=VM((7,) + cut, BF), mask=VM((rows // MOST, MOST, 2 * MOST), F32),
        qe=VM((MOST, width), BF), ae=VM((MOST, width), BF), sum=VM(small, F32),
        esem=dma(examples), wsem=dma(7), ksem=dma(examples, 2), **index_scratch,
    )
    ins = dict(x=decoder_in, enc=(encoder_out, HBM), **index)
    if comm:
        ins |= dict(q_s=query_self, k_s=key_self, v_s=value_self, o_s=out_self, q_c=query_cross,
                    o_c=out_cross, k_c=key_cross, v_c=value_cross, f_i=feed_in, f_o=feed_out.T,
                    gains_s=norm_gains, table_s=rel_table)
        fwd = run(
            functools.partial(forward_kernel, True), ins,
            acts | dict(sq=((8,) + cut, BF, HBM), fi=((4, 2, 2, 4, PIECE, width), BF, HBM),
                        fo=((4, 2, 2, PIECE, hidden), BF, HBM), gains=((3, width), F32),
                        dist=((HEADS, 2 * MOST), F32)),
            scratch | dict(
                xt=VM((12, 2, PIECE, 192), BF), xf=VM((2, PIECE, 768), BF), took=VM((12, PIECE, 192), BF),
                tookf=VM((PIECE, 768), BF), own=VM((UNITS, PIECE, WIDE), BF), gt=VM((8, 8, 128), F32),
                tt=VM((4, 8, 128), F32), xsem=dma(6), psem=dma(UNITS), smsem=dma(2, 10),
                ssem=dma(UNITS, 14), rsem=dma(UNITS, 14)),
            "forward", collective=0,
        )
        sq, fi, fo, gains, dist = fwd.sq, fwd.fi, fwd.fo, fwd.gains, fwd.dist
    else:
        order = (key_cross, value_cross, query_self, key_self, value_self, out_self, query_cross, out_cross)
        sq = jnp.stack([m.astype(BF).T for m in order])
        sq = lax.all_gather(sq, "fsdp", axis=1, tiled=True)
        sq = lax.all_gather(sq, "dp", axis=2, tiled=True).reshape((8,) + cut)
        fi = lax.all_gather(feed_in.astype(BF).T, "fsdp", axis=0, tiled=True)
        fi = lax.all_gather(fi, "dp", axis=1, tiled=True)
        fo = lax.all_gather(feed_out.astype(BF).T, "fsdp", axis=0, tiled=True)
        fo = lax.all_gather(fo, "dp", axis=1, tiled=True)
        gains = lax.all_gather(norm_gains.astype(BF), "fsdp", axis=1, tiled=True).astype(F32)
        table = lax.all_gather(rel_table.astype(BF), "dp", axis=0, tiled=True).astype(F32)
        dist = jnp.dot(distance_hot(0), table, precision=lax.Precision.HIGHEST).T
        fwd = run(
            functools.partial(forward_kernel, False),
            ins | dict(sq=(sq, HBM), gains=gains, dist=dist), acts, scratch, "forward",
        )

    feed = run(
        functools.partial(feed_kernel, comm),
        dict(a2=fwd.a2, h1=fwd.h1, c=upstream, gains=gains,
             w=(sq.reshape(8, width, width), pl.BlockSpec((1, width, width), lambda _: (7, 0, 0))),
             fi=fi.reshape(hidden, width), fo=fo.reshape(width, hidden)),
        dict(out=(small, BF), dfi=((hidden, width), BF), dfo=((4, 2, 2, PIECE, hidden), BF),
             dwoc=((width, width), BF), da2=(small, BF), dh2=(small, F32), gain=((1, width), F32))
        | (dict(fin=((2, PIECE, WIDE), BF)) if comm else {}),
        dict(h2=VM(small, F32), n3=VM(small, BF), sum=VM(small, F32), back=VM(small, F32),
             ct=VM((width, rows), BF), g=VM(small, BF), du=VM(small, BF))
        | (scatter_scratch(2, 1) if comm else {}),
        "feed", collective=3 if comm else None,
    )

    ins = dict(k2=(fwd.k2, HBM), v2=(fwd.v2, HBM), q2=fwd.q2, da2=feed.da2,
               **index)
    turned = (examples, width, keys_n)
    outs = dict(dk2=(turned, BF, HBM), dv2=(turned, BF, HBM), dq2=(small, BF))
    scratch = dict(
        k2v=VM(encoder_out.shape, BF), v2v=VM(encoder_out.shape, BF),
        qe=VM((MOST, width), BF), dae=VM((MOST, width), BF), dqe=VM((MOST, width), BF),
        dk=VM((2, width, keys_n), BF), dv=VM((2, width, keys_n), BF),
        sum=VM(small, F32), esem=dma(examples, 2), dsem=dma(2, 2),
        **index_scratch,
    )
    fins = {}
    if comm:
        dfi = feed.dfi.reshape(4, 2, 2, 4, PIECE, width)
        ins |= dict(dfi=(dfi, HBM),
                    dfo=(feed.dfo, HBM))
        fins = dict(fin=((5, PIECE, WIDE), BF))
        scratch |= scatter_scratch(5, 5)
    mid = run(functools.partial(cross_back_kernel, comm), ins, outs | fins, scratch, "cross_back",
              collective=1 if comm else None)

    seven = (7,) + cut if comm else (7, width, width)
    ins = dict(dq2=mid.dq2, n2=fwd.n2, h1=fwd.h1, dh2=feed.dh2, x=decoder_in, n1=fwd.n1, q1=fwd.q1,
               k1=fwd.k1, v1=fwd.v1, a1=fwd.a1, gains=gains, dist=dist, gain3=feed.gain,
               sq=(sq, HBM), enc=(encoder_out, HBM), dk2=(mid.dk2, HBM), dv2=(mid.dv2, HBM), lengths=decoder_lengths)
    outs = dict(dx=(small, BF), small=((16, width), F32), denc=(encoder_out.shape, BF, HBM))
    scratch = dict(
        mask=VM((rows // MOST, MOST, 2 * MOST), F32), dh1=VM(small, F32), b1=VM(small, BF),
        da1=VM(small, BF), dq=VM(small, BF), dk=VM((width, rows), BF), dv=VM((width, rows), BF),
        dksum=VM((128, rows + MOST), F32), dvsum=VM((128, rows + MOST), F32), back=VM(small, F32),
        gain=VM((2, width), F32), distsum=VM((HEADS, 2 * MOST), F32), w=VM((5,) + cut, BF),
        one=VM((2, width, keys_n), BF), two=VM((2, keys_n, width), BF), three=VM((2, width, keys_n), BF),
        dwsum=VM((width, width), F32), denv=VM((2, keys_n, width), BF), wsem=dma(7), esem=dma(2, 2),
        dsem=dma(2),
    )
    if comm:
        ins |= dict(dfi=(dfi, HBM), dwoc=(feed.dwoc.reshape(cut), HBM), finf=mid.fin, fing=feed.fin)
        outs |= dict(tsq=((8, 96, 192), BF), tfi=((384, 192), BF), tfo=((96, 768), BF), gains_own=((8, 128), F32),
                     table_own=((8, HEADS), F32))
        scratch |= dict(
            dw=VM(seven, BF), fin=VM((9, PIECE, WIDE), BF), all=VM((12, PIECE, WIDE), BF), give=VM((12, PIECE, 192), BF),
            take=VM((12, PIECE, 192), BF), giveo=VM((2, PIECE, WIDE), BF), takeo=VM((2, PIECE, WIDE), BF),
            given=VM((5, 16, width), F32), gotten=VM((5, 16, width), F32), smsem=dma(2, 5), xsem=dma(4),
        ) | scatter_scratch(9, 2)
    else:
        outs |= dict(dw=(seven, BF))
    last = run(functools.partial(self_back_kernel, comm), ins, outs, scratch, "self_back",
               collective=2 if comm else None)

    if comm:
        square = ((192, 96), F32)
        done = run(
            finish_kernel,
            dict(tsq=last.tsq, tfi=last.tfi, tfo=last.tfo, gains_in=last.gains_own, table_in=last.table_own,
                 dx_in=last.dx, out_in=feed.out, denc_in=(last.denc, HBM)),
            {n: square for n in ("k_c", "v_c", "q_s", "k_s", "v_s", "o_s", "q_c", "o_c")}
            | dict(f_i=((192, 384), F32), f_o=((96, 768), F32), gains=((3, 96), F32), table=((8, HEADS), F32),
                   dx=(small, BF), out=(small, BF), denc=(encoder_out.shape, BF, HBM)),
            dict(sem=dma(examples, 2), hold=VM(encoder_out.shape, BF)), "finish",
        )
        grads = (done.q_s, done.k_s, done.v_s, done.o_s, done.q_c, done.k_c, done.v_c, done.o_c,
                 done.f_i, done.f_o.T)
        gains_delta, table_delta, dx, denc, out = done.gains, done.table, done.dx, done.denc, done.out
    else:
        def owned(t, rows_axis=0):
            t = lax.psum_scatter(t, "dp", scatter_dimension=1, tiled=True)
            return lax.psum_scatter(t, "fsdp", scatter_dimension=0, tiled=True).astype(F32).T

        dw = last.dw
        grads = tuple(owned(t) for t in (dw[2], dw[3], dw[4], dw[1], dw[0], dw[5], dw[6],
                                         feed.dwoc, feed.dfi, feed.dfo.reshape(width, hidden)))
        gains_delta = lax.psum(last.small[0:3], "dp")
        gains_delta = lax.psum_scatter(gains_delta, "fsdp", scatter_dimension=1, tiled=True)
        table_delta = last.small[3 : 3 + HEADS, 0:BUCKETS].T
        table_delta = lax.psum_scatter(table_delta, "dp", scatter_dimension=0, tiled=True)
        table_delta = lax.psum(table_delta, "fsdp")
        dx, denc, out = last.dx, last.denc, feed.out
    return (out, dx, denc, gains_delta, table_delta) + grads


def solution(mesh):
    tokens = P(("dp", "fsdp"), None)
    weight = P("dp", "fsdp")
    comm = (mesh.shape["dp"], mesh.shape["fsdp"]) == (4, 8)
    return jax.shard_map(
        functools.partial(body, comm),
        mesh=mesh,
        in_specs=(tokens, P(("dp", "fsdp"), None, None), tokens, P(("dp", "fsdp")), P(None, "fsdp"),
                  P("dp", None)) + (weight,) * 10 + (tokens,),
        out_specs=(tokens, tokens, P(("dp", "fsdp"), None, None), P(None, "fsdp"), P("dp", None))
        + (weight,) * 10,
        check_vma=False,
    )
```

```python
import functools
import math
import types

import jax
import jax.numpy as jnp
from jax import lax
from jax.experimental import pallas as pl
from jax.experimental.pallas import tpu as pltpu
from jax.sharding import PartitionSpec as P

HEADS = 12
HEAD_DIM = 64
BUCKETS = 32
MAX_DIST = 128
MOST = 128
PAIRS = HEADS // 2
EPSILON = 1e-06
HIDDEN_SCORE = -1e30
BF = jnp.bfloat16
F32 = jnp.float32
VMEM_LIMIT = 60 * 1024 * 1024


def nn(a, b):
    return lax.dot_general(a, b, (((1,), (0,)), ((), ())), preferred_element_type=F32)


def nt(a, b):
    return lax.dot_general(a, b, (((1,), (1,)), ((), ())), preferred_element_type=F32)


def tn(a, b):
    return lax.dot_general(a, b, (((0,), (0,)), ((), ())), preferred_element_type=F32)


def rms(z, gain):
    factor = lax.rsqrt(jnp.mean(z * z, axis=-1, keepdims=True) + EPSILON)
    return z * factor * gain


def rms_back(z, gain, dy):
    factor = lax.rsqrt(jnp.mean(z * z, axis=-1, keepdims=True) + EPSILON)
    wdy = dy * gain
    inner = jnp.mean(z * wdy, axis=-1, keepdims=True)
    dz = factor * wdy - z * (factor * factor * factor * inner)
    return dz, jnp.sum(dy * z * factor, axis=0, keepdims=True)


def split_heads(rows):
    first = lax.broadcasted_iota(jnp.int32, rows.shape, 1) < HEAD_DIM
    zero = jnp.zeros_like(rows)
    return jnp.concatenate([jnp.where(first, rows, zero), jnp.where(first, zero, rows)], axis=0)


def join_heads(rows):
    half = rows.shape[0] // 2
    first = lax.broadcasted_iota(jnp.int32, (half, rows.shape[1]), 1) < HEAD_DIM
    return jnp.where(first, rows[:half], rows[half:])


def softmax(scores):
    raised = jnp.exp(scores - jnp.max(scores, axis=-1, keepdims=True))
    return raised * (1.0 / jnp.sum(raised, axis=-1, keepdims=True))


def lanes(index, width):
    return pl.ds(pl.multiple_of(index * width, width), width)


def loop(low, high, step, unroll=1):
    def run(index, carry):
        step(index)
        return carry

    lax.fori_loop(low, high, run, 0, unroll=unroll)


def quiet(act):
    act()


def bucket_of(distance):
    half_count = BUCKETS // 2
    counted = jnp.zeros_like(distance)
    for section_index in range(1, half_count):
        edge_at = int(
            math.ceil(half_count * (MAX_DIST / half_count) ** (section_index / half_count))
        )
        counted = counted + (distance >= edge_at).astype(jnp.int32)
    return jnp.where(distance < half_count, distance, half_count + counted)


def distance_hot(axis):
    shape = (2 * MOST, BUCKETS) if axis == 0 else (BUCKETS, 2 * MOST)
    distance = jnp.maximum(MOST - lax.broadcasted_iota(jnp.int32, shape, axis), 0)
    return (bucket_of(distance) == lax.broadcasted_iota(jnp.int32, shape, 1 - axis)).astype(F32)


def segments(lengths, shape, axis, shift=0):
    places = lax.broadcasted_iota(jnp.int32, shape, axis) - shift
    end = jnp.zeros((1, 1), jnp.int32)
    example = jnp.where(places < 0, -1, 0)
    start = jnp.zeros(shape, jnp.int32)
    for e in range(lengths.shape[1]):
        length = lengths[:, e : e + 1]
        end = end + length
        example = example + (places >= end).astype(jnp.int32)
        start = start + jnp.where(places >= end, length, 0)
    return example, places - start


def local(src, dst, sem):
    return pltpu.make_async_copy(src, dst, sem)


def w_rows(ref, m, j):
    return ref[m, pl.ds(2 * j, 2)].reshape(2 * WIDE // 2, ref.shape[-1])


def w_lanes(ref, m, at):
    part = ref[m, :, :, :, :, at]
    return part.reshape(-1, part.shape[-1])


MESH = pl.DeviceIdType.MESH
PIECE = 48
WIDE = 384
UNITS = 16
ALL = slice(None)
LOW, HIGH = slice(0, 2), slice(2, 4)


class Place:
    def __init__(self):
        self.d, self.f = lax.axis_index("dp"), lax.axis_index("fsdp")
        self.y, self.c = self.d // 2, self.d % 2
        self.z, self.x = self.f // 2, self.f % 2
        self.nx, self.ny, self.nc = 1 - self.x, 1 - self.y, 1 - self.c

    def at(self, z=None, x=None, y=None, c=None):
        z = self.z if z is None else z
        x = self.x if x is None else x
        y = self.y if y is None else y
        c = self.c if c is None else c
        return (y * 2 + c, z * 2 + x)

    def near(self):
        others = [self.at(z=(self.z + k) % 4) for k in (1, 2, 3)]
        return others + [self.at(x=1 - self.x), self.at(y=1 - self.y), self.at(c=1 - self.c)]


def greet(peers, between=lambda: None):
    barrier = pltpu.get_barrier_semaphore()
    for dev in peers:
        pl.semaphore_signal(barrier, inc=1, device_id=dev, device_id_type=MESH)
    between()
    pl.semaphore_wait(barrier, len(peers))


def eye(n):
    a = lax.broadcasted_iota(jnp.int32, (n, n), 0)
    b = lax.broadcasted_iota(jnp.int32, (n, n), 1)
    return (a == b).astype(F32).astype(BF)


def remote(src, dst, send, recv, dev):
    return pltpu.make_async_remote_copy(
        src_ref=src, dst_ref=dst, send_sem=send, recv_sem=recv, device_id=dev, device_id_type=MESH
    )


class Sends:
    def __init__(self, place, ssem, rsem):
        self.p, self.ssem, self.rsem, self.made = place, ssem, rsem, {}

    def to_x(self):
        return self.p.at(x=1 - self.p.x)

    def to_y(self):
        return self.p.at(y=1 - self.p.y)

    def to_c(self):
        return self.p.at(c=1 - self.p.c)

    def go(self, u, slot, src, dst, dev):
        def make():
            return remote(src(), dst(), self.ssem.at[u, slot], self.rsem.at[u, slot], dev())

        make().start()
        self.made[u, slot] = make

    def wait(self, u, *slots):
        for slot in slots:
            self.made[u, slot]().wait_recv()

    def drain(self):
        for make in self.made.values():
            make().wait_send()


class Gather(Sends):
    def __init__(self, place, own, sq, fi, fo, ssem, rsem):
        super().__init__(place, ssem, rsem)
        self.own, self.sq, self.fi, self.fo = own, sq, fi, fo

    def piece(self, u, z, x, c, y):
        if u < 8:
            return self.sq.at[u, z, x, c, :, pl.ds(pl.multiple_of(y * WIDE, WIDE), WIDE)]
        if u < 12:
            return self.fi.at[z, x, c, u - 8, :, pl.ds(pl.multiple_of(y * WIDE, WIDE), WIDE)]
        at = y * (4 * WIDE) + (u - 12) * WIDE
        return self.fo.at[z, x, c, :, pl.ds(pl.multiple_of(at, WIDE), WIDE)]

    def same(self, u, slot, dev, z, x, c, y):
        def here():
            return self.piece(u, z, x, c, y)

        self.go(u, slot, here, here, dev)

    def first(self, u):
        p = self.p
        if u in (8, 9):
            self.go(
                u, 0, lambda: self.own.at[u], lambda: self.piece(u, p.z, p.x, p.c, p.y),
                self.to_x if u == 8 else self.to_y,
            )
            return
        for k in (1, 2, 3):
            self.go(
                u, k - 1, lambda: self.own.at[u], lambda: self.piece(u, p.z, p.x, p.c, p.y),
                lambda k=k: p.at(z=(p.z + k) % 4),
            )

    def second(self, u):
        p = self.p
        if u == 8:
            self.wait(u, 0)
            self.same(u, 3, self.to_y, p.z, ALL, p.c, p.y)
            return
        if u == 9:
            self.wait(u, 0)
            for y in (0, 1):
                self.same(u, 3 + y, self.to_x, p.z, p.x, p.c, y)
            return
        self.wait(u, 0, 1, 2)
        self.same(u, 3, self.to_x, LOW, p.x, p.c, p.y)
        self.same(u, 4, self.to_y, HIGH, p.x, p.c, p.y)

    def third(self, u):
        p = self.p
        if u in (8, 9):
            self.wait(u, *((3, 4) if u == 9 else (3,)))
            for k in (1, 2, 3):
                for y in (0, 1):
                    self.same(
                        u, 3 + 2 * k + y, lambda k=k: p.at(z=(p.z + k) % 4), p.z, ALL, p.c, y
                    )
            return
        self.wait(u, 3, 4)
        self.same(u, 5, self.to_y, LOW, ALL, p.c, p.y)
        for y in (0, 1):
            self.same(u, 6 + y, self.to_x, HIGH, p.x, p.c, y)
        self.same(u, 8, self.to_c, LOW, ALL, p.c, p.y)
        for y in (0, 1):
            self.same(u, 9 + y, self.to_c, HIGH, p.x, p.c, y)

    def fourth(self, u):
        p = self.p
        if u in (8, 9):
            self.wait(u, 5, 6, 7, 8, 9, 10)
            for y in (0, 1):
                self.same(u, 11 + y, self.to_c, ALL, ALL, p.c, y)
            return
        self.wait(u, 5, 6, 7)
        self.same(u, 11, self.to_c, LOW, ALL, p.c, p.ny)
        for y in (0, 1):
            self.same(u, 12 + y, self.to_c, HIGH, p.nx, p.c, y)

    def fifth(self, u):
        if u in (8, 9):
            self.wait(u, 11, 12)
            return
        self.wait(u, *range(8, 14))

    def begin(self):
        for act, u in ((self.second, 8), (self.second, 9), (self.second, 0), (self.second, 1), (self.third, 0),
                       (self.third, 1), (self.second, 2), (self.second, 3), (self.fourth, 0), (self.fourth, 1),
                       (self.second, 4)):
            act(u)

    def tick(self, t):
        if 2 <= t and t not in (8, 9):
            self.fourth(t)
        if t + 2 < UNITS and t + 2 not in (8, 9):
            self.third(t + 2)
        if t + 5 < UNITS and t + 5 not in (8, 9):
            self.second(t + 5)
        if t == 3:
            self.third(8)
            self.third(9)
        if t == UNITS - 1:
            self.fourth(8)
            self.fourth(9)


class Scatter(Sends):
    def __init__(self, place, parts, staged, r):
        super().__init__(place, r.ssem, r.rsem)
        self.parts, self.staged, self.r = parts, staged, r

    def halves(self, u):
        p, r = self.p, self.r
        return [local(self.parts(u, p.c, y), r.stage.at[u, y], r.lsem.at[u, y]) for y in (0, 1)]

    def own(self, u, y):
        if u < self.staged:
            return self.r.stage[u, pl.ds(y, 1)]
        return self.parts(u, self.p.c, y)[...][None]

    def r0(self, u):
        p, r = self.p, self.r
        for y in (0, 1):
            self.go(
                u, y, lambda y=y: self.parts(u, p.nc, y), lambda y=y: r.land.at[u, y], self.to_c
            )
        if u < self.staged:
            for copy in self.halves(u):
                copy.start()

    def r1(self, u):
        p, r = self.p, self.r
        self.wait(u, 0, 1)
        if u < self.staged:
            for copy in self.halves(u):
                copy.wait()
        for y in (p.ny, p.y):
            at = pl.ds(y, 1)
            r.land[u, at] = r.land[u, at] + self.own(u, y)
            if y is p.ny:
                self.go(
                    u, 2, lambda: r.land.at[u, p.ny, LOW], lambda: r.land1.at[u, LOW], self.to_y
                )
        for y in (0, 1):
            self.go(
                u, 3 + y, lambda y=y: r.land.at[u, y, HIGH, p.nx], lambda y=y: r.land1.at[u, HIGH, y],
                self.to_x,
            )

    def r2(self, u):
        p, r = self.p, self.r
        self.wait(u, 2, 3, 4)
        own, x = pl.ds(p.y, 1), pl.ds(p.x, 1)
        r.land[u, own, LOW] = r.land[u, own, LOW] + r.land1[u, LOW][None]
        for y in (0, 1):
            r.land[u, y, HIGH, x] = r.land[u, y, HIGH, x] + r.land1[u, HIGH, y][:, None]
        self.go(u, 5, lambda: r.land.at[u, p.y, LOW, p.nx], lambda: r.land2.at[u, LOW], self.to_x)
        self.go(u, 6, lambda: r.land.at[u, p.ny, HIGH, p.x], lambda: r.land2.at[u, HIGH], self.to_y)

    def r3(self, u):
        p, r = self.p, self.r
        self.wait(u, 5, 6)
        y, x = pl.ds(p.y, 1), pl.ds(p.x, 1)
        r.land[u, y, :, x] = r.land[u, y, :, x] + r.land2[u][None, :, None]
        for k in (1, 2, 3):
            self.go(
                u, 6 + k, lambda k=k: r.land.at[u, p.y, (p.z + k) % 4, p.x],
                lambda k=k: r.land3.at[u, k - 1], lambda k=k: p.at(z=(p.z + k) % 4),
            )

    def r4(self, u):
        p, r = self.p, self.r
        self.wait(u, 7, 8, 9)
        part = r.land[u, pl.ds(p.y, 1), pl.ds(p.z, 1), pl.ds(p.x, 1)]
        total = part.reshape(PIECE, WIDE).astype(F32)
        for k in range(3):
            total = total + r.land3[u, k].astype(F32)
        r.fin[u] = total.astype(BF)

    def step(self, number, *units):
        act = (self.r0, self.r1, self.r2, self.r3, self.r4)[number]
        for u in units:
            act(u)


def scatter_scratch(count, staged):
    return dict(
        land=pltpu.VMEM((count, 2, 4, 2, PIECE, WIDE), BF),
        stage=pltpu.VMEM((staged, 2, 4, 2, PIECE, WIDE), BF),
        land1=pltpu.VMEM((count, 4, 2, PIECE, WIDE), BF),
        land2=pltpu.VMEM((count, 4, PIECE, WIDE), BF),
        land3=pltpu.VMEM((count, 3, PIECE, WIDE), BF),
        ssem=pltpu.SemaphoreType.DMA((count, 10)),
        rsem=pltpu.SemaphoreType.DMA((count, 10)),
        lsem=pltpu.SemaphoreType.DMA((staged, 2)),
    )


def self_masks(lengths, mask_ref):
    blocks = mask_ref.shape[0]
    seg_col = segments(lengths, (blocks * MOST, 1), 0)[0]
    seg_row = segments(lengths, (1, (blocks + 1) * MOST), 1, MOST)[0]
    a = lax.broadcasted_iota(jnp.int32, (MOST, 2 * MOST), 0)
    b = lax.broadcasted_iota(jnp.int32, (MOST, 2 * MOST), 1)
    causal = b <= a + MOST
    for i in range(blocks):
        same = seg_col[MOST * i : MOST * (i + 1), :] == seg_row[:, MOST * i : MOST * (i + 2)]
        mask_ref[i] = jnp.where(causal & same, 0.0, HIDDEN_SCORE)


def pair_bias(dist_ref, pair):
    parts = []
    for h in range(2):
        row = dist_ref[pl.ds(2 * pair + h, 1), :]
        parts.append(
            pltpu.roll(jnp.broadcast_to(row, (MOST, 2 * MOST)), 0, 1, stride=1, stride_axis=0)
        )
    return jnp.concatenate(parts, axis=0)


def masked_scores(scores, bias, mask):
    both = scores + bias
    return (both.reshape(2, MOST, 2 * MOST) + mask[None]).reshape(2 * MOST, 2 * MOST)


def example_rows(index_ref, example, total):
    place = lax.broadcasted_iota(jnp.int32, (MOST, total), 0)
    here = (index_ref[0:1, :] == example) & (index_ref[1:2, :] == place)
    return here.astype(F32).astype(BF)


def example_index(r, total):
    r.index[0:1, :], r.index[1:2, :] = segments(r.lengths[...], (1, total), 1)
    examples, keys_n = r.hidden.shape
    place = lax.broadcasted_iota(jnp.int32, (1, keys_n), 1)
    for e in range(examples):
        r.hidden[e : e + 1, :] = jnp.where(place < r.valid[:, e : e + 1], 0.0, HIDDEN_SCORE)


def turn_squares(r, *which):
    shards = (r.k_c, r.v_c, r.q_s, r.k_s, r.v_s, r.o_s, r.q_c, r.o_c)
    e96 = eye(96)
    for m in which:
        r.xt[m] = nt(e96, shards[m][...].astype(BF)).astype(BF).reshape(2, PIECE, 192)


def turn_feeds(r):
    t = nt(eye(384), r.f_i[...].astype(BF)).astype(BF).reshape(2, 4, PIECE, 192)
    for s in range(4):
        for h in range(2):
            r.xt[8 + s, h] = t[h, s]
    r.xf[...] = r.f_o[...].astype(BF).reshape(2, PIECE, 768)


def own_parts(p, r, low, high):
    first = p.c == 0
    mine = r.xt[low:high, pl.ds(p.c, 1)].reshape(high - low, PIECE, 192)
    other = r.took[low:high]
    r.own[low:high] = jnp.concatenate(
        [jnp.where(first, mine, other), jnp.where(first, other, mine)], axis=-1
    )


def small_sends(p, r):
    made = []
    for k in range(1, 8):
        dev = (p.d, (p.f + k) % 8)
        made.append(
            remote(r.gt.at[p.f], r.gt.at[p.f], r.smsem.at[0, k - 1], r.smsem.at[1, k - 1], dev)
        )
    for k in range(1, 4):
        dev = ((p.d + k) % 4, p.f)
        made.append(
            remote(r.tt.at[p.d], r.tt.at[p.d], r.smsem.at[0, 6 + k], r.smsem.at[1, 6 + k], dev)
        )
    return made


def forward_kernel(comm, r):
    rows, width = r.x.shape
    examples, keys_n = r.enc.shape[0], r.enc.shape[1]
    blocks = rows // MOST
    enc_copies = [local(r.enc.at[e], r.encv.at[e], r.esem.at[e]) for e in range(examples)]
    for copy in enc_copies:
        copy.start()
    if comm:
        p = Place()
        peers = [(p.d, (p.f + k) % 8) for k in range(1, 8)] + [((p.d + k) % 4, p.f) for k in range(1, 4)]

        def prepare():
            r.gt[pl.ds(p.f, 1)] = jnp.zeros((1, 8, 128), F32)
            r.gt[pl.ds(p.f, 1), 0:3, 0:96] = r.gains_s[...].astype(BF).astype(F32)[None]
            r.tt[pl.ds(p.d, 1)] = jnp.zeros((1, 8, 128), F32)
            r.tt[pl.ds(p.d, 1), :, 0:HEADS] = r.table_s[...].astype(BF).astype(F32)[None]
            turn_squares(r, 0, 1)

        greet(peers, prepare)
        sib = p.at(c=1 - p.c)
        trade = [
            remote(r.xt.at[0:2, 1 - p.c], r.took.at[0:2], r.xsem.at[0], r.xsem.at[1], sib),
            remote(r.xt.at[2:12, 1 - p.c], r.took.at[2:12], r.xsem.at[2], r.xsem.at[3], sib),
            remote(r.xf.at[1 - p.c], r.tookf, r.xsem.at[4], r.xsem.at[5], sib),
        ]
        small = small_sends(p, r)
        for copy in trade[0:1] + small:
            copy.start()
        turn_feeds(r)
        g = Gather(p, r.own, r.sq, r.fi, r.fo, r.ssem, r.rsem)
        placed = [
            local(r.own.at[u], g.piece(u, p.z, p.x, p.c, p.y), r.psem.at[u]) for u in range(UNITS)
        ]
        trade[0].wait_recv()
        own_parts(p, r, 0, 2)
        for u in (0, 1):
            g.first(u)
            placed[u].start()
        turn_squares(r, 2, 3, 4, 5, 6, 7)
        for copy in trade[1:]:
            copy.start()
        first = p.c == 0
        trade[1].wait_recv()
        own_parts(p, r, 2, 12)
        trade[2].wait_recv()
        mine, other = r.xf[pl.ds(p.c, 1)].reshape(PIECE, 768), r.tookf[...]
        low, high = jnp.where(first, mine, other), jnp.where(first, other, mine)
        r.own[12], r.own[13] = low[:, :WIDE], low[:, WIDE:]
        r.own[14], r.own[15] = high[:, :WIDE], high[:, WIDE:]
        for u in (8, 9, 2, 3, 4, 5, 6, 7, 10, 11, 12, 13, 14, 15):
            g.first(u)
            placed[u].start()
        for copy in small:
            copy.wait_recv()
        spot = lax.broadcasted_iota(jnp.int32, (128, width), 1)
        lane = lax.broadcasted_iota(jnp.int32, (128, width), 0)
        gains = jnp.zeros((8, width), F32)
        for f in range(8):
            put = ((spot == lane + 96 * f) & (lane < 96)).astype(F32).astype(BF)
            gains = gains + nn(r.gt[f].astype(BF), put)
        r.gains[...] = gains[0:3]
        table = r.tt[...].reshape(BUCKETS, 128).astype(BF)
        r.dist[...] = tn(table, distance_hot(1).astype(BF))[0:HEADS]
        for copy in placed:
            copy.wait()
        begin, tick, arrived = g.begin, g.tick, g.fifth
    else:
        begin, tick, arrived = (lambda *_: None,) * 3

    loads = [local(r.sq.at[m], r.wv.at[m], r.wsem.at[m]) for m in range(7)]

    def fetch(*which):
        for m in which:
            arrived(m)
            loads[m].start()

    def have(*which):
        for m in which:
            loads[m].wait()

    example_index(r, rows)
    r.n1[...] = rms(r.x[...].astype(F32), r.gains[0:1, :]).astype(BF)
    r.k1[0:MOST, :] = jnp.zeros((MOST, width), BF)
    r.v1[0:MOST, :] = jnp.zeros((MOST, width), BF)
    self_masks(r.lengths[...], r.mask)
    halves = width // WIDE

    def save(e):
        return [local(r.k2v.at[e], r.k2.at[e], r.ksem.at[e, 0]), local(r.v2v.at[e], r.v2.at[e], r.ksem.at[e, 1])]

    def project(e):
        local(r.enc.at[e], r.encv.at[e], r.esem.at[e]).wait()
        for j in range(halves):
            at = slice(WIDE * j, WIDE * (j + 1))
            r.k2v[e, :, at] = nt(r.encv[e], w_rows(r.wv, 0, j)).astype(BF)
            r.v2v[e, :, at] = nt(r.encv[e], w_rows(r.wv, 1, j)).astype(BF)
        for copy in save(e):
            copy.start()

    begin()
    fetch(0, 1)
    have(0, 1)
    for t in range(4):
        tick(t)
        loop(2 * t, 2 * t + 2, project)
    fetch(2, 3)
    tick(4)
    fetch(4)
    have(2, 3, 4)

    for j in range(halves):
        at = slice(WIDE * j, WIDE * (j + 1))
        r.q1[:, at] = nt(r.n1[...], w_rows(r.wv, 2, j)).astype(BF)
        r.k1[MOST:, at] = nt(r.n1[...], w_rows(r.wv, 3, j)).astype(BF)
        r.v1[MOST:, at] = nt(r.n1[...], w_rows(r.wv, 4, j)).astype(BF)

    def attend(pair):
        at = lanes(pair, 128)
        bias = pair_bias(r.dist, pair)
        for i in range(blocks):
            queries = split_heads(r.q1[MOST * i : MOST * (i + 1), at])
            keys = r.k1[MOST * i : MOST * (i + 2), at]
            values = r.v1[MOST * i : MOST * (i + 2), at]
            probs = softmax(masked_scores(nt(queries, keys), bias, r.mask[i])).astype(BF)
            r.a1[MOST * i : MOST * (i + 1), at] = join_heads(nn(probs, values)).astype(BF)

    tick(5)
    loop(0, PAIRS // 2, attend, PAIRS // 2)
    tick(6)
    fetch(5)
    loop(PAIRS // 2, PAIRS, attend, PAIRS // 2)
    tick(7)
    fetch(6)
    have(5, 6)
    for j in range(halves):
        at = slice(WIDE * j, WIDE * (j + 1))
        r.h1[:, at] = r.x[:, at].astype(F32) + nt(r.a1[...], w_rows(r.wv, 5, j))
    r.n2[...] = rms(r.h1[...], r.gains[1:2, :]).astype(BF)
    for j in range(halves):
        at = slice(WIDE * j, WIDE * (j + 1))
        r.q2[:, at] = nt(r.n2[...], w_rows(r.wv, 6, j)).astype(BF)

    r.sum[...] = jnp.zeros_like(r.sum)

    def cross(e):
        pick = example_rows(r.index, e, rows)
        r.qe[...] = nn(pick, r.q2[...]).astype(BF)
        hidden = r.hidden[pl.ds(e, 1), :]

        def pair_step(pair):
            at = lanes(pair, 128)
            probs = softmax(nt(split_heads(r.qe[:, at]), r.k2v[e, :, at]) + hidden).astype(BF)
            r.ae[:, at] = join_heads(nn(probs, r.v2v[e, :, at])).astype(BF)

        loop(0, PAIRS, pair_step, PAIRS)
        r.sum[...] += tn(pick, r.ae[...])

    def cross_tick(e):
        if comm:
            for t in range(examples):
                pl.when(e == t)(functools.partial(tick, t + 8))
        cross(e)

    loop(0, examples, cross_tick)
    r.a2[...] = r.sum[...].astype(BF)

    def saved(e):
        for copy in save(e):
            copy.wait()

    loop(0, examples, saved)
    if comm:
        for u in range(7, UNITS):
            g.fifth(u)
        g.drain()
        for copy in trade + small:
            copy.wait_send()


GELU_A = math.sqrt(2.0 / math.pi)
GELU_B = 0.044715


def feed_kernel(r):
    rows, width = r.a2.shape
    hidden = r.fi.shape[0]
    def cross_out(j):
        at = lanes(j, 256)
        r.h2[:, at] = r.h1[:, at] + nt(r.a2[...], r.w[0, at, :])

    loop(0, width // 256, cross_out)
    r.n3[...] = rms(r.h2[...], r.gains[2:3, :]).astype(BF)
    r.sum[...] = r.h2[...]
    r.back[...] = jnp.zeros_like(r.back)

    r.ct[...] = r.c[...].T

    def part(j):
        for i in range(3):
            at = pl.ds(pl.multiple_of(j * width + i * 256, 256), 256)
            here = slice(256 * i, 256 * (i + 1))
            u = nt(r.n3[...], r.fi[at, :])
            t = jnp.tanh(GELU_A * (u + GELU_B * (u * u * u)))
            r.g[:, here] = (0.5 * u * (1.0 + t)).astype(BF)
            slope = 0.5 * (1.0 + t) + 0.5 * u * (1.0 - t * t) * (
                GELU_A * (1.0 + (3.0 * GELU_B) * (u * u))
            )
            r.du[:, here] = (nn(r.c[...], r.fo[:, at]) * slope).astype(BF)
        whole_part = lanes(j, width)
        for i in range(3):
            at = pl.ds(pl.multiple_of(j * width + i * 256, 256), 256)
            here = slice(256 * i, 256 * (i + 1))
            r.dfo[:, :, :, :, at] = nn(r.ct[...], r.g[:, here]).astype(BF).reshape(4, 2, 2, PIECE, 256)
            r.dfi[at, :] = tn(r.du[:, here], r.n3[...]).astype(BF)
            r.sum[:, here] += nt(r.g[...], r.fo[here, whole_part])
            r.back[:, here] += nn(r.du[...], r.fi[whole_part, here])

    loop(0, hidden // width, part, 1)
    r.out[...] = r.sum[...].astype(BF)
    dz, dw = rms_back(r.h2[...], r.gains[2:3, :], r.back[...])
    r.gain[...] = dw
    r.dh2[...] = r.c[...].astype(F32) + dz

    def tail(j):
        at = lanes(j, 256)
        r.da2[:, at] = nn(r.dh2[...].astype(BF), r.w[0, :, at]).astype(BF)
        r.dwoc[at, :] = tn(r.dh2[:, at].astype(BF), r.a2[...]).astype(BF)

    loop(0, width // 256, tail)


STARTS = (0, 1, 2, 4, 5, 7, 8)
LAGS = (0, 1, 3, 5, 7)


def cross_back_kernel(comm, r):
    rows, width = r.q2.shape
    examples, keys_n = r.k2.shape[0], r.k2.shape[1]

    def fetches(e):
        return [local(getattr(r, a).at[e], getattr(r, b).at[e], r.esem.at[e, i])
                for i, (a, b) in enumerate((("k2", "k2v"), ("v2", "v2v")))]

    for e in range(examples):
        for copy in fetches(e):
            copy.start()
    if comm:
        p = Place()

        def parts(u, c, y):
            if u >= 4:
                return r.dfi.at[:, :, c, u - 4, :, y * WIDE : (y + 1) * WIDE]
            at = y * 4 * WIDE + u * WIDE
            return r.dfo.at[:, :, c, :, at : at + WIDE]

        s = Scatter(p, parts, 7, r)
        greet(p.near())
    example_index(r, rows)
    r.sum[...] = jnp.zeros_like(r.sum)

    def out_copies(e):
        return [
            local(r.dk.at[e % 2], r.dk2.at[e], r.dsem.at[e % 2, 0]),
            local(r.dv.at[e % 2], r.dv2.at[e], r.dsem.at[e % 2, 1]),
        ]

    def tick(at):
        if comm:
            for t in range(2 * examples):

                @pl.when(at == t)
                def _():
                    for number in (4, 3, 2, 1, 0):
                        for u, at_first in enumerate(STARTS):
                            if at_first + LAGS[number] == t:
                                s.step(number, u)

    def example(e):
        tick(2 * e)
        for copy in fetches(e):
            copy.wait()
        pick = example_rows(r.index, e, rows)
        r.qe[...] = nn(pick, r.q2[...]).astype(BF)
        r.dae[...] = nn(pick, r.da2[...]).astype(BF)
        hidden = r.hidden[pl.ds(e, 1), :]

        @pl.when(e >= 2)
        def _():
            for copy in out_copies(e - 2):
                copy.wait()

        def attend(pair):
            at = lanes(pair, 128)
            queries = split_heads(r.qe[:, at])
            deltas = split_heads(r.dae[:, at])
            keys = r.k2v[e, :, at]
            probs = softmax(nt(queries, keys) + hidden)
            dprobs = nt(deltas, r.v2v[e, :, at])
            low = (probs * (dprobs - jnp.sum(dprobs * probs, axis=-1, keepdims=True))).astype(BF)
            r.dv[e % 2, at, :] = tn(deltas, probs.astype(BF)).astype(BF)
            r.dk[e % 2, at, :] = tn(queries, low).astype(BF)
            r.dqe[:, at] = join_heads(nn(low, keys)).astype(BF)

        loop(0, PAIRS, attend, PAIRS)
        tick(2 * e + 1)
        for copy in out_copies(e):
            copy.start()
        r.sum[...] += tn(pick, r.dqe[...])

    loop(0, examples, example)
    r.dq2[...] = r.sum[...].astype(BF)
    for e in (examples - 2, examples - 1):
        for copy in out_copies(e):
            copy.wait()
    if comm:
        s.drain()


def self_back_kernel(comm, r):
    rows, width = r.x.shape
    blocks = rows // MOST
    thirds = width // 256
    if comm:
        p = Place()

        def parts(u, c, y):
            at = pl.ds(pl.multiple_of(y * WIDE, WIDE), WIDE)
            if u == 0:
                return r.dfi.at[:, :, c, 3, :, at]
            if u == 1:
                return r.dwoc.at[:, :, c, :, at]
            return r.dw.at[u - 2, :, :, c, :, at]

        s = Scatter(p, parts, 2, r)
        greet(p.near())
        step = s.step
    else:
        step = lambda *units: None

    def put(m, j, value):
        if comm:
            r.dw[m, 2 * j : 2 * j + 2] = value.astype(BF).reshape(2, 2, 2, PIECE, width)
        else:
            r.dw[m, WIDE * j : WIDE * (j + 1), :] = value.astype(BF)

    halves = width // WIDE
    examples = r.denc.shape[0]
    loads = [local(r.sq.at[2 + m], r.w.at[m], r.wsem.at[m]) for m in range(5)]
    late = [local(r.sq.at[m], r.w.at[3 + m], r.wsem.at[5 + m]) for m in range(2)]
    for copy in loads:
        copy.start()

    passes = ((r.dk2, r.enc), (r.dv2, r.enc), (r.dk2, r.dv2))

    def fetches(number, e):
        places = (r.one, r.three if number == 2 else r.two)
        return [local(passes[number][i].at[e], places[i].at[e % 2], r.esem.at[e % 2, i]) for i in (0, 1)]

    def pass_step(number, e, act):
        for copy in fetches(number, e):
            copy.wait()
        act(e)

        @pl.when(e + 2 < examples)
        def _():
            for copy in fetches(number, e + 2):
                copy.start()

        if number < 2:

            @pl.when(e + 2 >= examples)
            def _():
                for copy in fetches(number + 1, e + 2 - examples):
                    copy.start()

    def out_copy(e):
        return local(r.denv.at[e % 2], r.denc.at[e], r.dsem.at[e % 2])

    for e in (0, 1):
        for copy in fetches(0, e):
            copy.start()
    step(0, 0, 1)
    for j in range(halves):
        at = slice(WIDE * j, WIDE * (j + 1))
        put(0, j, tn(r.dq2[:, at], r.n2[...]))
    step(0, 2)
    for copy in loads:
        copy.wait()

    def query(j):
        at = lanes(j, 256)
        r.back[:, at] = nn(r.dq2[...], w_lanes(r.w, 4, at))

    loop(0, thirds, query)
    step(1, 0, 1)
    dz, dw = rms_back(r.h1[...], r.gains[1:2, :], r.back[...])
    r.gain[1:2, :] = dw
    r.dh1[...] = r.dh2[...] + dz
    r.b1[...] = r.dh1[...].astype(BF)
    for j in range(halves):
        at = slice(WIDE * j, WIDE * (j + 1))
        put(1, j, tn(r.b1[:, at], r.a1[...]))
    step(0, 3)

    def out(j):
        at = lanes(j, 256)
        r.da1[:, at] = nn(r.b1[...], w_lanes(r.w, 3, at)).astype(BF)

    loop(0, thirds, out)
    for copy in late:
        copy.start()
    if comm:
        pairs = [p.at(c=1 - p.c), p.at(y=1 - p.y), p.at(x=1 - p.x),
                 p.at(z=p.z + 1 - 2 * (p.z % 2)), p.at(z=(p.z + 2) % 4)]

        def share(i):
            return remote(r.given.at[i], r.gotten.at[i], r.smsem.at[0, i], r.smsem.at[1, i], pairs[i])

        def share_go(i):
            r.given[i] = r.small[...]
            share(i).start()

        def share_end(i):
            share(i).wait_recv()
            r.small[...] = r.small[...] + r.gotten[i]

        def share_next(i):
            share_end(i)
            share_go(i + 1)

    def passing(number, act, events):
        def one(e):
            pass_step(number, e, act)
            if comm:
                for at, happens in events.items():
                    pl.when(e == at)(functools.partial(quiet, happens))

        loop(0, examples, one)

    def weight_sum(e):
        def dense(j):
            at = lanes(j, 256)
            r.dwsum[at, :] = nn(r.one[e % 2, at, :], r.two[e % 2]) + jnp.where(e == 0, 0.0, r.dwsum[at, :])

        loop(0, thirds, dense, thirds)

    events = (
        {1: lambda: step(1, 2), 2: lambda: step(1, 3), 4: lambda: step(2, 0, 1), 6: lambda: step(2, 2),
         7: lambda: step(2, 3)},
        {0: lambda: share_next(0), 1: lambda: step(2, 4), 3: lambda: step(2, 5), 4: lambda: share_next(1),
         5: lambda: step(2, 6), 6: lambda: step(3, 4), 7: lambda: (step(3, 5), share_next(2))},
        {0: lambda: step(3, 6), 1: lambda: (step(1, 8), step(4, 4)), 2: lambda: step(4, 5),
         3: lambda: share_next(3), 4: lambda: step(4, 6), 5: lambda: step(2, 8), 6: lambda: share_end(4)},
    )

    passing(0, weight_sum, events[0])
    for j in range(halves):
        put(5, j, r.dwsum[WIDE * j : WIDE * (j + 1), :])
    step(0, 7)
    self_masks(r.lengths[...], r.mask)
    a = lax.broadcasted_iota(jnp.int32, (MOST, MOST), 0)
    b = lax.broadcasted_iota(jnp.int32, (MOST, MOST), 1)
    flip = (a + b == MOST - 1).astype(F32)

    def attend(pair):
        at = lanes(pair, 128)
        bias = pair_bias(r.dist, pair)
        r.dksum[...] = jnp.zeros_like(r.dksum)
        r.dvsum[...] = jnp.zeros_like(r.dvsum)
        skewed = jnp.zeros((2 * MOST, 2 * MOST), F32)
        for i in range(blocks):
            own = slice(MOST * i, MOST * (i + 1))
            band = slice(MOST * i, MOST * (i + 2))
            queries = split_heads(r.q1[own, at])
            deltas = split_heads(r.da1[own, at])
            keys = r.k1[band, at]
            probs = softmax(masked_scores(nt(queries, keys), bias, r.mask[i]))
            dprobs = nt(deltas, r.v1[band, at])
            dscores = probs * (dprobs - jnp.sum(dprobs * probs, axis=-1, keepdims=True))
            low = dscores.astype(BF)
            skewed = skewed + dscores
            r.dvsum[:, band] += tn(deltas, probs.astype(BF))
            r.dksum[:, band] += tn(queries, low)
            r.dq[own, at] = join_heads(nn(low, keys)).astype(BF)
        r.dk[at, :] = r.dksum[:, MOST:].astype(BF)
        r.dv[at, :] = r.dvsum[:, MOST:].astype(BF)
        for h in range(2):
            flipped = jnp.dot(
                flip,
                skewed[MOST * h : MOST * (h + 1)],
                precision=lax.Precision.HIGHEST,
                preferred_element_type=F32,
            )
            straight = pltpu.roll(flipped, MOST + 1, 1, stride=1, stride_axis=0)
            r.distsum[pl.ds(2 * pair + h, 1), :] = jnp.sum(straight, axis=0, keepdims=True)

    plan = {
        0: ((3, 0, 1),),
        1: ((1, 7), (3, 2)),
        2: ((3, 3), (4, 0, 1)),
        3: ((2, 7), (4, 2)),
        4: ((4, 3),),
        5: ((3, 7),),
    }

    def attend_tick(pair):
        if comm:
            for t, steps in plan.items():

                @pl.when(pair == t)
                def _():
                    for numbers in steps:
                        step(*numbers)

        attend(pair)

    loop(0, PAIRS, attend_tick)
    for m, ref in ((2, r.dq), (3, r.dk), (4, r.dv)):
        for j in range(halves):
            at = slice(WIDE * j, WIDE * (j + 1))
            put(m, j, tn(ref[:, at], r.n1[...]) if m == 2 else nn(ref[at, :], r.n1[...]))
        step(0, 2 + m)
    step(4, 7)
    step(1, 4, 5)

    r.b1[...] = r.dk[...].T
    r.da1[...] = r.dv[...].T

    def qkv(j):
        at = lanes(j, 256)
        r.back[:, at] = (
            nn(r.dq[...], w_lanes(r.w, 0, at))
            + nn(r.b1[...], w_lanes(r.w, 1, at))
            + nn(r.da1[...], w_lanes(r.w, 2, at))
        )

    loop(0, thirds, qkv, thirds)
    step(1, 6)
    dz, dw = rms_back(r.x[...].astype(F32), r.gains[0:1, :], r.back[...])
    r.gain[0:1, :] = dw
    r.dx[...] = (r.dh1[...] + dz).astype(BF)
    by_bucket = jnp.dot(
        r.distsum[...], distance_hot(0), precision=lax.Precision.HIGHEST, preferred_element_type=F32
    )
    r.small[...] = jnp.zeros_like(r.small)
    r.small[0:2, :] = r.gain[0:2, :]
    r.small[2:3, :] = r.gain3[...]
    r.small[3 : 3 + HEADS, 0:BUCKETS] = by_bucket

    if comm:
        share_go(0)

    passing(1, weight_sum, events[1])
    for j in range(halves):
        put(6, j, r.dwsum[WIDE * j : WIDE * (j + 1), :])
    step(0, 8)
    for copy in late:
        copy.wait()

    def encoder(e):
        @pl.when(e >= 2)
        def _():
            out_copy(e - 2).wait()

        r.b1[...] = r.one[e % 2].T
        r.da1[...] = r.three[e % 2].T

        def dense(j):
            at = lanes(j, 256)
            r.denv[e % 2, :, at] = (
                nn(r.b1[...], w_lanes(r.w, 3, at)) + nn(r.da1[...], w_lanes(r.w, 4, at))
            ).astype(BF)

        loop(0, thirds, dense, thirds)
        out_copy(e).start()

    passing(2, encoder, events[2])
    step(3, 8)
    step(4, 8)
    for e in (examples - 2, examples - 1):
        out_copy(e).wait()
    if not comm:
        return

    first = p.c == 0

    def split(ref, n):
        low, high = ref[0:n, :, :192], ref[0:n, :, 192:]
        return jnp.where(first, low, high), jnp.where(first, high, low)

    r.all[0:8] = r.fin[1:9]
    r.all[8:11] = r.finf[4:7]
    r.all[11] = r.fin[0]
    keep, r.give[...] = split(r.all, 12)
    r.giveo[...] = r.finf[pl.ds(2 * p.nc, 2)]
    sib = p.at(c=1 - p.c)
    trade = [
        remote(r.give, r.take, r.xsem.at[0], r.xsem.at[1], sib),
        remote(r.giveo, r.takeo, r.xsem.at[2], r.xsem.at[3], sib),
    ]
    for copy in trade:
        copy.start()
    for copy in trade:
        copy.wait_recv()

    def both(a, b, axis):
        return jnp.concatenate([jnp.where(first, a, b), jnp.where(first, b, a)], axis=axis)

    r.tsq[...] = both(keep[0:8], r.take[0:8], 1)
    r.tfi[...] = both(keep[8:12].reshape(192, 192), r.take[8:12].reshape(192, 192), 0)
    own = r.finf[pl.ds(2 * p.c, 2)]
    r.tfo[...] = both(
        jnp.concatenate([own[0], own[1]], axis=1), jnp.concatenate([r.takeo[0], r.takeo[1]], axis=1), 0
    )
    spot = lax.broadcasted_iota(jnp.int32, (width, 128), 0)
    lane = lax.broadcasted_iota(jnp.int32, (width, 128), 1)
    put_gains = ((spot == lane + 96 * p.f) & (lane < 96)).astype(F32)
    r.gains_own[...] = jnp.dot(
        r.small[0:8, :], put_gains, precision=lax.Precision.HIGHEST, preferred_element_type=F32
    )
    spot = lax.broadcasted_iota(jnp.int32, (8, BUCKETS), 1)
    line = lax.broadcasted_iota(jnp.int32, (8, BUCKETS), 0)
    r.table_own[...] = lax.dot_general(
        (spot == line + 8 * p.d).astype(F32), r.small[3 : 3 + HEADS, 0:BUCKETS], (((1,), (1,)), ((), ())),
        precision=lax.Precision.HIGHEST, preferred_element_type=F32,
    )
    s.drain()
    for i in range(5):
        share(i).wait_send()
    for copy in trade:
        copy.wait_send()


def finish_kernel(r):
    examples = r.denc.shape[0]
    ins = [local(r.denc_in.at[e], r.hold.at[e], r.sem.at[e, 0]) for e in range(examples)]
    outs = [local(r.hold.at[e], r.denc.at[e], r.sem.at[e, 1]) for e in range(examples)]
    for copy in ins:
        copy.start()
    r.dx[...] = r.dx_in[...]
    e192 = eye(192)
    for m, ref in enumerate((r.o_c, r.q_c, r.o_s, r.q_s, r.k_s, r.v_s, r.k_c, r.v_c)):
        ref[...] = nt(e192, r.tsq[m])
    r.f_i[...] = nt(e192, r.tfi[...])
    r.f_o[...] = r.tfo[...].astype(F32)
    r.gains[...] = r.gains_in[0:3, 0:96]
    r.table[...] = r.table_in[...]
    for e in range(examples):
        ins[e].wait()
        outs[e].start()
    for copy in outs:
        copy.wait()


VM = pltpu.VMEM
HBM = pl.ANY


def run(kernel, ins, outs, scratch, name, collective=None, flops=0):
    names = list(ins) + list(outs) + list(scratch)

    def wrapped(*refs):
        kernel(types.SimpleNamespace(**dict(zip(names, refs))))

    arrays, specs = [], []
    for value in ins.values():
        array, spec = value if isinstance(value, tuple) else (value, VM)
        arrays.append(array)
        specs.append(spec if isinstance(spec, pl.BlockSpec) else pl.BlockSpec(memory_space=spec))
    results = pl.pallas_call(
        wrapped,
        grid=(1,),
        in_specs=specs,
        out_specs=[pl.BlockSpec(memory_space=(o[2] if len(o) > 2 else VM)) for o in outs.values()],
        out_shape=[jax.ShapeDtypeStruct(o[0], o[1]) for o in outs.values()],
        scratch_shapes=list(scratch.values()),
        compiler_params=pltpu.CompilerParams(
            vmem_limit_bytes=VMEM_LIMIT,
            collective_id=collective,
            has_side_effects=collective is not None,
        ),
        cost_estimate=pl.CostEstimate(flops=flops, bytes_accessed=20_000_000, transcendentals=0),
        name=name,
    )(*arrays)
    return types.SimpleNamespace(**dict(zip(outs, results)))


def dma(*shape):
    return pltpu.SemaphoreType.DMA(shape)


def body(comm, decoder_in, encoder_out, decoder_lengths, encoder_lengths, norm_gains, rel_table,
         query_self, key_self, value_self, out_self, query_cross, key_cross, value_cross, out_cross,
         feed_in, feed_out, upstream):
    rows, width = decoder_in.shape
    row_count, examples = decoder_lengths.shape
    keys_n = encoder_out.shape[1]
    hidden = feed_in.shape[1] * lax.axis_size("fsdp")
    small = (rows, width)
    cut = (4, 2, 2, PIECE, width)

    index = dict(lengths=decoder_lengths, valid=encoder_lengths[None, :])
    index_scratch = dict(index=VM((2, rows), jnp.int32), hidden=VM((examples, keys_n), F32))

    acts = dict(n1=(small, BF), q1=(small, BF), k1=((rows + MOST, width), BF), v1=((rows + MOST, width), BF),
                a1=(small, BF), h1=(small, F32), n2=(small, BF), q2=(small, BF), a2=(small, BF),
                k2=(encoder_out.shape, BF, HBM), v2=(encoder_out.shape, BF, HBM))
    scratch = dict(
        encv=VM(encoder_out.shape, BF), k2v=VM(encoder_out.shape, BF), v2v=VM(encoder_out.shape, BF),
        wv=VM((7,) + cut, BF), mask=VM((rows // MOST, MOST, 2 * MOST), F32),
        qe=VM((MOST, width), BF), ae=VM((MOST, width), BF), sum=VM(small, F32),
        esem=dma(examples), wsem=dma(7), ksem=dma(examples, 2), **index_scratch,
    )
    ins = dict(x=decoder_in, enc=(encoder_out, HBM), **index)
    if comm:
        ins |= dict(q_s=query_self, k_s=key_self, v_s=value_self, o_s=out_self, q_c=query_cross,
                    o_c=out_cross, k_c=key_cross, v_c=value_cross, f_i=feed_in, f_o=feed_out.T,
                    gains_s=norm_gains, table_s=rel_table)
        fwd = run(
            functools.partial(forward_kernel, True), ins,
            acts | dict(sq=((8,) + cut, BF, HBM), fi=((4, 2, 2, 4, PIECE, width), BF, HBM),
                        fo=((4, 2, 2, PIECE, hidden), BF, HBM), gains=((3, width), F32),
                        dist=((HEADS, 2 * MOST), F32)),
            scratch | dict(
                xt=VM((12, 2, PIECE, 192), BF), xf=VM((2, PIECE, 768), BF), took=VM((12, PIECE, 192), BF),
                tookf=VM((PIECE, 768), BF), own=VM((UNITS, PIECE, WIDE), BF), gt=VM((8, 8, 128), F32),
                tt=VM((4, 8, 128), F32), xsem=dma(6), psem=dma(UNITS), smsem=dma(2, 10),
                ssem=dma(UNITS, 14), rsem=dma(UNITS, 14)),
            "forward", collective=0,
        )
        sq, fi, fo, gains, dist = fwd.sq, fwd.fi, fwd.fo, fwd.gains, fwd.dist
    else:
        order = (key_cross, value_cross, query_self, key_self, value_self, out_self, query_cross, out_cross)
        sq = jnp.stack([m.astype(BF).T for m in order])
        sq = lax.all_gather(sq, "fsdp", axis=1, tiled=True)
        sq = lax.all_gather(sq, "dp", axis=2, tiled=True).reshape((8,) + cut)
        fi = lax.all_gather(feed_in.astype(BF).T, "fsdp", axis=0, tiled=True)
        fi = lax.all_gather(fi, "dp", axis=1, tiled=True)
        fo = lax.all_gather(feed_out.astype(BF).T, "fsdp", axis=0, tiled=True)
        fo = lax.all_gather(fo, "dp", axis=1, tiled=True)
        gains = lax.all_gather(norm_gains.astype(BF), "fsdp", axis=1, tiled=True).astype(F32)
        table = lax.all_gather(rel_table.astype(BF), "dp", axis=0, tiled=True).astype(F32)
        dist = jnp.dot(distance_hot(0), table, precision=lax.Precision.HIGHEST).T
        fwd = run(
            functools.partial(forward_kernel, False),
            ins | dict(sq=(sq, HBM), gains=gains, dist=dist), acts, scratch, "forward",
        )

    feed = run(
        feed_kernel,
        dict(a2=fwd.a2, h1=fwd.h1, c=upstream, gains=gains,
             w=(sq.reshape(8, width, width), pl.BlockSpec((1, width, width), lambda _: (7, 0, 0))),
             fi=fi.reshape(hidden, width), fo=fo.reshape(width, hidden)),
        dict(out=(small, BF), dfi=((hidden, width), BF), dfo=((4, 2, 2, PIECE, hidden), BF),
             dwoc=((width, width), BF), da2=(small, BF), dh2=(small, F32), gain=((1, width), F32)),
        dict(h2=VM(small, F32), n3=VM(small, BF), sum=VM(small, F32), back=VM(small, F32),
             ct=VM((width, rows), BF), g=VM(small, BF), du=VM(small, BF)),
        "feed",
    )

    ins = dict(k2=(fwd.k2, HBM), v2=(fwd.v2, HBM), q2=fwd.q2, da2=feed.da2,
               **index)
    turned = (examples, width, keys_n)
    outs = dict(dk2=(turned, BF, HBM), dv2=(turned, BF, HBM), dq2=(small, BF))
    scratch = dict(
        k2v=VM(encoder_out.shape, BF), v2v=VM(encoder_out.shape, BF),
        qe=VM((MOST, width), BF), dae=VM((MOST, width), BF), dqe=VM((MOST, width), BF),
        dk=VM((2, width, keys_n), BF), dv=VM((2, width, keys_n), BF),
        sum=VM(small, F32), esem=dma(examples, 2), dsem=dma(2, 2),
        **index_scratch,
    )
    fins = {}
    if comm:
        dfi = feed.dfi.reshape(4, 2, 2, 4, PIECE, width)
        ins |= dict(dfi=(dfi, HBM),
                    dfo=(feed.dfo, HBM))
        fins = dict(fin=((7, PIECE, WIDE), BF))
        scratch |= scatter_scratch(7, 7)
    mid = run(functools.partial(cross_back_kernel, comm), ins, outs | fins, scratch, "cross_back",
              collective=1 if comm else None)

    seven = (7,) + cut if comm else (7, width, width)
    ins = dict(dq2=mid.dq2, n2=fwd.n2, h1=fwd.h1, dh2=feed.dh2, x=decoder_in, n1=fwd.n1, q1=fwd.q1,
               k1=fwd.k1, v1=fwd.v1, a1=fwd.a1, gains=gains, dist=dist, gain3=feed.gain,
               sq=(sq, HBM), enc=(encoder_out, HBM), dk2=(mid.dk2, HBM), dv2=(mid.dv2, HBM), lengths=decoder_lengths)
    outs = dict(dx=(small, BF), small=((16, width), F32), denc=(encoder_out.shape, BF, HBM))
    scratch = dict(
        mask=VM((rows // MOST, MOST, 2 * MOST), F32), dh1=VM(small, F32), b1=VM(small, BF),
        da1=VM(small, BF), dq=VM(small, BF), dk=VM((width, rows), BF), dv=VM((width, rows), BF),
        dksum=VM((128, rows + MOST), F32), dvsum=VM((128, rows + MOST), F32), back=VM(small, F32),
        gain=VM((2, width), F32), distsum=VM((HEADS, 2 * MOST), F32), w=VM((5,) + cut, BF),
        one=VM((2, width, keys_n), BF), two=VM((2, keys_n, width), BF), three=VM((2, width, keys_n), BF),
        dwsum=VM((width, width), F32), denv=VM((2, keys_n, width), BF), wsem=dma(7), esem=dma(2, 2),
        dsem=dma(2),
    )
    if comm:
        ins |= dict(dfi=(dfi, HBM), dwoc=(feed.dwoc.reshape(cut), HBM), finf=mid.fin)
        outs |= dict(tsq=((8, 96, 192), BF), tfi=((384, 192), BF), tfo=((96, 768), BF), gains_own=((8, 128), F32),
                     table_own=((8, HEADS), F32))
        scratch |= dict(
            dw=VM(seven, BF), fin=VM((9, PIECE, WIDE), BF), all=VM((12, PIECE, WIDE), BF), give=VM((12, PIECE, 192), BF),
            take=VM((12, PIECE, 192), BF), giveo=VM((2, PIECE, WIDE), BF), takeo=VM((2, PIECE, WIDE), BF),
            given=VM((5, 16, width), F32), gotten=VM((5, 16, width), F32), smsem=dma(2, 5), xsem=dma(4),
        ) | scatter_scratch(9, 2)
    else:
        outs |= dict(dw=(seven, BF))
    last = run(functools.partial(self_back_kernel, comm), ins, outs, scratch, "self_back",
               collective=2 if comm else None)

    if comm:
        square = ((192, 96), F32)
        done = run(
            finish_kernel,
            dict(tsq=last.tsq, tfi=last.tfi, tfo=last.tfo, gains_in=last.gains_own, table_in=last.table_own,
                 dx_in=last.dx, denc_in=(last.denc, HBM)),
            {n: square for n in ("k_c", "v_c", "q_s", "k_s", "v_s", "o_s", "q_c", "o_c")}
            | dict(f_i=((192, 384), F32), f_o=((96, 768), F32), gains=((3, 96), F32), table=((8, HEADS), F32),
                   dx=(small, BF), denc=(encoder_out.shape, BF, HBM)),
            dict(sem=dma(examples, 2), hold=VM(encoder_out.shape, BF)), "finish",
        )
        grads = (done.q_s, done.k_s, done.v_s, done.o_s, done.q_c, done.k_c, done.v_c, done.o_c,
                 done.f_i, done.f_o.T)
        gains_delta, table_delta, dx, denc = done.gains, done.table, done.dx, done.denc
    else:
        def owned(t, rows_axis=0):
            t = lax.psum_scatter(t, "dp", scatter_dimension=1, tiled=True)
            return lax.psum_scatter(t, "fsdp", scatter_dimension=0, tiled=True).astype(F32).T

        dw = last.dw
        grads = tuple(owned(t) for t in (dw[2], dw[3], dw[4], dw[1], dw[0], dw[5], dw[6],
                                         feed.dwoc, feed.dfi, feed.dfo.reshape(width, hidden)))
        gains_delta = lax.psum(last.small[0:3], "dp")
        gains_delta = lax.psum_scatter(gains_delta, "fsdp", scatter_dimension=1, tiled=True)
        table_delta = last.small[3 : 3 + HEADS, 0:BUCKETS].T
        table_delta = lax.psum_scatter(table_delta, "dp", scatter_dimension=0, tiled=True)
        table_delta = lax.psum(table_delta, "fsdp")
        dx, denc = last.dx, last.denc
    return (feed.out, dx, denc, gains_delta, table_delta) + grads


def solution(mesh):
    tokens = P(("dp", "fsdp"), None)
    weight = P("dp", "fsdp")
    comm = (mesh.shape["dp"], mesh.shape["fsdp"]) == (4, 8)
    return jax.shard_map(
        functools.partial(body, comm),
        mesh=mesh,
        in_specs=(tokens, P(("dp", "fsdp"), None, None), tokens, P(("dp", "fsdp")), P(None, "fsdp"),
                  P("dp", None)) + (weight,) * 10 + (tokens,),
        out_specs=(tokens, tokens, P(("dp", "fsdp"), None, None), P(None, "fsdp"), P("dp", None))
        + (weight,) * 10,
        check_vma=False,
    )
```

```python
import functools
import math
import types

import jax
import jax.numpy as jnp
from jax import lax
from jax.experimental import pallas as pl
from jax.experimental.pallas import tpu as pltpu
from jax.sharding import PartitionSpec as P

HEADS = 12
HEAD_DIM = 64
BUCKETS = 32
MAX_DIST = 128
MOST = 128
PAIRS = HEADS // 2
EPSILON = 1e-06
HIDDEN_SCORE = -1e30
BF = jnp.bfloat16
F32 = jnp.float32
VMEM_LIMIT = 60 * 1024 * 1024


def nn(a, b):
    return lax.dot_general(a, b, (((1,), (0,)), ((), ())), preferred_element_type=F32)


def nt(a, b):
    return lax.dot_general(a, b, (((1,), (1,)), ((), ())), preferred_element_type=F32)


def tn(a, b):
    return lax.dot_general(a, b, (((0,), (0,)), ((), ())), preferred_element_type=F32)


def rms(z, gain):
    factor = lax.rsqrt(jnp.mean(z * z, axis=-1, keepdims=True) + EPSILON)
    return z * factor * gain


def rms_back(z, gain, dy):
    factor = lax.rsqrt(jnp.mean(z * z, axis=-1, keepdims=True) + EPSILON)
    wdy = dy * gain
    inner = jnp.mean(z * wdy, axis=-1, keepdims=True)
    dz = factor * wdy - z * (factor * factor * factor * inner)
    return dz, jnp.sum(dy * z * factor, axis=0, keepdims=True)


def split_heads(rows):
    first = lax.broadcasted_iota(jnp.int32, rows.shape, 1) < HEAD_DIM
    zero = jnp.zeros_like(rows)
    return jnp.concatenate([jnp.where(first, rows, zero), jnp.where(first, zero, rows)], axis=0)


def join_heads(rows):
    half = rows.shape[0] // 2
    first = lax.broadcasted_iota(jnp.int32, (half, rows.shape[1]), 1) < HEAD_DIM
    return jnp.where(first, rows[:half], rows[half:])


def softmax(scores):
    raised = jnp.exp(scores - jnp.max(scores, axis=-1, keepdims=True))
    return raised * (1.0 / jnp.sum(raised, axis=-1, keepdims=True))


def lanes(index, width):
    return pl.ds(pl.multiple_of(index * width, width), width)


def loop(low, high, step, unroll=1):
    def run(index, carry):
        step(index)
        return carry

    lax.fori_loop(low, high, run, 0, unroll=unroll)


def quiet(act):
    act()


def bucket_of(distance):
    half_count = BUCKETS // 2
    counted = jnp.zeros_like(distance)
    for section_index in range(1, half_count):
        edge_at = int(
            math.ceil(half_count * (MAX_DIST / half_count) ** (section_index / half_count))
        )
        counted = counted + (distance >= edge_at).astype(jnp.int32)
    return jnp.where(distance < half_count, distance, half_count + counted)


def distance_hot(axis):
    shape = (2 * MOST, BUCKETS) if axis == 0 else (BUCKETS, 2 * MOST)
    distance = jnp.maximum(MOST - lax.broadcasted_iota(jnp.int32, shape, axis), 0)
    return (bucket_of(distance) == lax.broadcasted_iota(jnp.int32, shape, 1 - axis)).astype(F32)


def segments(lengths, shape, axis, shift=0):
    places = lax.broadcasted_iota(jnp.int32, shape, axis) - shift
    end = jnp.zeros((1, 1), jnp.int32)
    example = jnp.where(places < 0, -1, 0)
    start = jnp.zeros(shape, jnp.int32)
    for e in range(lengths.shape[1]):
        length = lengths[:, e : e + 1]
        end = end + length
        example = example + (places >= end).astype(jnp.int32)
        start = start + jnp.where(places >= end, length, 0)
    return example, places - start


def local(src, dst, sem):
    return pltpu.make_async_copy(src, dst, sem)


def w_rows(ref, m, j):
    return ref[m, pl.ds(2 * j, 2)].reshape(2 * WIDE // 2, ref.shape[-1])


def w_lanes(ref, m, at):
    part = ref[m, :, :, :, :, at]
    return part.reshape(-1, part.shape[-1])


MESH = pl.DeviceIdType.MESH
PIECE = 48
WIDE = 384
UNITS = 16
ALL = slice(None)
LOW, HIGH = slice(0, 2), slice(2, 4)


class Place:
    def __init__(self):
        self.d, self.f = lax.axis_index("dp"), lax.axis_index("fsdp")
        self.y, self.c = self.d // 2, self.d % 2
        self.z, self.x = self.f // 2, self.f % 2
        self.nx, self.ny, self.nc = 1 - self.x, 1 - self.y, 1 - self.c

    def at(self, z=None, x=None, y=None, c=None):
        z = self.z if z is None else z
        x = self.x if x is None else x
        y = self.y if y is None else y
        c = self.c if c is None else c
        return (y * 2 + c, z * 2 + x)

    def near(self):
        others = [self.at(z=(self.z + k) % 4) for k in (1, 2, 3)]
        return others + [self.at(x=1 - self.x), self.at(y=1 - self.y), self.at(c=1 - self.c)]


def greet(peers, between=lambda: None):
    barrier = pltpu.get_barrier_semaphore()
    for dev in peers:
        pl.semaphore_signal(barrier, inc=1, device_id=dev, device_id_type=MESH)
    between()
    pl.semaphore_wait(barrier, len(peers))


def eye(n):
    a = lax.broadcasted_iota(jnp.int32, (n, n), 0)
    b = lax.broadcasted_iota(jnp.int32, (n, n), 1)
    return (a == b).astype(F32).astype(BF)


def remote(src, dst, send, recv, dev):
    return pltpu.make_async_remote_copy(
        src_ref=src, dst_ref=dst, send_sem=send, recv_sem=recv, device_id=dev, device_id_type=MESH
    )


class Sends:
    def __init__(self, place, ssem, rsem):
        self.p, self.ssem, self.rsem, self.made = place, ssem, rsem, {}

    def to_x(self):
        return self.p.at(x=1 - self.p.x)

    def to_y(self):
        return self.p.at(y=1 - self.p.y)

    def to_c(self):
        return self.p.at(c=1 - self.p.c)

    def go(self, u, slot, src, dst, dev):
        def make():
            return remote(src(), dst(), self.ssem.at[u, slot], self.rsem.at[u, slot], dev())

        make().start()
        self.made[u, slot] = make

    def wait(self, u, *slots):
        for slot in slots:
            self.made[u, slot]().wait_recv()

    def drain(self):
        for make in self.made.values():
            make().wait_send()


class Gather(Sends):
    def __init__(self, place, own, sq, fi, fo, ssem, rsem):
        super().__init__(place, ssem, rsem)
        self.own, self.sq, self.fi, self.fo = own, sq, fi, fo

    def piece(self, u, z, x, c, y):
        if u < 8:
            return self.sq.at[u, z, x, c, :, pl.ds(pl.multiple_of(y * WIDE, WIDE), WIDE)]
        if u < 12:
            return self.fi.at[z, x, c, u - 8, :, pl.ds(pl.multiple_of(y * WIDE, WIDE), WIDE)]
        at = y * (4 * WIDE) + (u - 12) * WIDE
        return self.fo.at[z, x, c, :, pl.ds(pl.multiple_of(at, WIDE), WIDE)]

    def same(self, u, slot, dev, z, x, c, y):
        def here():
            return self.piece(u, z, x, c, y)

        self.go(u, slot, here, here, dev)

    def first(self, u):
        p = self.p
        if u in (8, 9):
            self.go(
                u, 0, lambda: self.own.at[u], lambda: self.piece(u, p.z, p.x, p.c, p.y),
                self.to_x if u == 8 else self.to_y,
            )
            return
        for k in (1, 2, 3):
            self.go(
                u, k - 1, lambda: self.own.at[u], lambda: self.piece(u, p.z, p.x, p.c, p.y),
                lambda k=k: p.at(z=(p.z + k) % 4),
            )

    def second(self, u):
        p = self.p
        if u == 8:
            self.wait(u, 0)
            self.same(u, 3, self.to_y, p.z, ALL, p.c, p.y)
            return
        if u == 9:
            self.wait(u, 0)
            for y in (0, 1):
                self.same(u, 3 + y, self.to_x, p.z, p.x, p.c, y)
            return
        self.wait(u, 0, 1, 2)
        self.same(u, 3, self.to_x, LOW, p.x, p.c, p.y)
        self.same(u, 4, self.to_y, HIGH, p.x, p.c, p.y)

    def third(self, u):
        p = self.p
        if u in (8, 9):
            self.wait(u, *((3, 4) if u == 9 else (3,)))
            for k in (1, 2, 3):
                for y in (0, 1):
                    self.same(
                        u, 3 + 2 * k + y, lambda k=k: p.at(z=(p.z + k) % 4), p.z, ALL, p.c, y
                    )
            return
        self.wait(u, 3, 4)
        self.same(u, 5, self.to_y, LOW, ALL, p.c, p.y)
        for y in (0, 1):
            self.same(u, 6 + y, self.to_x, HIGH, p.x, p.c, y)
        self.same(u, 8, self.to_c, LOW, ALL, p.c, p.y)
        for y in (0, 1):
            self.same(u, 9 + y, self.to_c, HIGH, p.x, p.c, y)

    def fourth(self, u):
        p = self.p
        if u in (8, 9):
            self.wait(u, 5, 6, 7, 8, 9, 10)
            for y in (0, 1):
                self.same(u, 11 + y, self.to_c, ALL, ALL, p.c, y)
            return
        self.wait(u, 5, 6, 7)
        self.same(u, 11, self.to_c, LOW, ALL, p.c, p.ny)
        for y in (0, 1):
            self.same(u, 12 + y, self.to_c, HIGH, p.nx, p.c, y)

    def fifth(self, u):
        if u in (8, 9):
            self.wait(u, 11, 12)
            return
        self.wait(u, *range(8, 14))

    def begin(self):
        for act, u in ((self.second, 8), (self.second, 9), (self.second, 0), (self.second, 1), (self.third, 0),
                       (self.third, 1), (self.second, 2), (self.second, 3), (self.fourth, 0), (self.fourth, 1),
                       (self.second, 4)):
            act(u)

    def tick(self, t):
        if 2 <= t and t not in (8, 9):
            self.fourth(t)
        if t + 2 < UNITS and t + 2 not in (8, 9):
            self.third(t + 2)
        if t + 5 < UNITS and t + 5 not in (8, 9):
            self.second(t + 5)
        if t == 5:
            self.third(8)
            self.third(9)
        if t == UNITS - 1:
            self.fourth(8)
            self.fourth(9)


class Scatter(Sends):
    def __init__(self, place, parts, staged, r):
        super().__init__(place, r.ssem, r.rsem)
        self.parts, self.staged, self.r = parts, staged, r

    def halves(self, u):
        p, r = self.p, self.r
        return [local(self.parts(u, p.c, y), r.stage.at[u, y], r.lsem.at[u, y]) for y in (0, 1)]

    def own(self, u, y):
        if u < self.staged:
            return self.r.stage[u, pl.ds(y, 1)]
        return self.parts(u, self.p.c, y)[...][None]

    def r0(self, u):
        p, r = self.p, self.r
        for y in (0, 1):
            self.go(
                u, y, lambda y=y: self.parts(u, p.nc, y), lambda y=y: r.land.at[u, y], self.to_c
            )
        if u < self.staged:
            for copy in self.halves(u):
                copy.start()

    def r1(self, u):
        p, r = self.p, self.r
        self.wait(u, 0, 1)
        if u < self.staged:
            for copy in self.halves(u):
                copy.wait()
        for y in (p.ny, p.y):
            at = pl.ds(y, 1)
            r.land[u, at] = r.land[u, at] + self.own(u, y)
            if y is p.ny:
                self.go(
                    u, 2, lambda: r.land.at[u, p.ny, LOW], lambda: r.land1.at[u, LOW], self.to_y
                )
        for y in (0, 1):
            self.go(
                u, 3 + y, lambda y=y: r.land.at[u, y, HIGH, p.nx], lambda y=y: r.land1.at[u, HIGH, y],
                self.to_x,
            )

    def r2(self, u):
        p, r = self.p, self.r
        self.wait(u, 2, 3, 4)
        own, x = pl.ds(p.y, 1), pl.ds(p.x, 1)
        r.land[u, own, LOW] = r.land[u, own, LOW] + r.land1[u, LOW][None]
        for y in (0, 1):
            r.land[u, y, HIGH, x] = r.land[u, y, HIGH, x] + r.land1[u, HIGH, y][:, None]
        self.go(u, 5, lambda: r.land.at[u, p.y, LOW, p.nx], lambda: r.land2.at[u, LOW], self.to_x)
        self.go(u, 6, lambda: r.land.at[u, p.ny, HIGH, p.x], lambda: r.land2.at[u, HIGH], self.to_y)

    def r3(self, u):
        p, r = self.p, self.r
        self.wait(u, 5, 6)
        y, x = pl.ds(p.y, 1), pl.ds(p.x, 1)
        r.land[u, y, :, x] = r.land[u, y, :, x] + r.land2[u][None, :, None]
        for k in (1, 2, 3):
            self.go(
                u, 6 + k, lambda k=k: r.land.at[u, p.y, (p.z + k) % 4, p.x],
                lambda k=k: r.land3.at[u, k - 1], lambda k=k: p.at(z=(p.z + k) % 4),
            )

    def r4(self, u):
        p, r = self.p, self.r
        self.wait(u, 7, 8, 9)
        part = r.land[u, pl.ds(p.y, 1), pl.ds(p.z, 1), pl.ds(p.x, 1)]
        total = part.reshape(PIECE, WIDE).astype(F32)
        for k in range(3):
            total = total + r.land3[u, k].astype(F32)
        r.fin[u] = total.astype(BF)

    def step(self, number, *units):
        act = (self.r0, self.r1, self.r2, self.r3, self.r4)[number]
        for u in units:
            act(u)


def scatter_scratch(count, staged):
    return dict(
        land=pltpu.VMEM((count, 2, 4, 2, PIECE, WIDE), BF),
        stage=pltpu.VMEM((staged, 2, 4, 2, PIECE, WIDE), BF),
        land1=pltpu.VMEM((count, 4, 2, PIECE, WIDE), BF),
        land2=pltpu.VMEM((count, 4, PIECE, WIDE), BF),
        land3=pltpu.VMEM((count, 3, PIECE, WIDE), BF),
        ssem=pltpu.SemaphoreType.DMA((count, 10)),
        rsem=pltpu.SemaphoreType.DMA((count, 10)),
        lsem=pltpu.SemaphoreType.DMA((staged, 2)),
    )


def self_masks(lengths, mask_ref):
    blocks = mask_ref.shape[0]
    seg_col = segments(lengths, (blocks * MOST, 1), 0)[0]
    seg_row = segments(lengths, (1, (blocks + 1) * MOST), 1, MOST)[0]
    a = lax.broadcasted_iota(jnp.int32, (MOST, 2 * MOST), 0)
    b = lax.broadcasted_iota(jnp.int32, (MOST, 2 * MOST), 1)
    causal = b <= a + MOST
    for i in range(blocks):
        same = seg_col[MOST * i : MOST * (i + 1), :] == seg_row[:, MOST * i : MOST * (i + 2)]
        mask_ref[i] = jnp.where(causal & same, 0.0, HIDDEN_SCORE)


def pair_bias(dist_ref, pair):
    parts = []
    for h in range(2):
        row = dist_ref[pl.ds(2 * pair + h, 1), :]
        parts.append(
            pltpu.roll(jnp.broadcast_to(row, (MOST, 2 * MOST)), 0, 1, stride=1, stride_axis=0)
        )
    return jnp.concatenate(parts, axis=0)


def masked_scores(scores, bias, mask):
    both = scores + bias
    return (both.reshape(2, MOST, 2 * MOST) + mask[None]).reshape(2 * MOST, 2 * MOST)


def example_rows(index_ref, example, total):
    place = lax.broadcasted_iota(jnp.int32, (MOST, total), 0)
    here = (index_ref[0:1, :] == example) & (index_ref[1:2, :] == place)
    return here.astype(F32).astype(BF)


def example_index(r, total):
    r.index[0:1, :], r.index[1:2, :] = segments(r.lengths[...], (1, total), 1)
    examples, keys_n = r.hidden.shape
    place = lax.broadcasted_iota(jnp.int32, (1, keys_n), 1)
    for e in range(examples):
        r.hidden[e : e + 1, :] = jnp.where(place < r.valid[:, e : e + 1], 0.0, HIDDEN_SCORE)


def turn_squares(r, *which):
    shards = (r.k_c, r.v_c, r.q_s, r.k_s, r.v_s, r.o_s, r.q_c, r.o_c)
    e96 = eye(96)
    for m in which:
        r.xt[m] = nt(e96, shards[m][...].astype(BF)).astype(BF).reshape(2, PIECE, 192)


def turn_feeds(r):
    t = nt(eye(384), r.f_i[...].astype(BF)).astype(BF).reshape(2, 4, PIECE, 192)
    for s in range(4):
        for h in range(2):
            r.xt[8 + s, h] = t[h, s]
    r.xf[...] = r.f_o[...].astype(BF).reshape(2, PIECE, 768)


def own_parts(p, r, low, high):
    first = p.c == 0
    mine = r.xt[low:high, pl.ds(p.c, 1)].reshape(high - low, PIECE, 192)
    other = r.took[low:high]
    r.own[low:high] = jnp.concatenate(
        [jnp.where(first, mine, other), jnp.where(first, other, mine)], axis=-1
    )


def small_sends(p, r):
    made = []
    for k in range(1, 8):
        dev = (p.d, (p.f + k) % 8)
        made.append(
            remote(r.gt.at[p.f], r.gt.at[p.f], r.smsem.at[0, k - 1], r.smsem.at[1, k - 1], dev)
        )
    for k in range(1, 4):
        dev = ((p.d + k) % 4, p.f)
        made.append(
            remote(r.tt.at[p.d], r.tt.at[p.d], r.smsem.at[0, 6 + k], r.smsem.at[1, 6 + k], dev)
        )
    return made


def forward_kernel(comm, r):
    rows, width = r.x.shape
    examples, keys_n = r.enc.shape[0], r.enc.shape[1]
    blocks = rows // MOST
    enc_copies = [local(r.enc.at[e], r.encv.at[e], r.esem.at[e]) for e in range(examples)]
    for copy in enc_copies:
        copy.start()
    if comm:
        p = Place()
        peers = [(p.d, (p.f + k) % 8) for k in range(1, 8)] + [((p.d + k) % 4, p.f) for k in range(1, 4)]

        def prepare():
            r.gt[pl.ds(p.f, 1)] = jnp.zeros((1, 8, 128), F32)
            r.gt[pl.ds(p.f, 1), 0:3, 0:96] = r.gains_s[...].astype(BF).astype(F32)[None]
            r.tt[pl.ds(p.d, 1)] = jnp.zeros((1, 8, 128), F32)
            r.tt[pl.ds(p.d, 1), :, 0:HEADS] = r.table_s[...].astype(BF).astype(F32)[None]
            turn_squares(r, 0, 1)

        greet(peers, prepare)
        sib = p.at(c=1 - p.c)
        trade = [
            remote(r.xt.at[0:2, 1 - p.c], r.took.at[0:2], r.xsem.at[0], r.xsem.at[1], sib),
            remote(r.xt.at[2:12, 1 - p.c], r.took.at[2:12], r.xsem.at[2], r.xsem.at[3], sib),
            remote(r.xf.at[1 - p.c], r.tookf, r.xsem.at[4], r.xsem.at[5], sib),
        ]
        small = small_sends(p, r)
        for copy in trade[0:1] + small:
            copy.start()
        turn_feeds(r)
        g = Gather(p, r.own, r.sq, r.fi, r.fo, r.ssem, r.rsem)
        placed = [
            local(r.own.at[u], g.piece(u, p.z, p.x, p.c, p.y), r.psem.at[u]) for u in range(UNITS)
        ]
        trade[0].wait_recv()
        own_parts(p, r, 0, 2)
        for u in (0, 1):
            g.first(u)
            placed[u].start()
        turn_squares(r, 2, 3, 4, 5, 6, 7)
        for copy in trade[1:]:
            copy.start()
        first = p.c == 0
        trade[1].wait_recv()
        own_parts(p, r, 2, 12)
        trade[2].wait_recv()
        mine, other = r.xf[pl.ds(p.c, 1)].reshape(PIECE, 768), r.tookf[...]
        low, high = jnp.where(first, mine, other), jnp.where(first, other, mine)
        r.own[12], r.own[13] = low[:, :WIDE], low[:, WIDE:]
        r.own[14], r.own[15] = high[:, :WIDE], high[:, WIDE:]
        for u in (8, 9, 2, 3, 4, 5, 6, 7, 10, 11, 12, 13, 14, 15):
            g.first(u)
            placed[u].start()
        for copy in small:
            copy.wait_recv()
        spot = lax.broadcasted_iota(jnp.int32, (128, width), 1)
        lane = lax.broadcasted_iota(jnp.int32, (128, width), 0)
        gains = jnp.zeros((8, width), F32)
        for f in range(8):
            put = ((spot == lane + 96 * f) & (lane < 96)).astype(F32).astype(BF)
            gains = gains + nn(r.gt[f].astype(BF), put)
        r.gains[...] = gains[0:3]
        table = r.tt[...].reshape(BUCKETS, 128).astype(BF)
        r.dist[...] = tn(table, distance_hot(1).astype(BF))[0:HEADS]
        for copy in placed:
            copy.wait()
        begin, tick, arrived = g.begin, g.tick, g.fifth
    else:
        begin, tick, arrived = (lambda *_: None,) * 3

    loads = [local(r.sq.at[m], r.wv.at[m], r.wsem.at[m]) for m in range(7)]

    def fetch(*which):
        for m in which:
            arrived(m)
            loads[m].start()

    def have(*which):
        for m in which:
            loads[m].wait()

    example_index(r, rows)
    r.n1[...] = rms(r.x[...].astype(F32), r.gains[0:1, :]).astype(BF)
    r.k1[0:MOST, :] = jnp.zeros((MOST, width), BF)
    r.v1[0:MOST, :] = jnp.zeros((MOST, width), BF)
    self_masks(r.lengths[...], r.mask)
    halves = width // WIDE

    def save(e):
        return [local(r.k2v.at[e], r.k2.at[e], r.ksem.at[e, 0]), local(r.v2v.at[e], r.v2.at[e], r.ksem.at[e, 1])]

    def project(e):
        local(r.enc.at[e], r.encv.at[e], r.esem.at[e]).wait()
        for j in range(halves):
            at = slice(WIDE * j, WIDE * (j + 1))
            r.k2v[e, :, at] = nt(r.encv[e], w_rows(r.wv, 0, j)).astype(BF)
            r.v2v[e, :, at] = nt(r.encv[e], w_rows(r.wv, 1, j)).astype(BF)
        for copy in save(e):
            copy.start()

    begin()
    fetch(0, 1)
    have(0, 1)
    for t in range(4):
        tick(t)
        loop(2 * t, 2 * t + 2, project)
    fetch(2, 3)
    tick(4)
    fetch(4)
    have(2, 3, 4)

    for j in range(halves):
        at = slice(WIDE * j, WIDE * (j + 1))
        r.q1[:, at] = nt(r.n1[...], w_rows(r.wv, 2, j)).astype(BF)
        r.k1[MOST:, at] = nt(r.n1[...], w_rows(r.wv, 3, j)).astype(BF)
        r.v1[MOST:, at] = nt(r.n1[...], w_rows(r.wv, 4, j)).astype(BF)

    def attend(pair):
        at = lanes(pair, 128)
        bias = pair_bias(r.dist, pair)
        for i in range(blocks):
            queries = split_heads(r.q1[MOST * i : MOST * (i + 1), at])
            keys = r.k1[MOST * i : MOST * (i + 2), at]
            values = r.v1[MOST * i : MOST * (i + 2), at]
            probs = softmax(masked_scores(nt(queries, keys), bias, r.mask[i])).astype(BF)
            r.a1[MOST * i : MOST * (i + 1), at] = join_heads(nn(probs, values)).astype(BF)

    tick(5)
    loop(0, PAIRS // 2, attend, PAIRS // 2)
    tick(6)
    fetch(5)
    loop(PAIRS // 2, PAIRS, attend, PAIRS // 2)
    tick(7)
    fetch(6)
    have(5, 6)
    for j in range(halves):
        at = slice(WIDE * j, WIDE * (j + 1))
        r.h1[:, at] = r.x[:, at].astype(F32) + nt(r.a1[...], w_rows(r.wv, 5, j))
    r.n2[...] = rms(r.h1[...], r.gains[1:2, :]).astype(BF)
    for j in range(halves):
        at = slice(WIDE * j, WIDE * (j + 1))
        r.q2[:, at] = nt(r.n2[...], w_rows(r.wv, 6, j)).astype(BF)

    r.sum[...] = jnp.zeros_like(r.sum)

    def cross(e):
        pick = example_rows(r.index, e, rows)
        r.qe[...] = nn(pick, r.q2[...]).astype(BF)
        hidden = r.hidden[pl.ds(e, 1), :]

        def pair_step(pair):
            at = lanes(pair, 128)
            probs = softmax(nt(split_heads(r.qe[:, at]), r.k2v[e, :, at]) + hidden).astype(BF)
            r.ae[:, at] = join_heads(nn(probs, r.v2v[e, :, at])).astype(BF)

        loop(0, PAIRS, pair_step, PAIRS)
        r.sum[...] += tn(pick, r.ae[...])

    def cross_tick(e):
        if comm:
            for t in range(examples):
                pl.when(e == t)(functools.partial(tick, t + 8))
        cross(e)

    loop(0, examples, cross_tick)
    r.a2[...] = r.sum[...].astype(BF)

    def saved(e):
        for copy in save(e):
            copy.wait()

    loop(0, examples, saved)
    if comm:
        for u in range(7, UNITS):
            g.fifth(u)
        g.drain()
        for copy in trade + small:
            copy.wait_send()


GELU_A = math.sqrt(2.0 / math.pi)
GELU_B = 0.044715


def feed_kernel(r):
    rows, width = r.a2.shape
    hidden = r.fi.shape[0]
    def cross_out(j):
        at = lanes(j, 256)
        r.h2[:, at] = r.h1[:, at] + nt(r.a2[...], r.w[0, at, :])

    loop(0, width // 256, cross_out)
    r.n3[...] = rms(r.h2[...], r.gains[2:3, :]).astype(BF)
    r.sum[...] = r.h2[...]
    r.back[...] = jnp.zeros_like(r.back)

    r.ct[...] = r.c[...].T

    def part(j):
        for i in range(3):
            at = pl.ds(pl.multiple_of(j * width + i * 256, 256), 256)
            here = slice(256 * i, 256 * (i + 1))
            u = nt(r.n3[...], r.fi[at, :])
            t = jnp.tanh(GELU_A * (u + GELU_B * (u * u * u)))
            r.g[:, here] = (0.5 * u * (1.0 + t)).astype(BF)
            slope = 0.5 * (1.0 + t) + 0.5 * u * (1.0 - t * t) * (
                GELU_A * (1.0 + (3.0 * GELU_B) * (u * u))
            )
            r.du[:, here] = (nn(r.c[...], r.fo[:, at]) * slope).astype(BF)
        whole_part = lanes(j, width)
        for i in range(3):
            at = pl.ds(pl.multiple_of(j * width + i * 256, 256), 256)
            here = slice(256 * i, 256 * (i + 1))
            r.dfo[:, :, :, :, at] = nn(r.ct[...], r.g[:, here]).astype(BF).reshape(4, 2, 2, PIECE, 256)
            r.dfi[at, :] = tn(r.du[:, here], r.n3[...]).astype(BF)
            r.sum[:, here] += nt(r.g[...], r.fo[here, whole_part])
            r.back[:, here] += nn(r.du[...], r.fi[whole_part, here])

    loop(0, hidden // width, part, 1)
    r.out[...] = r.sum[...].astype(BF)
    dz, dw = rms_back(r.h2[...], r.gains[2:3, :], r.back[...])
    r.gain[...] = dw
    r.dh2[...] = r.c[...].astype(F32) + dz

    def tail(j):
        at = lanes(j, 256)
        r.da2[:, at] = nn(r.dh2[...].astype(BF), r.w[0, :, at]).astype(BF)
        r.dwoc[at, :] = tn(r.dh2[:, at].astype(BF), r.a2[...]).astype(BF)

    loop(0, width // 256, tail)


STARTS = (0, 0, 1, 3, 4, 6, 7)
LAGS = (0, 1, 4, 6, 8)


def cross_back_kernel(comm, r):
    rows, width = r.q2.shape
    examples, keys_n = r.k2.shape[0], r.k2.shape[1]

    def fetches(e):
        return [local(getattr(r, a).at[e], getattr(r, b).at[e], r.esem.at[e, i])
                for i, (a, b) in enumerate((("k2", "k2v"), ("v2", "v2v")))]

    for e in range(examples):
        for copy in fetches(e):
            copy.start()
    if comm:
        p = Place()

        def parts(u, c, y):
            if u >= 4:
                return r.dfi.at[:, :, c, u - 4, :, y * WIDE : (y + 1) * WIDE]
            at = y * 4 * WIDE + u * WIDE
            return r.dfo.at[:, :, c, :, at : at + WIDE]

        s = Scatter(p, parts, 7, r)
        greet(p.near())
    example_index(r, rows)
    r.sum[...] = jnp.zeros_like(r.sum)

    def out_copies(e):
        return [
            local(r.dk.at[e % 2], r.dk2.at[e], r.dsem.at[e % 2, 0]),
            local(r.dv.at[e % 2], r.dv2.at[e], r.dsem.at[e % 2, 1]),
        ]

    def tick(at):
        if comm:
            for t in range(2 * examples):

                @pl.when(at == t)
                def _():
                    for number in (4, 3, 2, 1, 0):
                        for u, at_first in enumerate(STARTS):
                            if at_first + LAGS[number] == t:
                                s.step(number, u)

    def example(e):
        tick(2 * e)
        for copy in fetches(e):
            copy.wait()
        pick = example_rows(r.index, e, rows)
        r.qe[...] = nn(pick, r.q2[...]).astype(BF)
        r.dae[...] = nn(pick, r.da2[...]).astype(BF)
        hidden = r.hidden[pl.ds(e, 1), :]

        @pl.when(e >= 2)
        def _():
            for copy in out_copies(e - 2):
                copy.wait()

        def attend(pair):
            at = lanes(pair, 128)
            queries = split_heads(r.qe[:, at])
            deltas = split_heads(r.dae[:, at])
            keys = r.k2v[e, :, at]
            probs = softmax(nt(queries, keys) + hidden)
            dprobs = nt(deltas, r.v2v[e, :, at])
            low = (probs * (dprobs - jnp.sum(dprobs * probs, axis=-1, keepdims=True))).astype(BF)
            r.dv[e % 2, at, :] = tn(deltas, probs.astype(BF)).astype(BF)
            r.dk[e % 2, at, :] = tn(queries, low).astype(BF)
            r.dqe[:, at] = join_heads(nn(low, keys)).astype(BF)

        loop(0, PAIRS, attend, PAIRS)
        tick(2 * e + 1)
        for copy in out_copies(e):
            copy.start()
        r.sum[...] += tn(pick, r.dqe[...])

    loop(0, examples, example)
    r.dq2[...] = r.sum[...].astype(BF)
    for e in (examples - 2, examples - 1):
        for copy in out_copies(e):
            copy.wait()
    if comm:
        s.drain()


def self_back_kernel(comm, r):
    rows, width = r.x.shape
    blocks = rows // MOST
    thirds = width // 256
    if comm:
        p = Place()

        def parts(u, c, y):
            at = pl.ds(pl.multiple_of(y * WIDE, WIDE), WIDE)
            if u == 0:
                return r.dfi.at[:, :, c, 3, :, at]
            if u == 1:
                return r.dwoc.at[:, :, c, :, at]
            return r.dw.at[u - 2, :, :, c, :, at]

        s = Scatter(p, parts, 2, r)
        greet(p.near())
        step = s.step
    else:
        step = lambda *units: None

    def put(m, j, value):
        if comm:
            r.dw[m, 2 * j : 2 * j + 2] = value.astype(BF).reshape(2, 2, 2, PIECE, width)
        else:
            r.dw[m, WIDE * j : WIDE * (j + 1), :] = value.astype(BF)

    halves = width // WIDE
    examples = r.denc.shape[0]
    loads = [local(r.sq.at[2 + m], r.w.at[m], r.wsem.at[m]) for m in range(5)]
    late = [local(r.sq.at[m], r.w.at[3 + m], r.wsem.at[5 + m]) for m in range(2)]
    for copy in loads:
        copy.start()

    passes = ((r.dk2, r.enc), (r.dv2, r.enc), (r.dk2, r.dv2))

    def fetches(number, e):
        places = (r.one, r.three if number == 2 else r.two)
        return [local(passes[number][i].at[e], places[i].at[e % 2], r.esem.at[e % 2, i]) for i in (0, 1)]

    def pass_step(number, e, act):
        for copy in fetches(number, e):
            copy.wait()
        act(e)

        @pl.when(e + 2 < examples)
        def _():
            for copy in fetches(number, e + 2):
                copy.start()

        if number < 2:

            @pl.when(e + 2 >= examples)
            def _():
                for copy in fetches(number + 1, e + 2 - examples):
                    copy.start()

    def out_copy(e):
        return local(r.denv.at[e % 2], r.denc.at[e], r.dsem.at[e % 2])

    for e in (0, 1):
        for copy in fetches(0, e):
            copy.start()
    step(0, 0, 1)
    for j in range(halves):
        at = slice(WIDE * j, WIDE * (j + 1))
        put(0, j, tn(r.dq2[:, at], r.n2[...]))
    step(0, 2)
    for copy in loads:
        copy.wait()

    def query(j):
        at = lanes(j, 256)
        r.back[:, at] = nn(r.dq2[...], w_lanes(r.w, 4, at))

    loop(0, thirds, query)
    step(1, 0, 1)
    dz, dw = rms_back(r.h1[...], r.gains[1:2, :], r.back[...])
    r.gain[1:2, :] = dw
    r.dh1[...] = r.dh2[...] + dz
    r.b1[...] = r.dh1[...].astype(BF)
    for j in range(halves):
        at = slice(WIDE * j, WIDE * (j + 1))
        put(1, j, tn(r.b1[:, at], r.a1[...]))
    step(0, 3)

    def out(j):
        at = lanes(j, 256)
        r.da1[:, at] = nn(r.b1[...], w_lanes(r.w, 3, at)).astype(BF)

    loop(0, thirds, out)
    for copy in late:
        copy.start()
    if comm:
        pairs = [p.at(c=1 - p.c), p.at(y=1 - p.y), p.at(x=1 - p.x),
                 p.at(z=p.z + 1 - 2 * (p.z % 2)), p.at(z=(p.z + 2) % 4)]

        def share(i):
            return remote(r.given.at[i], r.gotten.at[i], r.smsem.at[0, i], r.smsem.at[1, i], pairs[i])

        def share_go(i):
            r.given[i] = r.small[...]
            share(i).start()

        def share_end(i):
            share(i).wait_recv()
            r.small[...] = r.small[...] + r.gotten[i]

        def share_next(i):
            share_end(i)
            share_go(i + 1)

    def passing(number, act, events):
        def one(e):
            pass_step(number, e, act)
            if comm:
                for at, happens in events.items():
                    pl.when(e == at)(functools.partial(quiet, happens))

        loop(0, examples, one)

    def weight_sum(e):
        def dense(j):
            at = lanes(j, 256)
            r.dwsum[at, :] = nn(r.one[e % 2, at, :], r.two[e % 2]) + jnp.where(e == 0, 0.0, r.dwsum[at, :])

        loop(0, thirds, dense, thirds)

    events = (
        {1: lambda: step(1, 2), 2: lambda: step(1, 3), 4: lambda: step(2, 0, 1), 6: lambda: step(2, 2),
         7: lambda: step(2, 3)},
        {0: lambda: share_next(0), 1: lambda: step(2, 4), 3: lambda: step(2, 5), 4: lambda: share_next(1),
         5: lambda: step(2, 6), 6: lambda: step(3, 4), 7: lambda: (step(3, 5), share_next(2))},
        {0: lambda: step(3, 6), 1: lambda: (step(1, 8), step(4, 4)), 2: lambda: step(4, 5),
         3: lambda: share_next(3), 4: lambda: step(4, 6), 5: lambda: step(2, 8), 6: lambda: share_end(4)},
    )

    passing(0, weight_sum, events[0])
    for j in range(halves):
        put(5, j, r.dwsum[WIDE * j : WIDE * (j + 1), :])
    step(0, 7)
    self_masks(r.lengths[...], r.mask)
    a = lax.broadcasted_iota(jnp.int32, (MOST, MOST), 0)
    b = lax.broadcasted_iota(jnp.int32, (MOST, MOST), 1)
    flip = (a + b == MOST - 1).astype(F32)

    def attend(pair):
        at = lanes(pair, 128)
        bias = pair_bias(r.dist, pair)
        r.dksum[...] = jnp.zeros_like(r.dksum)
        r.dvsum[...] = jnp.zeros_like(r.dvsum)
        skewed = jnp.zeros((2 * MOST, 2 * MOST), F32)
        for i in range(blocks):
            own = slice(MOST * i, MOST * (i + 1))
            band = slice(MOST * i, MOST * (i + 2))
            queries = split_heads(r.q1[own, at])
            deltas = split_heads(r.da1[own, at])
            keys = r.k1[band, at]
            probs = softmax(masked_scores(nt(queries, keys), bias, r.mask[i]))
            dprobs = nt(deltas, r.v1[band, at])
            dscores = probs * (dprobs - jnp.sum(dprobs * probs, axis=-1, keepdims=True))
            low = dscores.astype(BF)
            skewed = skewed + dscores
            r.dvsum[:, band] += tn(deltas, probs.astype(BF))
            r.dksum[:, band] += tn(queries, low)
            r.dq[own, at] = join_heads(nn(low, keys)).astype(BF)
        r.dk[at, :] = r.dksum[:, MOST:].astype(BF)
        r.dv[at, :] = r.dvsum[:, MOST:].astype(BF)
        for h in range(2):
            flipped = jnp.dot(
                flip,
                skewed[MOST * h : MOST * (h + 1)],
                precision=lax.Precision.HIGHEST,
                preferred_element_type=F32,
            )
            straight = pltpu.roll(flipped, MOST + 1, 1, stride=1, stride_axis=0)
            r.distsum[pl.ds(2 * pair + h, 1), :] = jnp.sum(straight, axis=0, keepdims=True)

    plan = {
        0: ((3, 0, 1),),
        1: ((1, 7), (3, 2)),
        2: ((3, 3), (4, 0, 1)),
        3: ((2, 7), (4, 2)),
        4: ((4, 3),),
        5: ((3, 7),),
    }

    def attend_tick(pair):
        if comm:
            for t, steps in plan.items():

                @pl.when(pair == t)
                def _():
                    for numbers in steps:
                        step(*numbers)

        attend(pair)

    loop(0, PAIRS, attend_tick)
    for m, ref in ((2, r.dq), (3, r.dk), (4, r.dv)):
        for j in range(halves):
            at = slice(WIDE * j, WIDE * (j + 1))
            put(m, j, tn(ref[:, at], r.n1[...]) if m == 2 else nn(ref[at, :], r.n1[...]))
        step(0, 2 + m)
    step(4, 7)
    step(1, 4, 5)

    r.b1[...] = r.dk[...].T
    r.da1[...] = r.dv[...].T

    def qkv(j):
        at = lanes(j, 256)
        r.back[:, at] = (
            nn(r.dq[...], w_lanes(r.w, 0, at))
            + nn(r.b1[...], w_lanes(r.w, 1, at))
            + nn(r.da1[...], w_lanes(r.w, 2, at))
        )

    loop(0, thirds, qkv, thirds)
    step(1, 6)
    dz, dw = rms_back(r.x[...].astype(F32), r.gains[0:1, :], r.back[...])
    r.gain[0:1, :] = dw
    r.dx[...] = (r.dh1[...] + dz).astype(BF)
    by_bucket = jnp.dot(
        r.distsum[...], distance_hot(0), precision=lax.Precision.HIGHEST, preferred_element_type=F32
    )
    r.small[...] = jnp.zeros_like(r.small)
    r.small[0:2, :] = r.gain[0:2, :]
    r.small[2:3, :] = r.gain3[...]
    r.small[3 : 3 + HEADS, 0:BUCKETS] = by_bucket

    if comm:
        share_go(0)

    passing(1, weight_sum, events[1])
    for j in range(halves):
        put(6, j, r.dwsum[WIDE * j : WIDE * (j + 1), :])
    step(0, 8)
    for copy in late:
        copy.wait()

    def encoder(e):
        @pl.when(e >= 2)
        def _():
            out_copy(e - 2).wait()

        r.b1[...] = r.one[e % 2].T
        r.da1[...] = r.three[e % 2].T

        def dense(j):
            at = lanes(j, 256)
            r.denv[e % 2, :, at] = (
                nn(r.b1[...], w_lanes(r.w, 3, at)) + nn(r.da1[...], w_lanes(r.w, 4, at))
            ).astype(BF)

        loop(0, thirds, dense, thirds)
        out_copy(e).start()

    passing(2, encoder, events[2])
    step(3, 8)
    for e in (examples - 2, examples - 1):
        out_copy(e).wait()
    if not comm:
        return

    first = p.c == 0

    def split(low, high):
        left, right = r.all[low:high, :, :192], r.all[low:high, :, 192:]
        r.give[low:high] = jnp.where(first, right, left)
        return jnp.where(first, left, right)

    def both(a, b, axis):
        return jnp.concatenate([jnp.where(first, a, b), jnp.where(first, b, a)], axis=axis)

    r.all[0:7] = r.fin[1:8]
    r.all[7:10] = r.finf[4:7]
    r.all[10] = r.fin[0]
    keep = split(0, 11)
    r.giveo[...] = r.finf[pl.ds(2 * p.nc, 2)]
    sib = p.at(c=1 - p.c)
    trade = [
        remote(r.give.at[0:11], r.take.at[0:11], r.xsem.at[0], r.xsem.at[1], sib),
        remote(r.giveo, r.takeo, r.xsem.at[2], r.xsem.at[3], sib),
        remote(r.give.at[11:12], r.take.at[11:12], r.xsem.at[4], r.xsem.at[5], sib),
    ]
    for copy in trade[0:2]:
        copy.start()
    spot = lax.broadcasted_iota(jnp.int32, (width, 128), 0)
    lane = lax.broadcasted_iota(jnp.int32, (width, 128), 1)
    put_gains = ((spot == lane + 96 * p.f) & (lane < 96)).astype(F32)
    r.gains_own[...] = jnp.dot(
        r.small[0:8, :], put_gains, precision=lax.Precision.HIGHEST, preferred_element_type=F32
    )
    spot = lax.broadcasted_iota(jnp.int32, (8, BUCKETS), 1)
    line = lax.broadcasted_iota(jnp.int32, (8, BUCKETS), 0)
    r.table_own[...] = lax.dot_general(
        (spot == line + 8 * p.d).astype(F32), r.small[3 : 3 + HEADS, 0:BUCKETS], (((1,), (1,)), ((), ())),
        precision=lax.Precision.HIGHEST, preferred_element_type=F32,
    )
    for copy in trade[0:2]:
        copy.wait_recv()
    r.tsq[0:7] = both(keep[0:7], r.take[0:7], 1)
    r.tfi[...] = both(keep[7:11].reshape(192, 192), r.take[7:11].reshape(192, 192), 0)
    own = r.finf[pl.ds(2 * p.c, 2)]
    r.tfo[...] = both(
        jnp.concatenate([own[0], own[1]], axis=1), jnp.concatenate([r.takeo[0], r.takeo[1]], axis=1), 0
    )
    step(4, 8)
    r.all[11] = r.fin[8]
    keep = split(11, 12)
    trade[2].start()
    trade[2].wait_recv()
    r.tsq[7:8] = both(keep, r.take[11:12], 1)
    s.drain()
    for i in range(5):
        share(i).wait_send()
    for copy in trade:
        copy.wait_send()


def finish_kernel(r):
    examples = r.denc.shape[0]
    ins = [local(r.denc_in.at[e], r.hold.at[e], r.sem.at[e, 0]) for e in range(examples)]
    outs = [local(r.hold.at[e], r.denc.at[e], r.sem.at[e, 1]) for e in range(examples)]
    for copy in ins:
        copy.start()
    r.dx[...] = r.dx_in[...]
    e192 = eye(192)
    for m, ref in enumerate((r.o_c, r.q_c, r.o_s, r.q_s, r.k_s, r.v_s, r.k_c, r.v_c)):
        ins[m].wait()
        outs[m].start()
        ref[...] = nt(e192, r.tsq[m])
    r.f_i[...] = nt(e192, r.tfi[...])
    r.f_o[...] = r.tfo[...].astype(F32)
    r.gains[...] = r.gains_in[0:3, 0:96]
    r.table[...] = r.table_in[...]
    for copy in outs:
        copy.wait()


VM = pltpu.VMEM
HBM = pl.ANY


def run(kernel, ins, outs, scratch, name, collective=None, flops=0):
    names = list(ins) + list(outs) + list(scratch)

    def wrapped(*refs):
        kernel(types.SimpleNamespace(**dict(zip(names, refs))))

    arrays, specs = [], []
    for value in ins.values():
        array, spec = value if isinstance(value, tuple) else (value, VM)
        arrays.append(array)
        specs.append(spec if isinstance(spec, pl.BlockSpec) else pl.BlockSpec(memory_space=spec))
    results = pl.pallas_call(
        wrapped,
        grid=(1,),
        in_specs=specs,
        out_specs=[pl.BlockSpec(memory_space=(o[2] if len(o) > 2 else VM)) for o in outs.values()],
        out_shape=[jax.ShapeDtypeStruct(o[0], o[1]) for o in outs.values()],
        scratch_shapes=list(scratch.values()),
        compiler_params=pltpu.CompilerParams(
            vmem_limit_bytes=VMEM_LIMIT,
            collective_id=collective,
            has_side_effects=collective is not None,
        ),
        cost_estimate=pl.CostEstimate(flops=flops, bytes_accessed=20_000_000, transcendentals=0),
        name=name,
    )(*arrays)
    return types.SimpleNamespace(**dict(zip(outs, results)))


def dma(*shape):
    return pltpu.SemaphoreType.DMA(shape)


def body(comm, decoder_in, encoder_out, decoder_lengths, encoder_lengths, norm_gains, rel_table,
         query_self, key_self, value_self, out_self, query_cross, key_cross, value_cross, out_cross,
         feed_in, feed_out, upstream):
    rows, width = decoder_in.shape
    row_count, examples = decoder_lengths.shape
    keys_n = encoder_out.shape[1]
    hidden = feed_in.shape[1] * lax.axis_size("fsdp")
    small = (rows, width)
    cut = (4, 2, 2, PIECE, width)

    index = dict(lengths=decoder_lengths, valid=encoder_lengths[None, :])
    index_scratch = dict(index=VM((2, rows), jnp.int32), hidden=VM((examples, keys_n), F32))

    acts = dict(n1=(small, BF), q1=(small, BF), k1=((rows + MOST, width), BF), v1=((rows + MOST, width), BF),
                a1=(small, BF), h1=(small, F32), n2=(small, BF), q2=(small, BF), a2=(small, BF),
                k2=(encoder_out.shape, BF, HBM), v2=(encoder_out.shape, BF, HBM))
    scratch = dict(
        encv=VM(encoder_out.shape, BF), k2v=VM(encoder_out.shape, BF), v2v=VM(encoder_out.shape, BF),
        wv=VM((7,) + cut, BF), mask=VM((rows // MOST, MOST, 2 * MOST), F32),
        qe=VM((MOST, width), BF), ae=VM((MOST, width), BF), sum=VM(small, F32),
        esem=dma(examples), wsem=dma(7), ksem=dma(examples, 2), **index_scratch,
    )
    ins = dict(x=decoder_in, enc=(encoder_out, HBM), **index)
    if comm:
        ins |= dict(q_s=query_self, k_s=key_self, v_s=value_self, o_s=out_self, q_c=query_cross,
                    o_c=out_cross, k_c=key_cross, v_c=value_cross, f_i=feed_in, f_o=feed_out.T,
                    gains_s=norm_gains, table_s=rel_table)
        fwd = run(
            functools.partial(forward_kernel, True), ins,
            acts | dict(sq=((8,) + cut, BF, HBM), fi=((4, 2, 2, 4, PIECE, width), BF, HBM),
                        fo=((4, 2, 2, PIECE, hidden), BF, HBM), gains=((3, width), F32),
                        dist=((HEADS, 2 * MOST), F32)),
            scratch | dict(
                xt=VM((12, 2, PIECE, 192), BF), xf=VM((2, PIECE, 768), BF), took=VM((12, PIECE, 192), BF),
                tookf=VM((PIECE, 768), BF), own=VM((UNITS, PIECE, WIDE), BF), gt=VM((8, 8, 128), F32),
                tt=VM((4, 8, 128), F32), xsem=dma(6), psem=dma(UNITS), smsem=dma(2, 10),
                ssem=dma(UNITS, 14), rsem=dma(UNITS, 14)),
            "forward", collective=0,
        )
        sq, fi, fo, gains, dist = fwd.sq, fwd.fi, fwd.fo, fwd.gains, fwd.dist
    else:
        order = (key_cross, value_cross, query_self, key_self, value_self, out_self, query_cross, out_cross)
        sq = jnp.stack([m.astype(BF).T for m in order])
        sq = lax.all_gather(sq, "fsdp", axis=1, tiled=True)
        sq = lax.all_gather(sq, "dp", axis=2, tiled=True).reshape((8,) + cut)
        fi = lax.all_gather(feed_in.astype(BF).T, "fsdp", axis=0, tiled=True)
        fi = lax.all_gather(fi, "dp", axis=1, tiled=True)
        fo = lax.all_gather(feed_out.astype(BF).T, "fsdp", axis=0, tiled=True)
        fo = lax.all_gather(fo, "dp", axis=1, tiled=True)
        gains = lax.all_gather(norm_gains.astype(BF), "fsdp", axis=1, tiled=True).astype(F32)
        table = lax.all_gather(rel_table.astype(BF), "dp", axis=0, tiled=True).astype(F32)
        dist = jnp.dot(distance_hot(0), table, precision=lax.Precision.HIGHEST).T
        fwd = run(
            functools.partial(forward_kernel, False),
            ins | dict(sq=(sq, HBM), gains=gains, dist=dist), acts, scratch, "forward",
        )

    feed = run(
        feed_kernel,
        dict(a2=fwd.a2, h1=fwd.h1, c=upstream, gains=gains,
             w=(sq.reshape(8, width, width), pl.BlockSpec((1, width, width), lambda _: (7, 0, 0))),
             fi=fi.reshape(hidden, width), fo=fo.reshape(width, hidden)),
        dict(out=(small, BF), dfi=((hidden, width), BF), dfo=((4, 2, 2, PIECE, hidden), BF),
             dwoc=((width, width), BF), da2=(small, BF), dh2=(small, F32), gain=((1, width), F32)),
        dict(h2=VM(small, F32), n3=VM(small, BF), sum=VM(small, F32), back=VM(small, F32),
             ct=VM((width, rows), BF), g=VM(small, BF), du=VM(small, BF)),
        "feed",
    )

    ins = dict(k2=(fwd.k2, HBM), v2=(fwd.v2, HBM), q2=fwd.q2, da2=feed.da2,
               **index)
    turned = (examples, width, keys_n)
    outs = dict(dk2=(turned, BF, HBM), dv2=(turned, BF, HBM), dq2=(small, BF))
    scratch = dict(
        k2v=VM(encoder_out.shape, BF), v2v=VM(encoder_out.shape, BF),
        qe=VM((MOST, width), BF), dae=VM((MOST, width), BF), dqe=VM((MOST, width), BF),
        dk=VM((2, width, keys_n), BF), dv=VM((2, width, keys_n), BF),
        sum=VM(small, F32), esem=dma(examples, 2), dsem=dma(2, 2),
        **index_scratch,
    )
    fins = {}
    if comm:
        dfi = feed.dfi.reshape(4, 2, 2, 4, PIECE, width)
        ins |= dict(dfi=(dfi, HBM),
                    dfo=(feed.dfo, HBM))
        fins = dict(fin=((7, PIECE, WIDE), BF))
        scratch |= scatter_scratch(7, 7)
    mid = run(functools.partial(cross_back_kernel, comm), ins, outs | fins, scratch, "cross_back",
              collective=1 if comm else None)

    seven = (7,) + cut if comm else (7, width, width)
    ins = dict(dq2=mid.dq2, n2=fwd.n2, h1=fwd.h1, dh2=feed.dh2, x=decoder_in, n1=fwd.n1, q1=fwd.q1,
               k1=fwd.k1, v1=fwd.v1, a1=fwd.a1, gains=gains, dist=dist, gain3=feed.gain,
               sq=(sq, HBM), enc=(encoder_out, HBM), dk2=(mid.dk2, HBM), dv2=(mid.dv2, HBM), lengths=decoder_lengths)
    outs = dict(dx=(small, BF), small=((16, width), F32), denc=(encoder_out.shape, BF, HBM))
    scratch = dict(
        mask=VM((rows // MOST, MOST, 2 * MOST), F32), dh1=VM(small, F32), b1=VM(small, BF),
        da1=VM(small, BF), dq=VM(small, BF), dk=VM((width, rows), BF), dv=VM((width, rows), BF),
        dksum=VM((128, rows + MOST), F32), dvsum=VM((128, rows + MOST), F32), back=VM(small, F32),
        gain=VM((2, width), F32), distsum=VM((HEADS, 2 * MOST), F32), w=VM((5,) + cut, BF),
        one=VM((2, width, keys_n), BF), two=VM((2, keys_n, width), BF), three=VM((2, width, keys_n), BF),
        dwsum=VM((width, width), F32), denv=VM((2, keys_n, width), BF), wsem=dma(7), esem=dma(2, 2),
        dsem=dma(2),
    )
    if comm:
        ins |= dict(dfi=(dfi, HBM), dwoc=(feed.dwoc.reshape(cut), HBM), finf=mid.fin)
        outs |= dict(tsq=((8, 96, 192), BF), tfi=((384, 192), BF), tfo=((96, 768), BF), gains_own=((8, 128), F32),
                     table_own=((8, HEADS), F32))
        scratch |= dict(
            dw=VM(seven, BF), fin=VM((9, PIECE, WIDE), BF), all=VM((12, PIECE, WIDE), BF), give=VM((12, PIECE, 192), BF),
            take=VM((12, PIECE, 192), BF), giveo=VM((2, PIECE, WIDE), BF), takeo=VM((2, PIECE, WIDE), BF),
            given=VM((5, 16, width), F32), gotten=VM((5, 16, width), F32), smsem=dma(2, 5), xsem=dma(6),
        ) | scatter_scratch(9, 2)
    else:
        outs |= dict(dw=(seven, BF))
    last = run(functools.partial(self_back_kernel, comm), ins, outs, scratch, "self_back",
               collective=2 if comm else None)

    if comm:
        square = ((192, 96), F32)
        done = run(
            finish_kernel,
            dict(tsq=last.tsq, tfi=last.tfi, tfo=last.tfo, gains_in=last.gains_own, table_in=last.table_own,
                 dx_in=last.dx, denc_in=(last.denc, HBM)),
            {n: square for n in ("k_c", "v_c", "q_s", "k_s", "v_s", "o_s", "q_c", "o_c")}
            | dict(f_i=((192, 384), F32), f_o=((96, 768), F32), gains=((3, 96), F32), table=((8, HEADS), F32),
                   dx=(small, BF), denc=(encoder_out.shape, BF, HBM)),
            dict(sem=dma(examples, 2), hold=VM(encoder_out.shape, BF)), "finish",
        )
        grads = (done.q_s, done.k_s, done.v_s, done.o_s, done.q_c, done.k_c, done.v_c, done.o_c,
                 done.f_i, done.f_o.T)
        gains_delta, table_delta, dx, denc = done.gains, done.table, done.dx, done.denc
    else:
        def owned(t, rows_axis=0):
            t = lax.psum_scatter(t, "dp", scatter_dimension=1, tiled=True)
            return lax.psum_scatter(t, "fsdp", scatter_dimension=0, tiled=True).astype(F32).T

        dw = last.dw
        grads = tuple(owned(t) for t in (dw[2], dw[3], dw[4], dw[1], dw[0], dw[5], dw[6],
                                         feed.dwoc, feed.dfi, feed.dfo.reshape(width, hidden)))
        gains_delta = lax.psum(last.small[0:3], "dp")
        gains_delta = lax.psum_scatter(gains_delta, "fsdp", scatter_dimension=1, tiled=True)
        table_delta = last.small[3 : 3 + HEADS, 0:BUCKETS].T
        table_delta = lax.psum_scatter(table_delta, "dp", scatter_dimension=0, tiled=True)
        table_delta = lax.psum(table_delta, "fsdp")
        dx, denc = last.dx, last.denc
    return (feed.out, dx, denc, gains_delta, table_delta) + grads


def solution(mesh):
    tokens = P(("dp", "fsdp"), None)
    weight = P("dp", "fsdp")
    comm = (mesh.shape["dp"], mesh.shape["fsdp"]) == (4, 8)
    return jax.shard_map(
        functools.partial(body, comm),
        mesh=mesh,
        in_specs=(tokens, P(("dp", "fsdp"), None, None), tokens, P(("dp", "fsdp")), P(None, "fsdp"),
                  P("dp", None)) + (weight,) * 10 + (tokens,),
        out_specs=(tokens, tokens, P(("dp", "fsdp"), None, None), P(None, "fsdp"), P("dp", None))
        + (weight,) * 10,
        check_vma=False,
    )
```

```python
import functools
import math
import types

import jax
import jax.numpy as jnp
from jax import lax
from jax.experimental import pallas as pl
from jax.experimental.pallas import tpu as pltpu
from jax.sharding import PartitionSpec as P

HEADS = 12
HEAD_DIM = 64
BUCKETS = 32
MAX_DIST = 128
MOST = 128
PAIRS = HEADS // 2
EPSILON = 1e-06
HIDDEN_SCORE = -1e30
BF = jnp.bfloat16
F32 = jnp.float32
VMEM_LIMIT = 60 * 1024 * 1024


def nn(a, b):
    return lax.dot_general(a, b, (((1,), (0,)), ((), ())), preferred_element_type=F32)


def nt(a, b):
    return lax.dot_general(a, b, (((1,), (1,)), ((), ())), preferred_element_type=F32)


def tn(a, b):
    return lax.dot_general(a, b, (((0,), (0,)), ((), ())), preferred_element_type=F32)


def rms(z, gain):
    factor = lax.rsqrt(jnp.mean(z * z, axis=-1, keepdims=True) + EPSILON)
    return z * factor * gain


def rms_back(z, gain, dy):
    factor = lax.rsqrt(jnp.mean(z * z, axis=-1, keepdims=True) + EPSILON)
    wdy = dy * gain
    inner = jnp.mean(z * wdy, axis=-1, keepdims=True)
    dz = factor * wdy - z * (factor * factor * factor * inner)
    return dz, jnp.sum(dy * z * factor, axis=0, keepdims=True)


def split_heads(rows):
    first = lax.broadcasted_iota(jnp.int32, rows.shape, 1) < HEAD_DIM
    zero = jnp.zeros_like(rows)
    return jnp.concatenate([jnp.where(first, rows, zero), jnp.where(first, zero, rows)], axis=0)


def join_heads(rows):
    half = rows.shape[0] // 2
    first = lax.broadcasted_iota(jnp.int32, (half, rows.shape[1]), 1) < HEAD_DIM
    return jnp.where(first, rows[:half], rows[half:])


def softmax(scores):
    raised = jnp.exp(scores - jnp.max(scores, axis=-1, keepdims=True))
    return raised * (1.0 / jnp.sum(raised, axis=-1, keepdims=True))


def lanes(index, width):
    return pl.ds(pl.multiple_of(index * width, width), width)


def loop(low, high, step, unroll=1):
    def run(index, carry):
        step(index)
        return carry

    lax.fori_loop(low, high, run, 0, unroll=unroll)


def quiet(act):
    act()


def bucket_of(distance):
    half_count = BUCKETS // 2
    counted = jnp.zeros_like(distance)
    for section_index in range(1, half_count):
        edge_at = int(
            math.ceil(half_count * (MAX_DIST / half_count) ** (section_index / half_count))
        )
        counted = counted + (distance >= edge_at).astype(jnp.int32)
    return jnp.where(distance < half_count, distance, half_count + counted)


def distance_hot(axis):
    shape = (2 * MOST, BUCKETS) if axis == 0 else (BUCKETS, 2 * MOST)
    distance = jnp.maximum(MOST - lax.broadcasted_iota(jnp.int32, shape, axis), 0)
    return (bucket_of(distance) == lax.broadcasted_iota(jnp.int32, shape, 1 - axis)).astype(F32)


def segments(lengths, shape, axis, shift=0):
    places = lax.broadcasted_iota(jnp.int32, shape, axis) - shift
    end = jnp.zeros((1, 1), jnp.int32)
    example = jnp.where(places < 0, -1, 0)
    start = jnp.zeros(shape, jnp.int32)
    for e in range(lengths.shape[1]):
        length = lengths[:, e : e + 1]
        end = end + length
        example = example + (places >= end).astype(jnp.int32)
        start = start + jnp.where(places >= end, length, 0)
    return example, places - start


def local(src, dst, sem):
    return pltpu.make_async_copy(src, dst, sem)


def w_rows(ref, m, j):
    return ref[m, pl.ds(2 * j, 2)].reshape(2 * WIDE // 2, ref.shape[-1])


def w_lanes(ref, m, at):
    part = ref[m, :, :, :, :, at]
    return part.reshape(-1, part.shape[-1])


MESH = pl.DeviceIdType.MESH
PIECE = 48
WIDE = 384
UNITS = 16
ALL = slice(None)
LOW, HIGH = slice(0, 2), slice(2, 4)


class Place:
    def __init__(self):
        self.d, self.f = lax.axis_index("dp"), lax.axis_index("fsdp")
        self.y, self.c = self.d // 2, self.d % 2
        self.z, self.x = self.f // 2, self.f % 2
        self.nx, self.ny, self.nc = 1 - self.x, 1 - self.y, 1 - self.c

    def at(self, z=None, x=None, y=None, c=None):
        z = self.z if z is None else z
        x = self.x if x is None else x
        y = self.y if y is None else y
        c = self.c if c is None else c
        return (y * 2 + c, z * 2 + x)

    def near(self):
        others = [self.at(z=(self.z + k) % 4) for k in (1, 2, 3)]
        return others + [self.at(x=1 - self.x), self.at(y=1 - self.y), self.at(c=1 - self.c)]


def greet(peers, between=lambda: None):
    barrier = pltpu.get_barrier_semaphore()
    for dev in peers:
        pl.semaphore_signal(barrier, inc=1, device_id=dev, device_id_type=MESH)
    between()
    pl.semaphore_wait(barrier, len(peers))


def eye(n):
    a = lax.broadcasted_iota(jnp.int32, (n, n), 0)
    b = lax.broadcasted_iota(jnp.int32, (n, n), 1)
    return (a == b).astype(F32).astype(BF)


def remote(src, dst, send, recv, dev):
    return pltpu.make_async_remote_copy(
        src_ref=src, dst_ref=dst, send_sem=send, recv_sem=recv, device_id=dev, device_id_type=MESH
    )


class Sends:
    def __init__(self, place, ssem, rsem):
        self.p, self.ssem, self.rsem, self.made = place, ssem, rsem, {}

    def to_x(self):
        return self.p.at(x=1 - self.p.x)

    def to_y(self):
        return self.p.at(y=1 - self.p.y)

    def to_c(self):
        return self.p.at(c=1 - self.p.c)

    def go(self, u, slot, src, dst, dev):
        def make():
            return remote(src(), dst(), self.ssem.at[u, slot], self.rsem.at[u, slot], dev())

        make().start()
        self.made[u, slot] = make

    def wait(self, u, *slots):
        for slot in slots:
            self.made[u, slot]().wait_recv()

    def drain(self):
        for make in self.made.values():
            make().wait_send()


class Gather(Sends):
    def __init__(self, place, own, sq, fi, fo, ssem, rsem):
        super().__init__(place, ssem, rsem)
        self.own, self.sq, self.fi, self.fo = own, sq, fi, fo

    def piece(self, u, z, x, c, y):
        if u < 8:
            return self.sq.at[u, z, x, c, :, pl.ds(pl.multiple_of(y * WIDE, WIDE), WIDE)]
        if u < 12:
            return self.fi.at[z, x, c, u - 8, :, pl.ds(pl.multiple_of(y * WIDE, WIDE), WIDE)]
        at = y * (4 * WIDE) + (u - 12) * WIDE
        return self.fo.at[z, x, c, :, pl.ds(pl.multiple_of(at, WIDE), WIDE)]

    def same(self, u, slot, dev, z, x, c, y):
        def here():
            return self.piece(u, z, x, c, y)

        self.go(u, slot, here, here, dev)

    def first(self, u):
        p = self.p
        if u in (8, 9):
            self.go(
                u, 0, lambda: self.own.at[u], lambda: self.piece(u, p.z, p.x, p.c, p.y),
                self.to_x if u == 8 else self.to_y,
            )
            return
        for k in (1, 2, 3):
            self.go(
                u, k - 1, lambda: self.own.at[u], lambda: self.piece(u, p.z, p.x, p.c, p.y),
                lambda k=k: p.at(z=(p.z + k) % 4),
            )

    def second(self, u):
        p = self.p
        if u == 8:
            self.wait(u, 0)
            self.same(u, 3, self.to_y, p.z, ALL, p.c, p.y)
            return
        if u == 9:
            self.wait(u, 0)
            for y in (0, 1):
                self.same(u, 3 + y, self.to_x, p.z, p.x, p.c, y)
            return
        self.wait(u, 0, 1, 2)
        self.same(u, 3, self.to_x, LOW, p.x, p.c, p.y)
        self.same(u, 4, self.to_y, HIGH, p.x, p.c, p.y)

    def third(self, u):
        p = self.p
        if u in (8, 9):
            self.wait(u, *((3, 4) if u == 9 else (3,)))
            for k in (1, 2, 3):
                for y in (0, 1):
                    self.same(
                        u, 3 + 2 * k + y, lambda k=k: p.at(z=(p.z + k) % 4), p.z, ALL, p.c, y
                    )
            return
        self.wait(u, 3, 4)
        self.same(u, 5, self.to_y, LOW, ALL, p.c, p.y)
        for y in (0, 1):
            self.same(u, 6 + y, self.to_x, HIGH, p.x, p.c, y)
        self.same(u, 8, self.to_c, LOW, ALL, p.c, p.y)
        for y in (0, 1):
            self.same(u, 9 + y, self.to_c, HIGH, p.x, p.c, y)

    def fourth(self, u):
        p = self.p
        if u in (8, 9):
            self.wait(u, 5, 6, 7, 8, 9, 10)
            for y in (0, 1):
                self.same(u, 11 + y, self.to_c, ALL, ALL, p.c, y)
            return
        self.wait(u, 5, 6, 7)
        self.same(u, 11, self.to_c, LOW, ALL, p.c, p.ny)
        for y in (0, 1):
            self.same(u, 12 + y, self.to_c, HIGH, p.nx, p.c, y)

    def fifth(self, u):
        if u in (8, 9):
            self.wait(u, 11, 12)
            return
        self.wait(u, *range(8, 14))

    def begin(self):
        for act, u in ((self.second, 8), (self.second, 9), (self.second, 0), (self.second, 1), (self.third, 0),
                       (self.third, 1), (self.second, 2), (self.second, 3), (self.fourth, 0), (self.fourth, 1),
                       (self.second, 4)):
            act(u)

    def tick(self, t):
        if 2 <= t and t not in (8, 9):
            self.fourth(t)
        if t + 2 < UNITS and t + 2 not in (8, 9):
            self.third(t + 2)
        if t + 5 < UNITS and t + 5 not in (8, 9):
            self.second(t + 5)
        if t == 5:
            self.third(8)
            self.third(9)
        if t == UNITS - 1:
            self.fourth(8)
            self.fourth(9)


class Scatter(Sends):
    def __init__(self, place, parts, staged, r):
        super().__init__(place, r.ssem, r.rsem)
        self.parts, self.staged, self.r = parts, staged, r

    def halves(self, u):
        p, r = self.p, self.r
        return [local(self.parts(u, p.c, y), r.stage.at[u, y], r.lsem.at[u, y]) for y in (0, 1)]

    def own(self, u, y):
        if u < self.staged:
            return self.r.stage[u, pl.ds(y, 1)]
        return self.parts(u, self.p.c, y)[...][None]

    def r0(self, u):
        p, r = self.p, self.r
        for y in (0, 1):
            self.go(
                u, y, lambda y=y: self.parts(u, p.nc, y), lambda y=y: r.land.at[u, y], self.to_c
            )
        if u < self.staged:
            for copy in self.halves(u):
                copy.start()

    def r1(self, u):
        p, r = self.p, self.r
        self.wait(u, 0, 1)
        if u < self.staged:
            for copy in self.halves(u):
                copy.wait()
        for y in (p.ny, p.y):
            at = pl.ds(y, 1)
            r.land[u, at] = r.land[u, at] + self.own(u, y)
            if y is p.ny:
                self.go(
                    u, 2, lambda: r.land.at[u, p.ny, LOW], lambda: r.land1.at[u, LOW], self.to_y
                )
        for y in (0, 1):
            self.go(
                u, 3 + y, lambda y=y: r.land.at[u, y, HIGH, p.nx], lambda y=y: r.land1.at[u, HIGH, y],
                self.to_x,
            )

    def r2(self, u):
        p, r = self.p, self.r
        self.wait(u, 2, 3, 4)
        own, x = pl.ds(p.y, 1), pl.ds(p.x, 1)
        r.land[u, own, LOW] = r.land[u, own, LOW] + r.land1[u, LOW][None]
        for y in (0, 1):
            r.land[u, y, HIGH, x] = r.land[u, y, HIGH, x] + r.land1[u, HIGH, y][:, None]
        self.go(u, 5, lambda: r.land.at[u, p.y, LOW, p.nx], lambda: r.land2.at[u, LOW], self.to_x)
        self.go(u, 6, lambda: r.land.at[u, p.ny, HIGH, p.x], lambda: r.land2.at[u, HIGH], self.to_y)

    def r3(self, u):
        p, r = self.p, self.r
        self.wait(u, 5, 6)
        y, x = pl.ds(p.y, 1), pl.ds(p.x, 1)
        r.land[u, y, :, x] = r.land[u, y, :, x] + r.land2[u][None, :, None]
        for k in (1, 2, 3):
            self.go(
                u, 6 + k, lambda k=k: r.land.at[u, p.y, (p.z + k) % 4, p.x],
                lambda k=k: r.land3.at[u, k - 1], lambda k=k: p.at(z=(p.z + k) % 4),
            )

    def r4(self, u):
        p, r = self.p, self.r
        self.wait(u, 7, 8, 9)
        part = r.land[u, pl.ds(p.y, 1), pl.ds(p.z, 1), pl.ds(p.x, 1)]
        total = part.reshape(PIECE, WIDE).astype(F32)
        for k in range(3):
            total = total + r.land3[u, k].astype(F32)
        r.fin[u] = total.astype(BF)

    def step(self, number, *units):
        act = (self.r0, self.r1, self.r2, self.r3, self.r4)[number]
        for u in units:
            act(u)


def scatter_scratch(count, staged):
    return dict(
        land=pltpu.VMEM((count, 2, 4, 2, PIECE, WIDE), BF),
        stage=pltpu.VMEM((staged, 2, 4, 2, PIECE, WIDE), BF),
        land1=pltpu.VMEM((count, 4, 2, PIECE, WIDE), BF),
        land2=pltpu.VMEM((count, 4, PIECE, WIDE), BF),
        land3=pltpu.VMEM((count, 3, PIECE, WIDE), BF),
        ssem=pltpu.SemaphoreType.DMA((count, 10)),
        rsem=pltpu.SemaphoreType.DMA((count, 10)),
        lsem=pltpu.SemaphoreType.DMA((staged, 2)),
    )


def self_masks(lengths, mask_ref):
    blocks = mask_ref.shape[0]
    seg_col = segments(lengths, (blocks * MOST, 1), 0)[0]
    seg_row = segments(lengths, (1, (blocks + 1) * MOST), 1, MOST)[0]
    a = lax.broadcasted_iota(jnp.int32, (MOST, 2 * MOST), 0)
    b = lax.broadcasted_iota(jnp.int32, (MOST, 2 * MOST), 1)
    causal = b <= a + MOST
    for i in range(blocks):
        same = seg_col[MOST * i : MOST * (i + 1), :] == seg_row[:, MOST * i : MOST * (i + 2)]
        mask_ref[i] = jnp.where(causal & same, 0.0, HIDDEN_SCORE)


def pair_bias(dist_ref, pair):
    parts = []
    for h in range(2):
        row = dist_ref[pl.ds(2 * pair + h, 1), :]
        parts.append(
            pltpu.roll(jnp.broadcast_to(row, (MOST, 2 * MOST)), 0, 1, stride=1, stride_axis=0)
        )
    return jnp.concatenate(parts, axis=0)


def masked_scores(scores, bias, mask):
    both = scores + bias
    return (both.reshape(2, MOST, 2 * MOST) + mask[None]).reshape(2 * MOST, 2 * MOST)


def example_rows(index_ref, example, total):
    place = lax.broadcasted_iota(jnp.int32, (MOST, total), 0)
    here = (index_ref[0:1, :] == example) & (index_ref[1:2, :] == place)
    return here.astype(F32).astype(BF)


def example_index(r, total):
    r.index[0:1, :], r.index[1:2, :] = segments(r.lengths[...], (1, total), 1)
    examples, keys_n = r.hidden.shape
    place = lax.broadcasted_iota(jnp.int32, (1, keys_n), 1)
    for e in range(examples):
        r.hidden[e : e + 1, :] = jnp.where(place < r.valid[:, e : e + 1], 0.0, HIDDEN_SCORE)


def turn_squares(r, *which):
    shards = (r.k_c, r.v_c, r.q_s, r.k_s, r.v_s, r.o_s, r.q_c, r.o_c)
    e96 = eye(96)
    for m in which:
        r.xt[m] = nt(e96, shards[m][...].astype(BF)).astype(BF).reshape(2, PIECE, 192)


def turn_feeds(r):
    t = nt(eye(384), r.f_i[...].astype(BF)).astype(BF).reshape(2, 4, PIECE, 192)
    for s in range(4):
        for h in range(2):
            r.xt[8 + s, h] = t[h, s]
    r.xf[...] = r.f_o[...].astype(BF).reshape(2, PIECE, 768)


def own_parts(p, r, low, high):
    first = p.c == 0
    mine = r.xt[low:high, pl.ds(p.c, 1)].reshape(high - low, PIECE, 192)
    other = r.took[low:high]
    r.own[low:high] = jnp.concatenate(
        [jnp.where(first, mine, other), jnp.where(first, other, mine)], axis=-1
    )


def small_sends(p, r):
    made = []
    for k in range(1, 8):
        dev = (p.d, (p.f + k) % 8)
        made.append(
            remote(r.gt.at[p.f], r.gt.at[p.f], r.smsem.at[0, k - 1], r.smsem.at[1, k - 1], dev)
        )
    for k in range(1, 4):
        dev = ((p.d + k) % 4, p.f)
        made.append(
            remote(r.tt.at[p.d], r.tt.at[p.d], r.smsem.at[0, 6 + k], r.smsem.at[1, 6 + k], dev)
        )
    return made


def forward_kernel(comm, r):
    rows, width = r.x.shape
    examples, keys_n = r.enc.shape[0], r.enc.shape[1]
    blocks = rows // MOST
    enc_copies = [local(r.enc.at[e], r.encv.at[e], r.esem.at[e]) for e in range(examples)]
    for copy in enc_copies:
        copy.start()
    if comm:
        p = Place()
        peers = [(p.d, (p.f + k) % 8) for k in range(1, 8)] + [((p.d + k) % 4, p.f) for k in range(1, 4)]

        def prepare():
            r.gt[pl.ds(p.f, 1)] = jnp.zeros((1, 8, 128), F32)
            r.gt[pl.ds(p.f, 1), 0:3, 0:96] = r.gains_s[...].astype(BF).astype(F32)[None]
            r.tt[pl.ds(p.d, 1)] = jnp.zeros((1, 8, 128), F32)
            r.tt[pl.ds(p.d, 1), :, 0:HEADS] = r.table_s[...].astype(BF).astype(F32)[None]
            turn_squares(r, 0, 1)

        greet(peers, prepare)
        sib = p.at(c=1 - p.c)
        trade = [
            remote(r.xt.at[0:2, 1 - p.c], r.took.at[0:2], r.xsem.at[0], r.xsem.at[1], sib),
            remote(r.xt.at[2:12, 1 - p.c], r.took.at[2:12], r.xsem.at[2], r.xsem.at[3], sib),
            remote(r.xf.at[1 - p.c], r.tookf, r.xsem.at[4], r.xsem.at[5], sib),
        ]
        small = small_sends(p, r)
        for copy in trade[0:1] + small:
            copy.start()
        turn_feeds(r)
        g = Gather(p, r.own, r.sq, r.fi, r.fo, r.ssem, r.rsem)
        placed = [
            local(r.own.at[u], g.piece(u, p.z, p.x, p.c, p.y), r.psem.at[u]) for u in range(UNITS)
        ]
        trade[0].wait_recv()
        own_parts(p, r, 0, 2)
        for u in (0, 1):
            g.first(u)
            placed[u].start()
        turn_squares(r, 2, 3, 4, 5, 6, 7)
        for copy in trade[1:]:
            copy.start()
        first = p.c == 0
        trade[1].wait_recv()
        own_parts(p, r, 2, 12)
        trade[2].wait_recv()
        mine, other = r.xf[pl.ds(p.c, 1)].reshape(PIECE, 768), r.tookf[...]
        low, high = jnp.where(first, mine, other), jnp.where(first, other, mine)
        r.own[12], r.own[13] = low[:, :WIDE], low[:, WIDE:]
        r.own[14], r.own[15] = high[:, :WIDE], high[:, WIDE:]
        for u in (8, 9, 2, 3, 4, 5, 6, 7, 10, 11, 12, 13, 14, 15):
            g.first(u)
            placed[u].start()
        for copy in small:
            copy.wait_recv()
        spot = lax.broadcasted_iota(jnp.int32, (128, width), 1)
        lane = lax.broadcasted_iota(jnp.int32, (128, width), 0)
        gains = jnp.zeros((8, width), F32)
        for f in range(8):
            put = ((spot == lane + 96 * f) & (lane < 96)).astype(F32).astype(BF)
            gains = gains + nn(r.gt[f].astype(BF), put)
        r.gains[...] = gains[0:3]
        table = r.tt[...].reshape(BUCKETS, 128).astype(BF)
        r.dist[...] = tn(table, distance_hot(1).astype(BF))[0:HEADS]
        for copy in placed:
            copy.wait()
        begin, tick, arrived = g.begin, g.tick, g.fifth
    else:
        begin, tick, arrived = (lambda *_: None,) * 3

    loads = [local(r.sq.at[m], r.wv.at[m], r.wsem.at[m]) for m in range(7)]

    def fetch(*which):
        for m in which:
            arrived(m)
            loads[m].start()

    def have(*which):
        for m in which:
            loads[m].wait()

    example_index(r, rows)
    r.n1[...] = rms(r.x[...].astype(F32), r.gains[0:1, :]).astype(BF)
    r.k1[0:MOST, :] = jnp.zeros((MOST, width), BF)
    r.v1[0:MOST, :] = jnp.zeros((MOST, width), BF)
    self_masks(r.lengths[...], r.mask)
    halves = width // WIDE

    def save(e):
        return [local(r.k2v.at[e], r.k2.at[e], r.ksem.at[e, 0]), local(r.v2v.at[e], r.v2.at[e], r.ksem.at[e, 1])]

    def project(e):
        local(r.enc.at[e], r.encv.at[e], r.esem.at[e]).wait()
        for j in range(halves):
            at = slice(WIDE * j, WIDE * (j + 1))
            r.k2v[e, :, at] = nt(r.encv[e], w_rows(r.wv, 0, j)).astype(BF)
            r.v2v[e, :, at] = nt(r.encv[e], w_rows(r.wv, 1, j)).astype(BF)
        for copy in save(e):
            copy.start()

    begin()
    fetch(0, 1)
    have(0, 1)
    for t in range(4):
        tick(t)
        loop(2 * t, 2 * t + 2, project)
    fetch(2, 3)
    tick(4)
    fetch(4)
    have(2, 3, 4)

    for j in range(halves):
        at = slice(WIDE * j, WIDE * (j + 1))
        r.q1[:, at] = nt(r.n1[...], w_rows(r.wv, 2, j)).astype(BF)
        r.k1[MOST:, at] = nt(r.n1[...], w_rows(r.wv, 3, j)).astype(BF)
        r.v1[MOST:, at] = nt(r.n1[...], w_rows(r.wv, 4, j)).astype(BF)

    def attend(pair):
        at = lanes(pair, 128)
        bias = pair_bias(r.dist, pair)
        for i in range(blocks):
            queries = split_heads(r.q1[MOST * i : MOST * (i + 1), at])
            keys = r.k1[MOST * i : MOST * (i + 2), at]
            values = r.v1[MOST * i : MOST * (i + 2), at]
            probs = softmax(masked_scores(nt(queries, keys), bias, r.mask[i])).astype(BF)
            r.a1[MOST * i : MOST * (i + 1), at] = join_heads(nn(probs, values)).astype(BF)

    tick(5)
    loop(0, PAIRS // 2, attend, PAIRS // 2)
    tick(6)
    fetch(5)
    loop(PAIRS // 2, PAIRS, attend, PAIRS // 2)
    tick(7)
    fetch(6)
    have(5, 6)
    for j in range(halves):
        at = slice(WIDE * j, WIDE * (j + 1))
        r.h1[:, at] = r.x[:, at].astype(F32) + nt(r.a1[...], w_rows(r.wv, 5, j))
    r.n2[...] = rms(r.h1[...], r.gains[1:2, :]).astype(BF)
    for j in range(halves):
        at = slice(WIDE * j, WIDE * (j + 1))
        r.q2[:, at] = nt(r.n2[...], w_rows(r.wv, 6, j)).astype(BF)

    r.sum[...] = jnp.zeros_like(r.sum)

    def cross(e):
        pick = example_rows(r.index, e, rows)
        r.qe[...] = nn(pick, r.q2[...]).astype(BF)
        hidden = r.hidden[pl.ds(e, 1), :]

        def pair_step(pair):
            at = lanes(pair, 128)
            probs = softmax(nt(split_heads(r.qe[:, at]), r.k2v[e, :, at]) + hidden).astype(BF)
            r.ae[:, at] = join_heads(nn(probs, r.v2v[e, :, at])).astype(BF)

        loop(0, PAIRS, pair_step, PAIRS)
        r.sum[...] += tn(pick, r.ae[...])

    def cross_tick(e):
        if comm:
            for t in range(examples):
                pl.when(e == t)(functools.partial(tick, t + 8))
        cross(e)

    loop(0, examples, cross_tick)
    r.a2[...] = r.sum[...].astype(BF)

    def saved(e):
        for copy in save(e):
            copy.wait()

    loop(0, examples, saved)
    if comm:
        for u in range(7, UNITS):
            g.fifth(u)
        g.drain()
        for copy in trade + small:
            copy.wait_send()


GELU_A = math.sqrt(2.0 / math.pi)
GELU_B = 0.044715


def feed_kernel(r):
    rows, width = r.a2.shape
    hidden = r.fi.shape[0]
    def cross_out(j):
        at = lanes(j, 256)
        r.h2[:, at] = r.h1[:, at] + nt(r.a2[...], r.w[0, at, :])

    loop(0, width // 256, cross_out, 3)
    r.n3[...] = rms(r.h2[...], r.gains[2:3, :]).astype(BF)
    r.sum[...] = r.h2[...]
    r.back[...] = jnp.zeros_like(r.back)

    r.ct[...] = r.c[...].T

    def part(j):
        for i in range(3):
            at = pl.ds(pl.multiple_of(j * width + i * 256, 256), 256)
            here = slice(256 * i, 256 * (i + 1))
            u = nt(r.n3[...], r.fi[at, :])
            t = jnp.tanh(GELU_A * (u + GELU_B * (u * u * u)))
            r.g[:, here] = (0.5 * u * (1.0 + t)).astype(BF)
            slope = 0.5 * (1.0 + t) + 0.5 * u * (1.0 - t * t) * (
                GELU_A * (1.0 + (3.0 * GELU_B) * (u * u))
            )
            r.du[:, here] = (nn(r.c[...], r.fo[:, at]) * slope).astype(BF)
        whole_part = lanes(j, width)
        for i in range(3):
            at = pl.ds(pl.multiple_of(j * width + i * 256, 256), 256)
            here = slice(256 * i, 256 * (i + 1))
            r.dfo[:, :, :, :, at] = nn(r.ct[...], r.g[:, here]).astype(BF).reshape(4, 2, 2, PIECE, 256)
            r.dfi[at, :] = tn(r.du[:, here], r.n3[...]).astype(BF)
            r.sum[:, here] += nt(r.g[...], r.fo[here, whole_part])
            r.back[:, here] += nn(r.du[...], r.fi[whole_part, here])

    loop(0, hidden // width, part, 1)
    r.out[...] = r.sum[...].astype(BF)
    dz, dw = rms_back(r.h2[...], r.gains[2:3, :], r.back[...])
    r.gain[...] = dw
    r.dh2[...] = r.c[...].astype(F32) + dz

    def tail(j):
        at = lanes(j, 256)
        r.da2[:, at] = nn(r.dh2[...].astype(BF), r.w[0, :, at]).astype(BF)
        r.dwoc[at, :] = tn(r.dh2[:, at].astype(BF), r.a2[...]).astype(BF)

    loop(0, width // 256, tail, 3)


STARTS = (0, 0, 1, 3, 4, 6, 7)
LAGS = (0, 1, 4, 6, 8)


def cross_back_kernel(comm, r):
    rows, width = r.q2.shape
    examples, keys_n = r.k2.shape[0], r.k2.shape[1]

    def fetches(e):
        return [local(getattr(r, a).at[e], getattr(r, b).at[e], r.esem.at[e, i])
                for i, (a, b) in enumerate((("k2", "k2v"), ("v2", "v2v")))]

    for e in range(examples):
        for copy in fetches(e):
            copy.start()
    if comm:
        p = Place()

        def parts(u, c, y):
            if u >= 4:
                return r.dfi.at[:, :, c, u - 4, :, y * WIDE : (y + 1) * WIDE]
            at = y * 4 * WIDE + u * WIDE
            return r.dfo.at[:, :, c, :, at : at + WIDE]

        s = Scatter(p, parts, 7, r)
        greet(p.near())
    example_index(r, rows)
    r.sum[...] = jnp.zeros_like(r.sum)

    def out_copies(e):
        return [
            local(r.dk.at[e % 2], r.dk2.at[e], r.dsem.at[e % 2, 0]),
            local(r.dv.at[e % 2], r.dv2.at[e], r.dsem.at[e % 2, 1]),
        ]

    def tick(at):
        if comm:
            for t in range(2 * examples):

                @pl.when(at == t)
                def _():
                    for number in (4, 3, 2, 1, 0):
                        for u, at_first in enumerate(STARTS):
                            if at_first + LAGS[number] == t:
                                s.step(number, u)

    def example(e):
        tick(2 * e)
        for copy in fetches(e):
            copy.wait()
        pick = example_rows(r.index, e, rows)
        r.qe[...] = nn(pick, r.q2[...]).astype(BF)
        r.dae[...] = nn(pick, r.da2[...]).astype(BF)
        hidden = r.hidden[pl.ds(e, 1), :]

        @pl.when(e >= 2)
        def _():
            for copy in out_copies(e - 2):
                copy.wait()

        def attend(pair):
            at = lanes(pair, 128)
            queries = split_heads(r.qe[:, at])
            deltas = split_heads(r.dae[:, at])
            keys = r.k2v[e, :, at]
            probs = softmax(nt(queries, keys) + hidden)
            dprobs = nt(deltas, r.v2v[e, :, at])
            low = (probs * (dprobs - jnp.sum(dprobs * probs, axis=-1, keepdims=True))).astype(BF)
            r.dv[e % 2, at, :] = tn(deltas, probs.astype(BF)).astype(BF)
            r.dk[e % 2, at, :] = tn(queries, low).astype(BF)
            r.dqe[:, at] = join_heads(nn(low, keys)).astype(BF)

        loop(0, PAIRS, attend, PAIRS)
        tick(2 * e + 1)
        for copy in out_copies(e):
            copy.start()
        r.sum[...] += tn(pick, r.dqe[...])

    loop(0, examples, example)
    r.dq2[...] = r.sum[...].astype(BF)
    for e in (examples - 2, examples - 1):
        for copy in out_copies(e):
            copy.wait()
    if comm:
        s.drain()


def self_back_kernel(comm, r):
    rows, width = r.x.shape
    blocks = rows // MOST
    thirds = width // 256
    if comm:
        p = Place()

        def parts(u, c, y):
            at = pl.ds(pl.multiple_of(y * WIDE, WIDE), WIDE)
            if u == 0:
                return r.dfi.at[:, :, c, 3, :, at]
            if u == 1:
                return r.dwoc.at[:, :, c, :, at]
            return r.dw.at[u - 2, :, :, c, :, at]

        s = Scatter(p, parts, 2, r)
        greet(p.near())
        step = s.step
    else:
        step = lambda *units: None

    def put(m, j, value):
        if comm:
            r.dw[m, 2 * j : 2 * j + 2] = value.astype(BF).reshape(2, 2, 2, PIECE, width)
        else:
            r.dw[m, WIDE * j : WIDE * (j + 1), :] = value.astype(BF)

    halves = width // WIDE
    examples = r.denc.shape[0]
    loads = [local(r.sq.at[2 + m], r.w.at[m], r.wsem.at[m]) for m in range(5)]
    late = [local(r.sq.at[m], r.w.at[3 + m], r.wsem.at[5 + m]) for m in range(2)]
    for copy in loads:
        copy.start()

    passes = ((r.dk2, r.enc), (r.dv2, r.enc), (r.dk2, r.dv2))

    def fetches(number, e):
        places = (r.one, r.three if number == 2 else r.two)
        return [local(passes[number][i].at[e], places[i].at[e % 2], r.esem.at[e % 2, i]) for i in (0, 1)]

    def pass_step(number, e, act):
        for copy in fetches(number, e):
            copy.wait()
        act(e)

        @pl.when(e + 2 < examples)
        def _():
            for copy in fetches(number, e + 2):
                copy.start()

        if number < 2:

            @pl.when(e + 2 >= examples)
            def _():
                for copy in fetches(number + 1, e + 2 - examples):
                    copy.start()

    def out_copy(e):
        return local(r.denv.at[e % 2], r.denc.at[e], r.dsem.at[e % 2])

    for e in (0, 1):
        for copy in fetches(0, e):
            copy.start()
    step(0, 0, 1)
    for j in range(halves):
        at = slice(WIDE * j, WIDE * (j + 1))
        put(0, j, tn(r.dq2[:, at], r.n2[...]))
    step(0, 2)
    for copy in loads:
        copy.wait()

    def query(j):
        at = lanes(j, 256)
        r.back[:, at] = nn(r.dq2[...], w_lanes(r.w, 4, at))

    loop(0, thirds, query, thirds)
    step(1, 0, 1)
    dz, dw = rms_back(r.h1[...], r.gains[1:2, :], r.back[...])
    r.gain[1:2, :] = dw
    r.dh1[...] = r.dh2[...] + dz
    r.b1[...] = r.dh1[...].astype(BF)
    for j in range(halves):
        at = slice(WIDE * j, WIDE * (j + 1))
        put(1, j, tn(r.b1[:, at], r.a1[...]))
    step(0, 3)

    def out(j):
        at = lanes(j, 256)
        r.da1[:, at] = nn(r.b1[...], w_lanes(r.w, 3, at)).astype(BF)

    loop(0, thirds, out, thirds)
    for copy in late:
        copy.start()
    if comm:
        pairs = [p.at(c=1 - p.c), p.at(y=1 - p.y), p.at(x=1 - p.x),
                 p.at(z=p.z + 1 - 2 * (p.z % 2)), p.at(z=(p.z + 2) % 4)]

        def share(i):
            return remote(r.given.at[i], r.gotten.at[i], r.smsem.at[0, i], r.smsem.at[1, i], pairs[i])

        def share_go(i):
            r.given[i] = r.small[...]
            share(i).start()

        def share_end(i):
            share(i).wait_recv()
            r.small[...] = r.small[...] + r.gotten[i]

        def share_next(i):
            share_end(i)
            share_go(i + 1)

    def passing(number, act, events):
        def one(e):
            pass_step(number, e, act)
            if comm:
                for at, happens in events.items():
                    pl.when(e == at)(functools.partial(quiet, happens))

        loop(0, examples, one)

    def weight_sum(e):
        def dense(j):
            at = lanes(j, 256)
            r.dwsum[at, :] = nn(r.one[e % 2, at, :], r.two[e % 2]) + jnp.where(e == 0, 0.0, r.dwsum[at, :])

        loop(0, thirds, dense, thirds)

    events = (
        {1: lambda: step(1, 2), 2: lambda: step(1, 3), 4: lambda: step(2, 0, 1), 6: lambda: step(2, 2),
         7: lambda: step(2, 3)},
        {0: lambda: share_next(0), 1: lambda: step(2, 4), 3: lambda: step(2, 5), 4: lambda: share_next(1),
         5: lambda: step(2, 6), 6: lambda: step(3, 4), 7: lambda: (step(3, 5), share_next(2))},
        {0: lambda: step(3, 6), 1: lambda: (step(1, 8), step(4, 4)), 2: lambda: step(4, 5),
         3: lambda: share_next(3), 4: lambda: step(4, 6), 5: lambda: step(2, 8), 6: lambda: share_end(4)},
    )

    passing(0, weight_sum, events[0])
    for j in range(halves):
        put(5, j, r.dwsum[WIDE * j : WIDE * (j + 1), :])
    step(0, 7)
    self_masks(r.lengths[...], r.mask)
    a = lax.broadcasted_iota(jnp.int32, (MOST, MOST), 0)
    b = lax.broadcasted_iota(jnp.int32, (MOST, MOST), 1)
    flip = (a + b == MOST - 1).astype(F32)

    def attend(pair):
        at = lanes(pair, 128)
        bias = pair_bias(r.dist, pair)
        r.dksum[...] = jnp.zeros_like(r.dksum)
        r.dvsum[...] = jnp.zeros_like(r.dvsum)
        skewed = jnp.zeros((2 * MOST, 2 * MOST), F32)
        for i in range(blocks):
            own = slice(MOST * i, MOST * (i + 1))
            band = slice(MOST * i, MOST * (i + 2))
            queries = split_heads(r.q1[own, at])
            deltas = split_heads(r.da1[own, at])
            keys = r.k1[band, at]
            probs = softmax(masked_scores(nt(queries, keys), bias, r.mask[i]))
            dprobs = nt(deltas, r.v1[band, at])
            dscores = probs * (dprobs - jnp.sum(dprobs * probs, axis=-1, keepdims=True))
            low = dscores.astype(BF)
            skewed = skewed + dscores
            r.dvsum[:, band] += tn(deltas, probs.astype(BF))
            r.dksum[:, band] += tn(queries, low)
            r.dq[own, at] = join_heads(nn(low, keys)).astype(BF)
        r.dk[at, :] = r.dksum[:, MOST:].astype(BF)
        r.dv[at, :] = r.dvsum[:, MOST:].astype(BF)
        for h in range(2):
            flipped = jnp.dot(
                flip,
                skewed[MOST * h : MOST * (h + 1)],
                precision=lax.Precision.HIGHEST,
                preferred_element_type=F32,
            )
            straight = pltpu.roll(flipped, MOST + 1, 1, stride=1, stride_axis=0)
            r.distsum[pl.ds(2 * pair + h, 1), :] = jnp.sum(straight, axis=0, keepdims=True)

    plan = {
        0: ((3, 0, 1),),
        1: ((1, 7), (3, 2)),
        2: ((3, 3), (4, 0, 1)),
        3: ((2, 7), (4, 2)),
        4: ((4, 3),),
        5: ((3, 7),),
    }

    def attend_tick(pair):
        if comm:
            for t, steps in plan.items():

                @pl.when(pair == t)
                def _():
                    for numbers in steps:
                        step(*numbers)

        attend(pair)

    loop(0, PAIRS, attend_tick)
    for m, ref in ((2, r.dq), (3, r.dk), (4, r.dv)):
        for j in range(halves):
            at = slice(WIDE * j, WIDE * (j + 1))
            put(m, j, tn(ref[:, at], r.n1[...]) if m == 2 else nn(ref[at, :], r.n1[...]))
        step(0, 2 + m)
    step(4, 7)
    step(1, 4, 5)

    r.b1[...] = r.dk[...].T
    r.da1[...] = r.dv[...].T

    def qkv(j):
        at = lanes(j, 256)
        r.back[:, at] = (
            nn(r.dq[...], w_lanes(r.w, 0, at))
            + nn(r.b1[...], w_lanes(r.w, 1, at))
            + nn(r.da1[...], w_lanes(r.w, 2, at))
        )

    loop(0, thirds, qkv, thirds)
    step(1, 6)
    dz, dw = rms_back(r.x[...].astype(F32), r.gains[0:1, :], r.back[...])
    r.gain[0:1, :] = dw
    r.dx[...] = (r.dh1[...] + dz).astype(BF)
    by_bucket = jnp.dot(
        r.distsum[...], distance_hot(0), precision=lax.Precision.HIGHEST, preferred_element_type=F32
    )
    r.small[...] = jnp.zeros_like(r.small)
    r.small[0:2, :] = r.gain[0:2, :]
    r.small[2:3, :] = r.gain3[...]
    r.small[3 : 3 + HEADS, 0:BUCKETS] = by_bucket

    if comm:
        share_go(0)

    passing(1, weight_sum, events[1])
    for j in range(halves):
        put(6, j, r.dwsum[WIDE * j : WIDE * (j + 1), :])
    step(0, 8)
    for copy in late:
        copy.wait()

    def encoder(e):
        @pl.when(e >= 2)
        def _():
            out_copy(e - 2).wait()

        r.b1[...] = r.one[e % 2].T
        r.da1[...] = r.three[e % 2].T

        def dense(j):
            at = lanes(j, 256)
            r.denv[e % 2, :, at] = (
                nn(r.b1[...], w_lanes(r.w, 3, at)) + nn(r.da1[...], w_lanes(r.w, 4, at))
            ).astype(BF)

        loop(0, thirds, dense, thirds)
        out_copy(e).start()

    passing(2, encoder, events[2])
    step(3, 8)
    for e in (examples - 2, examples - 1):
        out_copy(e).wait()
    if not comm:
        return

    first = p.c == 0

    def split(low, high):
        left, right = r.all[low:high, :, :192], r.all[low:high, :, 192:]
        r.give[low:high] = jnp.where(first, right, left)
        return jnp.where(first, left, right)

    def both(a, b, axis):
        return jnp.concatenate([jnp.where(first, a, b), jnp.where(first, b, a)], axis=axis)

    r.all[0:7] = r.fin[1:8]
    r.all[7:10] = r.finf[4:7]
    r.all[10] = r.fin[0]
    keep = split(0, 11)
    r.giveo[...] = r.finf[pl.ds(2 * p.nc, 2)]
    sib = p.at(c=1 - p.c)
    trade = [
        remote(r.give.at[0:11], r.take.at[0:11], r.xsem.at[0], r.xsem.at[1], sib),
        remote(r.giveo, r.takeo, r.xsem.at[2], r.xsem.at[3], sib),
        remote(r.give.at[11:12], r.take.at[11:12], r.xsem.at[4], r.xsem.at[5], sib),
    ]
    for copy in trade[0:2]:
        copy.start()
    spot = lax.broadcasted_iota(jnp.int32, (width, 128), 0)
    lane = lax.broadcasted_iota(jnp.int32, (width, 128), 1)
    put_gains = ((spot == lane + 96 * p.f) & (lane < 96)).astype(F32)
    r.gains_own[...] = jnp.dot(
        r.small[0:8, :], put_gains, precision=lax.Precision.HIGHEST, preferred_element_type=F32
    )
    spot = lax.broadcasted_iota(jnp.int32, (8, BUCKETS), 1)
    line = lax.broadcasted_iota(jnp.int32, (8, BUCKETS), 0)
    r.table_own[...] = lax.dot_general(
        (spot == line + 8 * p.d).astype(F32), r.small[3 : 3 + HEADS, 0:BUCKETS], (((1,), (1,)), ((), ())),
        precision=lax.Precision.HIGHEST, preferred_element_type=F32,
    )
    for copy in trade[0:2]:
        copy.wait_recv()
    r.tsq[0:7] = both(keep[0:7], r.take[0:7], 1)
    r.tfi[...] = both(keep[7:11].reshape(192, 192), r.take[7:11].reshape(192, 192), 0)
    own = r.finf[pl.ds(2 * p.c, 2)]
    r.tfo[...] = both(
        jnp.concatenate([own[0], own[1]], axis=1), jnp.concatenate([r.takeo[0], r.takeo[1]], axis=1), 0
    )
    step(4, 8)
    r.all[11] = r.fin[8]
    keep = split(11, 12)
    trade[2].start()
    trade[2].wait_recv()
    r.tsq[7:8] = both(keep, r.take[11:12], 1)
    s.drain()
    for i in range(5):
        share(i).wait_send()
    for copy in trade:
        copy.wait_send()


def finish_kernel(r):
    examples = r.denc.shape[0]
    ins = [local(r.denc_in.at[e], r.hold.at[e], r.sem.at[e, 0]) for e in range(examples)]
    outs = [local(r.hold.at[e], r.denc.at[e], r.sem.at[e, 1]) for e in range(examples)]
    for copy in ins:
        copy.start()
    r.dx[...] = r.dx_in[...]
    e192 = eye(192)
    for m, ref in enumerate((r.o_c, r.q_c, r.o_s, r.q_s, r.k_s, r.v_s, r.k_c, r.v_c)):
        ins[m].wait()
        outs[m].start()
        ref[...] = nt(e192, r.tsq[m])
    r.f_i[...] = nt(e192, r.tfi[...])
    r.f_o[...] = r.tfo[...].astype(F32)
    r.gains[...] = r.gains_in[0:3, 0:96]
    r.table[...] = r.table_in[...]
    for copy in outs:
        copy.wait()


VM = pltpu.VMEM
HBM = pl.ANY


def run(kernel, ins, outs, scratch, name, collective=None, flops=0):
    names = list(ins) + list(outs) + list(scratch)

    def wrapped(*refs):
        kernel(types.SimpleNamespace(**dict(zip(names, refs))))

    arrays, specs = [], []
    for value in ins.values():
        array, spec = value if isinstance(value, tuple) else (value, VM)
        arrays.append(array)
        specs.append(spec if isinstance(spec, pl.BlockSpec) else pl.BlockSpec(memory_space=spec))
    results = pl.pallas_call(
        wrapped,
        grid=(1,),
        in_specs=specs,
        out_specs=[pl.BlockSpec(memory_space=(o[2] if len(o) > 2 else VM)) for o in outs.values()],
        out_shape=[jax.ShapeDtypeStruct(o[0], o[1]) for o in outs.values()],
        scratch_shapes=list(scratch.values()),
        compiler_params=pltpu.CompilerParams(
            vmem_limit_bytes=VMEM_LIMIT,
            collective_id=collective,
            has_side_effects=collective is not None,
        ),
        cost_estimate=pl.CostEstimate(flops=flops, bytes_accessed=20_000_000, transcendentals=0),
        name=name,
    )(*arrays)
    return types.SimpleNamespace(**dict(zip(outs, results)))


def dma(*shape):
    return pltpu.SemaphoreType.DMA(shape)


def body(comm, decoder_in, encoder_out, decoder_lengths, encoder_lengths, norm_gains, rel_table,
         query_self, key_self, value_self, out_self, query_cross, key_cross, value_cross, out_cross,
         feed_in, feed_out, upstream):
    rows, width = decoder_in.shape
    row_count, examples = decoder_lengths.shape
    keys_n = encoder_out.shape[1]
    hidden = feed_in.shape[1] * lax.axis_size("fsdp")
    small = (rows, width)
    cut = (4, 2, 2, PIECE, width)

    index = dict(lengths=decoder_lengths, valid=encoder_lengths[None, :])
    index_scratch = dict(index=VM((2, rows), jnp.int32), hidden=VM((examples, keys_n), F32))

    acts = dict(n1=(small, BF), q1=(small, BF), k1=((rows + MOST, width), BF), v1=((rows + MOST, width), BF),
                a1=(small, BF), h1=(small, F32), n2=(small, BF), q2=(small, BF), a2=(small, BF),
                k2=(encoder_out.shape, BF, HBM), v2=(encoder_out.shape, BF, HBM))
    scratch = dict(
        encv=VM(encoder_out.shape, BF), k2v=VM(encoder_out.shape, BF), v2v=VM(encoder_out.shape, BF),
        wv=VM((7,) + cut, BF), mask=VM((rows // MOST, MOST, 2 * MOST), F32),
        qe=VM((MOST, width), BF), ae=VM((MOST, width), BF), sum=VM(small, F32),
        esem=dma(examples), wsem=dma(7), ksem=dma(examples, 2), **index_scratch,
    )
    ins = dict(x=decoder_in, enc=(encoder_out, HBM), **index)
    if comm:
        ins |= dict(q_s=query_self, k_s=key_self, v_s=value_self, o_s=out_self, q_c=query_cross,
                    o_c=out_cross, k_c=key_cross, v_c=value_cross, f_i=feed_in, f_o=feed_out.T,
                    gains_s=norm_gains, table_s=rel_table)
        fwd = run(
            functools.partial(forward_kernel, True), ins,
            acts | dict(sq=((8,) + cut, BF, HBM), fi=((4, 2, 2, 4, PIECE, width), BF, HBM),
                        fo=((4, 2, 2, PIECE, hidden), BF, HBM), gains=((3, width), F32),
                        dist=((HEADS, 2 * MOST), F32)),
            scratch | dict(
                xt=VM((12, 2, PIECE, 192), BF), xf=VM((2, PIECE, 768), BF), took=VM((12, PIECE, 192), BF),
                tookf=VM((PIECE, 768), BF), own=VM((UNITS, PIECE, WIDE), BF), gt=VM((8, 8, 128), F32),
                tt=VM((4, 8, 128), F32), xsem=dma(6), psem=dma(UNITS), smsem=dma(2, 10),
                ssem=dma(UNITS, 14), rsem=dma(UNITS, 14)),
            "forward", collective=0,
        )
        sq, fi, fo, gains, dist = fwd.sq, fwd.fi, fwd.fo, fwd.gains, fwd.dist
    else:
        order = (key_cross, value_cross, query_self, key_self, value_self, out_self, query_cross, out_cross)
        sq = jnp.stack([m.astype(BF).T for m in order])
        sq = lax.all_gather(sq, "fsdp", axis=1, tiled=True)
        sq = lax.all_gather(sq, "dp", axis=2, tiled=True).reshape((8,) + cut)
        fi = lax.all_gather(feed_in.astype(BF).T, "fsdp", axis=0, tiled=True)
        fi = lax.all_gather(fi, "dp", axis=1, tiled=True)
        fo = lax.all_gather(feed_out.astype(BF).T, "fsdp", axis=0, tiled=True)
        fo = lax.all_gather(fo, "dp", axis=1, tiled=True)
        gains = lax.all_gather(norm_gains.astype(BF), "fsdp", axis=1, tiled=True).astype(F32)
        table = lax.all_gather(rel_table.astype(BF), "dp", axis=0, tiled=True).astype(F32)
        dist = jnp.dot(distance_hot(0), table, precision=lax.Precision.HIGHEST).T
        fwd = run(
            functools.partial(forward_kernel, False),
            ins | dict(sq=(sq, HBM), gains=gains, dist=dist), acts, scratch, "forward",
        )

    feed = run(
        feed_kernel,
        dict(a2=fwd.a2, h1=fwd.h1, c=upstream, gains=gains,
             w=(sq.reshape(8, width, width), pl.BlockSpec((1, width, width), lambda _: (7, 0, 0))),
             fi=fi.reshape(hidden, width), fo=fo.reshape(width, hidden)),
        dict(out=(small, BF), dfi=((hidden, width), BF), dfo=((4, 2, 2, PIECE, hidden), BF),
             dwoc=((width, width), BF), da2=(small, BF), dh2=(small, F32), gain=((1, width), F32)),
        dict(h2=VM(small, F32), n3=VM(small, BF), sum=VM(small, F32), back=VM(small, F32),
             ct=VM((width, rows), BF), g=VM(small, BF), du=VM(small, BF)),
        "feed",
    )

    ins = dict(k2=(fwd.k2, HBM), v2=(fwd.v2, HBM), q2=fwd.q2, da2=feed.da2,
               **index)
    turned = (examples, width, keys_n)
    outs = dict(dk2=(turned, BF, HBM), dv2=(turned, BF, HBM), dq2=(small, BF))
    scratch = dict(
        k2v=VM(encoder_out.shape, BF), v2v=VM(encoder_out.shape, BF),
        qe=VM((MOST, width), BF), dae=VM((MOST, width), BF), dqe=VM((MOST, width), BF),
        dk=VM((2, width, keys_n), BF), dv=VM((2, width, keys_n), BF),
        sum=VM(small, F32), esem=dma(examples, 2), dsem=dma(2, 2),
        **index_scratch,
    )
    fins = {}
    if comm:
        dfi = feed.dfi.reshape(4, 2, 2, 4, PIECE, width)
        ins |= dict(dfi=(dfi, HBM),
                    dfo=(feed.dfo, HBM))
        fins = dict(fin=((7, PIECE, WIDE), BF))
        scratch |= scatter_scratch(7, 7)
    mid = run(functools.partial(cross_back_kernel, comm), ins, outs | fins, scratch, "cross_back",
              collective=1 if comm else None)

    seven = (7,) + cut if comm else (7, width, width)
    ins = dict(dq2=mid.dq2, n2=fwd.n2, h1=fwd.h1, dh2=feed.dh2, x=decoder_in, n1=fwd.n1, q1=fwd.q1,
               k1=fwd.k1, v1=fwd.v1, a1=fwd.a1, gains=gains, dist=dist, gain3=feed.gain,
               sq=(sq, HBM), enc=(encoder_out, HBM), dk2=(mid.dk2, HBM), dv2=(mid.dv2, HBM), lengths=decoder_lengths)
    outs = dict(dx=(small, BF), small=((16, width), F32), denc=(encoder_out.shape, BF, HBM))
    scratch = dict(
        mask=VM((rows // MOST, MOST, 2 * MOST), F32), dh1=VM(small, F32), b1=VM(small, BF),
        da1=VM(small, BF), dq=VM(small, BF), dk=VM((width, rows), BF), dv=VM((width, rows), BF),
        dksum=VM((128, rows + MOST), F32), dvsum=VM((128, rows + MOST), F32), back=VM(small, F32),
        gain=VM((2, width), F32), distsum=VM((HEADS, 2 * MOST), F32), w=VM((5,) + cut, BF),
        one=VM((2, width, keys_n), BF), two=VM((2, keys_n, width), BF), three=VM((2, width, keys_n), BF),
        dwsum=VM((width, width), F32), denv=VM((2, keys_n, width), BF), wsem=dma(7), esem=dma(2, 2),
        dsem=dma(2),
    )
    if comm:
        ins |= dict(dfi=(dfi, HBM), dwoc=(feed.dwoc.reshape(cut), HBM), finf=mid.fin)
        outs |= dict(tsq=((8, 96, 192), BF), tfi=((384, 192), BF), tfo=((96, 768), BF), gains_own=((8, 128), F32),
                     table_own=((8, HEADS), F32))
        scratch |= dict(
            dw=VM(seven, BF), fin=VM((9, PIECE, WIDE), BF), all=VM((12, PIECE, WIDE), BF), give=VM((12, PIECE, 192), BF),
            take=VM((12, PIECE, 192), BF), giveo=VM((2, PIECE, WIDE), BF), takeo=VM((2, PIECE, WIDE), BF),
            given=VM((5, 16, width), F32), gotten=VM((5, 16, width), F32), smsem=dma(2, 5), xsem=dma(6),
        ) | scatter_scratch(9, 2)
    else:
        outs |= dict(dw=(seven, BF))
    last = run(functools.partial(self_back_kernel, comm), ins, outs, scratch, "self_back",
               collective=2 if comm else None)

    if comm:
        square = ((192, 96), F32)
        done = run(
            finish_kernel,
            dict(tsq=last.tsq, tfi=last.tfi, tfo=last.tfo, gains_in=last.gains_own, table_in=last.table_own,
                 dx_in=last.dx, denc_in=(last.denc, HBM)),
            {n: square for n in ("k_c", "v_c", "q_s", "k_s", "v_s", "o_s", "q_c", "o_c")}
            | dict(f_i=((192, 384), F32), f_o=((96, 768), F32), gains=((3, 96), F32), table=((8, HEADS), F32),
                   dx=(small, BF), denc=(encoder_out.shape, BF, HBM)),
            dict(sem=dma(examples, 2), hold=VM(encoder_out.shape, BF)), "finish",
        )
        grads = (done.q_s, done.k_s, done.v_s, done.o_s, done.q_c, done.k_c, done.v_c, done.o_c,
                 done.f_i, done.f_o.T)
        gains_delta, table_delta, dx, denc = done.gains, done.table, done.dx, done.denc
    else:
        def owned(t, rows_axis=0):
            t = lax.psum_scatter(t, "dp", scatter_dimension=1, tiled=True)
            return lax.psum_scatter(t, "fsdp", scatter_dimension=0, tiled=True).astype(F32).T

        dw = last.dw
        grads = tuple(owned(t) for t in (dw[2], dw[3], dw[4], dw[1], dw[0], dw[5], dw[6],
                                         feed.dwoc, feed.dfi, feed.dfo.reshape(width, hidden)))
        gains_delta = lax.psum(last.small[0:3], "dp")
        gains_delta = lax.psum_scatter(gains_delta, "fsdp", scatter_dimension=1, tiled=True)
        table_delta = last.small[3 : 3 + HEADS, 0:BUCKETS].T
        table_delta = lax.psum_scatter(table_delta, "dp", scatter_dimension=0, tiled=True)
        table_delta = lax.psum(table_delta, "fsdp")
        dx, denc = last.dx, last.denc
    return (feed.out, dx, denc, gains_delta, table_delta) + grads


def solution(mesh):
    tokens = P(("dp", "fsdp"), None)
    weight = P("dp", "fsdp")
    comm = (mesh.shape["dp"], mesh.shape["fsdp"]) == (4, 8)
    return jax.shard_map(
        functools.partial(body, comm),
        mesh=mesh,
        in_specs=(tokens, P(("dp", "fsdp"), None, None), tokens, P(("dp", "fsdp")), P(None, "fsdp"),
                  P("dp", None)) + (weight,) * 10 + (tokens,),
        out_specs=(tokens, tokens, P(("dp", "fsdp"), None, None), P(None, "fsdp"), P("dp", None))
        + (weight,) * 10,
        check_vma=False,
    )
```
